32 devices in a mesh: ctx: 4 (over z), chan: 8 (over y, x, core).
Axes of the slice: x: 2, y: 2, z: 4, core: 2. Of those that a mesh axis runs over, the one named last changes fastest.
Arguments:
- conv_input: bfloat16 [512, 16384], P('ctx', 'chan'), may hold values from -6 to 6
- gate_input: bfloat16 [512, 16384], P('ctx', 'chan'), may hold values from -6 to 6
- out_grad: bfloat16 [512, 16384], P('ctx', 'chan'), may hold values from -6 to 6
- conv_weight: float32 [4, 16384], P(None, 'chan'), may hold values from -3 to 3
- conv_bias: float32 [16384], P('chan'), may hold values from -3 to 3
- proj_weight: bfloat16 [544, 16384], P(None, 'chan'), may hold values from -0.046875 to 0.046875
- step_weight: bfloat16 [512, 16384], P(None, 'chan'), may hold values from -0.25 to 0.25
- step_bias: float32 [16384], P('chan'), may hold values from -12 to -3
- decay_log: float32 [16, 16384], P(None, 'chan'), may hold values from -0.7 to 1.4
- skip_gain: float32 [16384], P('chan'), may hold values from 0.1 to 1.9
Outputs:
- grad_input: bfloat16 [512, 16384], P('ctx', 'chan')
- grad_gate: bfloat16 [512, 16384], P('ctx', 'chan')
- grad_proj: float32 [512, 16384], P('ctx', 'chan')
- grad_coef: float32 [32, 16384], P('ctx', 'chan')
- grad_step: float32 [512, 16384], P('ctx', 'chan')
- grad_conv_weight: float32 [4, 16384], P(None, 'chan')
- grad_conv_bias: float32 [16384], P('chan')
- grad_step_bias: float32 [16384], P('chan')
- grad_decay_log: float32 [16, 16384], P(None, 'chan')
- grad_skip: float32 [16384], P('chan')
The draws below stay inside these ranges and needn't reach their ends.
All inputs are finite; a program needn't handle non-finite values.
Results may differ from the reference program's by a relative error of at most 0.023.
Values may be sent and summed in bfloat16 or wider, within the bound.
No kernel may reach another device: no remote copies, remote signals or barrier semaphores. Data moves between devices by JAX's collectives and lax.ppermute only.
A program may use at most 128 MiB of HBM per device.

```python
import jax
import jax.numpy as jnp
from jax import lax

DI = 16384
R = 512
N = 16
K = 4
PROJ = 544
TOKENS = 512
N_CHAN = 8


def block_scale(stream_key, dims, split, least, largest):
    loudness = 1.0
    for dim, shards_of in split:
        heights = jax.random.uniform(jax.random.fold_in(jax.random.fold_in(stream_key, 6), dim), (shards_of,), jnp.float32, least / len(split), largest / len(split))
        loudness = loudness * jnp.repeat(jnp.exp(heights), dims[dim] // shards_of).reshape((-1,) + (1,) * (len(dims) - 1 - dim))
    return loudness


def centred(own_key, shape, deviation, most, split=(), dtype=jnp.bfloat16):
    factor_of = block_scale(own_key, shape, split, -0.22, 0.18) if split else 1.0
    drawn = jax.random.normal(own_key, shape, jnp.float32) * deviation * factor_of
    return jnp.minimum(jnp.maximum(drawn, -most), most).astype(dtype)


def setup_inputs(seed: int = 0) -> dict:
    splits = jax.random.split(jax.random.key(seed), 11)
    return {
        "conv_input": centred(splits[0], (TOKENS, DI), 1.0, 6.0, ((0, 4), (1, 8))),
        "gate_input": centred(splits[1], (TOKENS, DI), 1.0, 6.0, ((0, 4), (1, 8))),
        "out_grad": centred(splits[2], (TOKENS, DI), 1.0, 6.0, ((0, 4), (1, 8))),
        "conv_weight": centred(splits[3], (K, DI), K ** -0.5, 3.0, ((1, 8),), jnp.float32),
        "conv_bias": centred(splits[4], (DI,), 0.5, 3.0, ((0, 8),), jnp.float32),
        "proj_weight": centred(splits[5], (PROJ, DI), DI ** -0.5, 0.046875, ((1, 8),)),
        "step_weight": centred(splits[6], (R, DI), R ** -0.5, 0.25, ((1, 8),)),
        "step_bias": jnp.clip(-12.0 + 9.0 * jax.random.uniform(splits[7], (DI,), jnp.float32) ** block_scale(splits[7], (DI,), ((0, 8),), -0.2, 0.2), -12.0, -3.0),
        "decay_log": jnp.clip(-0.7 + 2.1 * jax.random.uniform(splits[8], (N, DI), jnp.float32) ** block_scale(splits[8], (N, DI), ((1, 8),), -0.2, 0.2), -0.7, 1.4),
        "skip_gain": jnp.clip(1.0 + 0.18 * jax.random.normal(splits[9], (DI,), jnp.float32), 0.1, 1.9),
    }


def silu_slope(values):
    sigma = jax.nn.sigmoid(values)
    return sigma * (1.0 + values * (1.0 - sigma))


def split_columns(array, pieces):
    piece_width = array.shape[-1] // pieces
    reshaped = array.reshape(array.shape[:-1] + (pieces, piece_width))
    return jnp.moveaxis(reshaped, -2, 0)


def join_columns(stacked):
    moved = jnp.moveaxis(stacked, 0, -2)
    return moved.reshape(moved.shape[:-2] + (moved.shape[-2] * moved.shape[-1],))


def conv_preact(inputs, weight, bias):
    length = inputs.shape[0]
    padded = jnp.pad(inputs.astype(jnp.float32), ((K - 1, 0), (0, 0)))
    result = jnp.zeros(inputs.shape, jnp.float32) + bias[None, :]
    for tap in range(K):
        result = result + weight[tap][None, :] * padded[tap:tap + length]
    return result


def reference(conv_input, gate_input, out_grad, conv_weight, conv_bias, proj_weight, step_weight, step_bias, decay_log, skip_gain):
    pieces = N_CHAN
    in_cols = split_columns(conv_input, pieces)
    gate_cols = split_columns(gate_input, pieces)
    grad_cols = split_columns(out_grad, pieces)
    conv_w_cols = split_columns(conv_weight, pieces)
    conv_b_cols = split_columns(conv_bias, pieces)
    proj_cols = split_columns(proj_weight, pieces)
    step_cols = split_columns(step_weight, pieces)
    bias_cols = split_columns(step_bias, pieces)
    decay_cols = split_columns(decay_log, pieces)
    skip_cols = split_columns(skip_gain, pieces)

    def project_piece(total, packed):
        in_part, w_part, b_part, p_part = packed
        conv_out = jax.nn.silu(conv_preact(in_part, w_part, b_part)).astype(jnp.bfloat16)
        term = lax.dot_general(conv_out, p_part, (((1,), (1,)), ((), ())), preferred_element_type=jnp.float32)
        return total + term, None

    projected_sum, _ = lax.scan(project_piece, jnp.zeros((TOKENS, PROJ), jnp.float32), (in_cols, conv_w_cols, conv_b_cols, proj_cols))
    projected = projected_sum.astype(jnp.bfloat16)
    step_low = projected[:, :R]
    input_coef = projected[:, R:R + N].astype(jnp.float32)
    output_coef = projected[:, R + N:].astype(jnp.float32)

    def scan_piece(total, packed):
        in_part, gate_part, grad_part, w_part, b_part, s_part, bias_part, decay_part, skip_part = packed
        conv_out = jax.nn.silu(conv_preact(in_part, w_part, b_part)).astype(jnp.bfloat16)
        conv_val = lax.optimization_barrier(conv_out).astype(jnp.float32)
        step_pre = jnp.dot(step_low, s_part, preferred_element_type=jnp.float32) + bias_part[None, :]
        step_size = jax.nn.softplus(step_pre)
        decay_rate = -jnp.exp(decay_part)
        scan_grad = grad_part.astype(jnp.float32) * jax.nn.silu(gate_part.astype(jnp.float32))
        zero_state = jnp.zeros((N, decay_part.shape[1]), jnp.float32)

        def forward_step(state, entry):
            size_now, conv_now, coef_now = entry
            state = jnp.exp(size_now[None, :] * decay_rate) * state + (size_now * conv_now)[None, :] * coef_now[:, None]
            return state, state

        _, history = lax.scan(forward_step, zero_state, (step_size, conv_val, input_coef))

        def adjoint_step(carried, entry):
            size_now, coef_now, grad_now = entry
            adjoint_now = coef_now[:, None] * grad_now[None, :] + carried
            return jnp.exp(size_now[None, :] * decay_rate) * adjoint_now, adjoint_now

        _, adjoint = lax.scan(adjoint_step, zero_state, (step_size, output_coef, scan_grad), reverse=True)
        prior = jnp.concatenate([zero_state[None], history[:-1]], axis=0)
        decayed = jnp.exp(step_size[:, None, :] * decay_rate[None]) * prior
        scan_out = jnp.sum(output_coef[:, :, None] * history, axis=1) + skip_part[None, :] * conv_val
        d_delta = jnp.sum(adjoint * (decay_rate[None] * decayed + input_coef[:, :, None] * conv_val[:, None, :]), axis=1)
        decay_grad = jnp.sum(adjoint * decayed * step_size[:, None, :], axis=0) * decay_rate
        coef_in_grad = jnp.sum(adjoint * (step_size * conv_val)[:, None, :], axis=2)
        coef_out_grad = jnp.sum(history * scan_grad[:, None, :], axis=2)
        conv_grad_scan = jnp.sum(adjoint * input_coef[:, :, None], axis=1) * step_size + skip_part[None, :] * scan_grad
        skip_grad = jnp.sum(scan_grad * conv_val, axis=0)
        gate_grad = (grad_part.astype(jnp.float32) * scan_out * silu_slope(gate_part.astype(jnp.float32))).astype(jnp.bfloat16)
        d_pre = d_delta * jax.nn.sigmoid(step_pre)
        bias_grad = jnp.sum(d_pre, axis=0)
        pre_bf = d_pre.astype(jnp.bfloat16)
        d_low = lax.dot_general(pre_bf, s_part, (((1,), (1,)), ((), ())), preferred_element_type=jnp.float32)
        step_grad = lax.dot_general(step_low, pre_bf, (((0,), (0,)), ((), ())), preferred_element_type=jnp.float32)
        total = total + jnp.concatenate([d_low, coef_in_grad, coef_out_grad], axis=1)
        return total, (gate_grad, conv_grad_scan, step_grad, decay_grad, bias_grad, skip_grad)

    back_sum, stacks = lax.scan(scan_piece, jnp.zeros((TOKENS, PROJ), jnp.float32), (in_cols, gate_cols, grad_cols, conv_w_cols, conv_b_cols, step_cols, bias_cols, decay_cols, skip_cols))
    gate_stack, scan_stack, step_stack, decay_stack, bias_stack, skip_stack = stacks
    back_proj = back_sum.astype(jnp.bfloat16)

    def conv_piece(packed):
        in_part, w_part, b_part, p_part, scan_part = packed
        conv_pre = conv_preact(in_part, w_part, b_part)
        conv_out = jax.nn.silu(conv_pre).astype(jnp.bfloat16)
        d_xc = scan_part + jnp.dot(back_proj, p_part, preferred_element_type=jnp.float32)
        proj_grad = lax.dot_general(back_proj, conv_out, (((0,), (0,)), ((), ())), preferred_element_type=jnp.float32)
        d_conv = d_xc * silu_slope(conv_pre)
        length = d_conv.shape[0]
        padded_in = jnp.pad(in_part.astype(jnp.float32), ((K - 1, 0), (0, 0)))
        padded_grad = jnp.pad(d_conv, ((0, K - 1), (0, 0)))
        conv_w_grad = jnp.stack([jnp.sum(d_conv * padded_in[tap:tap + length], axis=0) for tap in range(K)])
        input_grad = jnp.zeros(d_conv.shape, jnp.float32)
        for tap in range(K):
            input_grad = input_grad + w_part[tap][None, :] * padded_grad[K - 1 - tap:K - 1 - tap + length]
        return input_grad.astype(jnp.bfloat16), proj_grad, conv_w_grad, jnp.sum(d_conv, axis=0)

    input_stack, proj_stack, conv_w_stack, conv_b_stack = lax.map(conv_piece, (in_cols, conv_w_cols, conv_b_cols, proj_cols, scan_stack))
    return (join_columns(input_stack), join_columns(gate_stack), join_columns(proj_stack[:, :R]), join_columns(proj_stack[:, R:]), join_columns(step_stack), join_columns(conv_w_stack), join_columns(conv_b_stack), join_columns(bias_stack), join_columns(decay_stack), join_columns(skip_stack))
```

```python
import functools

import jax
import jax.numpy as jnp
from jax import lax
from jax.experimental import pallas as pl
from jax.experimental.pallas import tpu as pltpu
from jax.sharding import PartitionSpec as P

BF = jnp.bfloat16
F32 = jnp.float32
LOG2E = 1.4426950408889634
LN2 = 0.6931471805599453
VMEM_BYTES = 56 * 1024 * 1024
NT = (((1,), (1,)), ((), ()))
TN = (((0,), (0,)), ((), ()))


def group_rows(chans):
    for rows in (8, 4, 2, 1):
        if chans % (rows * 128) == 0:
            return rows
    return 1


def dot(a, b, dims=(((1,), (0,)), ((), ()))):
    return lax.dot_general(a, b, dims, preferred_element_type=F32)


def params(**more):
    return pltpu.CompilerParams(vmem_limit_bytes=VMEM_BYTES, **more)


def sds(shape, dtype):
    return jax.ShapeDtypeStruct(shape, dtype)


def whole(shape):
    return pl.BlockSpec(shape, lambda i: (0,) * len(shape))


def columns(rows, width):
    return pl.BlockSpec((rows, width), lambda i: (0, i))


def sigmoid(v):
    return 1.0 / (1.0 + jnp.exp(-v))


def piece_start(peers, mask, size):
    return 0 if peers == 1 else (lax.axis_index("chan") ^ mask) * size


def swap(block, axis, mask):
    count = lax.axis_size(axis)
    return lax.ppermute(block, axis, [(i, i ^ mask) for i in range(count)])


def rotate(block, axis, distance):
    count = lax.axis_size(axis)
    return lax.ppermute(block, axis, [(i, (i + distance) % count) for i in range(count)])


def shift(block, axis, distance):
    count = lax.axis_size(axis)
    route = [(i, i + distance) for i in range(count) if 0 <= i + distance < count]
    return lax.ppermute(block, axis, route)


def fill_extended(ext, rim_ref, input_ref, taps):
    rows = input_ref.shape[0]
    ext[8 - (taps - 1) : 8, :] = rim_ref[...].astype(F32)
    ext[8 : 8 + rows, :] = input_ref[...].astype(F32)


def conv_block(ext, weight, bias, taps, start, rows):
    total = bias + jnp.zeros((rows, ext.shape[1]), F32)
    for tap in range(taps):
        first = 8 - (taps - 1) + tap + start
        total = total + weight[tap : tap + 1, :] * ext[first : first + rows, :]
    return total


def conv_kernel(peers, input_ref, rim_ref, weight_ref, bias_ref, proj_ref, out_ref, *rest):
    pieces, (ext, acc) = rest[:peers], rest[peers:]
    step = pl.program_id(0)
    taps = weight_ref.shape[0]
    rows = input_ref.shape[0]
    fill_extended(ext, rim_ref, input_ref, taps)
    for start in range(0, rows, 16):
        pre = conv_block(ext, weight_ref, bias_ref[...], taps, start, 16)
        out_ref[start : start + 16, :] = (pre * sigmoid(pre)).astype(BF)
    part = dot(out_ref[...], proj_ref[...], NT)

    @pl.when(step == 0)
    def _():
        acc[...] = part

    @pl.when(step > 0)
    def _():
        acc[...] += part

    @pl.when(step == pl.num_programs(0) - 1)
    def _():
        size = rows // peers
        for mask in range(peers):
            first = piece_start(peers, mask, size)
            pieces[mask][...] = acc[pl.ds(first, size), :].astype(BF)


def conv_call(peers, conv_input, rim, weight, bias, proj_weight):
    rows, chans = conv_input.shape
    taps = weight.shape[0]
    wide = proj_weight.shape[0]
    width = min(512, chans)
    return pl.pallas_call(
        functools.partial(conv_kernel, peers),
        grid=(chans // width,),
        in_specs=[
            columns(rows, width),
            columns(taps - 1, width),
            columns(taps, width),
            columns(1, width),
            columns(wide, width),
        ],
        out_specs=[columns(rows, width)] + [whole((rows // peers, wide))] * peers,
        out_shape=[sds((rows, chans), BF)] + [sds((rows // peers, wide), BF)] * peers,
        scratch_shapes=[pltpu.VMEM((rows + 8, width), F32), pltpu.VMEM((rows, wide), F32)],
        compiler_params=params(),
        name="conv_project",
    )(conv_input, rim, weight, bias, proj_weight)


def tile_rows(value, target, lead, groups):
    rows = value.shape[0]
    for block in range(rows // 8):
        for group in range(groups):
            first = (block * groups + group) * 8
            target[lead, first : first + 8, :] = value[
                block * 8 : block * 8 + 8, group * 128 : group * 128 + 128
            ]


def local_kernel(
    peers, low_rank, states, *refs
):
    parts, refs = refs[:peers], refs[peers:]
    (weight_ref, bias_ref, decay_ref, conv_ref, gate_ref, grad_ref) = refs[:6]
    (dt_ref, fwd_ref, bwd_ref, coef_ref, low) = refs[6:11]
    (proj, coef_v, coef, dts, dxs, gs, fwd, bwd, sem) = refs[11:]
    step = pl.program_id(0)
    chunks = dts.shape[0]
    rows = conv_ref.shape[0]
    groups = decay_ref.shape[2]

    @pl.when(step == 0)
    def _():
        size = rows // peers
        for mask in range(peers):
            proj[pl.ds(piece_start(peers, mask, size), size), :] = parts[mask][...].astype(F32)
        low[...] = proj[:, :low_rank].astype(BF)
        coef_v[...] = jnp.zeros_like(coef_v)
        coef_v[:, : 2 * states] = proj[:, low_rank:]
        coef_ref[...] = coef_v[...]
        copy = pltpu.make_async_copy(coef_v, coef, sem)
        copy.start()
        copy.wait()

    pre = dot(low[...], weight_ref[...]) + bias_ref[...]
    for start in range(0, rows, 16):
        here = slice(start, start + 16)
        p = pre[here, :]
        size = jnp.maximum(p, 0.0) + jnp.log1p(jnp.exp(-jnp.abs(p)))
        gate = gate_ref[here, :].astype(F32)
        grad = grad_ref[here, :].astype(F32) * gate * sigmoid(gate)
        drive = size * conv_ref[here, :].astype(F32)
        for half in range(2):
            for group in range(groups):
                first = ((start // 8 + half) * groups + group) * 8
                lanes = slice(group * 128, group * 128 + 128)
                subs = slice(half * 8, half * 8 + 8)
                dts[step, first : first + 8, :] = size[subs, lanes]
                dt_ref[0, first : first + 8, :] = size[subs, lanes]
                dxs[step, first : first + 8, :] = drive[subs, lanes]
                gs[step, first : first + 8, :] = grad[subs, lanes]

    @pl.when(step == chunks - 1)
    def _():
        batch = 4
        span = groups * 8
        zero = jnp.zeros((groups, 128), F32)
        for lead in range(0, states, batch):
            pairs = [(n, v) for n in range(lead, lead + batch) for v in range(chunks)]
            rates = [-LOG2E * jnp.exp(decay_ref[v, n]) for n, v in pairs]

            def block(index, carry):
                state, run, head, total = (list(part) for part in carry)
                for sub in range(8):
                    token = index * 8 + sub
                    at = pl.ds(index * span + sub, groups, stride=8)
                    size = [dts[v, at, :] for v in range(chunks)]
                    drive = [dxs[v, at, :] for v in range(chunks)]
                    grad = [gs[v, at, :] for v in range(chunks)]
                    if lead == 0:
                        total = [a + b for a, b in zip(total, size)]
                    for k, (n, v) in enumerate(pairs):
                        factor = jnp.exp2(size[v] * rates[k])
                        state[k] = factor * state[k] + drive[v] * coef[token, n]
                        run[k] = run[k] * factor
                        head[k] = head[k] + run[k] * (grad[v] * coef[token, states + n])
                return state, run, head, total

            many = [zero] * len(pairs)
            state, run, head, total = lax.fori_loop(
                0,
                rows // 8,
                block,
                (many, [zero + 1.0] * len(pairs), many, [zero] * chunks),
            )
            for k, (n, v) in enumerate(pairs):
                fwd[v, n] = state[k]
                bwd[v, n] = head[k]
            if lead == 0:
                for v in range(chunks):
                    coarse = total[v].astype(BF).astype(F32)
                    for target in (fwd, bwd):
                        target[v, states] = coarse
                        target[v, states + 1] = total[v] - coarse
        fwd_ref[...] = fwd[...].astype(BF)
        bwd_ref[...] = bwd[...].astype(BF)


def local_call(parts, step_weight, step_bias, decay, conv_out, gate, grad, states):
    peers = len(parts)
    rows, chans = conv_out.shape
    wide = parts[0].shape[1]
    low_rank = step_weight.shape[0]
    chunks, _, groups, _ = decay.shape
    width = groups * 128
    message = (chunks, states + 2, groups, 128)
    big = pltpu.VMEM((chunks, rows * groups, 128), F32)
    return pl.pallas_call(
        functools.partial(local_kernel, peers, low_rank, states),
        grid=(chunks,),
        in_specs=[whole((rows // peers, wide))] * peers
        + [
            columns(low_rank, width),
            columns(1, width),
            whole(decay.shape),
            columns(rows, width),
            columns(rows, width),
            columns(rows, width),
        ],
        out_specs=[
            pl.BlockSpec((1, rows * groups, 128), lambda i: (i, 0, 0)),
            whole(message),
            whole(message),
            whole((rows, 128)),
            whole((rows, low_rank)),
        ],
        out_shape=[
            sds((chunks, rows * groups, 128), F32),
            sds(message, BF),
            sds(message, BF),
            sds((rows, 128), F32),
            sds((rows, low_rank), BF),
        ],
        scratch_shapes=[
            pltpu.VMEM((rows, wide), F32),
            pltpu.VMEM((rows, 128), F32),
            pltpu.SMEM((rows, 128), F32),
            big,
            big,
            big,
            pltpu.VMEM(message, F32),
            pltpu.VMEM(message, F32),
            pltpu.SemaphoreType.DMA,
        ],
        compiler_params=params(),
        name="local_ends",
    )(*parts, step_weight, step_bias, decay, conv_out, gate, grad)


def fold_sublanes(values):
    rows = lax.broadcasted_iota(jnp.int32, (8, 128), 0)
    if values[0].shape[0] != 8:
        result = jnp.zeros((8, 128), F32)
        for i, value in enumerate(values):
            result = jnp.where(rows == i, jnp.sum(value, axis=0, keepdims=True), result)
        return result
    distance = 4
    while len(values) > 1:
        half = len(values) // 2
        low = (rows & distance) == 0
        values = [
            jnp.where(low, a, b) + pltpu.roll(jnp.where(low, b, a), distance, 0)
            if distance == 4
            else jnp.where(low, a, pltpu.roll(b, distance, 0))
            + jnp.where(low, pltpu.roll(a, 8 - distance, 0), b)
            for a, b in zip(values[:half], values[half:])
        ]
        distance //= 2
    return values[0]


def scan_kernel(peers, hops, states, *refs):
    (coef, low_ref, dt_ref, decay_ref, conv_ref, gate_ref, grad_ref, weight_ref, skip_ref) = refs[:9]
    befores, refs = refs[9 : 9 + hops], refs[9 + hops :]
    afters, refs = refs[:hops], refs[hops:]
    (pre_ref, gate_out, scan_out, small_ref, prod_ref) = refs[:5]
    pieces, refs = refs[5 : 5 + peers], refs[5 + peers :]
    (xs, dxs, gs, ys, dds, qs, decayed, coef_out, coef_in, rate, decay_acc, acc, small) = refs
    step = pl.program_id(0)
    rows = conv_ref.shape[0]
    groups = decay_ref.shape[2]
    low_rank = weight_ref.shape[0]
    span = groups * 8

    for start in range(0, rows, 16):
        here = slice(start, start + 16)
        conv = conv_ref[here, :].astype(F32)
        gate = gate_ref[here, :].astype(F32)
        grad = grad_ref[here, :].astype(F32) * gate * sigmoid(gate)
        for half in range(2):
            for group in range(groups):
                first = ((start // 8 + half) * groups + group) * 8
                lanes = slice(group * 128, group * 128 + 128)
                subs = slice(half * 8, half * 8 + 8)
                xs[first : first + 8, :] = conv[subs, lanes]
                dxs[first : first + 8, :] = conv[subs, lanes] * dt_ref[0, first : first + 8, :]
                gs[first : first + 8, :] = grad[subs, lanes]

    state, carry = [], []
    for n in range(states):
        rate[n] = -LOG2E * jnp.exp(decay_ref[0, n])
    for n in range(states):
        now = jnp.zeros((groups, 128), F32)
        for message in befores[::-1]:
            total = message[0, states].astype(F32) + message[0, states + 1].astype(F32)
            now = jnp.exp2(rate[n] * total) * now + message[0, n].astype(F32)
        state.append(now)
        now = jnp.zeros((groups, 128), F32)
        for message in afters[::-1]:
            total = message[0, states].astype(F32) + message[0, states + 1].astype(F32)
            now = jnp.exp2(rate[n] * total) * now + message[0, n].astype(F32)
        carry.append(now)

    def forward(index, state):
        state = list(state)
        for sub in range(8):
            token = index * 8 + sub
            at = pl.ds(index * span + sub, groups, stride=8)
            size, drive, grad = dt_ref[0, at, :], dxs[at, :], gs[at, :]
            result = jnp.zeros((groups, 128), F32)
            for lead in range(0, states, 8):
                products = []
                for n in range(lead, lead + 8):
                    kept = jnp.exp2(size * rate[n]) * state[n]
                    decayed[token, n] = kept
                    state[n] = kept + drive * coef[token, n]
                    result = result + state[n] * coef[token, states + n]
                    products.append(state[n] * grad)
                coef_out[pl.ds(pl.multiple_of(token * states + lead, 8), 8), :] = fold_sublanes(
                    products
                )
            ys[at, :] = result
        return state

    lax.fori_loop(0, rows // 8, forward, state)

    def backward(hop, both):
        carry, gathered = list(both[0]), list(both[1])
        index = rows // 8 - 1 - hop
        for sub in range(7, -1, -1):
            token = index * 8 + sub
            at = pl.ds(index * span + sub, groups, stride=8)
            size, drive, grad = dt_ref[0, at, :], dxs[at, :], gs[at, :]
            slope = jnp.zeros((groups, 128), F32)
            inner = jnp.zeros((groups, 128), F32)
            for lead in range(0, states, 8):
                products = []
                for n in range(lead, lead + 8):
                    adjoint = carry[n] + grad * coef[token, states + n]
                    carry[n] = jnp.exp2(size * rate[n]) * adjoint
                    weighted = adjoint * decayed[token, n]
                    slope = slope + weighted * rate[n]
                    gathered[n] = gathered[n] + weighted * size
                    inner = inner + adjoint * coef[token, n]
                    products.append(adjoint * drive)
                coef_in[pl.ds(pl.multiple_of(token * states + lead, 8), 8), :] = fold_sublanes(
                    products
                )
            dds[at, :] = slope
            qs[at, :] = inner
        return carry, gathered

    zeros = [jnp.zeros((groups, 128), F32)] * states
    _, gathered = lax.fori_loop(0, rows // 8, backward, (carry, zeros))
    for n in range(states):
        decay_acc[n * groups : n * groups + groups, :] = gathered[n] * (rate[n] * LN2)

    small[...] = jnp.zeros_like(small)
    for group in range(groups):
        small[:states, group * 128 : group * 128 + 128] = decay_acc[
            pl.ds(group, states, stride=groups), :
        ]
    skip = skip_ref[...]
    bias_sum = jnp.zeros((1, conv_ref.shape[1]), F32)
    skip_sum = jnp.zeros((1, conv_ref.shape[1]), F32)
    for start in range(0, rows, 16):
        here = slice(start, start + 16)

        def natural(read):
            return jnp.concatenate(
                [
                    jnp.concatenate(
                        [
                            read(((start // 8 + half) * groups + group) * 8)
                            for group in range(groups)
                        ],
                        axis=1,
                    )
                    for half in range(2)
                ],
                axis=0,
            )

        size = natural(lambda first: dt_ref[0, first : first + 8, :])
        inner = natural(lambda first: qs[first : first + 8, :])
        slope = natural(lambda first: dds[first : first + 8, :])
        out = natural(lambda first: ys[first : first + 8, :])
        conv = conv_ref[here, :].astype(F32)
        gate = gate_ref[here, :].astype(F32)
        grad = grad_ref[here, :].astype(F32)
        sig = sigmoid(gate)
        scan_grad = grad * gate * sig
        tiny = size * (1.0 - 0.5 * size * (1.0 - size * (1.0 / 3.0) * (1.0 - 0.25 * size)))
        step_slope = jnp.where(size < 0.03, tiny, 1.0 - jnp.exp(-size))
        d_pre = (LN2 * slope + conv * inner) * step_slope
        pre_ref[here, :] = d_pre.astype(BF)
        bias_sum = bias_sum + jnp.sum(d_pre, axis=0, keepdims=True)
        skip_sum = skip_sum + jnp.sum(scan_grad * conv, axis=0, keepdims=True)
        scan_out[here, :] = (size * inner + skip * scan_grad).astype(BF)
        gate_out[here, :] = (
            grad * (out + skip * conv) * (sig * (1.0 + gate * (1.0 - sig)))
        ).astype(BF)
    small[states : states + 1, :] = bias_sum
    small[states + 1 : states + 2, :] = skip_sum
    small_ref[...] = small[...].astype(BF)

    pre_bf = pre_ref[...]
    prod_ref[...] = dot(low_ref[...], pre_bf, TN).astype(BF)
    lanes = lax.broadcasted_iota(jnp.int32, (2 * states, 128), 0)
    coefs = jnp.zeros((2 * states, rows), F32)
    for n in range(states):
        at = pl.ds(n, rows, stride=states)
        for kind, source in enumerate((coef_in, coef_out)):
            pick = jnp.where(lanes == kind * states + n, 1.0, 0.0).astype(BF)
            coefs = coefs + dot(pick, source[at, :].astype(BF), NT)
    wide = dot(weight_ref[...], pre_bf, NT)

    @pl.when(step == 0)
    def _():
        acc[:low_rank, :] = wide
        acc[low_rank:, :] = coefs

    @pl.when(step > 0)
    def _():
        acc[:low_rank, :] += wide
        acc[low_rank:, :] += coefs

    @pl.when(step == pl.num_programs(0) - 1)
    def _():
        size = acc.shape[0] // peers
        for mask in range(peers):
            first = piece_start(peers, mask, size)
            pieces[mask][...] = acc[pl.ds(first, size), :].astype(BF)


def scan_call(
    peers, coef, low, dt, decay, conv_out, gate, grad, step_weight, skip, befores, afters
):
    rows, chans = conv_out.shape
    low_rank = step_weight.shape[0]
    chunks, states, groups, _ = decay.shape
    width = groups * 128
    hops = len(befores)
    wide = low_rank + 2 * states
    lead = lambda *shape: pl.BlockSpec((1,) + shape, lambda i: (i,) + (0,) * len(shape))
    tall = pltpu.VMEM((rows * groups, 128), F32)
    return pl.pallas_call(
        functools.partial(scan_kernel, peers, hops, states),
        grid=(chunks,),
        in_specs=[
            pl.BlockSpec(memory_space=pltpu.SMEM),
            whole((rows, low_rank)),
            lead(rows * groups, 128),
            lead(states, groups, 128),
            columns(rows, width),
            columns(rows, width),
            columns(rows, width),
            columns(low_rank, width),
            columns(1, width),
        ]
        + [lead(states + 2, groups, 128)] * (2 * hops),
        out_specs=[
            columns(rows, width),
            columns(rows, width),
            columns(rows, width),
            columns(32, width),
            columns(low_rank, width),
        ]
        + [whole((wide // peers, rows))] * peers,
        out_shape=[
            sds((rows, chans), BF),
            sds((rows, chans), BF),
            sds((rows, chans), BF),
            sds((32, chans), BF),
            sds((low_rank, chans), BF),
        ]
        + [sds((wide // peers, rows), BF)] * peers,
        scratch_shapes=[
            tall,
            tall,
            tall,
            tall,
            tall,
            tall,
            pltpu.VMEM((rows, states, groups, 128), F32),
            pltpu.VMEM((rows * states, 128), F32),
            pltpu.VMEM((rows * states, 128), F32),
            pltpu.VMEM((states, groups, 128), F32),
            pltpu.VMEM((states * groups, 128), F32),
            pltpu.VMEM((wide, rows), F32),
            pltpu.VMEM((32, width), F32),
        ],
        compiler_params=params(),
        name="scan_gradients",
    )(coef, low, dt, decay, conv_out, gate, grad, step_weight, skip, *befores, *afters)


def gather_kernel(peers, places, low_rank, *refs):
    parts, refs = refs[:peers], refs[peers:]
    whole_ref, cuts, full = refs[0], refs[1 : 1 + places], refs[1 + places]
    place = lax.axis_index("ctx")
    size = full.shape[0] // peers
    for mask in range(peers):
        full[pl.ds(piece_start(peers, mask, size), size), :] = parts[mask][...].astype(F32)
    whole_ref[...] = full[...].astype(BF)
    rank_rows = low_rank // places
    coef_rows = (full.shape[0] - low_rank) // places
    for hop in range(places):
        target = lax.rem(place + hop, places)
        cuts[hop][...] = jnp.concatenate(
            [
                full[pl.ds(target * rank_rows, rank_rows), :],
                full[pl.ds(low_rank + target * coef_rows, coef_rows), :],
            ],
            axis=0,
        ).astype(BF)


def gather_call(parts, places, low_rank):
    size, rows = parts[0].shape
    peers = len(parts)
    cut = (size * peers // places, rows)
    return pl.pallas_call(
        functools.partial(gather_kernel, peers, places, low_rank),
        out_shape=[sds((size * peers, rows), BF)] + [sds(cut, BF)] * places,
        scratch_shapes=[pltpu.VMEM((size * peers, rows), F32)],
        compiler_params=params(),
        name="gather_back",
    )(*parts)


def conv_grad_kernel(back_ref, proj_ref, scan_ref, input_ref, rim_ref, weight_ref, bias_ref,
                     out_ref, tail_ref, head_ref, small_ref, ext, grad):
    taps = weight_ref.shape[0]
    rows = input_ref.shape[0]
    fill_extended(ext, rim_ref, input_ref, taps)
    d_xc = dot(back_ref[...], proj_ref[...], TN)
    sums = [jnp.zeros((1, input_ref.shape[1]), F32) for _ in range(taps + 1)]
    for start in range(0, rows, 16):
        here = slice(start, start + 16)
        pre = conv_block(ext, weight_ref, bias_ref[...], taps, start, 16)
        sig = sigmoid(pre)
        value = (d_xc[here, :] + scan_ref[here, :].astype(F32)) * (sig * (1.0 + pre * (1.0 - sig)))
        grad[here, :] = value
        for tap in range(taps):
            first = 8 - (taps - 1) + tap + start
            sums[tap] = sums[tap] + jnp.sum(value * ext[first : first + 16, :], axis=0, keepdims=True)
        sums[taps] = sums[taps] + jnp.sum(value, axis=0, keepdims=True)
    grad[rows : rows + 8, :] = jnp.zeros((8, grad.shape[1]), F32)
    for start in range(0, rows, 16):
        total = jnp.zeros((16, grad.shape[1]), F32)
        for tap in range(taps):
            first = start + taps - 1 - tap
            total = total + weight_ref[tap : tap + 1, :] * grad[first : first + 16, :]
        out_ref[start : start + 16, :] = total.astype(BF)
    tail_ref[...] = total
    head_ref[...] = grad[0:8, :]
    small_ref[...] = jnp.concatenate(
        sums + [jnp.zeros((small_ref.shape[0] - taps - 1, small_ref.shape[1]), F32)], axis=0
    )


def conv_grad_call(back, proj_weight, scan_part, conv_input, rim, weight, bias):
    rows, chans = conv_input.shape
    taps = weight.shape[0]
    wide = proj_weight.shape[0]
    width = min(512, chans)
    return pl.pallas_call(
        conv_grad_kernel,
        grid=(chans // width,),
        in_specs=[
            whole((wide, rows)),
            columns(wide, width),
            columns(rows, width),
            columns(rows, width),
            columns(taps - 1, width),
            columns(taps, width),
            columns(1, width),
        ],
        out_specs=[columns(rows, width), columns(16, width), columns(8, width), columns(8, width)],
        out_shape=[
            sds((rows, chans), BF),
            sds((16, chans), F32),
            sds((8, chans), F32),
            sds((8, chans), F32),
        ],
        scratch_shapes=[pltpu.VMEM((rows + 8, width), F32), pltpu.VMEM((rows + 8, width), F32)],
        compiler_params=params(),
        name="conv_gradients",
    )(back, proj_weight, scan_part, conv_input, rim, weight, bias)


def rows_kernel(places, rank_rows, *refs):
    cuts, conv_ref, out_ref, coef_ref = refs[:places], refs[places], refs[places + 1], refs[places + 2]
    place = lax.axis_index("ctx")
    total = None
    for hop in range(places):
        source = lax.rem(place + places - hop, places)
        part = dot(cuts[hop][...], conv_ref[source])
        total = part if total is None else total + part
    out_ref[...] = total[:rank_rows, :]
    coef_ref[...] = total[rank_rows:, :]


def rows_call(cuts, conv_all, rank_rows):
    places, rows, chans = conv_all.shape
    cut = cuts[0].shape
    width = min(512, chans)
    return pl.pallas_call(
        functools.partial(rows_kernel, places, rank_rows),
        grid=(chans // width,),
        in_specs=[whole(cut)] * places
        + [pl.BlockSpec((places, rows, width), lambda i: (0, 0, i))],
        out_specs=[columns(rank_rows, width), columns(cut[0] - rank_rows, width)],
        out_shape=[sds((rank_rows, chans), F32), sds((cut[0] - rank_rows, chans), F32)],
        compiler_params=params(),
        name="row_gradients",
    )(*cuts, conv_all)


def last_kernel(places, states, taps, *refs):
    (main_ref, tail_ref, next_ref, weight_ref) = refs[:4]
    early, refs = refs[4 : 4 + places], refs[4 + places :]
    late, refs = refs[:places], refs[places:]
    (out_ref, conv_w, conv_b, step_b, decay, skip, fix) = refs
    fix[...] = tail_ref[...]
    for row in range(taps - 1):
        extra = jnp.zeros((1, fix.shape[1]), F32)
        for tap in range(row + 1):
            extra = extra + weight_ref[tap : tap + 1, :] * next_ref[row - tap : row - tap + 1, :]
        at = 16 - (taps - 1) + row
        fix[at : at + 1, :] += extra
    out_ref[...] = fix[...].astype(BF)
    total = early[0][...].astype(F32)
    for part in early[1:]:
        total = total + part[...].astype(F32)
    decay[...] = total[:states, :]
    step_b[...] = total[states : states + 1, :]
    skip[...] = total[states + 1 : states + 2, :]
    total = late[0][...]
    for part in late[1:]:
        total = total + part[...]
    conv_w[...] = total[:taps, :]
    conv_b[...] = total[taps : taps + 1, :]


def last_call(main, tail, following, weight, early, late, states):
    rows, chans = main.shape
    taps = weight.shape[0]
    places = len(early)
    width = chans
    return pl.pallas_call(
        functools.partial(last_kernel, places, states, taps),
        grid=(1,),
        in_specs=[pl.BlockSpec(memory_space=pl.ANY), columns(16, width), columns(8, width), columns(taps, width)]
        + [columns(32, width)] * places
        + [columns(8, width)] * places,
        out_specs=[
            pl.BlockSpec((16, width), lambda i: (rows // 16 - 1, i)),
            columns(taps, width),
            columns(1, width),
            columns(1, width),
            columns(states, width),
            columns(1, width),
        ],
        out_shape=[
            sds((rows, chans), BF),
            sds((taps, chans), F32),
            sds((1, chans), F32),
            sds((1, chans), F32),
            sds((states, chans), F32),
            sds((1, chans), F32),
        ],
        scratch_shapes=[pltpu.VMEM((16, width), F32)],
        input_output_aliases={0: 0},
        compiler_params=params(),
        name="last_rows",
    )(main, tail, following, weight, *early, *late)


def chan_sum(pieces):
    if len(pieces) == 1:
        return [lax.psum(pieces[0], "chan")]
    total = pieces[0].astype(F32)
    for mask in range(1, len(pieces)):
        total = total + swap(pieces[mask], "chan", mask).astype(F32)
    total = total.astype(BF)
    return [total] + [swap(total, "chan", mask) for mask in range(1, len(pieces))]


def body(
    conv_input,
    gate_input,
    out_grad,
    conv_weight,
    conv_bias,
    proj_weight,
    step_weight,
    step_bias,
    decay_log,
    skip_gain,
):
    rows, chans = conv_input.shape
    taps = conv_weight.shape[0]
    low_rank = step_weight.shape[0]
    states = decay_log.shape[0]
    peers = lax.axis_size("chan")
    if rows % (16 * peers) or peers & (peers - 1):
        peers = 1
    places = lax.axis_size("ctx")
    groups = group_rows(chans)
    decay = decay_log.reshape(states, -1, groups, 128).transpose(1, 0, 2, 3)
    conv_bias = conv_bias[None, :]
    step_bias = step_bias[None, :]
    skip_gain = skip_gain[None, :]

    rim = shift(conv_input[rows - (taps - 1) :], "ctx", 1)
    conv_out, *pieces = conv_call(peers, conv_input, rim, conv_weight, conv_bias, proj_weight)
    conv_all = lax.all_gather(conv_out, "ctx")
    parts = chan_sum(pieces)
    dt, fwd, bwd, coef, low = local_call(
        parts, step_weight, step_bias, decay, conv_out, gate_input, out_grad, states
    )
    befores = [shift(fwd, "ctx", hop) for hop in range(1, places)]
    afters = [shift(bwd, "ctx", -hop) for hop in range(1, places)]
    pre_bf, grad_gate, scan_part, small, products, *pieces = scan_call(
        peers, coef, low, dt, decay, conv_out, gate_input, out_grad, step_weight, skip_gain,
        befores, afters,
    )
    grad_step = lax.psum_scatter(products, "ctx", scatter_dimension=0, tiled=True).astype(F32)
    early = [small] + [rotate(small, "ctx", hop) for hop in range(1, places)]
    back, *cuts = gather_call(chan_sum(pieces), places, low_rank)
    cuts = [cuts[0]] + [rotate(cuts[hop], "ctx", hop) for hop in range(1, places)]
    main, tail, head, sums = conv_grad_call(
        back, proj_weight, scan_part, conv_input, rim, conv_weight, conv_bias
    )
    following = shift(head, "ctx", -1)
    late = [sums] + [rotate(sums, "ctx", hop) for hop in range(1, places)]
    grad_proj, grad_coef = rows_call(cuts, conv_all, low_rank // places)
    grad_input, conv_w, conv_b, step_b, decay_grad, skip = last_call(
        main, tail, following, conv_weight, early, late, states
    )
    return (
        grad_input,
        grad_gate,
        grad_proj,
        grad_coef,
        grad_step,
        conv_w,
        conv_b[0],
        step_b[0],
        decay_grad,
        skip[0],
    )


def solution(mesh):
    tokens, columns_, chan = P("ctx", "chan"), P(None, "chan"), P("chan")
    in_specs = (
        tokens, tokens, tokens, columns_, chan, columns_, columns_, chan, columns_, chan,
    )
    out_specs = (
        tokens, tokens, tokens, tokens, tokens, columns_, chan, chan, columns_, chan,
    )
    return jax.shard_map(body, mesh=mesh, in_specs=in_specs, out_specs=out_specs, check_vma=False)
```

```python
import functools

import jax
import jax.numpy as jnp
from jax import lax
from jax.experimental import pallas as pl
from jax.experimental.pallas import tpu as pltpu
from jax.sharding import PartitionSpec as P

BF = jnp.bfloat16
F32 = jnp.float32
LOG2E = 1.4426950408889634
LN2 = 0.6931471805599453
VMEM_BYTES = 56 * 1024 * 1024
NT = (((1,), (1,)), ((), ()))
TN = (((0,), (0,)), ((), ()))


def group_rows(chans):
    for rows in (8, 4, 2, 1):
        if chans % (rows * 128) == 0:
            return rows
    return 1


def dot(a, b, dims=(((1,), (0,)), ((), ()))):
    return lax.dot_general(a, b, dims, preferred_element_type=F32)


def params(**more):
    return pltpu.CompilerParams(vmem_limit_bytes=VMEM_BYTES, **more)


def sds(shape, dtype):
    return jax.ShapeDtypeStruct(shape, dtype)


def whole(shape):
    return pl.BlockSpec(shape, lambda i: (0,) * len(shape))


def columns(rows, width):
    return pl.BlockSpec((rows, width), lambda i: (0, i))


def sigmoid(v):
    return 1.0 / (1.0 + jnp.exp(-v))


def rotate(block, axis, distance):
    count = lax.axis_size(axis)
    return lax.ppermute(block, axis, [(i, (i + distance) % count) for i in range(count)])


def shift(block, axis, distance):
    count = lax.axis_size(axis)
    route = [(i, i + distance) for i in range(count) if 0 <= i + distance < count]
    return lax.ppermute(block, axis, route)


def fill_extended(ext, rim_ref, input_ref, taps):
    rows = input_ref.shape[0]
    ext[8 - (taps - 1) : 8, :] = rim_ref[...].astype(F32)
    ext[8 : 8 + rows, :] = input_ref[...].astype(F32)


def conv_block(ext, weight, bias, taps, start, rows):
    total = bias + jnp.zeros((rows, ext.shape[1]), F32)
    for tap in range(taps):
        first = 8 - (taps - 1) + tap + start
        total = total + weight[tap : tap + 1, :] * ext[first : first + rows, :]
    return total


def conv_kernel(input_ref, rim_ref, weight_ref, bias_ref, proj_ref, out_ref, part_ref, ext, acc):
    step = pl.program_id(0)
    taps = weight_ref.shape[0]
    rows = input_ref.shape[0]
    fill_extended(ext, rim_ref, input_ref, taps)
    for start in range(0, rows, 16):
        pre = conv_block(ext, weight_ref, bias_ref[...], taps, start, 16)
        out_ref[start : start + 16, :] = (pre * sigmoid(pre)).astype(BF)
    part = dot(out_ref[...], proj_ref[...], NT)

    @pl.when(step == 0)
    def _():
        acc[...] = part

    @pl.when(step > 0)
    def _():
        acc[...] += part

    @pl.when(step == pl.num_programs(0) - 1)
    def _():
        part_ref[...] = acc[...].astype(BF)


def conv_call(conv_input, rim, weight, bias, proj_weight):
    rows, chans = conv_input.shape
    taps = weight.shape[0]
    wide = proj_weight.shape[0]
    width = min(512, chans)
    return pl.pallas_call(
        conv_kernel,
        grid=(chans // width,),
        in_specs=[
            columns(rows, width),
            columns(taps - 1, width),
            columns(taps, width),
            columns(1, width),
            columns(wide, width),
        ],
        out_specs=[columns(rows, width), whole((rows, wide))],
        out_shape=[sds((rows, chans), BF), sds((rows, wide), BF)],
        scratch_shapes=[pltpu.VMEM((rows + 8, width), F32), pltpu.VMEM((rows, wide), F32)],
        compiler_params=params(),
        name="conv_project",
    )(conv_input, rim, weight, bias, proj_weight)


def tile_rows(value, target, lead, groups):
    rows = value.shape[0]
    for block in range(rows // 8):
        for group in range(groups):
            first = (block * groups + group) * 8
            target[lead, first : first + 8, :] = value[
                block * 8 : block * 8 + 8, group * 128 : group * 128 + 128
            ]


def local_kernel(low_rank, states, places, *refs):
    part_ref, refs = refs[0], refs[1:]
    (weight_ref, bias_ref, decay_ref, conv_ref, gate_ref, grad_ref) = refs[:6]
    (dt_ref, ends_ref, coef_ref, low) = refs[6:10]
    (proj, coef_v, coef, dts, dxs, gs, fwd, bwd, sem) = refs[10:]
    step = pl.program_id(0)
    chunks = dts.shape[0]
    rows = conv_ref.shape[0]
    groups = decay_ref.shape[2]

    @pl.when(step == 0)
    def _():
        proj[...] = part_ref[...].astype(F32)
        low[...] = part_ref[:, :low_rank]
        coef_v[...] = jnp.zeros_like(coef_v)
        coef_v[:, : 2 * states] = proj[:, low_rank:]
        coef_ref[...] = coef_v[...]
        copy = pltpu.make_async_copy(coef_v, coef, sem)
        copy.start()
        copy.wait()

    pre = dot(low[...], weight_ref[...]) + bias_ref[...]
    for start in range(0, rows, 16):
        here = slice(start, start + 16)
        p = pre[here, :]
        size = jnp.maximum(p, 0.0) + jnp.log1p(jnp.exp(-jnp.abs(p)))
        gate = gate_ref[here, :].astype(F32)
        grad = grad_ref[here, :].astype(F32) * gate * sigmoid(gate)
        drive = size * conv_ref[here, :].astype(F32)
        for half in range(2):
            for group in range(groups):
                first = ((start // 8 + half) * groups + group) * 8
                lanes = slice(group * 128, group * 128 + 128)
                subs = slice(half * 8, half * 8 + 8)
                dts[step, first : first + 8, :] = size[subs, lanes]
                dt_ref[0, first : first + 8, :] = size[subs, lanes]
                dxs[step, first : first + 8, :] = drive[subs, lanes]
                gs[step, first : first + 8, :] = grad[subs, lanes]

    @pl.when(step == chunks - 1)
    def _():
        batch = 4
        span = groups * 8
        zero = jnp.zeros((groups, 128), F32)
        for lead in range(0, states, batch):
            pairs = [(n, v) for n in range(lead, lead + batch) for v in range(chunks)]
            rates = [-LOG2E * jnp.exp(decay_ref[v, n]) for n, v in pairs]

            def block(index, carry):
                state, run, head, total = (list(part) for part in carry)
                for sub in range(8):
                    token = index * 8 + sub
                    at = pl.ds(index * span + sub, groups, stride=8)
                    size = [dts[v, at, :] for v in range(chunks)]
                    drive = [dxs[v, at, :] for v in range(chunks)]
                    grad = [gs[v, at, :] for v in range(chunks)]
                    if lead == 0:
                        total = [a + b for a, b in zip(total, size)]
                    for k, (n, v) in enumerate(pairs):
                        factor = jnp.exp2(size[v] * rates[k])
                        state[k] = factor * state[k] + drive[v] * coef[token, n]
                        run[k] = run[k] * factor
                        head[k] = head[k] + run[k] * (grad[v] * coef[token, states + n])
                return state, run, head, total

            many = [zero] * len(pairs)
            state, run, head, total = lax.fori_loop(
                0,
                rows // 8,
                block,
                (many, [zero + 1.0] * len(pairs), many, [zero] * chunks),
            )
            for k, (n, v) in enumerate(pairs):
                fwd[v, n] = state[k]
                bwd[v, n] = head[k]
            if lead == 0:
                for v in range(chunks):
                    coarse = total[v].astype(BF).astype(F32)
                    for target in (fwd, bwd):
                        target[v, states] = coarse
                        target[v, states + 1] = total[v] - coarse
        place = lax.axis_index("ctx")
        for other in range(places):
            ends_ref[other] = jnp.where(other > place, fwd[...], bwd[...]).astype(BF)


def local_call(part, step_weight, step_bias, decay, conv_out, gate, grad, states, places):
    rows, chans = conv_out.shape
    wide = part.shape[1]
    low_rank = step_weight.shape[0]
    chunks, _, groups, _ = decay.shape
    width = groups * 128
    message = (chunks, states + 2, groups, 128)
    big = pltpu.VMEM((chunks, rows * groups, 128), F32)
    return pl.pallas_call(
        functools.partial(local_kernel, low_rank, states, places),
        grid=(chunks,),
        in_specs=[
            whole((rows, wide)),
            columns(low_rank, width),
            columns(1, width),
            whole(decay.shape),
            columns(rows, width),
            columns(rows, width),
            columns(rows, width),
        ],
        out_specs=[
            pl.BlockSpec((1, rows * groups, 128), lambda i: (i, 0, 0)),
            whole((places,) + message),
            whole((rows, 128)),
            whole((rows, low_rank)),
        ],
        out_shape=[
            sds((chunks, rows * groups, 128), F32),
            sds((places,) + message, BF),
            sds((rows, 128), F32),
            sds((rows, low_rank), BF),
        ],
        scratch_shapes=[
            pltpu.VMEM((rows, wide), F32),
            pltpu.VMEM((rows, 128), F32),
            pltpu.SMEM((rows, 128), F32),
            big,
            big,
            big,
            pltpu.VMEM(message, F32),
            pltpu.VMEM(message, F32),
            pltpu.SemaphoreType.DMA,
        ],
        compiler_params=params(),
        name="local_ends",
    )(part, step_weight, step_bias, decay, conv_out, gate, grad)


def fold_sublanes(values):
    rows = lax.broadcasted_iota(jnp.int32, (8, 128), 0)
    if values[0].shape[0] != 8:
        result = jnp.zeros((8, 128), F32)
        for i, value in enumerate(values):
            result = jnp.where(rows == i, jnp.sum(value, axis=0, keepdims=True), result)
        return result
    distance = 4
    while len(values) > 1:
        half = len(values) // 2
        low = (rows & distance) == 0
        values = [
            jnp.where(low, a, b) + pltpu.roll(jnp.where(low, b, a), distance, 0)
            if distance == 4
            else jnp.where(low, a, pltpu.roll(b, distance, 0))
            + jnp.where(low, pltpu.roll(a, 8 - distance, 0), b)
            for a, b in zip(values[:half], values[half:])
        ]
        distance //= 2
    return values[0]


def scan_kernel(places, states, *refs):
    (coef, low_ref, dt_ref, decay_ref, conv_ref, gate_ref, grad_ref, weight_ref, skip_ref) = refs[:9]
    ends, refs = refs[9], refs[10:]
    (pre_ref, gate_out, scan_out, small_ref, prod_ref, part_ref) = refs[:6]
    refs = refs[6:]
    (xs, dxs, gs, ys, dds, qs, decayed, coef_out, coef_in, rate, decay_acc, acc, small) = refs
    step = pl.program_id(0)
    rows = conv_ref.shape[0]
    groups = decay_ref.shape[2]
    low_rank = weight_ref.shape[0]
    span = groups * 8

    for start in range(0, rows, 16):
        here = slice(start, start + 16)
        conv = conv_ref[here, :].astype(F32)
        gate = gate_ref[here, :].astype(F32)
        grad = grad_ref[here, :].astype(F32) * gate * sigmoid(gate)
        for half in range(2):
            for group in range(groups):
                first = ((start // 8 + half) * groups + group) * 8
                lanes = slice(group * 128, group * 128 + 128)
                subs = slice(half * 8, half * 8 + 8)
                xs[first : first + 8, :] = conv[subs, lanes]
                dxs[first : first + 8, :] = conv[subs, lanes] * dt_ref[0, first : first + 8, :]
                gs[first : first + 8, :] = grad[subs, lanes]

    place = lax.axis_index("ctx")
    for n in range(states):
        rate[n] = -LOG2E * jnp.exp(decay_ref[0, n])
    totals = [
        ends[q, 0, states].astype(F32) + ends[q, 0, states + 1].astype(F32) for q in range(places)
    ]
    state, carry = [], []
    for n in range(states):
        before = jnp.zeros((groups, 128), F32)
        after = jnp.zeros((groups, 128), F32)
        for q in range(places - 1):
            reached = jnp.exp2(rate[n] * totals[q]) * before + ends[q, 0, n].astype(F32)
            before = jnp.where(q < place, reached, before)
        for q in range(places - 1, 0, -1):
            reached = jnp.exp2(rate[n] * totals[q]) * after + ends[q, 0, n].astype(F32)
            after = jnp.where(q > place, reached, after)
        state.append(before)
        carry.append(after)

    def forward(index, state):
        state = list(state)
        for sub in range(8):
            token = index * 8 + sub
            at = pl.ds(index * span + sub, groups, stride=8)
            size, drive, grad = dt_ref[0, at, :], dxs[at, :], gs[at, :]
            result = jnp.zeros((groups, 128), F32)
            for lead in range(0, states, 8):
                products = []
                for n in range(lead, lead + 8):
                    kept = jnp.exp2(size * rate[n]) * state[n]
                    decayed[token, n] = kept
                    state[n] = kept + drive * coef[token, n]
                    result = result + state[n] * coef[token, states + n]
                    products.append(state[n] * grad)
                coef_out[pl.ds(pl.multiple_of(token * states + lead, 8), 8), :] = fold_sublanes(
                    products
                )
            ys[at, :] = result
        return state

    lax.fori_loop(0, rows // 8, forward, state)

    def backward(hop, both):
        carry, gathered = list(both[0]), list(both[1])
        index = rows // 8 - 1 - hop
        for sub in range(7, -1, -1):
            token = index * 8 + sub
            at = pl.ds(index * span + sub, groups, stride=8)
            size, drive, grad = dt_ref[0, at, :], dxs[at, :], gs[at, :]
            slope = jnp.zeros((groups, 128), F32)
            inner = jnp.zeros((groups, 128), F32)
            for lead in range(0, states, 8):
                products = []
                for n in range(lead, lead + 8):
                    adjoint = carry[n] + grad * coef[token, states + n]
                    carry[n] = jnp.exp2(size * rate[n]) * adjoint
                    weighted = adjoint * decayed[token, n]
                    slope = slope + weighted * rate[n]
                    gathered[n] = gathered[n] + weighted * size
                    inner = inner + adjoint * coef[token, n]
                    products.append(adjoint * drive)
                coef_in[pl.ds(pl.multiple_of(token * states + lead, 8), 8), :] = fold_sublanes(
                    products
                )
            dds[at, :] = slope
            qs[at, :] = inner
        return carry, gathered

    zeros = [jnp.zeros((groups, 128), F32)] * states
    _, gathered = lax.fori_loop(0, rows // 8, backward, (carry, zeros))
    for n in range(states):
        decay_acc[n * groups : n * groups + groups, :] = gathered[n] * (rate[n] * LN2)

    small[...] = jnp.zeros_like(small)
    for group in range(groups):
        small[:states, group * 128 : group * 128 + 128] = decay_acc[
            pl.ds(group, states, stride=groups), :
        ]
    skip = skip_ref[...]
    bias_sum = jnp.zeros((1, conv_ref.shape[1]), F32)
    skip_sum = jnp.zeros((1, conv_ref.shape[1]), F32)
    for start in range(0, rows, 16):
        here = slice(start, start + 16)

        def natural(read):
            return jnp.concatenate(
                [
                    jnp.concatenate(
                        [
                            read(((start // 8 + half) * groups + group) * 8)
                            for group in range(groups)
                        ],
                        axis=1,
                    )
                    for half in range(2)
                ],
                axis=0,
            )

        size = natural(lambda first: dt_ref[0, first : first + 8, :])
        inner = natural(lambda first: qs[first : first + 8, :])
        slope = natural(lambda first: dds[first : first + 8, :])
        out = natural(lambda first: ys[first : first + 8, :])
        conv = conv_ref[here, :].astype(F32)
        gate = gate_ref[here, :].astype(F32)
        grad = grad_ref[here, :].astype(F32)
        sig = sigmoid(gate)
        scan_grad = grad * gate * sig
        tiny = size * (1.0 - 0.5 * size * (1.0 - size * (1.0 / 3.0) * (1.0 - 0.25 * size)))
        step_slope = jnp.where(size < 0.03, tiny, 1.0 - jnp.exp(-size))
        d_pre = (LN2 * slope + conv * inner) * step_slope
        pre_ref[here, :] = d_pre.astype(BF)
        bias_sum = bias_sum + jnp.sum(d_pre, axis=0, keepdims=True)
        skip_sum = skip_sum + jnp.sum(scan_grad * conv, axis=0, keepdims=True)
        scan_out[here, :] = (size * inner + skip * scan_grad).astype(BF)
        gate_out[here, :] = (
            grad * (out + skip * conv) * (sig * (1.0 + gate * (1.0 - sig)))
        ).astype(BF)
    small[states : states + 1, :] = bias_sum
    small[states + 1 : states + 2, :] = skip_sum
    small_ref[...] = small[...].astype(BF)

    pre_bf = pre_ref[...]
    prod_ref[...] = dot(low_ref[...], pre_bf, TN).astype(BF)
    lanes = lax.broadcasted_iota(jnp.int32, (2 * states, 128), 0)
    coefs = jnp.zeros((2 * states, rows), F32)
    for n in range(states):
        at = pl.ds(n, rows, stride=states)
        for kind, source in enumerate((coef_in, coef_out)):
            pick = jnp.where(lanes == kind * states + n, 1.0, 0.0).astype(BF)
            coefs = coefs + dot(pick, source[at, :].astype(BF), NT)
    wide = dot(weight_ref[...], pre_bf, NT)

    ranks, coef_rows, block = low_rank // places, 2 * states // places, acc.shape[0] // places

    @pl.when(step == 0)
    def _():
        acc[...] = jnp.zeros_like(acc)

    for q in range(places):
        first = q * block
        acc[first : first + ranks, :] += wide[q * ranks : (q + 1) * ranks, :]
        acc[first + ranks : first + ranks + coef_rows, :] += coefs[
            q * coef_rows : (q + 1) * coef_rows, :
        ]

    @pl.when(step == pl.num_programs(0) - 1)
    def _():
        part_ref[...] = acc[...].astype(BF)


def padded(wide):
    return (wide + 127) // 128 * 128


def scan_call(places, coef, low, dt, decay, conv_out, gate, grad, step_weight, skip, ends):
    rows, chans = conv_out.shape
    low_rank = step_weight.shape[0]
    chunks, states, groups, _ = decay.shape
    width = groups * 128
    wide = padded(low_rank + 2 * states)
    lead = lambda *shape: pl.BlockSpec((1,) + shape, lambda i: (i,) + (0,) * len(shape))
    tall = pltpu.VMEM((rows * groups, 128), F32)
    return pl.pallas_call(
        functools.partial(scan_kernel, places, states),
        grid=(chunks,),
        in_specs=[
            pl.BlockSpec(memory_space=pltpu.SMEM),
            whole((rows, low_rank)),
            lead(rows * groups, 128),
            lead(states, groups, 128),
            columns(rows, width),
            columns(rows, width),
            columns(rows, width),
            columns(low_rank, width),
            columns(1, width),
            pl.BlockSpec((places, 1, states + 2, groups, 128), lambda i: (0, i, 0, 0, 0)),
        ],
        out_specs=[
            columns(rows, width),
            columns(rows, width),
            columns(rows, width),
            columns(32, width),
            columns(low_rank, width),
            whole((wide, rows)),
        ],
        out_shape=[
            sds((rows, chans), BF),
            sds((rows, chans), BF),
            sds((rows, chans), BF),
            sds((32, chans), BF),
            sds((low_rank, chans), BF),
            sds((wide, rows), BF),
        ],
        scratch_shapes=[
            tall,
            tall,
            tall,
            tall,
            tall,
            tall,
            pltpu.VMEM((rows, states, groups, 128), F32),
            pltpu.VMEM((rows * states, 128), F32),
            pltpu.VMEM((rows * states, 128), F32),
            pltpu.VMEM((states, groups, 128), F32),
            pltpu.VMEM((states * groups, 128), F32),
            pltpu.VMEM((wide, rows), F32),
            pltpu.VMEM((32, width), F32),
        ],
        compiler_params=params(),
        name="scan_gradients",
    )(coef, low, dt, decay, conv_out, gate, grad, step_weight, skip, ends)


def conv_grad_kernel(places, low_rank, back_ref, proj_ref, scan_ref, input_ref, rim_ref, weight_ref, bias_ref,
                     out_ref, tail_ref, head_ref, small_ref, ext, grad):
    taps = weight_ref.shape[0]
    rows = input_ref.shape[0]
    fill_extended(ext, rim_ref, input_ref, taps)
    wide = proj_ref.shape[0]
    block = back_ref.shape[0] // places
    ranks, coef_rows = low_rank // places, (wide - low_rank) // places
    back = back_ref[...].astype(F32)
    order = [back[q * block : q * block + ranks, :] for q in range(places)]
    order += [back[q * block + ranks : q * block + ranks + coef_rows, :] for q in range(places)]
    d_xc = dot(jnp.concatenate(order, axis=0).astype(BF), proj_ref[...], TN)
    sums = [jnp.zeros((1, input_ref.shape[1]), F32) for _ in range(taps + 1)]
    for start in range(0, rows, 16):
        here = slice(start, start + 16)
        pre = conv_block(ext, weight_ref, bias_ref[...], taps, start, 16)
        sig = sigmoid(pre)
        value = (d_xc[here, :] + scan_ref[here, :].astype(F32)) * (sig * (1.0 + pre * (1.0 - sig)))
        grad[here, :] = value
        for tap in range(taps):
            first = 8 - (taps - 1) + tap + start
            sums[tap] = sums[tap] + jnp.sum(value * ext[first : first + 16, :], axis=0, keepdims=True)
        sums[taps] = sums[taps] + jnp.sum(value, axis=0, keepdims=True)
    grad[rows : rows + 8, :] = jnp.zeros((8, grad.shape[1]), F32)
    for start in range(0, rows, 16):
        total = jnp.zeros((16, grad.shape[1]), F32)
        for tap in range(taps):
            first = start + taps - 1 - tap
            total = total + weight_ref[tap : tap + 1, :] * grad[first : first + 16, :]
        out_ref[start : start + 16, :] = total.astype(BF)
    tail_ref[...] = total
    head_ref[...] = grad[0:8, :]
    small_ref[...] = jnp.concatenate(
        sums + [jnp.zeros((small_ref.shape[0] - taps - 1, small_ref.shape[1]), F32)], axis=0
    )


def conv_grad_call(places, low_rank, back, proj_weight, scan_part, conv_input, rim, weight, bias):
    rows, chans = conv_input.shape
    taps = weight.shape[0]
    wide = proj_weight.shape[0]
    width = min(512, chans)
    return pl.pallas_call(
        functools.partial(conv_grad_kernel, places, low_rank),
        grid=(chans // width,),
        in_specs=[
            whole(back.shape),
            columns(wide, width),
            columns(rows, width),
            columns(rows, width),
            columns(taps - 1, width),
            columns(taps, width),
            columns(1, width),
        ],
        out_specs=[columns(rows, width), columns(16, width), columns(8, width), columns(8, width)],
        out_shape=[
            sds((rows, chans), BF),
            sds((16, chans), F32),
            sds((8, chans), F32),
            sds((8, chans), F32),
        ],
        scratch_shapes=[pltpu.VMEM((rows + 8, width), F32), pltpu.VMEM((rows + 8, width), F32)],
        compiler_params=params(),
        name="conv_gradients",
    )(back, proj_weight, scan_part, conv_input, rim, weight, bias)


def rows_kernel(rank_rows, cut_ref, conv_ref, step_ref, out_ref, coef_ref, step_out):
    places = conv_ref.shape[0]
    block = cut_ref.shape[0] // places
    total = None
    for q in range(places):
        part = dot(cut_ref[q * block : (q + 1) * block, :], conv_ref[q])
        total = part if total is None else total + part
    out_ref[...] = total[:rank_rows, :]
    coef_ref[...] = total[rank_rows : rank_rows + coef_ref.shape[0], :]
    step_out[...] = step_ref[...].astype(F32)


def rows_call(cuts, conv_all, steps, coef_rows):
    places, rows, chans = conv_all.shape
    rank_rows = steps.shape[0]
    width = min(512, chans)
    return pl.pallas_call(
        functools.partial(rows_kernel, rank_rows),
        grid=(chans // width,),
        in_specs=[
            whole(cuts.shape),
            pl.BlockSpec((places, rows, width), lambda i: (0, 0, i)),
            columns(rank_rows, width),
        ],
        out_specs=[
            columns(rank_rows, width), columns(coef_rows, width), columns(rank_rows, width)
        ],
        out_shape=[
            sds((rank_rows, chans), F32), sds((coef_rows, chans), F32), sds((rank_rows, chans), F32)
        ],
        compiler_params=params(),
        name="row_gradients",
    )(cuts, conv_all, steps)


def last_kernel(places, states, taps, *refs):
    (main_ref, tail_ref, next_ref, weight_ref) = refs[:4]
    early, refs = refs[4 : 4 + places], refs[4 + places :]
    late, refs = refs[:places], refs[places:]
    (out_ref, conv_w, conv_b, step_b, decay, skip, fix) = refs
    fix[...] = tail_ref[...]
    for row in range(taps - 1):
        extra = jnp.zeros((1, fix.shape[1]), F32)
        for tap in range(row + 1):
            extra = extra + weight_ref[tap : tap + 1, :] * next_ref[row - tap : row - tap + 1, :]
        at = 16 - (taps - 1) + row
        fix[at : at + 1, :] += extra
    out_ref[...] = fix[...].astype(BF)
    total = early[0][...].astype(F32)
    for part in early[1:]:
        total = total + part[...].astype(F32)
    decay[...] = total[:states, :]
    step_b[...] = total[states : states + 1, :]
    skip[...] = total[states + 1 : states + 2, :]
    total = late[0][...]
    for part in late[1:]:
        total = total + part[...]
    conv_w[...] = total[:taps, :]
    conv_b[...] = total[taps : taps + 1, :]


def last_call(main, tail, following, weight, early, late, states):
    rows, chans = main.shape
    taps = weight.shape[0]
    places = len(early)
    width = chans
    return pl.pallas_call(
        functools.partial(last_kernel, places, states, taps),
        grid=(1,),
        in_specs=[pl.BlockSpec(memory_space=pl.ANY), columns(16, width), columns(8, width), columns(taps, width)]
        + [columns(32, width)] * places
        + [columns(8, width)] * places,
        out_specs=[
            pl.BlockSpec((16, width), lambda i: (rows // 16 - 1, i)),
            columns(taps, width),
            columns(1, width),
            columns(1, width),
            columns(states, width),
            columns(1, width),
        ],
        out_shape=[
            sds((rows, chans), BF),
            sds((taps, chans), F32),
            sds((1, chans), F32),
            sds((1, chans), F32),
            sds((states, chans), F32),
            sds((1, chans), F32),
        ],
        scratch_shapes=[pltpu.VMEM((16, width), F32)],
        input_output_aliases={0: 0},
        compiler_params=params(),
        name="last_rows",
    )(main, tail, following, weight, *early, *late)


def exchange(block, axis):
    return lax.all_to_all(block, axis, split_axis=0, concat_axis=0, tiled=True)


def chan_sum(part):
    peers = lax.axis_size("chan")
    pieces = exchange(part, "chan").reshape((peers, part.shape[0] // peers, part.shape[1]))
    total = jnp.sum(pieces.astype(F32), axis=0, keepdims=True).astype(BF)
    return exchange(jnp.broadcast_to(total, pieces.shape).reshape(part.shape), "chan")


def body(
    conv_input,
    gate_input,
    out_grad,
    conv_weight,
    conv_bias,
    proj_weight,
    step_weight,
    step_bias,
    decay_log,
    skip_gain,
):
    rows, chans = conv_input.shape
    taps = conv_weight.shape[0]
    low_rank = step_weight.shape[0]
    states = decay_log.shape[0]
    places = lax.axis_size("ctx")
    groups = group_rows(chans)
    decay = decay_log.reshape(states, -1, groups, 128).transpose(1, 0, 2, 3)
    conv_bias = conv_bias[None, :]
    step_bias = step_bias[None, :]
    skip_gain = skip_gain[None, :]

    rim = shift(conv_input[rows - (taps - 1) :], "ctx", 1)
    conv_out, part = conv_call(conv_input, rim, conv_weight, conv_bias, proj_weight)
    conv_all = lax.all_gather(conv_out, "ctx")
    dt, ends, coef, low = local_call(
        chan_sum(part), step_weight, step_bias, decay, conv_out, gate_input, out_grad, states, places
    )
    ends = exchange(ends, "ctx")
    pre_bf, grad_gate, scan_part, small, products, part = scan_call(
        places, coef, low, dt, decay, conv_out, gate_input, out_grad, step_weight, skip_gain, ends
    )
    steps = lax.psum_scatter(products, "ctx", scatter_dimension=0, tiled=True)
    early = [small] + [rotate(small, "ctx", hop) for hop in range(1, places)]
    back = chan_sum(part)
    cuts = exchange(back, "ctx")
    main, tail, head, sums = conv_grad_call(
        places, low_rank, back, proj_weight, scan_part, conv_input, rim, conv_weight, conv_bias
    )
    following = shift(head, "ctx", -1)
    late = [sums] + [rotate(sums, "ctx", hop) for hop in range(1, places)]
    grad_proj, grad_coef, grad_step = rows_call(cuts, conv_all, steps, 2 * states // places)
    grad_input, conv_w, conv_b, step_b, decay_grad, skip = last_call(
        main, tail, following, conv_weight, early, late, states
    )
    return (
        grad_input,
        grad_gate,
        grad_proj,
        grad_coef,
        grad_step,
        conv_w,
        conv_b[0],
        step_b[0],
        decay_grad,
        skip[0],
    )


def solution(mesh):
    tokens, columns_, chan = P("ctx", "chan"), P(None, "chan"), P("chan")
    in_specs = (
        tokens, tokens, tokens, columns_, chan, columns_, columns_, chan, columns_, chan,
    )
    out_specs = (
        tokens, tokens, tokens, tokens, tokens, columns_, chan, chan, columns_, chan,
    )
    return jax.shard_map(body, mesh=mesh, in_specs=in_specs, out_specs=out_specs, check_vma=False)
```

```python
import functools

import jax
import jax.numpy as jnp
from jax import lax
from jax.experimental import pallas as pl
from jax.experimental.pallas import tpu as pltpu
from jax.sharding import PartitionSpec as P

BF = jnp.bfloat16
F32 = jnp.float32
LOG2E = 1.4426950408889634
LN2 = 0.6931471805599453
VMEM_BYTES = 56 * 1024 * 1024
NT = (((1,), (1,)), ((), ()))
TN = (((0,), (0,)), ((), ()))


def group_rows(chans):
    for rows in (8, 4, 2, 1):
        if chans % (rows * 128) == 0:
            return rows
    return 1


def dot(a, b, dims=(((1,), (0,)), ((), ()))):
    return lax.dot_general(a, b, dims, preferred_element_type=F32)


def params(**more):
    return pltpu.CompilerParams(vmem_limit_bytes=VMEM_BYTES, **more)


def sds(shape, dtype):
    return jax.ShapeDtypeStruct(shape, dtype)


def whole(shape):
    return pl.BlockSpec(shape, lambda i: (0,) * len(shape))


def columns(rows, width):
    return pl.BlockSpec((rows, width), lambda i: (0, i))


def sigmoid(v):
    return 1.0 / (1.0 + jnp.exp(-v))


def rotate(block, axis, distance):
    count = lax.axis_size(axis)
    return lax.ppermute(block, axis, [(i, (i + distance) % count) for i in range(count)])


def shift(block, axis, distance):
    count = lax.axis_size(axis)
    route = [(i, i + distance) for i in range(count) if 0 <= i + distance < count]
    return lax.ppermute(block, axis, route)


def fill_extended(ext, rim_ref, input_ref, taps):
    rows = input_ref.shape[0]
    ext[8 - (taps - 1) : 8, :] = rim_ref[...].astype(F32)
    ext[8 : 8 + rows, :] = input_ref[...].astype(F32)


def conv_block(ext, weight, bias, taps, start, rows):
    total = bias + jnp.zeros((rows, ext.shape[1]), F32)
    for tap in range(taps):
        first = 8 - (taps - 1) + tap + start
        total = total + weight[tap : tap + 1, :] * ext[first : first + rows, :]
    return total


def conv_kernel(input_ref, rim_ref, weight_ref, bias_ref, proj_ref, out_ref, part_ref, ext, acc):
    step = pl.program_id(0)
    taps = weight_ref.shape[0]
    rows = input_ref.shape[0]
    fill_extended(ext, rim_ref, input_ref, taps)
    for start in range(0, rows, 16):
        pre = conv_block(ext, weight_ref, bias_ref[...], taps, start, 16)
        out_ref[start : start + 16, :] = (pre * sigmoid(pre)).astype(BF)
    part = dot(out_ref[...], proj_ref[...], NT)

    @pl.when(step == 0)
    def _():
        acc[...] = part

    @pl.when(step > 0)
    def _():
        acc[...] += part

    @pl.when(step == pl.num_programs(0) - 1)
    def _():
        part_ref[...] = acc[...].astype(BF)


def conv_call(conv_input, rim, weight, bias, proj_weight):
    rows, chans = conv_input.shape
    taps = weight.shape[0]
    wide = proj_weight.shape[0]
    width = min(512, chans)
    return pl.pallas_call(
        conv_kernel,
        grid=(chans // width,),
        in_specs=[
            columns(rows, width),
            columns(taps - 1, width),
            columns(taps, width),
            columns(1, width),
            columns(wide, width),
        ],
        out_specs=[columns(rows, width), whole((rows, wide))],
        out_shape=[sds((rows, chans), BF), sds((rows, wide), BF)],
        scratch_shapes=[pltpu.VMEM((rows + 8, width), F32), pltpu.VMEM((rows, wide), F32)],
        compiler_params=params(),
        name="conv_project",
    )(conv_input, rim, weight, bias, proj_weight)


def tile_rows(value, target, lead, groups):
    rows = value.shape[0]
    for block in range(rows // 8):
        for group in range(groups):
            first = (block * groups + group) * 8
            target[lead, first : first + 8, :] = value[
                block * 8 : block * 8 + 8, group * 128 : group * 128 + 128
            ]


def local_kernel(low_rank, states, places, *refs):
    parts, refs = refs[:2], refs[2:]
    (weight_ref, bias_ref, decay_ref, conv_ref, gate_ref, grad_ref) = refs[:6]
    (dt_ref, ends_ref, coef_ref, low) = refs[6:10]
    (proj, coef_v, coef, dts, dxs, gs, fwd, bwd, sem) = refs[10:]
    step = pl.program_id(0)
    chunks = dts.shape[0]
    rows = conv_ref.shape[0]
    groups = decay_ref.shape[2]

    @pl.when(step == 0)
    def _():
        total = (parts[0][...].astype(F32) + parts[1][...].astype(F32)).astype(BF)
        proj[...] = total.astype(F32)
        low[...] = total[:, :low_rank]
        coef_v[...] = jnp.zeros_like(coef_v)
        coef_v[:, : 2 * states] = proj[:, low_rank:]
        coef_ref[...] = coef_v[...]
        copy = pltpu.make_async_copy(coef_v, coef, sem)
        copy.start()
        copy.wait()

    pre = dot(low[...], weight_ref[...]) + bias_ref[...]
    for start in range(0, rows, 16):
        here = slice(start, start + 16)
        p = pre[here, :]
        size = jnp.maximum(p, 0.0) + jnp.log1p(jnp.exp(-jnp.abs(p)))
        gate = gate_ref[here, :].astype(F32)
        grad = grad_ref[here, :].astype(F32) * gate * sigmoid(gate)
        drive = size * conv_ref[here, :].astype(F32)
        for half in range(2):
            for group in range(groups):
                first = ((start // 8 + half) * groups + group) * 8
                lanes = slice(group * 128, group * 128 + 128)
                subs = slice(half * 8, half * 8 + 8)
                dts[step, first : first + 8, :] = size[subs, lanes]
                dt_ref[0, first : first + 8, :] = size[subs, lanes]
                dxs[step, first : first + 8, :] = drive[subs, lanes]
                gs[step, first : first + 8, :] = grad[subs, lanes]

    @pl.when(step == chunks - 1)
    def _():
        batch = 4
        span = groups * 8
        zero = jnp.zeros((groups, 128), F32)
        for lead in range(0, states, batch):
            pairs = [(n, v) for n in range(lead, lead + batch) for v in range(chunks)]
            rates = [-LOG2E * jnp.exp(decay_ref[v, n]) for n, v in pairs]

            def block(index, carry):
                state, run, head, total = (list(part) for part in carry)
                for sub in range(8):
                    token = index * 8 + sub
                    at = pl.ds(index * span + sub, groups, stride=8)
                    size = [dts[v, at, :] for v in range(chunks)]
                    drive = [dxs[v, at, :] for v in range(chunks)]
                    grad = [gs[v, at, :] for v in range(chunks)]
                    if lead == 0:
                        total = [a + b for a, b in zip(total, size)]
                    for k, (n, v) in enumerate(pairs):
                        factor = jnp.exp2(size[v] * rates[k])
                        state[k] = factor * state[k] + drive[v] * coef[token, n]
                        run[k] = run[k] * factor
                        head[k] = head[k] + run[k] * (grad[v] * coef[token, states + n])
                return state, run, head, total

            many = [zero] * len(pairs)
            state, run, head, total = lax.fori_loop(
                0,
                rows // 8,
                block,
                (many, [zero + 1.0] * len(pairs), many, [zero] * chunks),
            )
            for k, (n, v) in enumerate(pairs):
                fwd[v, n] = state[k]
                bwd[v, n] = head[k]
            if lead == 0:
                for v in range(chunks):
                    coarse = total[v].astype(BF).astype(F32)
                    for target in (fwd, bwd):
                        target[v, states] = coarse
                        target[v, states + 1] = total[v] - coarse
        place = lax.axis_index("ctx")
        for other in range(places):
            ends_ref[other] = jnp.where(other > place, fwd[...], bwd[...]).astype(BF)


def local_call(parts, step_weight, step_bias, decay, conv_out, gate, grad, states, places):
    rows, chans = conv_out.shape
    wide = parts[0].shape[1]
    low_rank = step_weight.shape[0]
    chunks, _, groups, _ = decay.shape
    width = groups * 128
    message = (chunks, states + 2, groups, 128)
    big = pltpu.VMEM((chunks, rows * groups, 128), F32)
    return pl.pallas_call(
        functools.partial(local_kernel, low_rank, states, places),
        grid=(chunks,),
        in_specs=[
            whole((rows, wide)),
            whole((rows, wide)),
            columns(low_rank, width),
            columns(1, width),
            whole(decay.shape),
            columns(rows, width),
            columns(rows, width),
            columns(rows, width),
        ],
        out_specs=[
            pl.BlockSpec((1, rows * groups, 128), lambda i: (i, 0, 0)),
            whole((places,) + message),
            whole((rows, 128)),
            whole((rows, low_rank)),
        ],
        out_shape=[
            sds((chunks, rows * groups, 128), F32),
            sds((places,) + message, BF),
            sds((rows, 128), F32),
            sds((rows, low_rank), BF),
        ],
        scratch_shapes=[
            pltpu.VMEM((rows, wide), F32),
            pltpu.VMEM((rows, 128), F32),
            pltpu.SMEM((rows, 128), F32),
            big,
            big,
            big,
            pltpu.VMEM(message, F32),
            pltpu.VMEM(message, F32),
            pltpu.SemaphoreType.DMA,
        ],
        compiler_params=params(),
        name="local_ends",
    )(*parts, step_weight, step_bias, decay, conv_out, gate, grad)


def fold_sublanes(values):
    rows = lax.broadcasted_iota(jnp.int32, (8, 128), 0)
    if values[0].shape[0] != 8:
        result = jnp.zeros((8, 128), F32)
        for i, value in enumerate(values):
            result = jnp.where(rows == i, jnp.sum(value, axis=0, keepdims=True), result)
        return result
    distance = 4
    while len(values) > 1:
        half = len(values) // 2
        low = (rows & distance) == 0
        values = [
            jnp.where(low, a, b) + pltpu.roll(jnp.where(low, b, a), distance, 0)
            if distance == 4
            else jnp.where(low, a, pltpu.roll(b, distance, 0))
            + jnp.where(low, pltpu.roll(a, 8 - distance, 0), b)
            for a, b in zip(values[:half], values[half:])
        ]
        distance //= 2
    return values[0]


def scan_kernel(places, states, opening, *refs):
    (coef, low_ref, dt_ref, decay_ref, conv_ref, gate_ref, grad_ref, weight_ref, skip_ref) = refs[:9]
    ends, refs = refs[9], refs[10:]
    if not opening:
        before_ref, refs = refs[0], refs[4:]
    (pre_ref, gate_out, scan_out, small_ref, prod_ref, part_ref) = refs[:6]
    refs = refs[6:]
    (xs, dxs, gs, ys, dds, qs, decayed, coef_out, coef_in, rate, decay_acc, acc, small) = refs
    rows = conv_ref.shape[0]
    groups = decay_ref.shape[2]
    low_rank = weight_ref.shape[0]
    span = groups * 8

    for start in range(0, rows, 16):
        here = slice(start, start + 16)
        conv = conv_ref[here, :].astype(F32)
        gate = gate_ref[here, :].astype(F32)
        grad = grad_ref[here, :].astype(F32) * gate * sigmoid(gate)
        for half in range(2):
            for group in range(groups):
                first = ((start // 8 + half) * groups + group) * 8
                lanes = slice(group * 128, group * 128 + 128)
                subs = slice(half * 8, half * 8 + 8)
                xs[first : first + 8, :] = conv[subs, lanes]
                dxs[first : first + 8, :] = conv[subs, lanes] * dt_ref[0, first : first + 8, :]
                gs[first : first + 8, :] = grad[subs, lanes]

    place = lax.axis_index("ctx")
    for n in range(states):
        rate[n] = -LOG2E * jnp.exp(decay_ref[0, n])
    totals = [
        ends[q, 0, states].astype(F32) + ends[q, 0, states + 1].astype(F32) for q in range(places)
    ]
    state, carry = [], []
    for n in range(states):
        before = jnp.zeros((groups, 128), F32)
        after = jnp.zeros((groups, 128), F32)
        for q in range(places - 1):
            reached = jnp.exp2(rate[n] * totals[q]) * before + ends[q, 0, n].astype(F32)
            before = jnp.where(q < place, reached, before)
        for q in range(places - 1, 0, -1):
            reached = jnp.exp2(rate[n] * totals[q]) * after + ends[q, 0, n].astype(F32)
            after = jnp.where(q > place, reached, after)
        state.append(before)
        carry.append(after)

    def forward(index, state):
        state = list(state)
        for sub in range(8):
            token = index * 8 + sub
            at = pl.ds(index * span + sub, groups, stride=8)
            size, drive, grad = dt_ref[0, at, :], dxs[at, :], gs[at, :]
            result = jnp.zeros((groups, 128), F32)
            for lead in range(0, states, 8):
                products = []
                for n in range(lead, lead + 8):
                    kept = jnp.exp2(size * rate[n]) * state[n]
                    decayed[token, n] = kept
                    state[n] = kept + drive * coef[token, n]
                    result = result + state[n] * coef[token, states + n]
                    products.append(state[n] * grad)
                coef_out[pl.ds(pl.multiple_of(token * states + lead, 8), 8), :] = fold_sublanes(
                    products
                )
            ys[at, :] = result
        return state

    lax.fori_loop(0, rows // 8, forward, state)

    def backward(hop, both):
        carry, gathered = list(both[0]), list(both[1])
        index = rows // 8 - 1 - hop
        for sub in range(7, -1, -1):
            token = index * 8 + sub
            at = pl.ds(index * span + sub, groups, stride=8)
            size, drive, grad = dt_ref[0, at, :], dxs[at, :], gs[at, :]
            slope = jnp.zeros((groups, 128), F32)
            inner = jnp.zeros((groups, 128), F32)
            for lead in range(0, states, 8):
                products = []
                for n in range(lead, lead + 8):
                    adjoint = carry[n] + grad * coef[token, states + n]
                    carry[n] = jnp.exp2(size * rate[n]) * adjoint
                    weighted = adjoint * decayed[token, n]
                    slope = slope + weighted * rate[n]
                    gathered[n] = gathered[n] + weighted * size
                    inner = inner + adjoint * coef[token, n]
                    products.append(adjoint * drive)
                coef_in[pl.ds(pl.multiple_of(token * states + lead, 8), 8), :] = fold_sublanes(
                    products
                )
            dds[at, :] = slope
            qs[at, :] = inner
        return carry, gathered

    zeros = [jnp.zeros((groups, 128), F32)] * states
    _, gathered = lax.fori_loop(0, rows // 8, backward, (carry, zeros))
    for n in range(states):
        decay_acc[n * groups : n * groups + groups, :] = gathered[n] * (rate[n] * LN2)

    small[...] = jnp.zeros_like(small)
    for group in range(groups):
        small[:states, group * 128 : group * 128 + 128] = decay_acc[
            pl.ds(group, states, stride=groups), :
        ]
    skip = skip_ref[...]
    bias_sum = jnp.zeros((1, conv_ref.shape[1]), F32)
    skip_sum = jnp.zeros((1, conv_ref.shape[1]), F32)
    for start in range(0, rows, 16):
        here = slice(start, start + 16)

        def natural(read):
            return jnp.concatenate(
                [
                    jnp.concatenate(
                        [
                            read(((start // 8 + half) * groups + group) * 8)
                            for group in range(groups)
                        ],
                        axis=1,
                    )
                    for half in range(2)
                ],
                axis=0,
            )

        size = natural(lambda first: dt_ref[0, first : first + 8, :])
        inner = natural(lambda first: qs[first : first + 8, :])
        slope = natural(lambda first: dds[first : first + 8, :])
        out = natural(lambda first: ys[first : first + 8, :])
        conv = conv_ref[here, :].astype(F32)
        gate = gate_ref[here, :].astype(F32)
        grad = grad_ref[here, :].astype(F32)
        sig = sigmoid(gate)
        scan_grad = grad * gate * sig
        tiny = size * (1.0 - 0.5 * size * (1.0 - size * (1.0 / 3.0) * (1.0 - 0.25 * size)))
        step_slope = jnp.where(size < 0.03, tiny, 1.0 - jnp.exp(-size))
        d_pre = (LN2 * slope + conv * inner) * step_slope
        pre_ref[here, :] = d_pre.astype(BF)
        bias_sum = bias_sum + jnp.sum(d_pre, axis=0, keepdims=True)
        skip_sum = skip_sum + jnp.sum(scan_grad * conv, axis=0, keepdims=True)
        scan_out[here, :] = (size * inner + skip * scan_grad).astype(BF)
        gate_out[here, :] = (
            grad * (out + skip * conv) * (sig * (1.0 + gate * (1.0 - sig)))
        ).astype(BF)
    small[states : states + 1, :] = bias_sum
    small[states + 1 : states + 2, :] = skip_sum
    small_ref[...] = small[...].astype(BF)

    pre_bf = pre_ref[...]
    prod_ref[...] = dot(low_ref[...], pre_bf, TN).astype(BF)
    lanes = lax.broadcasted_iota(jnp.int32, (2 * states, 128), 0)
    coefs = jnp.zeros((2 * states, rows), F32)
    for n in range(states):
        at = pl.ds(n, rows, stride=states)
        for kind, source in enumerate((coef_in, coef_out)):
            pick = jnp.where(lanes == kind * states + n, 1.0, 0.0).astype(BF)
            coefs = coefs + dot(pick, source[at, :].astype(BF), NT)
    wide = dot(weight_ref[...], pre_bf, NT)

    ranks, coef_rows, block = low_rank // places, 2 * states // places, acc.shape[0] // places

    acc[...] = jnp.zeros_like(acc) if opening else before_ref[...]
    for q in range(places):
        at = q * block
        acc[at : at + ranks, :] += wide[q * ranks : (q + 1) * ranks, :]
        acc[at + ranks : at + ranks + coef_rows, :] += coefs[
            q * coef_rows : (q + 1) * coef_rows, :
        ]
    part_ref[...] = acc[...].astype(part_ref.dtype)


def padded(wide):
    return (wide + 127) // 128 * 128


def scan_call(
    places, chunk, coef, low, dt, decay, conv_out, gate, grad, step_weight, skip, ends, previous
):
    rows, chans = conv_out.shape
    low_rank = step_weight.shape[0]
    chunks, states, groups, _ = decay.shape
    width = groups * 128
    wide = padded(low_rank + 2 * states)
    lead = lambda *shape: pl.BlockSpec((1,) + shape, lambda i: (chunk,) + (0,) * len(shape))
    here = lambda height: pl.BlockSpec((height, width), lambda i: (0, chunk))
    tall = pltpu.VMEM((rows * groups, 128), F32)
    first, last = chunk == 0, chunk == chunks - 1
    in_specs = [
        pl.BlockSpec(memory_space=pltpu.SMEM),
        whole((rows, low_rank)),
        lead(rows * groups, 128),
        lead(states, groups, 128),
        here(rows),
        here(rows),
        here(rows),
        here(low_rank),
        here(1),
        pl.BlockSpec((places, 1, states + 2, groups, 128), lambda i: (0, chunk, 0, 0, 0)),
    ]
    aliases = {}
    if not first:
        in_specs += [whole((wide, rows))] + [pl.BlockSpec(memory_space=pl.ANY)] * 3
        aliases = {11: 1, 12: 2, 13: 3}
    return pl.pallas_call(
        functools.partial(scan_kernel, places, states, first),
        grid=(1,),
        in_specs=in_specs,
        out_specs=[
            whole((rows, width)),
            here(rows),
            here(rows),
            here(32),
            whole((low_rank, width)),
            whole((wide, rows)),
        ],
        out_shape=[
            sds((rows, width), BF),
            sds((rows, chans), BF),
            sds((rows, chans), BF),
            sds((32, chans), BF),
            sds((low_rank, width), BF),
            sds((wide, rows), BF if last else F32),
        ],
        scratch_shapes=[
            tall,
            tall,
            tall,
            tall,
            tall,
            tall,
            pltpu.VMEM((rows, states, groups, 128), F32),
            pltpu.VMEM((rows * states, 128), F32),
            pltpu.VMEM((rows * states, 128), F32),
            pltpu.VMEM((states, groups, 128), F32),
            pltpu.VMEM((states * groups, 128), F32),
            pltpu.VMEM((wide, rows), F32),
            pltpu.VMEM((32, width), F32),
        ],
        input_output_aliases=aliases,
        compiler_params=params(),
        name="scan_gradients",
    )(coef, low, dt, decay, conv_out, gate, grad, step_weight, skip, ends, *previous)


def conv_grad_kernel(places, low_rank, back_a, back_b, proj_ref, scan_ref, input_ref, rim_ref, weight_ref, bias_ref,
                     out_ref, tail_ref, small_ref, ext, grad):
    taps = weight_ref.shape[0]
    rows = input_ref.shape[0]
    fill_extended(ext, rim_ref, input_ref, taps)
    wide = proj_ref.shape[0]
    block = back_a.shape[0] // places
    ranks, coef_rows = low_rank // places, (wide - low_rank) // places
    back = (back_a[...].astype(F32) + back_b[...].astype(F32)).astype(BF).astype(F32)
    order = [back[q * block : q * block + ranks, :] for q in range(places)]
    order += [back[q * block + ranks : q * block + ranks + coef_rows, :] for q in range(places)]
    d_xc = dot(jnp.concatenate(order, axis=0).astype(BF), proj_ref[...], TN)
    sums = [jnp.zeros((1, input_ref.shape[1]), F32) for _ in range(taps + 1)]
    for start in range(0, rows, 16):
        here = slice(start, start + 16)
        pre = conv_block(ext, weight_ref, bias_ref[...], taps, start, 16)
        sig = sigmoid(pre)
        value = (d_xc[here, :] + scan_ref[here, :].astype(F32)) * (sig * (1.0 + pre * (1.0 - sig)))
        grad[here, :] = value
        for tap in range(taps):
            first = 8 - (taps - 1) + tap + start
            sums[tap] = sums[tap] + jnp.sum(value * ext[first : first + 16, :], axis=0, keepdims=True)
        sums[taps] = sums[taps] + jnp.sum(value, axis=0, keepdims=True)
    grad[rows : rows + 8, :] = jnp.zeros((8, grad.shape[1]), F32)
    for start in range(0, rows, 16):
        total = jnp.zeros((16, grad.shape[1]), F32)
        for tap in range(taps):
            first = start + taps - 1 - tap
            total = total + weight_ref[tap : tap + 1, :] * grad[first : first + 16, :]
        out_ref[start : start + 16, :] = total.astype(BF)
    tail_ref[...] = total
    small_ref[...] = jnp.concatenate(
        sums + [jnp.zeros((8 - taps - 1, small_ref.shape[1]), F32), grad[0:8, :]], axis=0
    ).astype(BF)


def conv_grad_call(places, low_rank, backs, proj_weight, scan_part, conv_input, rim, weight, bias):
    rows, chans = conv_input.shape
    taps = weight.shape[0]
    wide = proj_weight.shape[0]
    width = min(512, chans)
    return pl.pallas_call(
        functools.partial(conv_grad_kernel, places, low_rank),
        grid=(chans // width,),
        in_specs=[
            whole(backs[0].shape),
            whole(backs[1].shape),
            columns(wide, width),
            columns(rows, width),
            columns(rows, width),
            columns(taps - 1, width),
            columns(taps, width),
            columns(1, width),
        ],
        out_specs=[columns(rows, width), columns(16, width), columns(16, width)],
        out_shape=[sds((rows, chans), BF), sds((16, chans), F32), sds((16, chans), BF)],
        scratch_shapes=[pltpu.VMEM((rows + 8, width), F32), pltpu.VMEM((rows + 8, width), F32)],
        compiler_params=params(),
        name="conv_gradients",
    )(*backs, proj_weight, scan_part, conv_input, rim, weight, bias)


def rows_kernel(places, rank_rows, chunks, *refs):
    cut_ref, refs = refs[0], refs[1:]
    blocks, refs = refs[: 2 * places - 1], refs[2 * places - 1 :]
    steps, (out_ref, coef_ref, step_out) = refs[:chunks], refs[chunks:]
    place = lax.axis_index("ctx")
    block = cut_ref.shape[0] // places
    total = None
    for hop, ref in zip([0] + [k for d in range(1, places) for k in (d, -d)], blocks):
        source = lax.rem(place + places - hop, places)
        cut = cut_ref[pl.ds(pl.multiple_of(source * block, 16 if block % 16 == 0 else 8), block), :]
        part = dot(cut, ref[...])
        total = part if total is None else total + part
    out_ref[...] = total[:rank_rows, :]
    coef_ref[...] = total[rank_rows : rank_rows + coef_ref.shape[0], :]
    for chunk in range(chunks):

        @pl.when(pl.program_id(0) == chunk)
        def _():
            step_out[...] = steps[chunk][...].astype(F32)


def rows_call(places, cuts, blocks, steps, coef_rows):
    rows, chans = blocks[0].shape
    rank_rows, width = steps[0].shape
    chunks = len(steps)
    return pl.pallas_call(
        functools.partial(rows_kernel, places, rank_rows, chunks),
        grid=(chunks,),
        in_specs=[whole(cuts.shape)]
        + [columns(rows, width)] * len(blocks)
        + [whole((rank_rows, width))] * chunks,
        out_specs=[
            columns(rank_rows, width), columns(coef_rows, width), columns(rank_rows, width)
        ],
        out_shape=[
            sds((rank_rows, chans), F32), sds((coef_rows, chans), F32), sds((rank_rows, chans), F32)
        ],
        compiler_params=params(),
        name="row_gradients",
    )(cuts, *blocks, *steps)


def last_kernel(places, states, taps, *refs):
    (_, tail_ref, weight_ref) = refs[:3]
    early, refs = refs[3 : 3 + places], refs[3 + places :]
    late, refs = refs[:places], refs[places:]
    (out_ref, conv_w, conv_b, step_b, decay, skip, fix) = refs
    fix[...] = tail_ref[...]
    inside = lax.axis_index("ctx") < places - 1
    following = jnp.where(inside, late[places - 1][8:16, :].astype(F32), 0.0)
    for row in range(taps - 1):
        extra = jnp.zeros((1, fix.shape[1]), F32)
        for tap in range(row + 1):
            extra = extra + weight_ref[tap : tap + 1, :] * following[row - tap : row - tap + 1, :]
        at = 16 - (taps - 1) + row
        fix[at : at + 1, :] += extra
    out_ref[...] = fix[...].astype(BF)
    total = early[0][...].astype(F32)
    for part in early[1:]:
        total = total + part[...].astype(F32)
    decay[...] = total[:states, :]
    step_b[...] = total[states : states + 1, :]
    skip[...] = total[states + 1 : states + 2, :]
    total = late[0][...].astype(F32)
    for part in late[1:]:
        total = total + part[...].astype(F32)
    conv_w[...] = total[:taps, :]
    conv_b[...] = total[taps : taps + 1, :]


def last_call(main, tail, weight, early, late, states):
    rows, chans = main.shape
    taps = weight.shape[0]
    places = len(early)
    width = chans
    return pl.pallas_call(
        functools.partial(last_kernel, places, states, taps),
        grid=(1,),
        in_specs=[pl.BlockSpec(memory_space=pl.ANY), columns(16, width), columns(taps, width)]
        + [columns(32, width)] * places
        + [columns(16, width)] * places,
        out_specs=[
            pl.BlockSpec((16, width), lambda i: (rows // 16 - 1, i)),
            columns(taps, width),
            columns(1, width),
            columns(1, width),
            columns(states, width),
            columns(1, width),
        ],
        out_shape=[
            sds((rows, chans), BF),
            sds((taps, chans), F32),
            sds((1, chans), F32),
            sds((1, chans), F32),
            sds((states, chans), F32),
            sds((1, chans), F32),
        ],
        scratch_shapes=[pltpu.VMEM((16, width), F32)],
        input_output_aliases={0: 0},
        compiler_params=params(),
        name="last_rows",
    )(main, tail, weight, *early, *late)


def exchange(block, axis):
    return lax.all_to_all(block, axis, split_axis=0, concat_axis=0, tiled=True)


def swap(block, axis, mask):
    return lax.ppermute(block, axis, [(i, i ^ mask) for i in range(lax.axis_size(axis))])


def chan_sum(part):
    mask, peers = 1, lax.axis_size("chan")
    while True:
        other = swap(part, "chan", mask)
        mask *= 2
        if mask == peers:
            return part, other
        part = (part.astype(F32) + other.astype(F32)).astype(BF)


def body(
    conv_input,
    gate_input,
    out_grad,
    conv_weight,
    conv_bias,
    proj_weight,
    step_weight,
    step_bias,
    decay_log,
    skip_gain,
):
    rows, chans = conv_input.shape
    taps = conv_weight.shape[0]
    low_rank = step_weight.shape[0]
    states = decay_log.shape[0]
    places = lax.axis_size("ctx")
    groups = group_rows(chans)
    decay = decay_log.reshape(states, -1, groups, 128).transpose(1, 0, 2, 3)
    conv_bias = conv_bias[None, :]
    step_bias = step_bias[None, :]
    skip_gain = skip_gain[None, :]

    chunks = decay.shape[0]
    rim = shift(conv_input[rows - (taps - 1) :], "ctx", 1)
    conv_out, part = conv_call(conv_input, rim, conv_weight, conv_bias, proj_weight)
    blocks = [conv_out]
    right, left = shift(conv_out, "ctx", 1), shift(conv_out, "ctx", -1)
    blocks += [right, left]
    parts = chan_sum(part)
    for hop in range(2, places):
        if hop == 2:
            parts, right, left = lax.optimization_barrier((parts, right, left))
            right, left = shift(right, "ctx", 1), shift(left, "ctx", -1)
            blocks += [right, left]
    dt, ends, coef, low = local_call(
        parts, step_weight, step_bias, decay, conv_out, gate_input, out_grad, states, places
    )
    ends = exchange(ends, "ctx")
    for hop in range(3, places):
        ends, right, left = lax.optimization_barrier((ends, right, left))
        right, left = shift(right, "ctx", 1), shift(left, "ctx", -1)
        blocks += [right, left]
    previous, steps = [], []
    for chunk in range(chunks):
        pre_bf, grad_gate, scan_part, small, products, part = scan_call(
            places, chunk, coef, low, dt, decay, conv_out, gate_input, out_grad, step_weight,
            skip_gain, ends, previous,
        )
        previous = [part, grad_gate, scan_part, small]
        steps.append(lax.psum_scatter(products, "ctx", scatter_dimension=0, tiled=True))
    early = [small] + [rotate(small, "ctx", hop) for hop in range(1, places)]
    backs = chan_sum(part)
    back = (backs[0].astype(F32) + backs[1].astype(F32)).astype(BF)
    cuts = exchange(back, "ctx")
    main, tail, sums = conv_grad_call(
        places, low_rank, backs, proj_weight, scan_part, conv_input, rim, conv_weight, conv_bias
    )
    late = [sums] + [rotate(sums, "ctx", hop) for hop in range(1, places)]
    grad_proj, grad_coef, grad_step = rows_call(places, cuts, blocks, steps, 2 * states // places)
    grad_input, conv_w, conv_b, step_b, decay_grad, skip = last_call(
        main, tail, conv_weight, early, late, states
    )
    return (
        grad_input,
        grad_gate,
        grad_proj,
        grad_coef,
        grad_step,
        conv_w,
        conv_b[0],
        step_b[0],
        decay_grad,
        skip[0],
    )


def solution(mesh):
    tokens, columns_, chan = P("ctx", "chan"), P(None, "chan"), P("chan")
    in_specs = (
        tokens, tokens, tokens, columns_, chan, columns_, columns_, chan, columns_, chan,
    )
    out_specs = (
        tokens, tokens, tokens, tokens, tokens, columns_, chan, chan, columns_, chan,
    )
    return jax.shard_map(body, mesh=mesh, in_specs=in_specs, out_specs=out_specs, check_vma=False)
```

```python
import functools

import jax
import jax.numpy as jnp
from jax import lax
from jax.experimental import pallas as pl
from jax.experimental.pallas import tpu as pltpu
from jax.sharding import PartitionSpec as P

BF = jnp.bfloat16
F32 = jnp.float32
LOG2E = 1.4426950408889634
LN2 = 0.6931471805599453
VMEM_BYTES = 56 * 1024 * 1024
NT = (((1,), (1,)), ((), ()))
TN = (((0,), (0,)), ((), ()))


def group_rows(chans):
    for rows in (8, 4, 2, 1):
        if chans % (rows * 128) == 0:
            return rows
    return 1


def dot(a, b, dims=(((1,), (0,)), ((), ()))):
    return lax.dot_general(a, b, dims, preferred_element_type=F32)


def params(**more):
    return pltpu.CompilerParams(vmem_limit_bytes=VMEM_BYTES, **more)


def sds(shape, dtype):
    return jax.ShapeDtypeStruct(shape, dtype)


def whole(shape):
    return pl.BlockSpec(shape, lambda i: (0,) * len(shape))


def columns(rows, width):
    return pl.BlockSpec((rows, width), lambda i: (0, i))


def sigmoid(v):
    return 1.0 / (1.0 + jnp.exp(-v))


def rotate(block, axis, distance):
    count = lax.axis_size(axis)
    return lax.ppermute(block, axis, [(i, (i + distance) % count) for i in range(count)])


def shift(block, axis, distance):
    count = lax.axis_size(axis)
    route = [(i, i + distance) for i in range(count) if 0 <= i + distance < count]
    return lax.ppermute(block, axis, route)


def fill_extended(ext, rim_ref, input_ref, taps):
    rows = input_ref.shape[0]
    ext[8 - (taps - 1) : 8, :] = rim_ref[...].astype(F32)
    ext[8 : 8 + rows, :] = input_ref[...].astype(F32)


def conv_block(ext, weight, bias, taps, start, rows):
    total = bias + jnp.zeros((rows, ext.shape[1]), F32)
    for tap in range(taps):
        first = 8 - (taps - 1) + tap + start
        total = total + weight[tap : tap + 1, :] * ext[first : first + rows, :]
    return total


def conv_kernel(input_ref, rim_ref, weight_ref, bias_ref, proj_ref, out_ref, part_ref, ext, acc):
    step = pl.program_id(0)
    taps = weight_ref.shape[0]
    rows = input_ref.shape[0]
    fill_extended(ext, rim_ref, input_ref, taps)
    for start in range(0, rows, 16):
        pre = conv_block(ext, weight_ref, bias_ref[...], taps, start, 16)
        out_ref[start : start + 16, :] = (pre * sigmoid(pre)).astype(BF)
    part = dot(out_ref[...], proj_ref[...], NT)

    @pl.when(step == 0)
    def _():
        acc[...] = part

    @pl.when(step > 0)
    def _():
        acc[...] += part

    @pl.when(step == pl.num_programs(0) - 1)
    def _():
        part_ref[...] = acc[...].astype(BF)


def conv_call(conv_input, rim, weight, bias, proj_weight):
    rows, chans = conv_input.shape
    taps = weight.shape[0]
    wide = proj_weight.shape[0]
    width = min(512, chans)
    return pl.pallas_call(
        conv_kernel,
        grid=(chans // width,),
        in_specs=[
            columns(rows, width),
            columns(taps - 1, width),
            columns(taps, width),
            columns(1, width),
            columns(wide, width),
        ],
        out_specs=[columns(rows, width), whole((rows, wide))],
        out_shape=[sds((rows, chans), BF), sds((rows, wide), BF)],
        scratch_shapes=[pltpu.VMEM((rows + 8, width), F32), pltpu.VMEM((rows, wide), F32)],
        compiler_params=params(),
        name="conv_project",
    )(conv_input, rim, weight, bias, proj_weight)


def tile_rows(value, target, lead, groups):
    rows = value.shape[0]
    for block in range(rows // 8):
        for group in range(groups):
            first = (block * groups + group) * 8
            target[lead, first : first + 8, :] = value[
                block * 8 : block * 8 + 8, group * 128 : group * 128 + 128
            ]


def local_kernel(low_rank, states, places, *refs):
    parts, refs = refs[:2], refs[2:]
    (weight_ref, bias_ref, decay_ref, conv_ref, gate_ref, grad_ref) = refs[:6]
    (dt_ref, coef_ref, low, low_t) = refs[6:10]
    messages, refs = refs[10 : 9 + places], refs[9 + places :]
    (proj, coef_v, coef, dts, dxs, gs, fwd, bwd, sem) = refs
    step = pl.program_id(0)
    chunks = dts.shape[0]
    rows = conv_ref.shape[0]
    groups = decay_ref.shape[2]

    @pl.when(step == 0)
    def _():
        total = (parts[0][...].astype(F32) + parts[1][...].astype(F32)).astype(BF)
        proj[...] = total.astype(F32)
        low[...] = total[:, :low_rank]
        low_t[...] = jnp.transpose(proj[:, :low_rank]).astype(BF)
        coef_v[...] = jnp.zeros_like(coef_v)
        coef_v[:, : 2 * states] = proj[:, low_rank:]
        coef_ref[...] = coef_v[...]
        copy = pltpu.make_async_copy(coef_v, coef, sem)
        copy.start()
        copy.wait()

    pre = dot(low[...], weight_ref[...]) + bias_ref[...]
    for start in range(0, rows, 16):
        here = slice(start, start + 16)
        p = pre[here, :]
        size = jnp.maximum(p, 0.0) + jnp.log1p(jnp.exp(-jnp.abs(p)))
        gate = gate_ref[here, :].astype(F32)
        grad = grad_ref[here, :].astype(F32) * gate * sigmoid(gate)
        drive = size * conv_ref[here, :].astype(F32)
        for half in range(2):
            for group in range(groups):
                first = ((start // 8 + half) * groups + group) * 8
                lanes = slice(group * 128, group * 128 + 128)
                subs = slice(half * 8, half * 8 + 8)
                dts[step, first : first + 8, :] = size[subs, lanes]
                dt_ref[0, first : first + 8, :] = size[subs, lanes]
                dxs[step, first : first + 8, :] = drive[subs, lanes]
                gs[step, first : first + 8, :] = grad[subs, lanes]

    @pl.when(step == chunks - 1)
    def _():
        batch = 4
        span = groups * 8
        zero = jnp.zeros((groups, 128), F32)
        for lead in range(0, states, batch):
            pairs = [(n, v) for n in range(lead, lead + batch) for v in range(chunks)]
            rates = [-LOG2E * jnp.exp(decay_ref[v, n]) for n, v in pairs]

            def block(index, carry):
                state, run, head, total = (list(part) for part in carry)
                for sub in range(8):
                    token = index * 8 + sub
                    at = pl.ds(index * span + sub, groups, stride=8)
                    size = [dts[v, at, :] for v in range(chunks)]
                    drive = [dxs[v, at, :] for v in range(chunks)]
                    grad = [gs[v, at, :] for v in range(chunks)]
                    if lead == 0:
                        total = [a + b for a, b in zip(total, size)]
                    for k, (n, v) in enumerate(pairs):
                        factor = jnp.exp2(size[v] * rates[k])
                        state[k] = factor * state[k] + drive[v] * coef[token, n]
                        run[k] = run[k] * factor
                        head[k] = head[k] + run[k] * (grad[v] * coef[token, states + n])
                return state, run, head, total

            many = [zero] * len(pairs)
            state, run, head, total = lax.fori_loop(
                0,
                rows // 8,
                block,
                (many, [zero + 1.0] * len(pairs), many, [zero] * chunks),
            )
            for k, (n, v) in enumerate(pairs):
                fwd[v, n] = state[k]
                bwd[v, n] = head[k]
            if lead == 0:
                for v in range(chunks):
                    coarse = total[v].astype(BF).astype(F32)
                    for target in (fwd, bwd):
                        target[v, states] = coarse
                        target[v, states + 1] = total[v] - coarse
        place = lax.axis_index("ctx")
        for mask, message in enumerate(messages, 1):
            message[...] = jnp.where((place ^ mask) > place, fwd[...], bwd[...]).astype(BF)


def local_call(parts, step_weight, step_bias, decay, conv_out, gate, grad, states, places):
    rows, chans = conv_out.shape
    wide = parts[0].shape[1]
    low_rank = step_weight.shape[0]
    chunks, _, groups, _ = decay.shape
    width = groups * 128
    message = (chunks, states + 2, groups, 128)
    big = pltpu.VMEM((chunks, rows * groups, 128), F32)
    return pl.pallas_call(
        functools.partial(local_kernel, low_rank, states, places),
        grid=(chunks,),
        in_specs=[
            whole((rows, wide)),
            whole((rows, wide)),
            columns(low_rank, width),
            columns(1, width),
            whole(decay.shape),
            columns(rows, width),
            columns(rows, width),
            columns(rows, width),
        ],
        out_specs=[
            pl.BlockSpec((1, rows * groups, 128), lambda i: (i, 0, 0)),
            whole((rows, 128)),
            whole((rows, low_rank)),
            whole((low_rank, rows)),
        ]
        + [whole(message)] * (places - 1),
        out_shape=[
            sds((chunks, rows * groups, 128), F32),
            sds((rows, 128), F32),
            sds((rows, low_rank), BF),
            sds((low_rank, rows), BF),
        ]
        + [sds(message, BF)] * (places - 1),
        scratch_shapes=[
            pltpu.VMEM((rows, wide), F32),
            pltpu.VMEM((rows, 128), F32),
            pltpu.SMEM((rows, 128), F32),
            big,
            big,
            big,
            pltpu.VMEM(message, F32),
            pltpu.VMEM(message, F32),
            pltpu.SemaphoreType.DMA,
        ],
        compiler_params=params(),
        name="local_ends",
    )(*parts, step_weight, step_bias, decay, conv_out, gate, grad)


def fold_sublanes(values):
    rows = lax.broadcasted_iota(jnp.int32, (8, 128), 0)
    if values[0].shape[0] != 8:
        result = jnp.zeros((8, 128), F32)
        for i, value in enumerate(values):
            result = jnp.where(rows == i, jnp.sum(value, axis=0, keepdims=True), result)
        return result
    distance = 4
    while len(values) > 1:
        half = len(values) // 2
        low = (rows & distance) == 0
        values = [
            jnp.where(low, a, b) + pltpu.roll(jnp.where(low, b, a), distance, 0)
            if distance == 4
            else jnp.where(low, a, pltpu.roll(b, distance, 0))
            + jnp.where(low, pltpu.roll(a, 8 - distance, 0), b)
            for a, b in zip(values[:half], values[half:])
        ]
        distance //= 2
    return values[0]


def scan_kernel(places, states, opening, *refs):
    (coef, dt_ref, decay_ref, conv_ref, gate_ref, grad_ref, weight_ref, skip_ref) = refs[:8]
    messages, refs = refs[8 : 7 + places], refs[7 + places :]
    if not opening:
        before_ref, refs = refs[0], refs[4:]
    (pre_ref, gate_out, scan_out, small_ref, part_ref) = refs[:5]
    refs = refs[5:]
    (xs, dxs, gs, ys, dds, qs, decayed, coef_out, coef_in, rate, decay_acc, acc, ends) = refs
    rows = conv_ref.shape[0]
    groups = decay_ref.shape[2]
    low_rank = weight_ref.shape[0]
    span = groups * 8

    for start in range(0, rows, 16):
        here = slice(start, start + 16)
        conv = conv_ref[here, :].astype(F32)
        gate = gate_ref[here, :].astype(F32)
        grad = grad_ref[here, :].astype(F32) * gate * sigmoid(gate)
        for half in range(2):
            for group in range(groups):
                first = ((start // 8 + half) * groups + group) * 8
                lanes = slice(group * 128, group * 128 + 128)
                subs = slice(half * 8, half * 8 + 8)
                xs[first : first + 8, :] = conv[subs, lanes]
                dxs[first : first + 8, :] = conv[subs, lanes] * dt_ref[0, first : first + 8, :]
                gs[first : first + 8, :] = grad[subs, lanes]

    place = lax.axis_index("ctx")
    for n in range(states):
        rate[n] = -LOG2E * jnp.exp(decay_ref[0, n])
    ends[place] = jnp.zeros(ends.shape[1:], F32)
    for mask, message in enumerate(messages, 1):
        ends[place ^ mask] = message[0].astype(F32)
    totals = [ends[q, states] + ends[q, states + 1] for q in range(places)]
    state, carry = [], []
    for n in range(states):
        before = jnp.zeros((groups, 128), F32)
        after = jnp.zeros((groups, 128), F32)
        for q in range(places - 1):
            reached = jnp.exp2(rate[n] * totals[q]) * before + ends[q, n]
            before = jnp.where(q < place, reached, before)
        for q in range(places - 1, 0, -1):
            reached = jnp.exp2(rate[n] * totals[q]) * after + ends[q, n]
            after = jnp.where(q > place, reached, after)
        state.append(before)
        carry.append(after)

    def forward(index, state):
        state = list(state)
        for sub in range(8):
            token = index * 8 + sub
            at = pl.ds(index * span + sub, groups, stride=8)
            size, drive, grad = dt_ref[0, at, :], dxs[at, :], gs[at, :]
            result = jnp.zeros((groups, 128), F32)
            for lead in range(0, states, 8):
                products = []
                for n in range(lead, lead + 8):
                    kept = jnp.exp2(size * rate[n]) * state[n]
                    decayed[token, n] = kept
                    state[n] = kept + drive * coef[token, n]
                    result = result + state[n] * coef[token, states + n]
                    products.append(state[n] * grad)
                coef_out[pl.ds(pl.multiple_of(token * states + lead, 8), 8), :] = fold_sublanes(
                    products
                )
            ys[at, :] = result
        return state

    lax.fori_loop(0, rows // 8, forward, state)

    def backward(hop, both):
        carry, gathered = list(both[0]), list(both[1])
        index = rows // 8 - 1 - hop
        for sub in range(7, -1, -1):
            token = index * 8 + sub
            at = pl.ds(index * span + sub, groups, stride=8)
            size, drive, grad = dt_ref[0, at, :], dxs[at, :], gs[at, :]
            slope = jnp.zeros((groups, 128), F32)
            inner = jnp.zeros((groups, 128), F32)
            for lead in range(0, states, 8):
                products = []
                for n in range(lead, lead + 8):
                    adjoint = carry[n] + grad * coef[token, states + n]
                    carry[n] = jnp.exp2(size * rate[n]) * adjoint
                    weighted = adjoint * decayed[token, n]
                    slope = slope + weighted * rate[n]
                    gathered[n] = gathered[n] + weighted * size
                    inner = inner + adjoint * coef[token, n]
                    products.append(adjoint * drive)
                coef_in[pl.ds(pl.multiple_of(token * states + lead, 8), 8), :] = fold_sublanes(
                    products
                )
            dds[at, :] = slope
            qs[at, :] = inner
        return carry, gathered

    zeros = [jnp.zeros((groups, 128), F32)] * states
    _, gathered = lax.fori_loop(0, rows // 8, backward, (carry, zeros))
    for n in range(states):
        decay_acc[n * groups : n * groups + groups, :] = gathered[n] * (rate[n] * LN2)

    for group in range(groups):
        pre_ref[rows : rows + states, group * 128 : group * 128 + 128] = decay_acc[
            pl.ds(group, states, stride=groups), :
        ].astype(BF)
    skip = skip_ref[...]
    bias_sum = jnp.zeros((1, conv_ref.shape[1]), F32)
    skip_sum = jnp.zeros((1, conv_ref.shape[1]), F32)
    for start in range(0, rows, 16):
        here = slice(start, start + 16)

        def natural(read):
            return jnp.concatenate(
                [
                    jnp.concatenate(
                        [
                            read(((start // 8 + half) * groups + group) * 8)
                            for group in range(groups)
                        ],
                        axis=1,
                    )
                    for half in range(2)
                ],
                axis=0,
            )

        size = natural(lambda first: dt_ref[0, first : first + 8, :])
        inner = natural(lambda first: qs[first : first + 8, :])
        slope = natural(lambda first: dds[first : first + 8, :])
        out = natural(lambda first: ys[first : first + 8, :])
        conv = conv_ref[here, :].astype(F32)
        gate = gate_ref[here, :].astype(F32)
        grad = grad_ref[here, :].astype(F32)
        sig = sigmoid(gate)
        scan_grad = grad * gate * sig
        tiny = size * (1.0 - 0.5 * size * (1.0 - size * (1.0 / 3.0) * (1.0 - 0.25 * size)))
        step_slope = jnp.where(size < 0.03, tiny, 1.0 - jnp.exp(-size))
        d_pre = (LN2 * slope + conv * inner) * step_slope
        pre_ref[here, :] = d_pre.astype(BF)
        bias_sum = bias_sum + jnp.sum(d_pre, axis=0, keepdims=True)
        skip_sum = skip_sum + jnp.sum(scan_grad * conv, axis=0, keepdims=True)
        scan_out[here, :] = (size * inner + skip * scan_grad).astype(BF)
        gate_out[here, :] = (
            grad * (out + skip * conv) * (sig * (1.0 + gate * (1.0 - sig)))
        ).astype(BF)
    small_ref[...] = jnp.concatenate(
        [bias_sum, skip_sum, jnp.zeros((6, bias_sum.shape[1]), F32)], axis=0
    )

    pre_bf = pre_ref[:rows, :]
    lanes = lax.broadcasted_iota(jnp.int32, (2 * states, 128), 0)
    coefs = jnp.zeros((2 * states, rows), F32)
    for n in range(states):
        at = pl.ds(n, rows, stride=states)
        for kind, source in enumerate((coef_in, coef_out)):
            pick = jnp.where(lanes == kind * states + n, 1.0, 0.0).astype(BF)
            coefs = coefs + dot(pick, source[at, :].astype(BF), NT)
    wide = dot(weight_ref[...], pre_bf, NT)

    ranks, coef_rows, block = low_rank // places, 2 * states // places, acc.shape[0] // places

    acc[...] = jnp.zeros_like(acc) if opening else before_ref[...]
    for q in range(places):
        at = q * block
        acc[at : at + ranks, :] += wide[q * ranks : (q + 1) * ranks, :]
        acc[at + ranks : at + ranks + coef_rows, :] += coefs[
            q * coef_rows : (q + 1) * coef_rows, :
        ]
    part_ref[...] = acc[...].astype(part_ref.dtype)


def padded(wide):
    return (wide + 127) // 128 * 128


def scan_call(
    places, chunk, coef, dt, decay, conv_out, gate, grad, step_weight, skip, messages, previous
):
    rows, chans = conv_out.shape
    low_rank = step_weight.shape[0]
    chunks, states, groups, _ = decay.shape
    width = groups * 128
    wide = padded(low_rank + 2 * states)
    lead = lambda *shape: pl.BlockSpec((1,) + shape, lambda i: (chunk,) + (0,) * len(shape))
    here = lambda height: pl.BlockSpec((height, width), lambda i: (0, chunk))
    tall = pltpu.VMEM((rows * groups, 128), F32)
    first, last = chunk == 0, chunk == chunks - 1
    in_specs = [
        pl.BlockSpec(memory_space=pltpu.SMEM),
        lead(rows * groups, 128),
        lead(states, groups, 128),
        here(rows),
        here(rows),
        here(rows),
        here(low_rank),
        here(1),
    ]
    in_specs += [lead(states + 2, groups, 128)] * (places - 1)
    aliases = {}
    if not first:
        in_specs += [whole((wide, rows))] + [pl.BlockSpec(memory_space=pl.ANY)] * 3
        aliases = {8 + places: 1, 9 + places: 2, 10 + places: 3}
    return pl.pallas_call(
        functools.partial(scan_kernel, places, states, first),
        grid=(1,),
        in_specs=in_specs,
        out_specs=[
            whole((rows + states, width)),
            here(rows),
            here(rows),
            here(8),
            whole((wide, rows)),
        ],
        out_shape=[
            sds((rows + states, width), BF),
            sds((rows, chans), BF),
            sds((rows, chans), BF),
            sds((8, chans), F32),
            sds((wide, rows), BF if last else F32),
        ],
        scratch_shapes=[
            tall,
            tall,
            tall,
            tall,
            tall,
            tall,
            pltpu.VMEM((rows, states, groups, 128), F32),
            pltpu.VMEM((rows * states, 128), F32),
            pltpu.VMEM((rows * states, 128), F32),
            pltpu.VMEM((states, groups, 128), F32),
            pltpu.VMEM((states * groups, 128), F32),
            pltpu.VMEM((wide, rows), F32),
            pltpu.VMEM((places, states + 2, groups, 128), F32),
        ],
        input_output_aliases=aliases,
        compiler_params=params(),
        name="scan_gradients",
    )(coef, dt, decay, conv_out, gate, grad, step_weight, skip, *messages, *previous)


def conv_grad_kernel(places, low_rank, back_a, back_b, proj_ref, scan_ref, small_in, input_ref, rim_ref, weight_ref, bias_ref,
                     out_ref, tail_ref, small_ref, ext, grad):
    taps = weight_ref.shape[0]
    rows = input_ref.shape[0]
    fill_extended(ext, rim_ref, input_ref, taps)
    wide = proj_ref.shape[0]
    block = back_a.shape[0] // places
    ranks, coef_rows = low_rank // places, (wide - low_rank) // places
    back = (back_a[...].astype(F32) + back_b[...].astype(F32)).astype(BF).astype(F32)
    order = [back[q * block : q * block + ranks, :] for q in range(places)]
    order += [back[q * block + ranks : q * block + ranks + coef_rows, :] for q in range(places)]
    d_xc = dot(jnp.concatenate(order, axis=0).astype(BF), proj_ref[...], TN)
    sums = [jnp.zeros((1, input_ref.shape[1]), F32) for _ in range(taps + 1)]
    for start in range(0, rows, 16):
        here = slice(start, start + 16)
        pre = conv_block(ext, weight_ref, bias_ref[...], taps, start, 16)
        sig = sigmoid(pre)
        value = (d_xc[here, :] + scan_ref[here, :].astype(F32)) * (sig * (1.0 + pre * (1.0 - sig)))
        grad[here, :] = value
        for tap in range(taps):
            first = 8 - (taps - 1) + tap + start
            sums[tap] = sums[tap] + jnp.sum(value * ext[first : first + 16, :], axis=0, keepdims=True)
        sums[taps] = sums[taps] + jnp.sum(value, axis=0, keepdims=True)
    grad[rows : rows + 8, :] = jnp.zeros((8, grad.shape[1]), F32)
    for start in range(0, rows, 16):
        total = jnp.zeros((16, grad.shape[1]), F32)
        for tap in range(taps):
            first = start + taps - 1 - tap
            total = total + weight_ref[tap : tap + 1, :] * grad[first : first + 16, :]
        out_ref[start : start + 16, :] = total.astype(BF)
    tail_ref[...] = total
    small_ref[...] = jnp.concatenate(
        sums + [small_in[0 : 7 - taps, :], grad[0:8, :]], axis=0
    ).astype(BF)


def conv_grad_call(places, low_rank, backs, proj_weight, scan_part, small, conv_input, rim, weight, bias):
    rows, chans = conv_input.shape
    taps = weight.shape[0]
    wide = proj_weight.shape[0]
    width = min(512, chans)
    return pl.pallas_call(
        functools.partial(conv_grad_kernel, places, low_rank),
        grid=(chans // width,),
        in_specs=[
            whole(backs[0].shape),
            whole(backs[1].shape),
            columns(wide, width),
            columns(rows, width),
            columns(8, width),
            columns(rows, width),
            columns(taps - 1, width),
            columns(taps, width),
            columns(1, width),
        ],
        out_specs=[columns(rows, width), columns(16, width), columns(16, width)],
        out_shape=[sds((rows, chans), BF), sds((16, chans), F32), sds((16, chans), BF)],
        scratch_shapes=[pltpu.VMEM((rows + 8, width), F32), pltpu.VMEM((rows + 8, width), F32)],
        compiler_params=params(),
        name="conv_gradients",
    )(*backs, proj_weight, scan_part, small, conv_input, rim, weight, bias)


def rows_kernel(places, rank_rows, chunks, *refs):
    cut_ref, refs = refs[0], refs[1:]
    blocks, refs = refs[:places], refs[places:]
    steps, refs = refs[: chunks * places], refs[chunks * places :]
    out_ref, coef_ref, step_ref, decay_ref = refs
    place = lax.axis_index("ctx")
    rows = blocks[0].shape[0]
    back_rows = cut_ref.shape[1] - rank_rows
    total = jnp.zeros((back_rows, out_ref.shape[1]), F32)
    for mask in range(places):
        total = total + dot(cut_ref[place ^ mask, :back_rows, :], blocks[mask][...])
    out_ref[...] = total[:rank_rows, :]
    coef_ref[...] = total[rank_rows : rank_rows + coef_ref.shape[0], :]
    for chunk in range(chunks):

        @pl.when(pl.program_id(0) == chunk)
        def _():
            total = jnp.zeros(step_ref.shape, F32)
            decay = jnp.zeros(decay_ref.shape, F32)
            for mask in range(places):
                step = steps[chunk * places + mask]
                total = total + dot(cut_ref[place ^ mask, back_rows:, :], step[:rows, :])
                decay = decay + step[rows:, :].astype(F32)
            step_ref[...] = total
            decay_ref[...] = decay


def rows_call(places, rank_rows, coef_rows, cuts, blocks, steps):
    rows, chans = blocks[0].shape
    chunks = len(steps) // places
    tall, width = steps[0].shape
    heights = (rank_rows, coef_rows, rank_rows, tall - rows)
    return pl.pallas_call(
        functools.partial(rows_kernel, places, rank_rows, chunks),
        grid=(chunks,),
        in_specs=[whole(cuts.shape)]
        + [columns(rows, width)] * places
        + [whole((tall, width))] * (chunks * places),
        out_specs=[columns(height, width) for height in heights],
        out_shape=[sds((height, chans), F32) for height in heights],
        compiler_params=params(),
        name="row_gradients",
    )(cuts, *blocks, *steps)


def last_kernel(places, taps, *refs):
    (_, tail_ref, weight_ref) = refs[:3]
    late, refs = refs[3 : 3 + places], refs[3 + places :]
    (out_ref, conv_w, conv_b, step_b, skip, fix) = refs
    fix[...] = tail_ref[...]
    inside = lax.axis_index("ctx") < places - 1
    following = jnp.where(inside, late[places - 1][8:16, :].astype(F32), 0.0)
    for row in range(taps - 1):
        extra = jnp.zeros((1, fix.shape[1]), F32)
        for tap in range(row + 1):
            extra = extra + weight_ref[tap : tap + 1, :] * following[row - tap : row - tap + 1, :]
        at = 16 - (taps - 1) + row
        fix[at : at + 1, :] += extra
    out_ref[...] = fix[...].astype(BF)
    total = late[0][...].astype(F32)
    for part in late[1:]:
        total = total + part[...].astype(F32)
    conv_w[...] = total[:taps, :]
    conv_b[...] = total[taps : taps + 1, :]
    step_b[...] = total[taps + 1 : taps + 2, :]
    skip[...] = total[taps + 2 : taps + 3, :]


def last_call(main, tail, weight, late):
    rows, chans = main.shape
    taps = weight.shape[0]
    places = len(late)
    return pl.pallas_call(
        functools.partial(last_kernel, places, taps),
        grid=(1,),
        in_specs=[pl.BlockSpec(memory_space=pl.ANY), columns(16, chans), columns(taps, chans)]
        + [columns(16, chans)] * places,
        out_specs=[
            pl.BlockSpec((16, chans), lambda i: (rows // 16 - 1, i)),
            columns(taps, chans),
        ]
        + [columns(1, chans)] * 3,
        out_shape=[sds((rows, chans), BF), sds((taps, chans), F32)] + [sds((1, chans), F32)] * 3,
        scratch_shapes=[pltpu.VMEM((16, chans), F32)],
        input_output_aliases={0: 0},
        compiler_params=params(),
        name="last_rows",
    )(main, tail, weight, *late)


def exchange(block, axis):
    return lax.all_to_all(block, axis, split_axis=0, concat_axis=0, tiled=True)


def swap(block, axis, mask):
    return lax.ppermute(block, axis, [(i, i ^ mask) for i in range(lax.axis_size(axis))])


def chan_sum(part):
    mask, peers = 1, lax.axis_size("chan")
    while True:
        other = swap(part, "chan", mask)
        mask *= 2
        if mask == peers:
            return part, other
        part = (part.astype(F32) + other.astype(F32)).astype(BF)


def body(
    conv_input,
    gate_input,
    out_grad,
    conv_weight,
    conv_bias,
    proj_weight,
    step_weight,
    step_bias,
    decay_log,
    skip_gain,
):
    rows, chans = conv_input.shape
    taps = conv_weight.shape[0]
    low_rank = step_weight.shape[0]
    states = decay_log.shape[0]
    places = lax.axis_size("ctx")
    groups = group_rows(chans)
    decay = decay_log.reshape(states, -1, groups, 128).transpose(1, 0, 2, 3)
    conv_bias = conv_bias[None, :]
    step_bias = step_bias[None, :]
    skip_gain = skip_gain[None, :]

    chunks = decay.shape[0]
    rim = shift(conv_input[rows - (taps - 1) :], "ctx", 1)
    conv_out, part = conv_call(conv_input, rim, conv_weight, conv_bias, proj_weight)
    blocks = [conv_out] + [swap(conv_out, "ctx", mask) for mask in range(1, min(places, 3))]
    parts = chan_sum(part)
    dt, coef, low, low_t, *messages = local_call(
        parts, step_weight, step_bias, decay, conv_out, gate_input, out_grad, states, places
    )
    messages = [swap(message, "ctx", mask) for mask, message in enumerate(messages, 1)]
    messages, held = lax.optimization_barrier((messages, conv_out))
    blocks += [swap(held, "ctx", mask) for mask in range(3, places)]
    previous, steps = [], []
    for chunk in range(chunks):
        pre_bf, grad_gate, scan_part, small, part = scan_call(
            places, chunk, coef, dt, decay, conv_out, gate_input, out_grad, step_weight,
            skip_gain, messages, previous,
        )
        previous = [part, grad_gate, scan_part, small]
        steps += [pre_bf] + [swap(pre_bf, "ctx", mask) for mask in range(1, places)]
    backs = chan_sum(part)
    cuts = jnp.concatenate(
        [
            (backs[0].astype(F32) + backs[1].astype(F32)).astype(BF).reshape(places, -1, rows),
            low_t.reshape(places, -1, rows),
        ],
        axis=1,
    )
    cuts = exchange(cuts, "ctx")
    main, tail, sums = conv_grad_call(
        places, low_rank, backs, proj_weight, scan_part, small, conv_input, rim, conv_weight,
        conv_bias,
    )
    late = [sums] + [rotate(sums, "ctx", hop) for hop in range(1, places)]
    grad_proj, grad_coef, grad_step, decay_grad = rows_call(
        places, low_rank // places, 2 * states // places, cuts, blocks, steps
    )
    grad_input, conv_w, conv_b, step_b, skip = last_call(main, tail, conv_weight, late)
    return (
        grad_input,
        grad_gate,
        grad_proj,
        grad_coef,
        grad_step,
        conv_w,
        conv_b[0],
        step_b[0],
        decay_grad,
        skip[0],
    )


def solution(mesh):
    tokens, columns_, chan = P("ctx", "chan"), P(None, "chan"), P("chan")
    in_specs = (
        tokens, tokens, tokens, columns_, chan, columns_, columns_, chan, columns_, chan,
    )
    out_specs = (
        tokens, tokens, tokens, tokens, tokens, columns_, chan, chan, columns_, chan,
    )
    return jax.shard_map(body, mesh=mesh, in_specs=in_specs, out_specs=out_specs, check_vma=False)
```

```python
import functools

import jax
import jax.numpy as jnp
from jax import lax
from jax.experimental import pallas as pl
from jax.experimental.pallas import tpu as pltpu
from jax.sharding import PartitionSpec as P

BF = jnp.bfloat16
F32 = jnp.float32
LOG2E = 1.4426950408889634
LN2 = 0.6931471805599453
VMEM_BYTES = 56 * 1024 * 1024
NT = (((1,), (1,)), ((), ()))
TN = (((0,), (0,)), ((), ()))


def group_rows(chans):
    for rows in (8, 4, 2, 1):
        if chans % (rows * 128) == 0:
            return rows
    return 1


def dot(a, b, dims=(((1,), (0,)), ((), ()))):
    return lax.dot_general(a, b, dims, preferred_element_type=F32)


def params(**more):
    return pltpu.CompilerParams(vmem_limit_bytes=VMEM_BYTES, **more)


def sds(shape, dtype):
    return jax.ShapeDtypeStruct(shape, dtype)


def whole(shape):
    return pl.BlockSpec(shape, lambda i: (0,) * len(shape))


def columns(rows, width):
    return pl.BlockSpec((rows, width), lambda i: (0, i))


def sigmoid(v):
    return 1.0 / (1.0 + jnp.exp(-v))


def rotate(block, axis, distance):
    count = lax.axis_size(axis)
    return lax.ppermute(block, axis, [(i, (i + distance) % count) for i in range(count)])


def shift(block, axis, distance):
    count = lax.axis_size(axis)
    route = [(i, i + distance) for i in range(count) if 0 <= i + distance < count]
    return lax.ppermute(block, axis, route)


def fill_extended(ext, rim_ref, input_ref, taps):
    rows = input_ref.shape[0]
    ext[8 - (taps - 1) : 8, :] = rim_ref[...].astype(F32)
    ext[8 : 8 + rows, :] = input_ref[...].astype(F32)


def conv_block(ext, weight, bias, taps, start, rows):
    total = bias + jnp.zeros((rows, ext.shape[1]), F32)
    for tap in range(taps):
        first = 8 - (taps - 1) + tap + start
        total = total + weight[tap : tap + 1, :] * ext[first : first + rows, :]
    return total


def conv_kernel(input_ref, rim_ref, weight_ref, bias_ref, proj_ref, out_ref, part_ref, ext, acc):
    step = pl.program_id(0)
    taps = weight_ref.shape[0]
    rows = input_ref.shape[0]
    fill_extended(ext, rim_ref, input_ref, taps)
    for start in range(0, rows, 16):
        pre = conv_block(ext, weight_ref, bias_ref[...], taps, start, 16)
        out_ref[start : start + 16, :] = (pre * sigmoid(pre)).astype(BF)
    part = dot(out_ref[...], proj_ref[...], NT)

    @pl.when(step == 0)
    def _():
        acc[...] = part

    @pl.when(step > 0)
    def _():
        acc[...] += part

    @pl.when(step == pl.num_programs(0) - 1)
    def _():
        part_ref[...] = acc[...].astype(BF)


def conv_call(conv_input, rim, weight, bias, proj_weight):
    rows, chans = conv_input.shape
    taps = weight.shape[0]
    wide = proj_weight.shape[0]
    width = min(512, chans)
    return pl.pallas_call(
        conv_kernel,
        grid=(chans // width,),
        in_specs=[
            columns(rows, width),
            columns(taps - 1, width),
            columns(taps, width),
            columns(1, width),
            columns(wide, width),
        ],
        out_specs=[columns(rows, width), whole((rows, wide))],
        out_shape=[sds((rows, chans), BF), sds((rows, wide), BF)],
        scratch_shapes=[pltpu.VMEM((rows + 8, width), F32), pltpu.VMEM((rows, wide), F32)],
        compiler_params=params(),
        name="conv_project",
    )(conv_input, rim, weight, bias, proj_weight)


def tile_rows(value, target, lead, groups):
    rows = value.shape[0]
    for block in range(rows // 8):
        for group in range(groups):
            first = (block * groups + group) * 8
            target[lead, first : first + 8, :] = value[
                block * 8 : block * 8 + 8, group * 128 : group * 128 + 128
            ]


def local_kernel(low_rank, states, places, *refs):
    parts, refs = refs[:2], refs[2:]
    (weight_ref, bias_ref, decay_ref, conv_ref, gate_ref, grad_ref) = refs[:6]
    (dt_ref, coef_ref, low, low_t) = refs[6:10]
    messages, refs = refs[10 : 9 + places], refs[9 + places :]
    (proj, coef_v, coef, dts, dxs, gs, fwd, bwd, sem) = refs
    step = pl.program_id(0)
    chunks = dts.shape[0]
    rows = conv_ref.shape[0]
    groups = decay_ref.shape[2]

    @pl.when(step == 0)
    def _():
        total = (parts[0][...].astype(F32) + parts[1][...].astype(F32)).astype(BF)
        proj[...] = total.astype(F32)
        low[...] = total[:, :low_rank]
        low_t[...] = jnp.transpose(proj[:, :low_rank]).astype(BF)
        coef_v[...] = jnp.zeros_like(coef_v)
        coef_v[:, : 2 * states] = proj[:, low_rank:]
        coef_ref[...] = coef_v[...]
        copy = pltpu.make_async_copy(coef_v, coef, sem)
        copy.start()
        copy.wait()

    pre = dot(low[...], weight_ref[...]) + bias_ref[...]
    for start in range(0, rows, 16):
        here = slice(start, start + 16)
        p = pre[here, :]
        size = jnp.maximum(p, 0.0) + jnp.log1p(jnp.exp(-jnp.abs(p)))
        gate = gate_ref[here, :].astype(F32)
        grad = grad_ref[here, :].astype(F32) * gate * sigmoid(gate)
        drive = size * conv_ref[here, :].astype(F32)
        for half in range(2):
            for group in range(groups):
                first = ((start // 8 + half) * groups + group) * 8
                lanes = slice(group * 128, group * 128 + 128)
                subs = slice(half * 8, half * 8 + 8)
                dts[step, first : first + 8, :] = size[subs, lanes]
                dt_ref[0, first : first + 8, :] = size[subs, lanes]
                dxs[step, first : first + 8, :] = drive[subs, lanes]
                gs[step, first : first + 8, :] = grad[subs, lanes]

    @pl.when(step == chunks - 1)
    def _():
        batch = 4
        span = groups * 8
        zero = jnp.zeros((groups, 128), F32)
        for lead in range(0, states, batch):
            pairs = [(n, v) for n in range(lead, lead + batch) for v in range(chunks)]
            rates = [-LOG2E * jnp.exp(decay_ref[v, n]) for n, v in pairs]

            def block(index, carry):
                state, run, head, total = (list(part) for part in carry)
                for sub in range(8):
                    token = index * 8 + sub
                    at = pl.ds(index * span + sub, groups, stride=8)
                    size = [dts[v, at, :] for v in range(chunks)]
                    drive = [dxs[v, at, :] for v in range(chunks)]
                    grad = [gs[v, at, :] for v in range(chunks)]
                    if lead == 0:
                        total = [a + b for a, b in zip(total, size)]
                    for k, (n, v) in enumerate(pairs):
                        factor = jnp.exp2(size[v] * rates[k])
                        state[k] = factor * state[k] + drive[v] * coef[token, n]
                        run[k] = run[k] * factor
                        head[k] = head[k] + run[k] * (grad[v] * coef[token, states + n])
                return state, run, head, total

            many = [zero] * len(pairs)
            state, run, head, total = lax.fori_loop(
                0,
                rows // 8,
                block,
                (many, [zero + 1.0] * len(pairs), many, [zero] * chunks),
            )
            for k, (n, v) in enumerate(pairs):
                fwd[v, n] = state[k]
                bwd[v, n] = head[k]
            if lead == 0:
                for v in range(chunks):
                    coarse = total[v].astype(BF).astype(F32)
                    for target in (fwd, bwd):
                        target[v, states] = coarse
                        target[v, states + 1] = total[v] - coarse
        place = lax.axis_index("ctx")
        for mask, message in enumerate(messages, 1):
            message[...] = jnp.where((place ^ mask) > place, fwd[...], bwd[...]).astype(BF)


def local_call(parts, step_weight, step_bias, decay, conv_out, gate, grad, states, places):
    rows, chans = conv_out.shape
    wide = parts[0].shape[1]
    low_rank = step_weight.shape[0]
    chunks, _, groups, _ = decay.shape
    width = groups * 128
    message = (chunks, states + 2, groups, 128)
    big = pltpu.VMEM((chunks, rows * groups, 128), F32)
    return pl.pallas_call(
        functools.partial(local_kernel, low_rank, states, places),
        grid=(chunks,),
        in_specs=[
            whole((rows, wide)),
            whole((rows, wide)),
            columns(low_rank, width),
            columns(1, width),
            whole(decay.shape),
            columns(rows, width),
            columns(rows, width),
            columns(rows, width),
        ],
        out_specs=[
            pl.BlockSpec((1, rows * groups, 128), lambda i: (i, 0, 0)),
            whole((rows, 128)),
            whole((rows, low_rank)),
            whole((low_rank, rows)),
        ]
        + [whole(message)] * (places - 1),
        out_shape=[
            sds((chunks, rows * groups, 128), F32),
            sds((rows, 128), F32),
            sds((rows, low_rank), BF),
            sds((low_rank, rows), BF),
        ]
        + [sds(message, BF)] * (places - 1),
        scratch_shapes=[
            pltpu.VMEM((rows, wide), F32),
            pltpu.VMEM((rows, 128), F32),
            pltpu.SMEM((rows, 128), F32),
            big,
            big,
            big,
            pltpu.VMEM(message, F32),
            pltpu.VMEM(message, F32),
            pltpu.SemaphoreType.DMA,
        ],
        compiler_params=params(),
        name="local_ends",
    )(*parts, step_weight, step_bias, decay, conv_out, gate, grad)


def fold_sublanes(values):
    rows = lax.broadcasted_iota(jnp.int32, (8, 128), 0)
    if values[0].shape[0] != 8:
        result = jnp.zeros((8, 128), F32)
        for i, value in enumerate(values):
            result = jnp.where(rows == i, jnp.sum(value, axis=0, keepdims=True), result)
        return result
    distance = 4
    while len(values) > 1:
        half = len(values) // 2
        low = (rows & distance) == 0
        values = [
            jnp.where(low, a, b) + pltpu.roll(jnp.where(low, b, a), distance, 0)
            if distance == 4
            else jnp.where(low, a, pltpu.roll(b, distance, 0))
            + jnp.where(low, pltpu.roll(a, 8 - distance, 0), b)
            for a, b in zip(values[:half], values[half:])
        ]
        distance //= 2
    return values[0]


def scan_kernel(places, states, opening, *refs):
    (coef, dt_ref, decay_ref, conv_ref, gate_ref, grad_ref, weight_ref, skip_ref) = refs[:8]
    messages, refs = refs[8 : 7 + places], refs[7 + places :]
    if not opening:
        before_ref, refs = refs[0], refs[4:]
    (pre_ref, gate_out, scan_out, small_ref, part_ref) = refs[:5]
    refs = refs[5:]
    (xs, dxs, gs, ys, dds, qs, decayed, coef_out, coef_in, rate, decay_acc, acc, ends) = refs
    rows = conv_ref.shape[0]
    groups = decay_ref.shape[2]
    low_rank = weight_ref.shape[0]
    span = groups * 8

    for start in range(0, rows, 16):
        here = slice(start, start + 16)
        conv = conv_ref[here, :].astype(F32)
        gate = gate_ref[here, :].astype(F32)
        grad = grad_ref[here, :].astype(F32) * gate * sigmoid(gate)
        for half in range(2):
            for group in range(groups):
                first = ((start // 8 + half) * groups + group) * 8
                lanes = slice(group * 128, group * 128 + 128)
                subs = slice(half * 8, half * 8 + 8)
                xs[first : first + 8, :] = conv[subs, lanes]
                dxs[first : first + 8, :] = conv[subs, lanes] * dt_ref[0, first : first + 8, :]
                gs[first : first + 8, :] = grad[subs, lanes]

    place = lax.axis_index("ctx")
    for n in range(states):
        rate[n] = -LOG2E * jnp.exp(decay_ref[0, n])
    ends[place] = jnp.zeros(ends.shape[1:], F32)
    for mask, message in enumerate(messages, 1):
        ends[place ^ mask] = message[0].astype(F32)
    totals = [ends[q, states] + ends[q, states + 1] for q in range(places)]
    state, carry = [], []
    for n in range(states):
        before = jnp.zeros((groups, 128), F32)
        after = jnp.zeros((groups, 128), F32)
        for q in range(places - 1):
            reached = jnp.exp2(rate[n] * totals[q]) * before + ends[q, n]
            before = jnp.where(q < place, reached, before)
        for q in range(places - 1, 0, -1):
            reached = jnp.exp2(rate[n] * totals[q]) * after + ends[q, n]
            after = jnp.where(q > place, reached, after)
        state.append(before)
        carry.append(after)

    def forward(index, state):
        state = list(state)
        for sub in range(8):
            token = index * 8 + sub
            at = pl.ds(index * span + sub, groups, stride=8)
            size, drive, grad = dt_ref[0, at, :], dxs[at, :], gs[at, :]
            result = jnp.zeros((groups, 128), F32)
            for lead in range(0, states, 8):
                products = []
                for n in range(lead, lead + 8):
                    kept = jnp.exp2(size * rate[n]) * state[n]
                    decayed[token, n] = kept
                    state[n] = kept + drive * coef[token, n]
                    result = result + state[n] * coef[token, states + n]
                    products.append(state[n] * grad)
                coef_out[pl.ds(pl.multiple_of(token * states + lead, 8), 8), :] = fold_sublanes(
                    products
                )
            ys[at, :] = result
        return state

    lax.fori_loop(0, rows // 8, forward, state)

    def backward(hop, both):
        carry, gathered = list(both[0]), list(both[1])
        index = rows // 8 - 1 - hop
        for sub in range(7, -1, -1):
            token = index * 8 + sub
            at = pl.ds(index * span + sub, groups, stride=8)
            size, drive, grad = dt_ref[0, at, :], dxs[at, :], gs[at, :]
            slope = jnp.zeros((groups, 128), F32)
            inner = jnp.zeros((groups, 128), F32)
            for lead in range(0, states, 8):
                products = []
                for n in range(lead, lead + 8):
                    adjoint = carry[n] + grad * coef[token, states + n]
                    carry[n] = jnp.exp2(size * rate[n]) * adjoint
                    weighted = adjoint * decayed[token, n]
                    slope = slope + weighted * rate[n]
                    gathered[n] = gathered[n] + weighted * size
                    inner = inner + adjoint * coef[token, n]
                    products.append(adjoint * drive)
                coef_in[pl.ds(pl.multiple_of(token * states + lead, 8), 8), :] = fold_sublanes(
                    products
                )
            dds[at, :] = slope
            qs[at, :] = inner
        return carry, gathered

    zeros = [jnp.zeros((groups, 128), F32)] * states
    _, gathered = lax.fori_loop(0, rows // 8, backward, (carry, zeros))
    for n in range(states):
        decay_acc[n * groups : n * groups + groups, :] = gathered[n] * (rate[n] * LN2)

    for group in range(groups):
        pre_ref[rows : rows + states, group * 128 : group * 128 + 128] = decay_acc[
            pl.ds(group, states, stride=groups), :
        ].astype(BF)
    skip = skip_ref[...]
    bias_sum = jnp.zeros((1, conv_ref.shape[1]), F32)
    skip_sum = jnp.zeros((1, conv_ref.shape[1]), F32)
    for start in range(0, rows, 16):
        here = slice(start, start + 16)

        def natural(read):
            return jnp.concatenate(
                [
                    jnp.concatenate(
                        [
                            read(((start // 8 + half) * groups + group) * 8)
                            for group in range(groups)
                        ],
                        axis=1,
                    )
                    for half in range(2)
                ],
                axis=0,
            )

        size = natural(lambda first: dt_ref[0, first : first + 8, :])
        inner = natural(lambda first: qs[first : first + 8, :])
        slope = natural(lambda first: dds[first : first + 8, :])
        out = natural(lambda first: ys[first : first + 8, :])
        conv = conv_ref[here, :].astype(F32)
        gate = gate_ref[here, :].astype(F32)
        grad = grad_ref[here, :].astype(F32)
        sig = sigmoid(gate)
        scan_grad = grad * gate * sig
        tiny = size * (1.0 - 0.5 * size * (1.0 - size * (1.0 / 3.0) * (1.0 - 0.25 * size)))
        step_slope = jnp.where(size < 0.03, tiny, 1.0 - jnp.exp(-size))
        d_pre = (LN2 * slope + conv * inner) * step_slope
        pre_ref[here, :] = d_pre.astype(BF)
        bias_sum = bias_sum + jnp.sum(d_pre, axis=0, keepdims=True)
        skip_sum = skip_sum + jnp.sum(scan_grad * conv, axis=0, keepdims=True)
        scan_out[here, :] = (size * inner + skip * scan_grad).astype(BF)
        gate_out[here, :] = (
            grad * (out + skip * conv) * (sig * (1.0 + gate * (1.0 - sig)))
        ).astype(BF)
    small_ref[...] = jnp.concatenate(
        [bias_sum, skip_sum, jnp.zeros((6, bias_sum.shape[1]), F32)], axis=0
    )

    pre_bf = pre_ref[:rows, :]
    lanes = lax.broadcasted_iota(jnp.int32, (2 * states, 128), 0)
    coefs = jnp.zeros((2 * states, rows), F32)
    for n in range(states):
        at = pl.ds(n, rows, stride=states)
        for kind, source in enumerate((coef_in, coef_out)):
            pick = jnp.where(lanes == kind * states + n, 1.0, 0.0).astype(BF)
            coefs = coefs + dot(pick, source[at, :].astype(BF), NT)
    wide = dot(weight_ref[...], pre_bf, NT)

    ranks, coef_rows, block = low_rank // places, 2 * states // places, acc.shape[0] // places

    acc[...] = jnp.zeros_like(acc) if opening else before_ref[...]
    for q in range(places):
        at = q * block
        acc[at : at + ranks, :] += wide[q * ranks : (q + 1) * ranks, :]
        acc[at + ranks : at + ranks + coef_rows, :] += coefs[
            q * coef_rows : (q + 1) * coef_rows, :
        ]
    part_ref[...] = acc[...].astype(part_ref.dtype)


def padded(wide):
    return (wide + 127) // 128 * 128


def scan_call(
    places, chunk, coef, dt, decay, conv_out, gate, grad, step_weight, skip, messages, previous
):
    rows, chans = conv_out.shape
    low_rank = step_weight.shape[0]
    chunks, states, groups, _ = decay.shape
    width = groups * 128
    wide = padded(low_rank + 2 * states)
    lead = lambda *shape: pl.BlockSpec((1,) + shape, lambda i: (chunk,) + (0,) * len(shape))
    here = lambda height: pl.BlockSpec((height, width), lambda i: (0, chunk))
    tall = pltpu.VMEM((rows * groups, 128), F32)
    first, last = chunk == 0, chunk == chunks - 1
    in_specs = [
        pl.BlockSpec(memory_space=pltpu.SMEM),
        lead(rows * groups, 128),
        lead(states, groups, 128),
        here(rows),
        here(rows),
        here(rows),
        here(low_rank),
        here(1),
    ]
    in_specs += [lead(states + 2, groups, 128)] * (places - 1)
    aliases = {}
    if not first:
        in_specs += [whole((wide, rows))] + [pl.BlockSpec(memory_space=pl.ANY)] * 3
        aliases = {8 + places: 1, 9 + places: 2, 10 + places: 3}
    return pl.pallas_call(
        functools.partial(scan_kernel, places, states, first),
        grid=(1,),
        in_specs=in_specs,
        out_specs=[
            whole((rows + states, width)),
            here(rows),
            here(rows),
            here(8),
            whole((wide, rows)),
        ],
        out_shape=[
            sds((rows + states, width), BF),
            sds((rows, chans), BF),
            sds((rows, chans), BF),
            sds((8, chans), F32),
            sds((wide, rows), BF if last else F32),
        ],
        scratch_shapes=[
            tall,
            tall,
            tall,
            tall,
            tall,
            tall,
            pltpu.VMEM((rows, states, groups, 128), F32),
            pltpu.VMEM((rows * states, 128), F32),
            pltpu.VMEM((rows * states, 128), F32),
            pltpu.VMEM((states, groups, 128), F32),
            pltpu.VMEM((states * groups, 128), F32),
            pltpu.VMEM((wide, rows), F32),
            pltpu.VMEM((places, states + 2, groups, 128), F32),
        ],
        input_output_aliases=aliases,
        compiler_params=params(),
        name="scan_gradients",
    )(coef, dt, decay, conv_out, gate, grad, step_weight, skip, *messages, *previous)


def conv_grad_kernel(places, low_rank, back_a, back_b, proj_ref, scan_ref, small_in, input_ref, rim_ref, weight_ref, bias_ref,
                     out_ref, tail_ref, small_ref, ext, grad):
    taps = weight_ref.shape[0]
    rows = input_ref.shape[0]
    fill_extended(ext, rim_ref, input_ref, taps)
    wide = proj_ref.shape[0]
    block = back_a.shape[0] // places
    ranks, coef_rows = low_rank // places, (wide - low_rank) // places
    back = (back_a[...].astype(F32) + back_b[...].astype(F32)).astype(BF).astype(F32)
    order = [back[q * block : q * block + ranks, :] for q in range(places)]
    order += [back[q * block + ranks : q * block + ranks + coef_rows, :] for q in range(places)]
    d_xc = dot(jnp.concatenate(order, axis=0).astype(BF), proj_ref[...], TN)
    sums = [jnp.zeros((1, input_ref.shape[1]), F32) for _ in range(taps + 1)]
    for start in range(0, rows, 16):
        here = slice(start, start + 16)
        pre = conv_block(ext, weight_ref, bias_ref[...], taps, start, 16)
        sig = sigmoid(pre)
        value = (d_xc[here, :] + scan_ref[here, :].astype(F32)) * (sig * (1.0 + pre * (1.0 - sig)))
        grad[here, :] = value
        for tap in range(taps):
            first = 8 - (taps - 1) + tap + start
            sums[tap] = sums[tap] + jnp.sum(value * ext[first : first + 16, :], axis=0, keepdims=True)
        sums[taps] = sums[taps] + jnp.sum(value, axis=0, keepdims=True)
    grad[rows : rows + 8, :] = jnp.zeros((8, grad.shape[1]), F32)
    for start in range(0, rows, 16):
        total = jnp.zeros((16, grad.shape[1]), F32)
        for tap in range(taps):
            first = start + taps - 1 - tap
            total = total + weight_ref[tap : tap + 1, :] * grad[first : first + 16, :]
        out_ref[start : start + 16, :] = total.astype(BF)
    tail_ref[...] = total
    small_ref[...] = jnp.concatenate(
        sums + [small_in[0 : 7 - taps, :], grad[0:8, :]], axis=0
    ).astype(BF)


def conv_grad_call(places, low_rank, backs, proj_weight, scan_part, small, conv_input, rim, weight, bias):
    rows, chans = conv_input.shape
    taps = weight.shape[0]
    wide = proj_weight.shape[0]
    width = min(512, chans)
    return pl.pallas_call(
        functools.partial(conv_grad_kernel, places, low_rank),
        grid=(chans // width,),
        in_specs=[
            whole(backs[0].shape),
            whole(backs[1].shape),
            columns(wide, width),
            columns(rows, width),
            columns(8, width),
            columns(rows, width),
            columns(taps - 1, width),
            columns(taps, width),
            columns(1, width),
        ],
        out_specs=[columns(rows, width), columns(16, width), columns(16, width)],
        out_shape=[sds((rows, chans), BF), sds((16, chans), F32), sds((16, chans), BF)],
        scratch_shapes=[pltpu.VMEM((rows + 8, width), F32), pltpu.VMEM((rows + 8, width), F32)],
        compiler_params=params(),
        name="conv_gradients",
    )(*backs, proj_weight, scan_part, small, conv_input, rim, weight, bias)


def cut_kernel(places, *refs):
    back_a, back_b, low_t = refs[:3]
    cuts, (back,) = refs[3 : 3 + places], refs[3 + places :]
    place = lax.axis_index("ctx")
    back_rows, ranks = back.shape[0] // places, low_t.shape[0] // places
    back[...] = back_a[...].astype(F32) + back_b[...].astype(F32)
    for mask in range(places):
        other = place ^ mask
        cuts[mask][:back_rows, :] = back[pl.ds(other * back_rows, back_rows), :].astype(BF)
        cuts[mask][back_rows:, :] = low_t[pl.ds(pl.multiple_of(other * ranks, 16), ranks), :]


def cut_call(places, backs, low_t):
    wide, rows = backs[0].shape
    cut = ((wide + low_t.shape[0]) // places, rows)
    return pl.pallas_call(
        functools.partial(cut_kernel, places),
        out_shape=[sds(cut, BF)] * places,
        scratch_shapes=[pltpu.VMEM((wide, rows), F32)],
        compiler_params=params(),
        name="cut_rows",
    )(*backs, low_t)


def rows_kernel(places, rank_rows, chunks, *refs):
    cuts, refs = refs[:places], refs[places:]
    blocks, refs = refs[:places], refs[places:]
    steps, refs = refs[: chunks * places], refs[chunks * places :]
    out_ref, coef_ref, step_ref, decay_ref = refs
    place = lax.axis_index("ctx")
    rows = blocks[0].shape[0]
    back_rows = cuts[0].shape[0] - rank_rows
    total = jnp.zeros((back_rows, out_ref.shape[1]), F32)
    for cut, block in zip(cuts, blocks):
        total = total + dot(cut[:back_rows, :], block[...])
    out_ref[...] = total[:rank_rows, :]
    coef_ref[...] = total[rank_rows : rank_rows + coef_ref.shape[0], :]
    for chunk in range(chunks):

        @pl.when(pl.program_id(0) == chunk)
        def _():
            total = jnp.zeros(step_ref.shape, F32)
            decay = jnp.zeros(decay_ref.shape, F32)
            for mask in range(places):
                step = steps[chunk * places + mask]
                total = total + dot(cuts[mask][back_rows:, :], step[:rows, :])
                decay = decay + step[rows:, :].astype(F32)
            step_ref[...] = total
            decay_ref[...] = decay


def rows_call(places, rank_rows, coef_rows, cuts, blocks, steps):
    rows, chans = blocks[0].shape
    tall, width = steps[0].shape
    chunks = chans // width
    heights = (rank_rows, coef_rows, rank_rows, tall - rows)
    return pl.pallas_call(
        functools.partial(rows_kernel, places, rank_rows, chunks),
        grid=(chunks,),
        in_specs=[whole(cuts[0].shape)] * places
        + [columns(rows, width)] * places
        + [whole((tall, width))] * len(steps),
        out_specs=[columns(height, width) for height in heights],
        out_shape=[sds((height, chans), F32) for height in heights],
        compiler_params=params(),
        name="row_gradients",
    )(*cuts, *blocks, *steps)


def last_kernel(places, taps, *refs):
    (_, tail_ref, weight_ref) = refs[:3]
    late, refs = refs[3 : 3 + places], refs[3 + places :]
    (out_ref, conv_w, conv_b, step_b, skip, fix) = refs
    fix[...] = tail_ref[...]
    inside = lax.axis_index("ctx") < places - 1
    following = jnp.where(inside, late[places - 1][8:16, :].astype(F32), 0.0)
    for row in range(taps - 1):
        extra = jnp.zeros((1, fix.shape[1]), F32)
        for tap in range(row + 1):
            extra = extra + weight_ref[tap : tap + 1, :] * following[row - tap : row - tap + 1, :]
        at = 16 - (taps - 1) + row
        fix[at : at + 1, :] += extra
    out_ref[...] = fix[...].astype(BF)
    total = late[0][...].astype(F32)
    for part in late[1:]:
        total = total + part[...].astype(F32)
    conv_w[...] = total[:taps, :]
    conv_b[...] = total[taps : taps + 1, :]
    step_b[...] = total[taps + 1 : taps + 2, :]
    skip[...] = total[taps + 2 : taps + 3, :]


def last_call(main, tail, weight, late):
    rows, chans = main.shape
    taps = weight.shape[0]
    places = len(late)
    return pl.pallas_call(
        functools.partial(last_kernel, places, taps),
        grid=(1,),
        in_specs=[pl.BlockSpec(memory_space=pl.ANY), columns(16, chans), columns(taps, chans)]
        + [columns(16, chans)] * places,
        out_specs=[
            pl.BlockSpec((16, chans), lambda i: (rows // 16 - 1, i)),
            columns(taps, chans),
        ]
        + [columns(1, chans)] * 3,
        out_shape=[sds((rows, chans), BF), sds((taps, chans), F32)] + [sds((1, chans), F32)] * 3,
        scratch_shapes=[pltpu.VMEM((16, chans), F32)],
        input_output_aliases={0: 0},
        compiler_params=params(),
        name="last_rows",
    )(main, tail, weight, *late)


def exchange(block, axis):
    return lax.all_to_all(block, axis, split_axis=0, concat_axis=0, tiled=True)


def swap(block, axis, mask):
    return lax.ppermute(block, axis, [(i, i ^ mask) for i in range(lax.axis_size(axis))])


tie = lax.optimization_barrier


def spread(block):
    return [block] + [swap(block, "ctx", mask) for mask in range(1, min(lax.axis_size("ctx"), 3))]


def spread_on(blocks):
    places = lax.axis_size("ctx")
    if places == 4:
        return blocks + [swap(blocks[2], "ctx", 1)]
    return blocks + [swap(blocks[0], "ctx", mask) for mask in range(3, places)]


def chan_sum(part):
    mask, peers = 1, lax.axis_size("chan")
    while True:
        other = swap(part, "chan", mask)
        mask *= 2
        if mask == peers:
            return part, other
        part = (part.astype(F32) + other.astype(F32)).astype(BF)


def body(
    conv_input,
    gate_input,
    out_grad,
    conv_weight,
    conv_bias,
    proj_weight,
    step_weight,
    step_bias,
    decay_log,
    skip_gain,
):
    rows, chans = conv_input.shape
    taps = conv_weight.shape[0]
    low_rank = step_weight.shape[0]
    states = decay_log.shape[0]
    places = lax.axis_size("ctx")
    groups = group_rows(chans)
    decay = decay_log.reshape(states, -1, groups, 128).transpose(1, 0, 2, 3)
    conv_bias = conv_bias[None, :]
    step_bias = step_bias[None, :]
    skip_gain = skip_gain[None, :]

    chunks = decay.shape[0]
    rim = shift(conv_input[rows - (taps - 1) :], "ctx", 1)
    conv_out, part = conv_call(conv_input, rim, conv_weight, conv_bias, proj_weight)
    blocks = spread(conv_out)
    parts = chan_sum(part)
    dt, coef, low, low_t, *messages = local_call(
        parts, step_weight, step_bias, decay, conv_out, gate_input, out_grad, states, places
    )
    messages, blocks = tie((messages, blocks))
    messages = [swap(message, "ctx", mask) for mask, message in enumerate(messages, 1)]
    messages, blocks = tie((messages, blocks))
    blocks = spread_on(blocks)
    previous, steps, fresh = [], [], None
    for chunk in range(chunks):
        message, grad_gate, scan_part, small, part = scan_call(
            places, chunk, coef, dt, decay, conv_out, gate_input, out_grad, step_weight,
            skip_gain, messages, previous,
        )
        previous = [part, grad_gate, scan_part, small]
        if chunk == 0:
            previous, blocks = tie((previous, blocks))
        if fresh is not None:
            previous, fresh = tie((previous, fresh))
            steps += spread_on(fresh)
        fresh = spread(message)
    part, grad_gate, scan_part, small = previous
    backs = chan_sum(part)
    backs, steps, fresh = tie((backs, steps, fresh))
    steps += spread_on(fresh)
    cuts = cut_call(places, backs, low_t)
    cuts = [cuts[0]] + [swap(cut, "ctx", mask) for mask, cut in enumerate(cuts[1:], 1)]
    main, tail, sums = conv_grad_call(
        places, low_rank, backs, proj_weight, scan_part, small, conv_input, rim, conv_weight,
        conv_bias,
    )
    sums, cuts, steps = tie((sums, cuts, steps))
    late = [sums] + [rotate(sums, "ctx", hop) for hop in range(1, places)]
    grad_proj, grad_coef, grad_step, decay_grad = rows_call(
        places, low_rank // places, 2 * states // places, cuts, blocks, steps
    )
    grad_input, conv_w, conv_b, step_b, skip = last_call(main, tail, conv_weight, late)
    return (
        grad_input,
        grad_gate,
        grad_proj,
        grad_coef,
        grad_step,
        conv_w,
        conv_b[0],
        step_b[0],
        decay_grad,
        skip[0],
    )


def solution(mesh):
    tokens, columns_, chan = P("ctx", "chan"), P(None, "chan"), P("chan")
    in_specs = (
        tokens, tokens, tokens, columns_, chan, columns_, columns_, chan, columns_, chan,
    )
    out_specs = (
        tokens, tokens, tokens, tokens, tokens, columns_, chan, chan, columns_, chan,
    )
    return jax.shard_map(body, mesh=mesh, in_specs=in_specs, out_specs=out_specs, check_vma=False)
```

```python
import functools

import jax
import jax.numpy as jnp
from jax import lax
from jax.experimental import pallas as pl
from jax.experimental.pallas import tpu as pltpu
from jax.sharding import PartitionSpec as P

BF = jnp.bfloat16
F32 = jnp.float32
LOG2E = 1.4426950408889634
LN2 = 0.6931471805599453
VMEM_BYTES = 56 * 1024 * 1024
NT = (((1,), (1,)), ((), ()))
TN = (((0,), (0,)), ((), ()))


def group_rows(chans):
    for rows in (8, 4, 2, 1):
        if chans % (rows * 128) == 0:
            return rows
    return 1


def dot(a, b, dims=(((1,), (0,)), ((), ()))):
    return lax.dot_general(a, b, dims, preferred_element_type=F32)


def params(**more):
    return pltpu.CompilerParams(vmem_limit_bytes=VMEM_BYTES, **more)


def sds(shape, dtype):
    return jax.ShapeDtypeStruct(shape, dtype)


def whole(shape):
    return pl.BlockSpec(shape, lambda i: (0,) * len(shape))


def columns(rows, width):
    return pl.BlockSpec((rows, width), lambda i: (0, i))


def sigmoid(v):
    return 0.5 + 0.5 * jnp.tanh(0.5 * v)


def rotate(block, axis, distance):
    count = lax.axis_size(axis)
    return lax.ppermute(block, axis, [(i, (i + distance) % count) for i in range(count)])


def shift(block, axis, distance):
    count = lax.axis_size(axis)
    route = [(i, i + distance) for i in range(count) if 0 <= i + distance < count]
    return lax.ppermute(block, axis, route)


def fill_extended(ext, rim_ref, input_ref, taps):
    rows = input_ref.shape[0]
    ext[8 - (taps - 1) : 8, :] = rim_ref[...].astype(F32)
    ext[8 : 8 + rows, :] = input_ref[...].astype(F32)


def conv_block(ext, weight, bias, taps, start, rows):
    total = bias + jnp.zeros((rows, ext.shape[1]), F32)
    for tap in range(taps):
        first = 8 - (taps - 1) + tap + start
        total = total + weight[tap : tap + 1, :] * ext[first : first + rows, :]
    return total


def conv_kernel(input_ref, rim_ref, weight_ref, bias_ref, proj_ref, out_ref, part_ref, ext, acc):
    step = pl.program_id(0)
    taps = weight_ref.shape[0]
    rows = input_ref.shape[0]
    fill_extended(ext, rim_ref, input_ref, taps)
    for start in range(0, rows, 16):
        pre = conv_block(ext, weight_ref, bias_ref[...], taps, start, 16)
        out_ref[start : start + 16, :] = (pre * sigmoid(pre)).astype(BF)
    part = dot(out_ref[...], proj_ref[...], NT)

    @pl.when(step == 0)
    def _():
        acc[...] = part

    @pl.when(step > 0)
    def _():
        acc[...] += part

    @pl.when(step == pl.num_programs(0) - 1)
    def _():
        part_ref[...] = acc[...].astype(BF)


def conv_call(conv_input, rim, weight, bias, proj_weight):
    rows, chans = conv_input.shape
    taps = weight.shape[0]
    wide = proj_weight.shape[0]
    width = min(512, chans)
    return pl.pallas_call(
        conv_kernel,
        grid=(chans // width,),
        in_specs=[
            columns(rows, width),
            columns(taps - 1, width),
            columns(taps, width),
            columns(1, width),
            columns(wide, width),
        ],
        out_specs=[columns(rows, width), whole((rows, wide))],
        out_shape=[sds((rows, chans), BF), sds((rows, wide), BF)],
        scratch_shapes=[pltpu.VMEM((rows + 8, width), F32), pltpu.VMEM((rows, wide), F32)],
        compiler_params=params(),
        name="conv_project",
    )(conv_input, rim, weight, bias, proj_weight)


def tile_rows(value, target, lead, groups):
    rows = value.shape[0]
    for block in range(rows // 8):
        for group in range(groups):
            first = (block * groups + group) * 8
            target[lead, first : first + 8, :] = value[
                block * 8 : block * 8 + 8, group * 128 : group * 128 + 128
            ]


def local_kernel(low_rank, states, places, *refs):
    parts, refs = refs[:2], refs[2:]
    (weight_ref, bias_ref, decay_ref, conv_ref, gate_ref, grad_ref) = refs[:6]
    (dt_ref, coef_ref, low, low_t) = refs[6:10]
    messages, refs = refs[10 : 9 + places], refs[9 + places :]
    (proj, coef_v, coef, dts, dxs, gs, fwd, bwd, sem) = refs
    step = pl.program_id(0)
    chunks = dts.shape[0]
    rows = conv_ref.shape[0]
    groups = decay_ref.shape[2]

    @pl.when(step == 0)
    def _():
        total = (parts[0][...].astype(F32) + parts[1][...].astype(F32)).astype(BF)
        proj[...] = total.astype(F32)
        low[...] = total[:, :low_rank]
        low_t[...] = jnp.transpose(proj[:, :low_rank]).astype(BF)
        coef_v[...] = jnp.zeros_like(coef_v)
        coef_v[:, : 2 * states] = proj[:, low_rank:]
        coef_ref[...] = coef_v[...]
        copy = pltpu.make_async_copy(coef_v, coef, sem)
        copy.start()
        copy.wait()

    pre = dot(low[...], weight_ref[...]) + bias_ref[...]
    for start in range(0, rows, 16):
        here = slice(start, start + 16)
        p = pre[here, :]
        size = jnp.maximum(p, 0.0) + jnp.log1p(jnp.exp(-jnp.abs(p)))
        gate = gate_ref[here, :].astype(F32)
        grad = grad_ref[here, :].astype(F32) * gate * sigmoid(gate)
        drive = size * conv_ref[here, :].astype(F32)
        for half in range(2):
            for group in range(groups):
                first = ((start // 8 + half) * groups + group) * 8
                lanes = slice(group * 128, group * 128 + 128)
                subs = slice(half * 8, half * 8 + 8)
                dts[step, first : first + 8, :] = size[subs, lanes]
                dt_ref[0, first : first + 8, :] = size[subs, lanes]
                dxs[step, first : first + 8, :] = drive[subs, lanes]
                gs[step, first : first + 8, :] = grad[subs, lanes]

    @pl.when(step == chunks - 1)
    def _():
        batch = 4
        span = groups * 8
        zero = jnp.zeros((groups, 128), F32)
        for lead in range(0, states, batch):
            pairs = [(n, v) for n in range(lead, lead + batch) for v in range(chunks)]
            rates = [-LOG2E * jnp.exp(decay_ref[v, n]) for n, v in pairs]

            def block(index, carry):
                state, run, head, total = (list(part) for part in carry)
                for sub in range(8):
                    token = index * 8 + sub
                    at = pl.ds(index * span + sub, groups, stride=8)
                    size = [dts[v, at, :] for v in range(chunks)]
                    drive = [dxs[v, at, :] for v in range(chunks)]
                    grad = [gs[v, at, :] for v in range(chunks)]
                    if lead == 0:
                        total = [a + b for a, b in zip(total, size)]
                    for k, (n, v) in enumerate(pairs):
                        factor = jnp.exp2(size[v] * rates[k])
                        state[k] = factor * state[k] + drive[v] * coef[token, n]
                        run[k] = run[k] * factor
                        head[k] = head[k] + run[k] * (grad[v] * coef[token, states + n])
                return state, run, head, total

            many = [zero] * len(pairs)
            state, run, head, total = lax.fori_loop(
                0,
                rows // 8,
                block,
                (many, [zero + 1.0] * len(pairs), many, [zero] * chunks),
            )
            for k, (n, v) in enumerate(pairs):
                fwd[v, n] = state[k]
                bwd[v, n] = head[k]
            if lead == 0:
                for v in range(chunks):
                    coarse = total[v].astype(BF).astype(F32)
                    for target in (fwd, bwd):
                        target[v, states] = coarse
                        target[v, states + 1] = total[v] - coarse
        place = lax.axis_index("ctx")
        for mask, message in enumerate(messages, 1):
            message[...] = jnp.where((place ^ mask) > place, fwd[...], bwd[...]).astype(BF)


def local_call(parts, step_weight, step_bias, decay, conv_out, gate, grad, states, places):
    rows, chans = conv_out.shape
    wide = parts[0].shape[1]
    low_rank = step_weight.shape[0]
    chunks, _, groups, _ = decay.shape
    width = groups * 128
    message = (chunks, states + 2, groups, 128)
    big = pltpu.VMEM((chunks, rows * groups, 128), F32)
    return pl.pallas_call(
        functools.partial(local_kernel, low_rank, states, places),
        grid=(chunks,),
        in_specs=[
            whole((rows, wide)),
            whole((rows, wide)),
            columns(low_rank, width),
            columns(1, width),
            whole(decay.shape),
            columns(rows, width),
            columns(rows, width),
            columns(rows, width),
        ],
        out_specs=[
            pl.BlockSpec((1, rows * groups, 128), lambda i: (i, 0, 0)),
            whole((rows, 128)),
            whole((rows, low_rank)),
            whole((low_rank, rows)),
        ]
        + [whole(message)] * (places - 1),
        out_shape=[
            sds((chunks, rows * groups, 128), F32),
            sds((rows, 128), F32),
            sds((rows, low_rank), BF),
            sds((low_rank, rows), BF),
        ]
        + [sds(message, BF)] * (places - 1),
        scratch_shapes=[
            pltpu.VMEM((rows, wide), F32),
            pltpu.VMEM((rows, 128), F32),
            pltpu.SMEM((rows, 128), F32),
            big,
            big,
            big,
            pltpu.VMEM(message, F32),
            pltpu.VMEM(message, F32),
            pltpu.SemaphoreType.DMA,
        ],
        compiler_params=params(),
        name="local_ends",
    )(*parts, step_weight, step_bias, decay, conv_out, gate, grad)


def fold_rows(products, base, groups, target, first):
    total = products[pl.ds(base, 8, stride=groups), :]
    for row in range(1, groups):
        total = total + products[pl.ds(base + row, 8, stride=groups), :]
    target[pl.ds(pl.multiple_of(first, 8), 8), :] = total


def scan_kernel(places, states, opening, *refs):
    (coef, dt_ref, decay_ref, conv_ref, gate_ref, grad_ref, weight_ref, skip_ref) = refs[:8]
    messages, refs = refs[8 : 7 + places], refs[7 + places :]
    if not opening:
        before_ref, refs = refs[0], refs[4:]
    (pre_ref, gate_out, scan_out, small_ref, part_ref) = refs[:5]
    refs = refs[5:]
    (xs, dxs, gs, ys, dds, qs, decayed, coef_out, coef_in, rate, decay_acc, acc, ends, products) = refs
    rows = conv_ref.shape[0]
    groups = decay_ref.shape[2]
    low_rank = weight_ref.shape[0]
    span = groups * 8

    for start in range(0, rows, 16):
        here = slice(start, start + 16)
        conv = conv_ref[here, :].astype(F32)
        gate = gate_ref[here, :].astype(F32)
        grad = grad_ref[here, :].astype(F32) * gate * sigmoid(gate)
        for half in range(2):
            for group in range(groups):
                first = ((start // 8 + half) * groups + group) * 8
                lanes = slice(group * 128, group * 128 + 128)
                subs = slice(half * 8, half * 8 + 8)
                xs[first : first + 8, :] = conv[subs, lanes]
                dxs[first : first + 8, :] = conv[subs, lanes] * dt_ref[0, first : first + 8, :]
                gs[first : first + 8, :] = grad[subs, lanes]

    place = lax.axis_index("ctx")
    for n in range(states):
        rate[n] = -LOG2E * jnp.exp(decay_ref[0, n])
    ends[place] = jnp.zeros(ends.shape[1:], F32)
    for mask, message in enumerate(messages, 1):
        ends[place ^ mask] = message[0].astype(F32)
    totals = [ends[q, states] + ends[q, states + 1] for q in range(places)]
    state, carry = [], []
    for n in range(states):
        before = jnp.zeros((groups, 128), F32)
        after = jnp.zeros((groups, 128), F32)
        for q in range(places - 1):
            reached = jnp.exp2(rate[n] * totals[q]) * before + ends[q, n]
            before = jnp.where(q < place, reached, before)
        for q in range(places - 1, 0, -1):
            reached = jnp.exp2(rate[n] * totals[q]) * after + ends[q, n]
            after = jnp.where(q > place, reached, after)
        state.append(before)
        carry.append(after)

    def forward(index, state):
        state = list(state)
        for sub in range(8):
            token = index * 8 + sub
            at = pl.ds(index * span + sub, groups, stride=8)
            size, drive, grad = dt_ref[0, at, :], dxs[at, :], gs[at, :]
            result = jnp.zeros((groups, 128), F32)
            for lead in range(0, states, 8):
                base = (sub * states + lead) * groups
                for n in range(lead, lead + 8):
                    kept = jnp.exp2(size * rate[n]) * state[n]
                    decayed[token, n] = kept
                    state[n] = kept + drive * coef[token, n]
                    result = result + state[n] * coef[token, states + n]
                    row = base + (n - lead) * groups
                    products[row : row + groups, :] = state[n] * grad
                fold_rows(products, base, groups, coef_out, token * states + lead)
            ys[at, :] = result
        return state

    lax.fori_loop(0, rows // 8, forward, state)

    def backward(hop, both):
        carry, gathered = list(both[0]), list(both[1])
        index = rows // 8 - 1 - hop
        for sub in range(7, -1, -1):
            token = index * 8 + sub
            at = pl.ds(index * span + sub, groups, stride=8)
            size, drive, grad = dt_ref[0, at, :], dxs[at, :], gs[at, :]
            slope = jnp.zeros((groups, 128), F32)
            inner = jnp.zeros((groups, 128), F32)
            for lead in range(0, states, 8):
                base = (sub * states + lead) * groups
                for n in range(lead, lead + 8):
                    adjoint = carry[n] + grad * coef[token, states + n]
                    power = size * rate[n]
                    carry[n] = jnp.exp2(power) * adjoint
                    weighted = adjoint * decayed[token, n] * power
                    slope = slope + weighted
                    gathered[n] = gathered[n] + weighted
                    inner = inner + adjoint * coef[token, n]
                    row = base + (n - lead) * groups
                    products[row : row + groups, :] = adjoint * drive
                fold_rows(products, base, groups, coef_in, token * states + lead)
            dds[at, :] = slope
            qs[at, :] = inner
        return carry, gathered

    zeros = [jnp.zeros((groups, 128), F32)] * states
    _, gathered = lax.fori_loop(0, rows // 8, backward, (carry, zeros))
    for n in range(states):
        decay_acc[n * groups : n * groups + groups, :] = gathered[n] * LN2

    for group in range(groups):
        pre_ref[rows : rows + states, group * 128 : group * 128 + 128] = decay_acc[
            pl.ds(group, states, stride=groups), :
        ].astype(BF)
    skip = skip_ref[...]
    bias_sum = jnp.zeros((1, conv_ref.shape[1]), F32)
    skip_sum = jnp.zeros((1, conv_ref.shape[1]), F32)
    for start in range(0, rows, 16):
        here = slice(start, start + 16)

        def natural(read):
            return jnp.concatenate(
                [
                    jnp.concatenate(
                        [
                            read(((start // 8 + half) * groups + group) * 8)
                            for group in range(groups)
                        ],
                        axis=1,
                    )
                    for half in range(2)
                ],
                axis=0,
            )

        size = natural(lambda first: dt_ref[0, first : first + 8, :])
        inner = natural(lambda first: qs[first : first + 8, :])
        slope = natural(lambda first: dds[first : first + 8, :])
        out = natural(lambda first: ys[first : first + 8, :])
        conv = conv_ref[here, :].astype(F32)
        gate = gate_ref[here, :].astype(F32)
        grad = grad_ref[here, :].astype(F32)
        sig = sigmoid(gate)
        scan_grad = grad * gate * sig
        tiny = 1.0 - 0.5 * size * (1.0 - size * (1.0 / 3.0) * (1.0 - 0.25 * size))
        ratio = jnp.where(size < 0.03, tiny, (1.0 - jnp.exp(-size)) / jnp.maximum(size, 0.03))
        d_pre = (LN2 * slope + conv * inner * size) * ratio
        pre_ref[here, :] = d_pre.astype(BF)
        bias_sum = bias_sum + jnp.sum(d_pre, axis=0, keepdims=True)
        skip_sum = skip_sum + jnp.sum(scan_grad * conv, axis=0, keepdims=True)
        scan_out[here, :] = (size * inner + skip * scan_grad).astype(BF)
        gate_out[here, :] = (
            grad * (out + skip * conv) * (sig * (1.0 + gate * (1.0 - sig)))
        ).astype(BF)
    small_ref[...] = jnp.concatenate(
        [bias_sum, skip_sum, jnp.zeros((6, bias_sum.shape[1]), F32)], axis=0
    )

    pre_bf = pre_ref[:rows, :]
    lanes = lax.broadcasted_iota(jnp.int32, (2 * states, 128), 0)
    coefs = jnp.zeros((2 * states, rows), F32)
    for n in range(states):
        at = pl.ds(n, rows, stride=states)
        for kind, source in enumerate((coef_in, coef_out)):
            pick = jnp.where(lanes == kind * states + n, 1.0, 0.0).astype(BF)
            coefs = coefs + dot(pick, source[at, :].astype(BF), NT)
    wide = dot(weight_ref[...], pre_bf, NT)

    ranks, coef_rows, block = low_rank // places, 2 * states // places, acc.shape[0] // places

    acc[...] = jnp.zeros_like(acc) if opening else before_ref[...]
    for q in range(places):
        at = q * block
        acc[at : at + ranks, :] += wide[q * ranks : (q + 1) * ranks, :]
        acc[at + ranks : at + ranks + coef_rows, :] += coefs[
            q * coef_rows : (q + 1) * coef_rows, :
        ]
    part_ref[...] = acc[...].astype(part_ref.dtype)


def padded(wide):
    return (wide + 127) // 128 * 128


def scan_call(
    places, chunk, coef, dt, decay, conv_out, gate, grad, step_weight, skip, messages, previous
):
    rows, chans = conv_out.shape
    low_rank = step_weight.shape[0]
    chunks, states, groups, _ = decay.shape
    width = groups * 128
    wide = padded(low_rank + 2 * states)
    lead = lambda *shape: pl.BlockSpec((1,) + shape, lambda i: (chunk,) + (0,) * len(shape))
    here = lambda height: pl.BlockSpec((height, width), lambda i: (0, chunk))
    tall = pltpu.VMEM((rows * groups, 128), F32)
    first, last = chunk == 0, chunk == chunks - 1
    in_specs = [
        pl.BlockSpec(memory_space=pltpu.SMEM),
        lead(rows * groups, 128),
        lead(states, groups, 128),
        here(rows),
        here(rows),
        here(rows),
        here(low_rank),
        here(1),
    ]
    in_specs += [lead(states + 2, groups, 128)] * (places - 1)
    aliases = {}
    if not first:
        in_specs += [whole((wide, rows))] + [pl.BlockSpec(memory_space=pl.ANY)] * 3
        aliases = {8 + places: 1, 9 + places: 2, 10 + places: 3}
    return pl.pallas_call(
        functools.partial(scan_kernel, places, states, first),
        grid=(1,),
        in_specs=in_specs,
        out_specs=[
            whole((rows + states, width)),
            here(rows),
            here(rows),
            here(8),
            whole((wide, rows)),
        ],
        out_shape=[
            sds((rows + states, width), BF),
            sds((rows, chans), BF),
            sds((rows, chans), BF),
            sds((8, chans), F32),
            sds((wide, rows), BF if last else F32),
        ],
        scratch_shapes=[
            tall,
            tall,
            tall,
            tall,
            tall,
            tall,
            pltpu.VMEM((rows, states, groups, 128), F32),
            pltpu.VMEM((rows * states, 128), F32),
            pltpu.VMEM((rows * states, 128), F32),
            pltpu.VMEM((states, groups, 128), F32),
            pltpu.VMEM((states * groups, 128), F32),
            pltpu.VMEM((wide, rows), F32),
            pltpu.VMEM((places, states + 2, groups, 128), F32),
            pltpu.VMEM((8 * states * groups, 128), F32),
        ],
        input_output_aliases=aliases,
        compiler_params=params(),
        name="scan_gradients",
    )(coef, dt, decay, conv_out, gate, grad, step_weight, skip, *messages, *previous)


def conv_grad_kernel(places, low_rank, back_a, back_b, proj_ref, scan_ref, small_in, input_ref, rim_ref, weight_ref, bias_ref,
                     out_ref, tail_ref, small_ref, ext, grad):
    taps = weight_ref.shape[0]
    rows = input_ref.shape[0]
    fill_extended(ext, rim_ref, input_ref, taps)
    wide = proj_ref.shape[0]
    block = back_a.shape[0] // places
    ranks, coef_rows = low_rank // places, (wide - low_rank) // places
    back = (back_a[...].astype(F32) + back_b[...].astype(F32)).astype(BF).astype(F32)
    order = [back[q * block : q * block + ranks, :] for q in range(places)]
    order += [back[q * block + ranks : q * block + ranks + coef_rows, :] for q in range(places)]
    d_xc = dot(jnp.concatenate(order, axis=0).astype(BF), proj_ref[...], TN)
    sums = [jnp.zeros((1, input_ref.shape[1]), F32) for _ in range(taps + 1)]
    for start in range(0, rows, 16):
        here = slice(start, start + 16)
        pre = conv_block(ext, weight_ref, bias_ref[...], taps, start, 16)
        sig = sigmoid(pre)
        value = (d_xc[here, :] + scan_ref[here, :].astype(F32)) * (sig * (1.0 + pre * (1.0 - sig)))
        grad[here, :] = value
        for tap in range(taps):
            first = 8 - (taps - 1) + tap + start
            sums[tap] = sums[tap] + jnp.sum(value * ext[first : first + 16, :], axis=0, keepdims=True)
        sums[taps] = sums[taps] + jnp.sum(value, axis=0, keepdims=True)
    grad[rows : rows + 8, :] = jnp.zeros((8, grad.shape[1]), F32)
    for start in range(0, rows, 16):
        total = jnp.zeros((16, grad.shape[1]), F32)
        for tap in range(taps):
            first = start + taps - 1 - tap
            total = total + weight_ref[tap : tap + 1, :] * grad[first : first + 16, :]
        out_ref[start : start + 16, :] = total.astype(BF)
    tail_ref[...] = total
    small_ref[...] = jnp.concatenate(
        sums + [small_in[0 : 7 - taps, :], grad[0:8, :]], axis=0
    ).astype(BF)


def conv_grad_call(places, low_rank, backs, proj_weight, scan_part, small, conv_input, rim, weight, bias):
    rows, chans = conv_input.shape
    taps = weight.shape[0]
    wide = proj_weight.shape[0]
    width = min(512, chans)
    return pl.pallas_call(
        functools.partial(conv_grad_kernel, places, low_rank),
        grid=(chans // width,),
        in_specs=[
            whole(backs[0].shape),
            whole(backs[1].shape),
            columns(wide, width),
            columns(rows, width),
            columns(8, width),
            columns(rows, width),
            columns(taps - 1, width),
            columns(taps, width),
            columns(1, width),
        ],
        out_specs=[columns(rows, width), columns(16, width), columns(16, width)],
        out_shape=[sds((rows, chans), BF), sds((16, chans), F32), sds((16, chans), BF)],
        scratch_shapes=[pltpu.VMEM((rows + 8, width), F32), pltpu.VMEM((rows + 8, width), F32)],
        compiler_params=params(),
        name="conv_gradients",
    )(*backs, proj_weight, scan_part, small, conv_input, rim, weight, bias)


def cut_kernel(places, *refs):
    back_a, back_b, low_t = refs[:3]
    cuts, (back,) = refs[3 : 3 + places], refs[3 + places :]
    place = lax.axis_index("ctx")
    back_rows, ranks = back.shape[0] // places, low_t.shape[0] // places
    back[...] = back_a[...].astype(F32) + back_b[...].astype(F32)
    for mask in range(places):
        other = place ^ mask
        cuts[mask][:back_rows, :] = back[pl.ds(other * back_rows, back_rows), :].astype(BF)
        cuts[mask][back_rows:, :] = low_t[pl.ds(pl.multiple_of(other * ranks, 16), ranks), :]


def cut_call(places, backs, low_t):
    wide, rows = backs[0].shape
    cut = ((wide + low_t.shape[0]) // places, rows)
    return pl.pallas_call(
        functools.partial(cut_kernel, places),
        out_shape=[sds(cut, BF)] * places,
        scratch_shapes=[pltpu.VMEM((wide, rows), F32)],
        compiler_params=params(),
        name="cut_rows",
    )(*backs, low_t)


def rows_kernel(places, rank_rows, chunks, *refs):
    cuts, refs = refs[:places], refs[places:]
    blocks, refs = refs[:places], refs[places:]
    steps, refs = refs[: chunks * places], refs[chunks * places :]
    out_ref, coef_ref, step_ref, decay_ref = refs
    place = lax.axis_index("ctx")
    rows = blocks[0].shape[0]
    back_rows = cuts[0].shape[0] - rank_rows
    total = jnp.zeros((back_rows, out_ref.shape[1]), F32)
    for cut, block in zip(cuts, blocks):
        total = total + dot(cut[:back_rows, :], block[...])
    out_ref[...] = total[:rank_rows, :]
    coef_ref[...] = total[rank_rows : rank_rows + coef_ref.shape[0], :]
    for chunk in range(chunks):

        @pl.when(pl.program_id(0) == chunk)
        def _():
            total = jnp.zeros(step_ref.shape, F32)
            decay = jnp.zeros(decay_ref.shape, F32)
            for mask in range(places):
                step = steps[chunk * places + mask]
                total = total + dot(cuts[mask][back_rows:, :], step[:rows, :])
                decay = decay + step[rows:, :].astype(F32)
            step_ref[...] = total
            decay_ref[...] = decay


def rows_call(places, rank_rows, coef_rows, cuts, blocks, steps):
    rows, chans = blocks[0].shape
    tall, width = steps[0].shape
    chunks = chans // width
    heights = (rank_rows, coef_rows, rank_rows, tall - rows)
    return pl.pallas_call(
        functools.partial(rows_kernel, places, rank_rows, chunks),
        grid=(chunks,),
        in_specs=[whole(cuts[0].shape)] * places
        + [columns(rows, width)] * places
        + [whole((tall, width))] * len(steps),
        out_specs=[columns(height, width) for height in heights],
        out_shape=[sds((height, chans), F32) for height in heights],
        compiler_params=params(),
        name="row_gradients",
    )(*cuts, *blocks, *steps)


def last_kernel(places, taps, *refs):
    (_, tail_ref, weight_ref) = refs[:3]
    late, refs = refs[3 : 3 + places], refs[3 + places :]
    (out_ref, conv_w, conv_b, step_b, skip, fix) = refs
    fix[...] = tail_ref[...]
    inside = lax.axis_index("ctx") < places - 1
    following = jnp.where(inside, late[places - 1][8:16, :].astype(F32), 0.0)
    for row in range(taps - 1):
        extra = jnp.zeros((1, fix.shape[1]), F32)
        for tap in range(row + 1):
            extra = extra + weight_ref[tap : tap + 1, :] * following[row - tap : row - tap + 1, :]
        at = 16 - (taps - 1) + row
        fix[at : at + 1, :] += extra
    out_ref[...] = fix[...].astype(BF)
    total = late[0][...].astype(F32)
    for part in late[1:]:
        total = total + part[...].astype(F32)
    conv_w[...] = total[:taps, :]
    conv_b[...] = total[taps : taps + 1, :]
    step_b[...] = total[taps + 1 : taps + 2, :]
    skip[...] = total[taps + 2 : taps + 3, :]


def last_call(main, tail, weight, late):
    rows, chans = main.shape
    taps = weight.shape[0]
    places = len(late)
    return pl.pallas_call(
        functools.partial(last_kernel, places, taps),
        grid=(1,),
        in_specs=[pl.BlockSpec(memory_space=pl.ANY), columns(16, chans), columns(taps, chans)]
        + [columns(16, chans)] * places,
        out_specs=[
            pl.BlockSpec((16, chans), lambda i: (rows // 16 - 1, i)),
            columns(taps, chans),
        ]
        + [columns(1, chans)] * 3,
        out_shape=[sds((rows, chans), BF), sds((taps, chans), F32)] + [sds((1, chans), F32)] * 3,
        scratch_shapes=[pltpu.VMEM((16, chans), F32)],
        input_output_aliases={0: 0},
        compiler_params=params(),
        name="last_rows",
    )(main, tail, weight, *late)


def exchange(block, axis):
    return lax.all_to_all(block, axis, split_axis=0, concat_axis=0, tiled=True)


def swap(block, axis, mask):
    return lax.ppermute(block, axis, [(i, i ^ mask) for i in range(lax.axis_size(axis))])


tie = lax.optimization_barrier


def spread(block):
    return [block] + [swap(block, "ctx", mask) for mask in range(1, min(lax.axis_size("ctx"), 3))]


def spread_on(blocks):
    places = lax.axis_size("ctx")
    if places == 4:
        return blocks + [swap(blocks[2], "ctx", 1)]
    return blocks + [swap(blocks[0], "ctx", mask) for mask in range(3, places)]


def chan_sum(part):
    mask, peers = 1, lax.axis_size("chan")
    while True:
        other = swap(part, "chan", mask)
        mask *= 2
        if mask == peers:
            return part, other
        part = (part.astype(F32) + other.astype(F32)).astype(BF)


def body(
    conv_input,
    gate_input,
    out_grad,
    conv_weight,
    conv_bias,
    proj_weight,
    step_weight,
    step_bias,
    decay_log,
    skip_gain,
):
    rows, chans = conv_input.shape
    taps = conv_weight.shape[0]
    low_rank = step_weight.shape[0]
    states = decay_log.shape[0]
    places = lax.axis_size("ctx")
    groups = group_rows(chans)
    decay = decay_log.reshape(states, -1, groups, 128).transpose(1, 0, 2, 3)
    conv_bias = conv_bias[None, :]
    step_bias = step_bias[None, :]
    skip_gain = skip_gain[None, :]

    chunks = decay.shape[0]
    rim = shift(conv_input[rows - (taps - 1) :], "ctx", 1)
    conv_out, part = conv_call(conv_input, rim, conv_weight, conv_bias, proj_weight)
    blocks = spread(conv_out)
    parts = chan_sum(part)
    dt, coef, low, low_t, *messages = local_call(
        parts, step_weight, step_bias, decay, conv_out, gate_input, out_grad, states, places
    )
    messages, blocks = tie((messages, blocks))
    messages = [swap(message, "ctx", mask) for mask, message in enumerate(messages, 1)]
    messages, blocks = tie((messages, blocks))
    blocks = spread_on(blocks)
    previous, steps, fresh = [], [], None
    for chunk in range(chunks):
        message, grad_gate, scan_part, small, part = scan_call(
            places, chunk, coef, dt, decay, conv_out, gate_input, out_grad, step_weight,
            skip_gain, messages, previous,
        )
        previous = [part, grad_gate, scan_part, small]
        if chunk == 0:
            previous, blocks = tie((previous, blocks))
        if fresh is not None:
            previous, fresh = tie((previous, fresh))
            steps += spread_on(fresh)
        fresh = spread(message)
    part, grad_gate, scan_part, small = previous
    backs = chan_sum(part)
    if places == 4:
        backs, steps, far = tie((backs, steps, fresh[2]))
        fresh = fresh[:2] + [far]
    else:
        backs, steps, fresh = tie((backs, steps, fresh))
    steps += spread_on(fresh)
    cuts = cut_call(places, backs, low_t)
    cuts = [cuts[0]] + [swap(cut, "ctx", mask) for mask, cut in enumerate(cuts[1:], 1)]
    main, tail, sums = conv_grad_call(
        places, low_rank, backs, proj_weight, scan_part, small, conv_input, rim, conv_weight,
        conv_bias,
    )
    sums, cuts, steps = tie((sums, cuts, steps))
    late = [sums] + [rotate(sums, "ctx", hop) for hop in range(1, places)]
    grad_proj, grad_coef, grad_step, decay_grad = rows_call(
        places, low_rank // places, 2 * states // places, cuts, blocks, steps
    )
    grad_input, conv_w, conv_b, step_b, skip = last_call(main, tail, conv_weight, late)
    return (
        grad_input,
        grad_gate,
        grad_proj,
        grad_coef,
        grad_step,
        conv_w,
        conv_b[0],
        step_b[0],
        decay_grad,
        skip[0],
    )


def solution(mesh):
    tokens, columns_, chan = P("ctx", "chan"), P(None, "chan"), P("chan")
    in_specs = (
        tokens, tokens, tokens, columns_, chan, columns_, columns_, chan, columns_, chan,
    )
    out_specs = (
        tokens, tokens, tokens, tokens, tokens, columns_, chan, chan, columns_, chan,
    )
    return jax.shard_map(body, mesh=mesh, in_specs=in_specs, out_specs=out_specs, check_vma=False)
```

```python
import functools

import jax
import jax.numpy as jnp
from jax import lax
from jax.experimental import pallas as pl
from jax.experimental.pallas import tpu as pltpu
from jax.sharding import PartitionSpec as P

BF = jnp.bfloat16
F32 = jnp.float32
LOG2E = 1.4426950408889634
LN2 = 0.6931471805599453
VMEM_BYTES = 56 * 1024 * 1024
NT = (((1,), (1,)), ((), ()))
TN = (((0,), (0,)), ((), ()))


def group_rows(chans):
    for rows in (8, 4, 2, 1):
        if chans % (rows * 128) == 0:
            return rows
    return 1


def dot(a, b, dims=(((1,), (0,)), ((), ()))):
    return lax.dot_general(a, b, dims, preferred_element_type=F32)


def params(**more):
    return pltpu.CompilerParams(vmem_limit_bytes=VMEM_BYTES, **more)


def sds(shape, dtype):
    return jax.ShapeDtypeStruct(shape, dtype)


def whole(shape):
    return pl.BlockSpec(shape, lambda i: (0,) * len(shape))


def columns(rows, width):
    return pl.BlockSpec((rows, width), lambda i: (0, i))


def sigmoid(v):
    return 0.5 + 0.5 * jnp.tanh(0.5 * v)


def rotate(block, axis, distance):
    count = lax.axis_size(axis)
    return lax.ppermute(block, axis, [(i, (i + distance) % count) for i in range(count)])


def shift(block, axis, distance):
    count = lax.axis_size(axis)
    route = [(i, i + distance) for i in range(count) if 0 <= i + distance < count]
    return lax.ppermute(block, axis, route)


def fill_extended(ext, rim_ref, input_ref, taps):
    rows = input_ref.shape[0]
    ext[8 - (taps - 1) : 8, :] = rim_ref[...].astype(F32)
    ext[8 : 8 + rows, :] = input_ref[...].astype(F32)


def conv_block(ext, weight, bias, taps, start, rows):
    total = bias + jnp.zeros((rows, ext.shape[1]), F32)
    for tap in range(taps):
        first = 8 - (taps - 1) + tap + start
        total = total + weight[tap : tap + 1, :] * ext[first : first + rows, :]
    return total


def conv_kernel(input_ref, rim_ref, weight_ref, bias_ref, proj_ref, out_ref, part_ref, ext, acc):
    step = pl.program_id(0)
    taps = weight_ref.shape[0]
    rows = input_ref.shape[0]
    fill_extended(ext, rim_ref, input_ref, taps)
    for start in range(0, rows, 16):
        pre = conv_block(ext, weight_ref, bias_ref[...], taps, start, 16)
        out_ref[start : start + 16, :] = (pre * sigmoid(pre)).astype(BF)
    part = dot(out_ref[...], proj_ref[...], NT)

    @pl.when(step == 0)
    def _():
        acc[...] = part

    @pl.when(step > 0)
    def _():
        acc[...] += part

    @pl.when(step == pl.num_programs(0) - 1)
    def _():
        part_ref[...] = acc[...].astype(BF)


def conv_call(conv_input, rim, weight, bias, proj_weight):
    rows, chans = conv_input.shape
    taps = weight.shape[0]
    wide = proj_weight.shape[0]
    width = min(512, chans)
    return pl.pallas_call(
        conv_kernel,
        grid=(chans // width,),
        in_specs=[
            columns(rows, width),
            columns(taps - 1, width),
            columns(taps, width),
            columns(1, width),
            columns(wide, width),
        ],
        out_specs=[columns(rows, width), whole((rows, wide))],
        out_shape=[sds((rows, chans), BF), sds((rows, wide), BF)],
        scratch_shapes=[pltpu.VMEM((rows + 8, width), F32), pltpu.VMEM((rows, wide), F32)],
        compiler_params=params(),
        name="conv_project",
    )(conv_input, rim, weight, bias, proj_weight)


def tile_rows(value, target, lead, groups):
    rows = value.shape[0]
    for block in range(rows // 8):
        for group in range(groups):
            first = (block * groups + group) * 8
            target[lead, first : first + 8, :] = value[
                block * 8 : block * 8 + 8, group * 128 : group * 128 + 128
            ]


def local_kernel(low_rank, states, places, *refs):
    parts, refs = refs[:2], refs[2:]
    (weight_ref, bias_ref, decay_ref, conv_ref, gate_ref, grad_ref) = refs[:6]
    (dt_ref, coef_ref, low, low_t) = refs[6:10]
    messages, refs = refs[10 : 9 + places], refs[9 + places :]
    (proj, coef_v, coef, dts, dxs, gs, fwd, bwd, sem) = refs
    step = pl.program_id(0)
    chunks = dts.shape[0]
    rows = conv_ref.shape[0]
    groups = decay_ref.shape[2]

    @pl.when(step == 0)
    def _():
        total = (parts[0][...].astype(F32) + parts[1][...].astype(F32)).astype(BF)
        proj[...] = total.astype(F32)
        low[...] = total[:, :low_rank]
        low_t[...] = jnp.transpose(proj[:, :low_rank]).astype(BF)
        coef_v[...] = jnp.zeros_like(coef_v)
        coef_v[:, : 2 * states] = proj[:, low_rank:]
        coef_ref[...] = coef_v[...]
        copy = pltpu.make_async_copy(coef_v, coef, sem)
        copy.start()
        copy.wait()

    pre = dot(low[...], weight_ref[...]) + bias_ref[...]
    for start in range(0, rows, 16):
        here = slice(start, start + 16)
        p = pre[here, :]
        size = jnp.maximum(p, 0.0) + jnp.log1p(jnp.exp(-jnp.abs(p)))
        gate = gate_ref[here, :].astype(F32)
        grad = grad_ref[here, :].astype(F32) * gate * sigmoid(gate)
        drive = size * conv_ref[here, :].astype(F32)
        for half in range(2):
            for group in range(groups):
                first = ((start // 8 + half) * groups + group) * 8
                lanes = slice(group * 128, group * 128 + 128)
                subs = slice(half * 8, half * 8 + 8)
                dts[step, first : first + 8, :] = size[subs, lanes]
                dt_ref[0, first : first + 8, :] = size[subs, lanes]
                dxs[step, first : first + 8, :] = drive[subs, lanes]
                gs[step, first : first + 8, :] = grad[subs, lanes]

    @pl.when(step == chunks - 1)
    def _():
        batch = 4
        span = groups * 8
        zero = jnp.zeros((groups, 128), F32)
        for lead in range(0, states, batch):
            pairs = [(n, v) for n in range(lead, lead + batch) for v in range(chunks)]
            rates = [-LOG2E * jnp.exp(decay_ref[v, n]) for n, v in pairs]

            def block(index, carry):
                state, run, head, total = (list(part) for part in carry)
                for sub in range(8):
                    token = index * 8 + sub
                    at = pl.ds(index * span + sub, groups, stride=8)
                    size = [dts[v, at, :] for v in range(chunks)]
                    drive = [dxs[v, at, :] for v in range(chunks)]
                    grad = [gs[v, at, :] for v in range(chunks)]
                    if lead == 0:
                        total = [a + b for a, b in zip(total, size)]
                    for k, (n, v) in enumerate(pairs):
                        factor = jnp.exp2(size[v] * rates[k])
                        state[k] = factor * state[k] + drive[v] * coef[token, n]
                        run[k] = run[k] * factor
                        head[k] = head[k] + run[k] * (grad[v] * coef[token, states + n])
                return state, run, head, total

            many = [zero] * len(pairs)
            state, run, head, total = lax.fori_loop(
                0,
                rows // 8,
                block,
                (many, [zero + 1.0] * len(pairs), many, [zero] * chunks),
            )
            for k, (n, v) in enumerate(pairs):
                fwd[v, n] = state[k]
                bwd[v, n] = head[k]
            if lead == 0:
                for v in range(chunks):
                    coarse = total[v].astype(BF).astype(F32)
                    for target in (fwd, bwd):
                        target[v, states] = coarse
                        target[v, states + 1] = total[v] - coarse
        place = lax.axis_index("ctx")
        for mask, message in enumerate(messages, 1):
            message[...] = jnp.where((place ^ mask) > place, fwd[...], bwd[...]).astype(BF)


def local_call(parts, step_weight, step_bias, decay, conv_out, gate, grad, states, places):
    rows, chans = conv_out.shape
    wide = parts[0].shape[1]
    low_rank = step_weight.shape[0]
    chunks, _, groups, _ = decay.shape
    width = groups * 128
    message = (chunks, states + 2, groups, 128)
    big = pltpu.VMEM((chunks, rows * groups, 128), F32)
    return pl.pallas_call(
        functools.partial(local_kernel, low_rank, states, places),
        grid=(chunks,),
        in_specs=[
            whole((rows, wide)),
            whole((rows, wide)),
            columns(low_rank, width),
            columns(1, width),
            whole(decay.shape),
            columns(rows, width),
            columns(rows, width),
            columns(rows, width),
        ],
        out_specs=[
            pl.BlockSpec((1, rows * groups, 128), lambda i: (i, 0, 0)),
            whole((rows, 128)),
            whole((rows, low_rank)),
            whole((low_rank, rows)),
        ]
        + [whole(message)] * (places - 1),
        out_shape=[
            sds((chunks, rows * groups, 128), F32),
            sds((rows, 128), F32),
            sds((rows, low_rank), BF),
            sds((low_rank, rows), BF),
        ]
        + [sds(message, BF)] * (places - 1),
        scratch_shapes=[
            pltpu.VMEM((rows, wide), F32),
            pltpu.VMEM((rows, 128), F32),
            pltpu.SMEM((rows, 128), F32),
            big,
            big,
            big,
            pltpu.VMEM(message, F32),
            pltpu.VMEM(message, F32),
            pltpu.SemaphoreType.DMA,
        ],
        compiler_params=params(),
        name="local_ends",
    )(*parts, step_weight, step_bias, decay, conv_out, gate, grad)


def fold_rows(products, base, groups, target, first):
    total = products[pl.ds(base, 8, stride=groups), :]
    for row in range(1, groups):
        total = total + products[pl.ds(base + row, 8, stride=groups), :]
    target[pl.ds(pl.multiple_of(first, 8), 8), :] = total


def scan_kernel(places, states, opening, *refs):
    (coef, dt_ref, decay_ref, conv_ref, gate_ref, grad_ref, weight_ref, skip_ref) = refs[:8]
    messages, refs = refs[8 : 7 + places], refs[7 + places :]
    if not opening:
        before_ref, refs = refs[0], refs[4:]
    (pre_ref, gate_out, scan_out, small_ref, part_ref) = refs[:5]
    refs = refs[5:]
    (xs, dxs, gs, ys, dds, qs, decayed, coef_out, coef_in, rate, decay_acc, acc, ends, products, factors) = refs
    rows = conv_ref.shape[0]
    groups = decay_ref.shape[2]
    low_rank = weight_ref.shape[0]
    span = groups * 8

    for start in range(0, rows, 16):
        here = slice(start, start + 16)
        conv = conv_ref[here, :].astype(F32)
        gate = gate_ref[here, :].astype(F32)
        grad = grad_ref[here, :].astype(F32) * gate * sigmoid(gate)
        for half in range(2):
            for group in range(groups):
                first = ((start // 8 + half) * groups + group) * 8
                lanes = slice(group * 128, group * 128 + 128)
                subs = slice(half * 8, half * 8 + 8)
                xs[first : first + 8, :] = conv[subs, lanes]
                dxs[first : first + 8, :] = conv[subs, lanes] * dt_ref[0, first : first + 8, :]
                gs[first : first + 8, :] = grad[subs, lanes]

    place = lax.axis_index("ctx")
    for n in range(states):
        rate[n] = -LOG2E * jnp.exp(decay_ref[0, n])
    ends[place] = jnp.zeros(ends.shape[1:], F32)
    for mask, message in enumerate(messages, 1):
        ends[place ^ mask] = message[0].astype(F32)
    totals = [ends[q, states] + ends[q, states + 1] for q in range(places)]
    state, carry = [], []
    for n in range(states):
        before = jnp.zeros((groups, 128), F32)
        after = jnp.zeros((groups, 128), F32)
        for q in range(places - 1):
            reached = jnp.exp2(rate[n] * totals[q]) * before + ends[q, n]
            before = jnp.where(q < place, reached, before)
        for q in range(places - 1, 0, -1):
            reached = jnp.exp2(rate[n] * totals[q]) * after + ends[q, n]
            after = jnp.where(q > place, reached, after)
        state.append(before)
        carry.append(after)

    def forward(index, state):
        state = list(state)
        for sub in range(8):
            token = index * 8 + sub
            at = pl.ds(index * span + sub, groups, stride=8)
            size, drive, grad = dt_ref[0, at, :], dxs[at, :], gs[at, :]
            result = jnp.zeros((groups, 128), F32)
            for lead in range(0, states, 8):
                base = (sub * states + lead) * groups
                for n in range(lead, lead + 8):
                    factor = jnp.exp2(size * rate[n])
                    kept = factor * state[n]
                    factors[token, n] = factor
                    decayed[token, n] = kept
                    state[n] = kept + drive * coef[token, n]
                    result = result + state[n] * coef[token, states + n]
                    row = base + (n - lead) * groups
                    products[row : row + groups, :] = state[n] * grad
                fold_rows(products, base, groups, coef_out, token * states + lead)
            ys[at, :] = result
        return state

    lax.fori_loop(0, rows // 8, forward, state)

    def backward(hop, both):
        carry, gathered = list(both[0]), list(both[1])
        index = rows // 8 - 1 - hop
        for sub in range(7, -1, -1):
            token = index * 8 + sub
            at = pl.ds(index * span + sub, groups, stride=8)
            size, drive, grad = dt_ref[0, at, :], dxs[at, :], gs[at, :]
            slope = jnp.zeros((groups, 128), F32)
            inner = jnp.zeros((groups, 128), F32)
            for lead in range(0, states, 8):
                base = (sub * states + lead) * groups
                for n in range(lead, lead + 8):
                    adjoint = carry[n] + grad * coef[token, states + n]
                    carry[n] = factors[token, n] * adjoint
                    weighted = adjoint * decayed[token, n] * (size * rate[n])
                    slope = slope + weighted
                    gathered[n] = gathered[n] + weighted
                    inner = inner + adjoint * coef[token, n]
                    row = base + (n - lead) * groups
                    products[row : row + groups, :] = adjoint * drive
                fold_rows(products, base, groups, coef_in, token * states + lead)
            dds[at, :] = slope
            qs[at, :] = inner
        return carry, gathered

    zeros = [jnp.zeros((groups, 128), F32)] * states
    _, gathered = lax.fori_loop(0, rows // 8, backward, (carry, zeros))
    for n in range(states):
        decay_acc[n * groups : n * groups + groups, :] = gathered[n] * LN2

    for group in range(groups):
        pre_ref[rows : rows + states, group * 128 : group * 128 + 128] = decay_acc[
            pl.ds(group, states, stride=groups), :
        ].astype(BF)
    skip = skip_ref[...]
    bias_sum = jnp.zeros((1, conv_ref.shape[1]), F32)
    skip_sum = jnp.zeros((1, conv_ref.shape[1]), F32)
    for start in range(0, rows, 16):
        here = slice(start, start + 16)

        def natural(read):
            return jnp.concatenate(
                [
                    jnp.concatenate(
                        [
                            read(((start // 8 + half) * groups + group) * 8)
                            for group in range(groups)
                        ],
                        axis=1,
                    )
                    for half in range(2)
                ],
                axis=0,
            )

        size = natural(lambda first: dt_ref[0, first : first + 8, :])
        inner = natural(lambda first: qs[first : first + 8, :])
        slope = natural(lambda first: dds[first : first + 8, :])
        out = natural(lambda first: ys[first : first + 8, :])
        conv = conv_ref[here, :].astype(F32)
        gate = gate_ref[here, :].astype(F32)
        grad = grad_ref[here, :].astype(F32)
        sig = sigmoid(gate)
        scan_grad = grad * gate * sig
        tiny = 1.0 - 0.5 * size * (1.0 - size * (1.0 / 3.0) * (1.0 - 0.25 * size))
        ratio = jnp.where(size < 0.03, tiny, (1.0 - jnp.exp(-size)) / jnp.maximum(size, 0.03))
        d_pre = (LN2 * slope + conv * inner * size) * ratio
        pre_ref[here, :] = d_pre.astype(BF)
        bias_sum = bias_sum + jnp.sum(d_pre, axis=0, keepdims=True)
        skip_sum = skip_sum + jnp.sum(scan_grad * conv, axis=0, keepdims=True)
        scan_out[here, :] = (size * inner + skip * scan_grad).astype(BF)
        gate_out[here, :] = (
            grad * (out + skip * conv) * (sig * (1.0 + gate * (1.0 - sig)))
        ).astype(BF)
    small_ref[...] = jnp.concatenate(
        [bias_sum, skip_sum, jnp.zeros((6, bias_sum.shape[1]), F32)], axis=0
    )

    pre_bf = pre_ref[:rows, :]
    lanes = lax.broadcasted_iota(jnp.int32, (2 * states, 128), 0)
    coefs = jnp.zeros((2 * states, rows), F32)
    for n in range(states):
        at = pl.ds(n, rows, stride=states)
        for kind, source in enumerate((coef_in, coef_out)):
            pick = jnp.where(lanes == kind * states + n, 1.0, 0.0).astype(BF)
            coefs = coefs + dot(pick, source[at, :].astype(BF), NT)
    wide = dot(weight_ref[...], pre_bf, NT)

    ranks, coef_rows, block = low_rank // places, 2 * states // places, acc.shape[0] // places

    acc[...] = jnp.zeros_like(acc) if opening else before_ref[...]
    for q in range(places):
        at = q * block
        acc[at : at + ranks, :] += wide[q * ranks : (q + 1) * ranks, :]
        acc[at + ranks : at + ranks + coef_rows, :] += coefs[
            q * coef_rows : (q + 1) * coef_rows, :
        ]
    part_ref[...] = acc[...].astype(part_ref.dtype)


def padded(wide):
    return (wide + 127) // 128 * 128


def scan_call(
    places, chunk, coef, dt, decay, conv_out, gate, grad, step_weight, skip, messages, previous
):
    rows, chans = conv_out.shape
    low_rank = step_weight.shape[0]
    chunks, states, groups, _ = decay.shape
    width = groups * 128
    wide = padded(low_rank + 2 * states)
    lead = lambda *shape: pl.BlockSpec((1,) + shape, lambda i: (chunk,) + (0,) * len(shape))
    here = lambda height: pl.BlockSpec((height, width), lambda i: (0, chunk))
    tall = pltpu.VMEM((rows * groups, 128), F32)
    first, last = chunk == 0, chunk == chunks - 1
    in_specs = [
        pl.BlockSpec(memory_space=pltpu.SMEM),
        lead(rows * groups, 128),
        lead(states, groups, 128),
        here(rows),
        here(rows),
        here(rows),
        here(low_rank),
        here(1),
    ]
    in_specs += [lead(states + 2, groups, 128)] * (places - 1)
    aliases = {}
    if not first:
        in_specs += [whole((wide, rows))] + [pl.BlockSpec(memory_space=pl.ANY)] * 3
        aliases = {8 + places: 1, 9 + places: 2, 10 + places: 3}
    return pl.pallas_call(
        functools.partial(scan_kernel, places, states, first),
        grid=(1,),
        in_specs=in_specs,
        out_specs=[
            whole((rows + states, width)),
            here(rows),
            here(rows),
            here(8),
            whole((wide, rows)),
        ],
        out_shape=[
            sds((rows + states, width), BF),
            sds((rows, chans), BF),
            sds((rows, chans), BF),
            sds((8, chans), F32),
            sds((wide, rows), BF if last else F32),
        ],
        scratch_shapes=[
            tall,
            tall,
            tall,
            tall,
            tall,
            tall,
            pltpu.VMEM((rows, states, groups, 128), F32),
            pltpu.VMEM((rows * states, 128), F32),
            pltpu.VMEM((rows * states, 128), F32),
            pltpu.VMEM((states, groups, 128), F32),
            pltpu.VMEM((states * groups, 128), F32),
            pltpu.VMEM((wide, rows), F32),
            pltpu.VMEM((places, states + 2, groups, 128), F32),
            pltpu.VMEM((8 * states * groups, 128), F32),
            pltpu.VMEM((rows, states, groups, 128), F32),
        ],
        input_output_aliases=aliases,
        compiler_params=params(),
        name="scan_gradients",
    )(coef, dt, decay, conv_out, gate, grad, step_weight, skip, *messages, *previous)


def conv_grad_kernel(places, low_rank, back_a, back_b, proj_ref, scan_ref, small_in, input_ref, rim_ref, weight_ref, bias_ref,
                     out_ref, tail_ref, small_ref, ext, grad):
    taps = weight_ref.shape[0]
    rows = input_ref.shape[0]
    fill_extended(ext, rim_ref, input_ref, taps)
    wide = proj_ref.shape[0]
    block = back_a.shape[0] // places
    ranks, coef_rows = low_rank // places, (wide - low_rank) // places
    back = (back_a[...].astype(F32) + back_b[...].astype(F32)).astype(BF).astype(F32)
    order = [back[q * block : q * block + ranks, :] for q in range(places)]
    order += [back[q * block + ranks : q * block + ranks + coef_rows, :] for q in range(places)]
    d_xc = dot(jnp.concatenate(order, axis=0).astype(BF), proj_ref[...], TN)
    sums = [jnp.zeros((1, input_ref.shape[1]), F32) for _ in range(taps + 1)]
    for start in range(0, rows, 16):
        here = slice(start, start + 16)
        pre = conv_block(ext, weight_ref, bias_ref[...], taps, start, 16)
        sig = sigmoid(pre)
        value = (d_xc[here, :] + scan_ref[here, :].astype(F32)) * (sig * (1.0 + pre * (1.0 - sig)))
        grad[here, :] = value
        for tap in range(taps):
            first = 8 - (taps - 1) + tap + start
            sums[tap] = sums[tap] + jnp.sum(value * ext[first : first + 16, :], axis=0, keepdims=True)
        sums[taps] = sums[taps] + jnp.sum(value, axis=0, keepdims=True)
    grad[rows : rows + 8, :] = jnp.zeros((8, grad.shape[1]), F32)
    for start in range(0, rows, 16):
        total = jnp.zeros((16, grad.shape[1]), F32)
        for tap in range(taps):
            first = start + taps - 1 - tap
            total = total + weight_ref[tap : tap + 1, :] * grad[first : first + 16, :]
        out_ref[start : start + 16, :] = total.astype(BF)
    tail_ref[...] = total
    small_ref[...] = jnp.concatenate(
        sums + [small_in[0 : 7 - taps, :], grad[0:8, :]], axis=0
    ).astype(BF)


def conv_grad_call(places, low_rank, backs, proj_weight, scan_part, small, conv_input, rim, weight, bias):
    rows, chans = conv_input.shape
    taps = weight.shape[0]
    wide = proj_weight.shape[0]
    width = min(512, chans)
    return pl.pallas_call(
        functools.partial(conv_grad_kernel, places, low_rank),
        grid=(chans // width,),
        in_specs=[
            whole(backs[0].shape),
            whole(backs[1].shape),
            columns(wide, width),
            columns(rows, width),
            columns(8, width),
            columns(rows, width),
            columns(taps - 1, width),
            columns(taps, width),
            columns(1, width),
        ],
        out_specs=[columns(rows, width), columns(16, width), columns(16, width)],
        out_shape=[sds((rows, chans), BF), sds((16, chans), F32), sds((16, chans), BF)],
        scratch_shapes=[pltpu.VMEM((rows + 8, width), F32), pltpu.VMEM((rows + 8, width), F32)],
        compiler_params=params(),
        name="conv_gradients",
    )(*backs, proj_weight, scan_part, small, conv_input, rim, weight, bias)


def cut_kernel(places, *refs):
    back_a, back_b, low_t = refs[:3]
    cuts, (back,) = refs[3 : 3 + places], refs[3 + places :]
    place = lax.axis_index("ctx")
    back_rows, ranks = back.shape[0] // places, low_t.shape[0] // places
    back[...] = back_a[...].astype(F32) + back_b[...].astype(F32)
    for mask in range(places):
        other = place ^ mask
        cuts[mask][:back_rows, :] = back[pl.ds(other * back_rows, back_rows), :].astype(BF)
        cuts[mask][back_rows:, :] = low_t[pl.ds(pl.multiple_of(other * ranks, 16), ranks), :]


def cut_call(places, backs, low_t):
    wide, rows = backs[0].shape
    cut = ((wide + low_t.shape[0]) // places, rows)
    return pl.pallas_call(
        functools.partial(cut_kernel, places),
        out_shape=[sds(cut, BF)] * places,
        scratch_shapes=[pltpu.VMEM((wide, rows), F32)],
        compiler_params=params(),
        name="cut_rows",
    )(*backs, low_t)


def rows_kernel(places, rank_rows, chunks, *refs):
    cuts, refs = refs[:places], refs[places:]
    blocks, refs = refs[:places], refs[places:]
    steps, refs = refs[: chunks * places], refs[chunks * places :]
    out_ref, coef_ref, step_ref, decay_ref = refs
    place = lax.axis_index("ctx")
    rows = blocks[0].shape[0]
    back_rows = cuts[0].shape[0] - rank_rows
    total = jnp.zeros((back_rows, out_ref.shape[1]), F32)
    for cut, block in zip(cuts, blocks):
        total = total + dot(cut[:back_rows, :], block[...])
    out_ref[...] = total[:rank_rows, :]
    coef_ref[...] = total[rank_rows : rank_rows + coef_ref.shape[0], :]
    for chunk in range(chunks):

        @pl.when(pl.program_id(0) == chunk)
        def _():
            total = jnp.zeros(step_ref.shape, F32)
            decay = jnp.zeros(decay_ref.shape, F32)
            for mask in range(places):
                step = steps[chunk * places + mask]
                total = total + dot(cuts[mask][back_rows:, :], step[:rows, :])
                decay = decay + step[rows:, :].astype(F32)
            step_ref[...] = total
            decay_ref[...] = decay


def rows_call(places, rank_rows, coef_rows, cuts, blocks, steps):
    rows, chans = blocks[0].shape
    tall, width = steps[0].shape
    chunks = chans // width
    heights = (rank_rows, coef_rows, rank_rows, tall - rows)
    return pl.pallas_call(
        functools.partial(rows_kernel, places, rank_rows, chunks),
        grid=(chunks,),
        in_specs=[whole(cuts[0].shape)] * places
        + [columns(rows, width)] * places
        + [whole((tall, width))] * len(steps),
        out_specs=[columns(height, width) for height in heights],
        out_shape=[sds((height, chans), F32) for height in heights],
        compiler_params=params(),
        name="row_gradients",
    )(*cuts, *blocks, *steps)


def last_kernel(places, taps, *refs):
    (_, tail_ref, weight_ref) = refs[:3]
    late, refs = refs[3 : 3 + places], refs[3 + places :]
    (out_ref, conv_w, conv_b, step_b, skip, fix) = refs
    fix[...] = tail_ref[...]
    inside = lax.axis_index("ctx") < places - 1
    following = jnp.where(inside, late[places - 1][8:16, :].astype(F32), 0.0)
    for row in range(taps - 1):
        extra = jnp.zeros((1, fix.shape[1]), F32)
        for tap in range(row + 1):
            extra = extra + weight_ref[tap : tap + 1, :] * following[row - tap : row - tap + 1, :]
        at = 16 - (taps - 1) + row
        fix[at : at + 1, :] += extra
    out_ref[...] = fix[...].astype(BF)
    total = late[0][...].astype(F32)
    for part in late[1:]:
        total = total + part[...].astype(F32)
    conv_w[...] = total[:taps, :]
    conv_b[...] = total[taps : taps + 1, :]
    step_b[...] = total[taps + 1 : taps + 2, :]
    skip[...] = total[taps + 2 : taps + 3, :]


def last_call(main, tail, weight, late):
    rows, chans = main.shape
    taps = weight.shape[0]
    places = len(late)
    return pl.pallas_call(
        functools.partial(last_kernel, places, taps),
        grid=(1,),
        in_specs=[pl.BlockSpec(memory_space=pl.ANY), columns(16, chans), columns(taps, chans)]
        + [columns(16, chans)] * places,
        out_specs=[
            pl.BlockSpec((16, chans), lambda i: (rows // 16 - 1, i)),
            columns(taps, chans),
        ]
        + [columns(1, chans)] * 3,
        out_shape=[sds((rows, chans), BF), sds((taps, chans), F32)] + [sds((1, chans), F32)] * 3,
        scratch_shapes=[pltpu.VMEM((16, chans), F32)],
        input_output_aliases={0: 0},
        compiler_params=params(),
        name="last_rows",
    )(main, tail, weight, *late)


def exchange(block, axis):
    return lax.all_to_all(block, axis, split_axis=0, concat_axis=0, tiled=True)


def swap(block, axis, mask):
    return lax.ppermute(block, axis, [(i, i ^ mask) for i in range(lax.axis_size(axis))])


tie = lax.optimization_barrier


def spread(block):
    return [block] + [swap(block, "ctx", mask) for mask in range(1, min(lax.axis_size("ctx"), 3))]


def spread_on(blocks):
    places = lax.axis_size("ctx")
    if places == 4:
        return blocks + [swap(blocks[2], "ctx", 1)]
    return blocks + [swap(blocks[0], "ctx", mask) for mask in range(3, places)]


def chan_sum(part):
    mask, peers = 1, lax.axis_size("chan")
    while True:
        other = swap(part, "chan", mask)
        mask *= 2
        if mask == peers:
            return part, other
        part = (part.astype(F32) + other.astype(F32)).astype(BF)


def body(
    conv_input,
    gate_input,
    out_grad,
    conv_weight,
    conv_bias,
    proj_weight,
    step_weight,
    step_bias,
    decay_log,
    skip_gain,
):
    rows, chans = conv_input.shape
    taps = conv_weight.shape[0]
    low_rank = step_weight.shape[0]
    states = decay_log.shape[0]
    places = lax.axis_size("ctx")
    groups = group_rows(chans)
    decay = decay_log.reshape(states, -1, groups, 128).transpose(1, 0, 2, 3)
    conv_bias = conv_bias[None, :]
    step_bias = step_bias[None, :]
    skip_gain = skip_gain[None, :]

    chunks = decay.shape[0]
    rim = shift(conv_input[rows - (taps - 1) :], "ctx", 1)
    conv_out, part = conv_call(conv_input, rim, conv_weight, conv_bias, proj_weight)
    blocks = spread(conv_out)
    parts = chan_sum(part)
    dt, coef, low, low_t, *messages = local_call(
        parts, step_weight, step_bias, decay, conv_out, gate_input, out_grad, states, places
    )
    messages, blocks = tie((messages, blocks))
    messages = [swap(message, "ctx", mask) for mask, message in enumerate(messages, 1)]
    messages, blocks = tie((messages, blocks))
    blocks = spread_on(blocks)
    previous, steps = [], []
    for chunk in range(chunks):
        message, grad_gate, scan_part, small, part = scan_call(
            places, chunk, coef, dt, decay, conv_out, gate_input, out_grad, step_weight,
            skip_gain, messages, previous,
        )
        previous = [part, grad_gate, scan_part, small]
        if chunk == 0:
            previous, blocks = tie((previous, blocks))
        else:
            previous, steps[-1] = tie((previous, steps[-1]))
        steps.append(spread(message))
    part, grad_gate, scan_part, small = previous
    backs = chan_sum(part)
    backs, steps = tie((backs, steps))
    steps = [block for step in steps for block in spread_on(step)]
    cuts = cut_call(places, backs, low_t)
    cuts = [cuts[0]] + [swap(cut, "ctx", mask) for mask, cut in enumerate(cuts[1:], 1)]
    main, tail, sums = conv_grad_call(
        places, low_rank, backs, proj_weight, scan_part, small, conv_input, rim, conv_weight,
        conv_bias,
    )
    sums, cuts, steps = tie((sums, cuts, steps))
    late = [sums] + [rotate(sums, "ctx", hop) for hop in range(1, places)]
    grad_proj, grad_coef, grad_step, decay_grad = rows_call(
        places, low_rank // places, 2 * states // places, cuts, blocks, steps
    )
    grad_input, conv_w, conv_b, step_b, skip = last_call(main, tail, conv_weight, late)
    return (
        grad_input,
        grad_gate,
        grad_proj,
        grad_coef,
        grad_step,
        conv_w,
        conv_b[0],
        step_b[0],
        decay_grad,
        skip[0],
    )


def solution(mesh):
    tokens, columns_, chan = P("ctx", "chan"), P(None, "chan"), P("chan")
    in_specs = (
        tokens, tokens, tokens, columns_, chan, columns_, columns_, chan, columns_, chan,
    )
    out_specs = (
        tokens, tokens, tokens, tokens, tokens, columns_, chan, chan, columns_, chan,
    )
    return jax.shard_map(body, mesh=mesh, in_specs=in_specs, out_specs=out_specs, check_vma=False)
```

```python
import functools

import jax
import jax.numpy as jnp
from jax import lax
from jax.experimental import pallas as pl
from jax.experimental.pallas import tpu as pltpu
from jax.sharding import PartitionSpec as P

BF = jnp.bfloat16
F32 = jnp.float32
LOG2E = 1.4426950408889634
LN2 = 0.6931471805599453
VMEM_BYTES = 56 * 1024 * 1024
NT = (((1,), (1,)), ((), ()))
TN = (((0,), (0,)), ((), ()))


def group_rows(chans):
    for rows in (8, 4, 2, 1):
        if chans % (rows * 128) == 0:
            return rows
    return 1


def dot(a, b, dims=(((1,), (0,)), ((), ()))):
    return lax.dot_general(a, b, dims, preferred_element_type=F32)


def params(**more):
    return pltpu.CompilerParams(vmem_limit_bytes=VMEM_BYTES, **more)


def sds(shape, dtype):
    return jax.ShapeDtypeStruct(shape, dtype)


def whole(shape):
    return pl.BlockSpec(shape, lambda i: (0,) * len(shape))


def columns(rows, width):
    return pl.BlockSpec((rows, width), lambda i: (0, i))


def sigmoid(v):
    return 0.5 + 0.5 * jnp.tanh(0.5 * v)


def rotate(block, axis, distance):
    count = lax.axis_size(axis)
    return lax.ppermute(block, axis, [(i, (i + distance) % count) for i in range(count)])


def shift(block, axis, distance):
    count = lax.axis_size(axis)
    route = [(i, i + distance) for i in range(count) if 0 <= i + distance < count]
    return lax.ppermute(block, axis, route)


def fill_extended(ext, rim_ref, input_ref, taps):
    rows = input_ref.shape[0]
    ext[8 - (taps - 1) : 8, :] = rim_ref[...].astype(F32)
    ext[8 : 8 + rows, :] = input_ref[...].astype(F32)


def conv_block(ext, weight, bias, taps, start, rows):
    total = bias + jnp.zeros((rows, ext.shape[1]), F32)
    for tap in range(taps):
        first = 8 - (taps - 1) + tap + start
        total = total + weight[tap : tap + 1, :] * ext[first : first + rows, :]
    return total


def conv_kernel(input_ref, rim_ref, weight_ref, bias_ref, proj_ref, out_ref, part_ref, ext, acc):
    step = pl.program_id(0)
    taps = weight_ref.shape[0]
    rows = input_ref.shape[0]
    fill_extended(ext, rim_ref, input_ref, taps)
    for start in range(0, rows, 16):
        pre = conv_block(ext, weight_ref, bias_ref[...], taps, start, 16)
        out_ref[start : start + 16, :] = (pre * sigmoid(pre)).astype(BF)
    part = dot(out_ref[...], proj_ref[...], NT)

    @pl.when(step == 0)
    def _():
        acc[...] = part

    @pl.when(step > 0)
    def _():
        acc[...] += part

    @pl.when(step == pl.num_programs(0) - 1)
    def _():
        part_ref[...] = acc[...].astype(BF)


def conv_call(conv_input, rim, weight, bias, proj_weight):
    rows, chans = conv_input.shape
    taps = weight.shape[0]
    wide = proj_weight.shape[0]
    width = min(512, chans)
    return pl.pallas_call(
        conv_kernel,
        grid=(chans // width,),
        in_specs=[
            columns(rows, width),
            columns(taps - 1, width),
            columns(taps, width),
            columns(1, width),
            columns(wide, width),
        ],
        out_specs=[columns(rows, width), whole((rows, wide))],
        out_shape=[sds((rows, chans), BF), sds((rows, wide), BF)],
        scratch_shapes=[pltpu.VMEM((rows + 8, width), F32), pltpu.VMEM((rows, wide), F32)],
        compiler_params=params(),
        name="conv_project",
    )(conv_input, rim, weight, bias, proj_weight)


def tile_rows(value, target, lead, groups):
    rows = value.shape[0]
    for block in range(rows // 8):
        for group in range(groups):
            first = (block * groups + group) * 8
            target[lead, first : first + 8, :] = value[
                block * 8 : block * 8 + 8, group * 128 : group * 128 + 128
            ]


def local_kernel(low_rank, states, places, *refs):
    parts, refs = refs[:2], refs[2:]
    (weight_ref, bias_ref, decay_ref, conv_ref, gate_ref, grad_ref) = refs[:6]
    (dt_ref, coef_ref, low) = refs[6:9]
    messages, refs = refs[9 : 8 + places], refs[8 + places :]
    (coef_v, coef, dts, dxs, gs, fwd, bwd, sem) = refs
    step = pl.program_id(0)
    chunks = dts.shape[0]
    rows = conv_ref.shape[0]
    groups = decay_ref.shape[2]

    @pl.when(step == 0)
    def _():
        total = (parts[0][...].astype(F32) + parts[1][...].astype(F32)).astype(BF)
        low[...] = total[:, :low_rank]
        coef_v[...] = jnp.zeros_like(coef_v)
        coef_v[:, : 2 * states] = total[:, low_rank:].astype(F32)
        coef_ref[...] = jnp.transpose(coef_v[...])[: 2 * states, :]
        copy = pltpu.make_async_copy(coef_ref, coef, sem)
        copy.start()
        copy.wait()

    pre = dot(low[...], weight_ref[...]) + bias_ref[...]
    for start in range(0, rows, 16):
        here = slice(start, start + 16)
        p = pre[here, :]
        size = jnp.maximum(p, 0.0) + jnp.log1p(jnp.exp(-jnp.abs(p)))
        gate = gate_ref[here, :].astype(F32)
        grad = grad_ref[here, :].astype(F32) * gate * sigmoid(gate)
        drive = size * conv_ref[here, :].astype(F32)
        for half in range(2):
            for group in range(groups):
                first = ((start // 8 + half) * groups + group) * 8
                lanes = slice(group * 128, group * 128 + 128)
                subs = slice(half * 8, half * 8 + 8)
                dts[step, first : first + 8, :] = size[subs, lanes]
                dt_ref[0, first : first + 8, :] = size[subs, lanes]
                dxs[step, first : first + 8, :] = drive[subs, lanes]
                gs[step, first : first + 8, :] = grad[subs, lanes]

    @pl.when(step == chunks - 1)
    def _():
        batch = 4
        span = groups * 8
        zero = jnp.zeros((groups, 128), F32)
        for lead in range(0, states, batch):
            pairs = [(n, v) for n in range(lead, lead + batch) for v in range(chunks)]
            rates = [-LOG2E * jnp.exp(decay_ref[v, n]) for n, v in pairs]

            def block(index, carry):
                state, run, head, total = (list(part) for part in carry)
                for sub in range(8):
                    token = index * 8 + sub
                    at = pl.ds(index * span + sub, groups, stride=8)
                    size = [dts[v, at, :] for v in range(chunks)]
                    drive = [dxs[v, at, :] for v in range(chunks)]
                    grad = [gs[v, at, :] for v in range(chunks)]
                    if lead == 0:
                        total = [a + b for a, b in zip(total, size)]
                    for k, (n, v) in enumerate(pairs):
                        factor = jnp.exp2(size[v] * rates[k])
                        state[k] = factor * state[k] + drive[v] * coef[n, token]
                        run[k] = run[k] * factor
                        head[k] = head[k] + run[k] * (grad[v] * coef[states + n, token])
                return state, run, head, total

            many = [zero] * len(pairs)
            state, run, head, total = lax.fori_loop(
                0,
                rows // 8,
                block,
                (many, [zero + 1.0] * len(pairs), many, [zero] * chunks),
            )
            for k, (n, v) in enumerate(pairs):
                fwd[v, n] = state[k]
                bwd[v, n] = head[k]
            if lead == 0:
                for v in range(chunks):
                    coarse = total[v].astype(BF).astype(F32)
                    for target in (fwd, bwd):
                        target[v, states] = coarse
                        target[v, states + 1] = total[v] - coarse
        place = lax.axis_index("ctx")
        for mask, message in enumerate(messages, 1):
            message[...] = jnp.where((place ^ mask) > place, fwd[...], bwd[...]).astype(BF)


def local_call(parts, step_weight, step_bias, decay, conv_out, gate, grad, states, places):
    rows, chans = conv_out.shape
    wide = parts[0].shape[1]
    low_rank = step_weight.shape[0]
    chunks, _, groups, _ = decay.shape
    width = groups * 128
    message = (chunks, states + 2, groups, 128)
    big = pltpu.VMEM((chunks, rows * groups, 128), F32)
    return pl.pallas_call(
        functools.partial(local_kernel, low_rank, states, places),
        grid=(chunks,),
        in_specs=[
            whole((rows, wide)),
            whole((rows, wide)),
            columns(low_rank, width),
            columns(1, width),
            whole(decay.shape),
            columns(rows, width),
            columns(rows, width),
            columns(rows, width),
        ],
        out_specs=[
            pl.BlockSpec((1, rows * groups, 128), lambda i: (i, 0, 0)),
            whole((2 * states, rows)),
            whole((rows, low_rank)),
        ]
        + [whole(message)] * (places - 1),
        out_shape=[
            sds((chunks, rows * groups, 128), F32),
            sds((2 * states, rows), F32),
            sds((rows, low_rank), BF),
        ]
        + [sds(message, BF)] * (places - 1),
        scratch_shapes=[
            pltpu.VMEM((rows, 128), F32),
            pltpu.SMEM((2 * states, rows), F32),
            big,
            big,
            big,
            pltpu.VMEM(message, F32),
            pltpu.VMEM(message, F32),
            pltpu.SemaphoreType.DMA,
        ],
        compiler_params=params(),
        name="local_ends",
    )(*parts, step_weight, step_bias, decay, conv_out, gate, grad)


def fold_rows(products, base, groups, target, first, stride):
    total = products[pl.ds(base, 8, stride=groups), :]
    for row in range(1, groups):
        total = total + products[pl.ds(base + row, 8, stride=groups), :]
    target[pl.ds(first, 8, stride=stride), :] = total


def scan_kernel(places, states, opening, *refs):
    (coef, dt_ref, decay_ref, conv_ref, gate_ref, grad_ref, weight_ref, skip_ref) = refs[:8]
    messages, refs = refs[8 : 7 + places], refs[7 + places :]
    if not opening:
        before_ref, refs = refs[0], refs[4:]
    (pre_ref, gate_out, scan_out, small_ref, part_ref) = refs[:5]
    refs = refs[5:]
    (xs, dxs, gs, ys, dds, qs, decayed, coef_out, coef_in, rate, decay_acc, acc, ends, products, factors) = refs
    rows = conv_ref.shape[0]
    groups = decay_ref.shape[2]
    low_rank = weight_ref.shape[0]
    span = groups * 8

    for start in range(0, rows, 16):
        here = slice(start, start + 16)
        conv = conv_ref[here, :].astype(F32)
        gate = gate_ref[here, :].astype(F32)
        grad = grad_ref[here, :].astype(F32) * gate * sigmoid(gate)
        for half in range(2):
            for group in range(groups):
                first = ((start // 8 + half) * groups + group) * 8
                lanes = slice(group * 128, group * 128 + 128)
                subs = slice(half * 8, half * 8 + 8)
                xs[first : first + 8, :] = conv[subs, lanes]
                dxs[first : first + 8, :] = conv[subs, lanes] * dt_ref[0, first : first + 8, :]
                gs[first : first + 8, :] = grad[subs, lanes]

    place = lax.axis_index("ctx")
    for n in range(states):
        rate[n] = -LOG2E * jnp.exp(decay_ref[0, n])
    ends[place] = jnp.zeros(ends.shape[1:], F32)
    for mask, message in enumerate(messages, 1):
        ends[place ^ mask] = message[0].astype(F32)
    totals = [ends[q, states] + ends[q, states + 1] for q in range(places)]
    state, carry = [], []
    for n in range(states):
        before = jnp.zeros((groups, 128), F32)
        after = jnp.zeros((groups, 128), F32)
        for q in range(places - 1):
            reached = jnp.exp2(rate[n] * totals[q]) * before + ends[q, n]
            before = jnp.where(q < place, reached, before)
        for q in range(places - 1, 0, -1):
            reached = jnp.exp2(rate[n] * totals[q]) * after + ends[q, n]
            after = jnp.where(q > place, reached, after)
        state.append(before)
        carry.append(after)

    def forward(index, state):
        state = list(state)
        for sub in range(8):
            token = index * 8 + sub
            at = pl.ds(index * span + sub, groups, stride=8)
            size, drive, grad = dt_ref[0, at, :], dxs[at, :], gs[at, :]
            result = jnp.zeros((groups, 128), F32)
            for lead in range(0, states, 8):
                base = (sub * states + lead) * groups
                for n in range(lead, lead + 8):
                    factor = jnp.exp2(size * rate[n])
                    kept = factor * state[n]
                    factors[token, n] = factor
                    decayed[token, n] = kept
                    state[n] = kept + drive * coef[n, token]
                    result = result + state[n] * coef[states + n, token]
                    row = base + (n - lead) * groups
                    products[row : row + groups, :] = state[n] * grad
                fold_rows(products, base, groups, coef_out, lead * rows + token, rows)
            ys[at, :] = result
        return state

    lax.fori_loop(0, rows // 8, forward, state)

    def backward(hop, both):
        carry, gathered = list(both[0]), list(both[1])
        index = rows // 8 - 1 - hop
        for sub in range(7, -1, -1):
            token = index * 8 + sub
            at = pl.ds(index * span + sub, groups, stride=8)
            size, drive, grad = dt_ref[0, at, :], dxs[at, :], gs[at, :]
            slope = jnp.zeros((groups, 128), F32)
            inner = jnp.zeros((groups, 128), F32)
            for lead in range(0, states, 8):
                base = (sub * states + lead) * groups
                for n in range(lead, lead + 8):
                    adjoint = carry[n] + grad * coef[states + n, token]
                    carry[n] = factors[token, n] * adjoint
                    weighted = adjoint * decayed[token, n] * (size * rate[n])
                    slope = slope + weighted
                    gathered[n] = gathered[n] + weighted
                    inner = inner + adjoint * coef[n, token]
                    row = base + (n - lead) * groups
                    products[row : row + groups, :] = adjoint * drive
                fold_rows(products, base, groups, coef_in, lead * rows + token, rows)
            dds[at, :] = slope
            qs[at, :] = inner
        return carry, gathered

    zeros = [jnp.zeros((groups, 128), F32)] * states
    _, gathered = lax.fori_loop(0, rows // 8, backward, (carry, zeros))
    for n in range(states):
        decay_acc[n * groups : n * groups + groups, :] = gathered[n] * LN2

    for group in range(groups):
        pre_ref[rows : rows + states, group * 128 : group * 128 + 128] = decay_acc[
            pl.ds(group, states, stride=groups), :
        ].astype(BF)
    skip = skip_ref[...]
    bias_sum = jnp.zeros((1, conv_ref.shape[1]), F32)
    skip_sum = jnp.zeros((1, conv_ref.shape[1]), F32)
    for start in range(0, rows, 16):
        here = slice(start, start + 16)

        def natural(read):
            return jnp.concatenate(
                [
                    jnp.concatenate(
                        [
                            read(((start // 8 + half) * groups + group) * 8)
                            for group in range(groups)
                        ],
                        axis=1,
                    )
                    for half in range(2)
                ],
                axis=0,
            )

        size = natural(lambda first: dt_ref[0, first : first + 8, :])
        inner = natural(lambda first: qs[first : first + 8, :])
        slope = natural(lambda first: dds[first : first + 8, :])
        out = natural(lambda first: ys[first : first + 8, :])
        conv = conv_ref[here, :].astype(F32)
        gate = gate_ref[here, :].astype(F32)
        grad = grad_ref[here, :].astype(F32)
        sig = sigmoid(gate)
        scan_grad = grad * gate * sig
        tiny = 1.0 - 0.5 * size * (1.0 - size * (1.0 / 3.0) * (1.0 - 0.25 * size))
        ratio = jnp.where(size < 0.03, tiny, (1.0 - jnp.exp(-size)) / jnp.maximum(size, 0.03))
        d_pre = (LN2 * slope + conv * inner * size) * ratio
        pre_ref[here, :] = d_pre.astype(BF)
        bias_sum = bias_sum + jnp.sum(d_pre, axis=0, keepdims=True)
        skip_sum = skip_sum + jnp.sum(scan_grad * conv, axis=0, keepdims=True)
        scan_out[here, :] = (size * inner + skip * scan_grad).astype(BF)
        gate_out[here, :] = (
            grad * (out + skip * conv) * (sig * (1.0 + gate * (1.0 - sig)))
        ).astype(BF)
    small_ref[...] = jnp.concatenate(
        [bias_sum, skip_sum, jnp.zeros((6, bias_sum.shape[1]), F32)], axis=0
    )

    pre_bf = pre_ref[:rows, :]
    ones = jnp.ones((8, 128), BF)
    coefs = jnp.concatenate(
        [
            sums[:1, n * rows : n * rows + rows]
            for sums in (dot(ones, source[...].astype(BF), NT) for source in (coef_in, coef_out))
            for n in range(states)
        ],
        axis=0,
    )
    wide = dot(weight_ref[...], pre_bf, NT)

    ranks, coef_rows, block = low_rank // places, 2 * states // places, acc.shape[0] // places

    acc[...] = jnp.zeros_like(acc) if opening else before_ref[...]
    for q in range(places):
        at = q * block
        acc[at : at + ranks, :] += wide[q * ranks : (q + 1) * ranks, :]
        acc[at + ranks : at + ranks + coef_rows, :] += coefs[
            q * coef_rows : (q + 1) * coef_rows, :
        ]
    part_ref[...] = acc[...].astype(part_ref.dtype)


def padded(wide):
    return (wide + 127) // 128 * 128


def scan_call(
    places, chunk, coef, dt, decay, conv_out, gate, grad, step_weight, skip, messages, previous
):
    rows, chans = conv_out.shape
    low_rank = step_weight.shape[0]
    chunks, states, groups, _ = decay.shape
    width = groups * 128
    wide = padded(low_rank + 2 * states)
    lead = lambda *shape: pl.BlockSpec((1,) + shape, lambda i: (chunk,) + (0,) * len(shape))
    here = lambda height: pl.BlockSpec((height, width), lambda i: (0, chunk))
    tall = pltpu.VMEM((rows * groups, 128), F32)
    first, last = chunk == 0, chunk == chunks - 1
    in_specs = [
        pl.BlockSpec(memory_space=pltpu.SMEM),
        lead(rows * groups, 128),
        lead(states, groups, 128),
        here(rows),
        here(rows),
        here(rows),
        here(low_rank),
        here(1),
    ]
    in_specs += [lead(states + 2, groups, 128)] * (places - 1)
    aliases = {}
    if not first:
        in_specs += [whole((wide, rows))] + [pl.BlockSpec(memory_space=pl.ANY)] * 3
        aliases = {8 + places: 1, 9 + places: 2, 10 + places: 3}
    return pl.pallas_call(
        functools.partial(scan_kernel, places, states, first),
        grid=(1,),
        in_specs=in_specs,
        out_specs=[
            whole((rows + states, width)),
            here(rows),
            here(rows),
            here(8),
            whole((wide, rows)),
        ],
        out_shape=[
            sds((rows + states, width), BF),
            sds((rows, chans), BF),
            sds((rows, chans), BF),
            sds((8, chans), F32),
            sds((wide, rows), BF if last else F32),
        ],
        scratch_shapes=[
            tall,
            tall,
            tall,
            tall,
            tall,
            tall,
            pltpu.VMEM((rows, states, groups, 128), F32),
            pltpu.VMEM((rows * states, 128), F32),
            pltpu.VMEM((rows * states, 128), F32),
            pltpu.VMEM((states, groups, 128), F32),
            pltpu.VMEM((states * groups, 128), F32),
            pltpu.VMEM((wide, rows), F32),
            pltpu.VMEM((places, states + 2, groups, 128), F32),
            pltpu.VMEM((8 * states * groups, 128), F32),
            pltpu.VMEM((rows, states, groups, 128), F32),
        ],
        input_output_aliases=aliases,
        compiler_params=params(),
        name="scan_gradients",
    )(coef, dt, decay, conv_out, gate, grad, step_weight, skip, *messages, *previous)


def conv_grad_kernel(places, low_rank, back_a, back_b, proj_ref, scan_ref, small_in, input_ref, rim_ref, weight_ref, bias_ref,
                     out_ref, tail_ref, small_ref, ext, grad):
    taps = weight_ref.shape[0]
    rows = input_ref.shape[0]
    fill_extended(ext, rim_ref, input_ref, taps)
    wide = proj_ref.shape[0]
    block = back_a.shape[0] // places
    ranks, coef_rows = low_rank // places, (wide - low_rank) // places
    back = (back_a[...].astype(F32) + back_b[...].astype(F32)).astype(BF).astype(F32)
    order = [back[q * block : q * block + ranks, :] for q in range(places)]
    order += [back[q * block + ranks : q * block + ranks + coef_rows, :] for q in range(places)]
    d_xc = dot(jnp.concatenate(order, axis=0).astype(BF), proj_ref[...], TN)
    sums = [jnp.zeros((1, input_ref.shape[1]), F32) for _ in range(taps + 1)]
    for start in range(0, rows, 16):
        here = slice(start, start + 16)
        pre = conv_block(ext, weight_ref, bias_ref[...], taps, start, 16)
        sig = sigmoid(pre)
        value = (d_xc[here, :] + scan_ref[here, :].astype(F32)) * (sig * (1.0 + pre * (1.0 - sig)))
        grad[here, :] = value
        for tap in range(taps):
            first = 8 - (taps - 1) + tap + start
            sums[tap] = sums[tap] + jnp.sum(value * ext[first : first + 16, :], axis=0, keepdims=True)
        sums[taps] = sums[taps] + jnp.sum(value, axis=0, keepdims=True)
    grad[rows : rows + 8, :] = jnp.zeros((8, grad.shape[1]), F32)
    for start in range(0, rows, 16):
        total = jnp.zeros((16, grad.shape[1]), F32)
        for tap in range(taps):
            first = start + taps - 1 - tap
            total = total + weight_ref[tap : tap + 1, :] * grad[first : first + 16, :]
        out_ref[start : start + 16, :] = total.astype(BF)
    tail_ref[...] = total
    small_ref[...] = jnp.concatenate(
        sums + [small_in[0 : 7 - taps, :], grad[0:8, :]], axis=0
    ).astype(BF)


def conv_grad_call(places, low_rank, backs, proj_weight, scan_part, small, conv_input, rim, weight, bias):
    rows, chans = conv_input.shape
    taps = weight.shape[0]
    wide = proj_weight.shape[0]
    width = min(512, chans)
    return pl.pallas_call(
        functools.partial(conv_grad_kernel, places, low_rank),
        grid=(chans // width,),
        in_specs=[
            whole(backs[0].shape),
            whole(backs[1].shape),
            columns(wide, width),
            columns(rows, width),
            columns(8, width),
            columns(rows, width),
            columns(taps - 1, width),
            columns(taps, width),
            columns(1, width),
        ],
        out_specs=[columns(rows, width), columns(16, width), columns(16, width)],
        out_shape=[sds((rows, chans), BF), sds((16, chans), F32), sds((16, chans), BF)],
        scratch_shapes=[pltpu.VMEM((rows + 8, width), F32), pltpu.VMEM((rows + 8, width), F32)],
        compiler_params=params(),
        name="conv_gradients",
    )(*backs, proj_weight, scan_part, small, conv_input, rim, weight, bias)


def cut_kernel(places, back_a, back_b, *refs):
    cuts, (back,) = refs[:places], refs[places:]
    place = lax.axis_index("ctx")
    height = back.shape[0] // places
    back[...] = back_a[...].astype(F32) + back_b[...].astype(F32)
    for mask in range(places):
        cuts[mask][...] = back[pl.ds((place ^ mask) * height, height), :].astype(BF)


def cut_call(places, backs):
    wide, rows = backs[0].shape
    return pl.pallas_call(
        functools.partial(cut_kernel, places),
        out_shape=[sds((wide // places, rows), BF)] * places,
        scratch_shapes=[pltpu.VMEM((wide, rows), F32)],
        compiler_params=params(),
        name="cut_rows",
    )(*backs)


def step_kernel(chunks, ranks, near, *refs):
    lows, steps, (mine_ref, theirs_ref) = refs[:near], refs[near:-2], refs[-2:]
    place = lax.axis_index("ctx")
    rows = lows[0].shape[1]
    pair = pl.ds(pl.multiple_of(lax.div(place, 2) * (2 * ranks), 16), 2 * ranks)
    odd = lax.rem(place, 2) == 1
    for chunk in range(chunks):

        @pl.when(pl.program_id(0) == chunk)
        def _():
            total = jnp.zeros((2 * ranks, mine_ref.shape[1]), F32)
            decay = jnp.zeros((mine_ref.shape[0] - ranks, mine_ref.shape[1]), F32)
            for low, step in zip(lows, steps[chunk * near : (chunk + 1) * near]):
                total = total + dot(low[pair, :], step[:rows, :])
                decay = decay + step[rows:, :].astype(F32)
            mine_ref[:ranks, :] = jnp.where(odd, total[ranks:, :], total[:ranks, :])
            theirs_ref[:ranks, :] = jnp.where(odd, total[:ranks, :], total[ranks:, :]).astype(BF)
            mine_ref[ranks:, :] = decay
            theirs_ref[ranks:, :] = decay.astype(BF)


def step_call(ranks, lows, steps):
    rows = lows[0].shape[1]
    chunks = len(steps) // len(lows)
    tall, width = steps[0].shape
    height = ranks + tall - rows
    return pl.pallas_call(
        functools.partial(step_kernel, chunks, ranks, len(lows)),
        grid=(chunks,),
        in_specs=[whole(lows[0].shape)] * len(lows) + [whole((tall, width))] * len(steps),
        out_specs=[columns(height, width)] * 2,
        out_shape=[sds((height, width * chunks), F32), sds((height, width * chunks), BF)],
        compiler_params=params(),
        name="step_products",
    )(*lows, *steps)


def rows_kernel(ranks, places, *refs):
    cuts, blocks, refs = refs[:places], refs[places : 2 * places], refs[2 * places :]
    mine_ref, theirs_ref, out_ref, coef_ref, step_ref, decay_ref = refs
    total = jnp.zeros((cuts[0].shape[0], out_ref.shape[1]), F32)
    for cut, block in zip(cuts, blocks):
        total = total + dot(cut[...], block[...])
    out_ref[...] = total[:ranks, :]
    coef_ref[...] = total[ranks : ranks + coef_ref.shape[0], :]
    step_ref[...] = mine_ref[:ranks, :] + theirs_ref[:ranks, :].astype(F32)
    decay_ref[...] = mine_ref[ranks:, :] + theirs_ref[ranks:, :].astype(F32)


def rows_call(ranks, coef_rows, cuts, blocks, mine, theirs):
    rows, chans = blocks[0].shape
    width = min(1024, chans)
    heights = (ranks, coef_rows, ranks, mine.shape[0] - ranks)
    return pl.pallas_call(
        functools.partial(rows_kernel, ranks, len(cuts)),
        grid=(chans // width,),
        in_specs=[whole(cuts[0].shape)] * len(cuts)
        + [columns(rows, width)] * len(blocks)
        + [columns(mine.shape[0], width)] * 2,
        out_specs=[columns(height, width) for height in heights],
        out_shape=[sds((height, chans), F32) for height in heights],
        compiler_params=params(),
        name="row_gradients",
    )(*cuts, *blocks, mine, theirs)


def last_kernel(places, taps, *refs):
    (_, tail_ref, weight_ref) = refs[:3]
    late, refs = refs[3 : 3 + places], refs[3 + places :]
    (out_ref, conv_w, conv_b, step_b, skip, fix) = refs
    fix[...] = tail_ref[...]
    inside = lax.axis_index("ctx") < places - 1
    following = jnp.where(inside, late[places - 1][8:16, :].astype(F32), 0.0)
    for row in range(taps - 1):
        extra = jnp.zeros((1, fix.shape[1]), F32)
        for tap in range(row + 1):
            extra = extra + weight_ref[tap : tap + 1, :] * following[row - tap : row - tap + 1, :]
        at = 16 - (taps - 1) + row
        fix[at : at + 1, :] += extra
    out_ref[...] = fix[...].astype(BF)
    total = late[0][...].astype(F32)
    for part in late[1:]:
        total = total + part[...].astype(F32)
    conv_w[...] = total[:taps, :]
    conv_b[...] = total[taps : taps + 1, :]
    step_b[...] = total[taps + 1 : taps + 2, :]
    skip[...] = total[taps + 2 : taps + 3, :]


def last_call(main, tail, weight, late):
    rows, chans = main.shape
    taps = weight.shape[0]
    places = len(late)
    return pl.pallas_call(
        functools.partial(last_kernel, places, taps),
        grid=(1,),
        in_specs=[pl.BlockSpec(memory_space=pl.ANY), columns(16, chans), columns(taps, chans)]
        + [columns(16, chans)] * places,
        out_specs=[
            pl.BlockSpec((16, chans), lambda i: (rows // 16 - 1, i)),
            columns(taps, chans),
        ]
        + [columns(1, chans)] * 3,
        out_shape=[sds((rows, chans), BF), sds((taps, chans), F32)] + [sds((1, chans), F32)] * 3,
        scratch_shapes=[pltpu.VMEM((16, chans), F32)],
        input_output_aliases={0: 0},
        compiler_params=params(),
        name="last_rows",
    )(main, tail, weight, *late)


def exchange(block, axis):
    return lax.all_to_all(block, axis, split_axis=0, concat_axis=0, tiled=True)


def swap(block, axis, mask):
    return lax.ppermute(block, axis, [(i, i ^ mask) for i in range(lax.axis_size(axis))])


tie = lax.optimization_barrier


def spread(block):
    return [block] + [swap(block, "ctx", mask) for mask in range(1, min(lax.axis_size("ctx"), 3))]


def spread_on(blocks):
    places = lax.axis_size("ctx")
    if places == 4:
        return blocks + [swap(blocks[2], "ctx", 1)]
    return blocks + [swap(blocks[0], "ctx", mask) for mask in range(3, places)]


def gather_near(block):
    return [block] + [swap(block, "ctx", mask) for mask in range(2, lax.axis_size("ctx"), 2)]


def chan_sum(part):
    mask, peers = 1, lax.axis_size("chan")
    while True:
        other = swap(part, "chan", mask)
        mask *= 2
        if mask == peers:
            return part, other
        part = (part.astype(F32) + other.astype(F32)).astype(BF)


def body(
    conv_input,
    gate_input,
    out_grad,
    conv_weight,
    conv_bias,
    proj_weight,
    step_weight,
    step_bias,
    decay_log,
    skip_gain,
):
    rows, chans = conv_input.shape
    taps = conv_weight.shape[0]
    low_rank = step_weight.shape[0]
    states = decay_log.shape[0]
    places = lax.axis_size("ctx")
    groups = group_rows(chans)
    decay = decay_log.reshape(states, -1, groups, 128).transpose(1, 0, 2, 3)
    conv_bias = conv_bias[None, :]
    step_bias = step_bias[None, :]
    skip_gain = skip_gain[None, :]

    chunks = decay.shape[0]
    rim = shift(conv_input[rows - (taps - 1) :], "ctx", 1)
    conv_out, part = conv_call(conv_input, rim, conv_weight, conv_bias, proj_weight)
    blocks = spread(conv_out)
    parts = chan_sum(part)
    dt, coef, low, *messages = local_call(
        parts, step_weight, step_bias, decay, conv_out, gate_input, out_grad, states, places
    )
    messages, blocks = tie((messages, blocks))
    messages = [swap(message, "ctx", mask) for mask, message in enumerate(messages, 1)]
    messages, blocks, low = tie((messages, blocks, low))
    blocks = spread_on(blocks)
    lows = gather_near(jnp.transpose(low))
    previous, steps = [], []
    for chunk in range(chunks):
        message, grad_gate, scan_part, small, part = scan_call(
            places, chunk, coef, dt, decay, conv_out, gate_input, out_grad, step_weight,
            skip_gain, messages, previous,
        )
        previous = [part, grad_gate, scan_part, small]
        if chunk == 0:
            previous, blocks = tie((previous, blocks))
        else:
            previous, steps, lows = tie((previous, steps, lows))
        steps += gather_near(message)
    part, grad_gate, scan_part, small = previous
    backs = chan_sum(part)
    cuts = cut_call(places, backs)
    cuts, lows = tie((cuts, lows))
    cuts = [cuts[0]] + [swap(cut, "ctx", mask) for mask, cut in enumerate(cuts[1:], 1)]
    mine, theirs = step_call(low_rank // places, lows, steps)
    backs, theirs = tie((backs, theirs))
    theirs = swap(theirs, "ctx", 1)
    main, tail, sums = conv_grad_call(
        places, low_rank, backs, proj_weight, scan_part, small, conv_input, rim, conv_weight,
        conv_bias,
    )
    sums, cuts = tie((sums, cuts))
    late = [sums] + [rotate(sums, "ctx", hop) for hop in range(1, places)]
    grad_proj, grad_coef, grad_step, decay_grad = rows_call(
        low_rank // places, 2 * states // places, cuts, blocks, mine, theirs
    )
    grad_input, conv_w, conv_b, step_b, skip = last_call(main, tail, conv_weight, late)
    return (
        grad_input,
        grad_gate,
        grad_proj,
        grad_coef,
        grad_step,
        conv_w,
        conv_b[0],
        step_b[0],
        decay_grad,
        skip[0],
    )


def solution(mesh):
    tokens, columns_, chan = P("ctx", "chan"), P(None, "chan"), P("chan")
    in_specs = (
        tokens, tokens, tokens, columns_, chan, columns_, columns_, chan, columns_, chan,
    )
    out_specs = (
        tokens, tokens, tokens, tokens, tokens, columns_, chan, chan, columns_, chan,
    )
    return jax.shard_map(body, mesh=mesh, in_specs=in_specs, out_specs=out_specs, check_vma=False)
```

```python
import functools

import jax
import jax.numpy as jnp
from jax import lax
from jax.experimental import pallas as pl
from jax.experimental.pallas import tpu as pltpu
from jax.sharding import PartitionSpec as P

BF = jnp.bfloat16
F32 = jnp.float32
LOG2E = 1.4426950408889634
LN2 = 0.6931471805599453
VMEM_BYTES = 56 * 1024 * 1024
NT = (((1,), (1,)), ((), ()))
TN = (((0,), (0,)), ((), ()))


def group_rows(chans):
    for rows in (8, 4, 2, 1):
        if chans % (rows * 128) == 0:
            return rows
    return 1


def dot(a, b, dims=(((1,), (0,)), ((), ()))):
    return lax.dot_general(a, b, dims, preferred_element_type=F32)


def params(**more):
    return pltpu.CompilerParams(vmem_limit_bytes=VMEM_BYTES, **more)


def sds(shape, dtype):
    return jax.ShapeDtypeStruct(shape, dtype)


def whole(shape):
    return pl.BlockSpec(shape, lambda i: (0,) * len(shape))


def columns(rows, width):
    return pl.BlockSpec((rows, width), lambda i: (0, i))


def sigmoid(v):
    return 0.5 + 0.5 * jnp.tanh(0.5 * v)


def rotate(block, axis, distance):
    count = lax.axis_size(axis)
    return lax.ppermute(block, axis, [(i, (i + distance) % count) for i in range(count)])


def shift(block, axis, distance):
    count = lax.axis_size(axis)
    route = [(i, i + distance) for i in range(count) if 0 <= i + distance < count]
    return lax.ppermute(block, axis, route)


def fill_extended(ext, rim_ref, input_ref, taps):
    rows = input_ref.shape[0]
    ext[8 - (taps - 1) : 8, :] = rim_ref[...].astype(F32)
    ext[8 : 8 + rows, :] = input_ref[...].astype(F32)


def conv_block(ext, weight, bias, taps, start, rows):
    total = bias + jnp.zeros((rows, ext.shape[1]), F32)
    for tap in range(taps):
        first = 8 - (taps - 1) + tap + start
        total = total + weight[tap : tap + 1, :] * ext[first : first + rows, :]
    return total


def conv_kernel(input_ref, rim_ref, weight_ref, bias_ref, proj_ref, out_ref, part_ref, ext, acc):
    step = pl.program_id(0)
    taps = weight_ref.shape[0]
    rows = input_ref.shape[0]
    fill_extended(ext, rim_ref, input_ref, taps)
    for start in range(0, rows, 16):
        pre = conv_block(ext, weight_ref, bias_ref[...], taps, start, 16)
        out_ref[start : start + 16, :] = (pre * sigmoid(pre)).astype(BF)
    part = dot(out_ref[...], proj_ref[...], NT)

    @pl.when(step == 0)
    def _():
        acc[...] = part

    @pl.when(step > 0)
    def _():
        acc[...] += part

    @pl.when(step == pl.num_programs(0) - 1)
    def _():
        part_ref[...] = acc[...].astype(BF)


def conv_call(conv_input, rim, weight, bias, proj_weight):
    rows, chans = conv_input.shape
    taps = weight.shape[0]
    wide = proj_weight.shape[0]
    width = min(512, chans)
    return pl.pallas_call(
        conv_kernel,
        grid=(chans // width,),
        in_specs=[
            columns(rows, width),
            columns(taps - 1, width),
            columns(taps, width),
            columns(1, width),
            columns(wide, width),
        ],
        out_specs=[columns(rows, width), whole((rows, wide))],
        out_shape=[sds((rows, chans), BF), sds((rows, wide), BF)],
        scratch_shapes=[pltpu.VMEM((rows + 8, width), F32), pltpu.VMEM((rows, wide), F32)],
        compiler_params=params(),
        name="conv_project",
    )(conv_input, rim, weight, bias, proj_weight)


def tile_rows(value, target, lead, groups):
    rows = value.shape[0]
    for block in range(rows // 8):
        for group in range(groups):
            first = (block * groups + group) * 8
            target[lead, first : first + 8, :] = value[
                block * 8 : block * 8 + 8, group * 128 : group * 128 + 128
            ]


def local_kernel(low_rank, states, places, *refs):
    parts, refs = refs[:2], refs[2:]
    (weight_ref, bias_ref, decay_ref, conv_ref, gate_ref, grad_ref) = refs[:6]
    (dt_ref, dx_ref, g_ref, coef_ref, low) = refs[6:11]
    messages, refs = refs[11 : 10 + places], refs[10 + places :]
    (coef_v, coef, tiles, dts, dxs, gs, fwd, bwd, sem) = refs
    step = pl.program_id(0)
    chunks = dts.shape[0]
    rows = conv_ref.shape[0]
    groups = decay_ref.shape[2]

    @pl.when(step == 0)
    def _():
        total = (parts[0][...].astype(F32) + parts[1][...].astype(F32)).astype(BF)
        low[...] = total[:, :low_rank]
        coef_v[...] = jnp.zeros_like(coef_v)
        coef_v[:, : 2 * states] = total[:, low_rank:].astype(F32)
        coef_ref[...] = jnp.transpose(coef_v[...])[: 2 * states, :]
        copy = pltpu.make_async_copy(coef_ref, coef, sem)
        copy.start()
        copy.wait()

    pre = dot(low[...], weight_ref[...]) + bias_ref[...]
    for start in range(0, rows, 16):
        here = slice(start, start + 16)
        p = pre[here, :]
        size = jnp.maximum(p, 0.0) + jnp.log1p(jnp.exp(-jnp.abs(p)))
        gate = gate_ref[here, :].astype(F32)
        grad = grad_ref[here, :].astype(F32) * gate * sigmoid(gate)
        drive = size * conv_ref[here, :].astype(F32)
        for half in range(2):
            for group in range(groups):
                first = ((start // 8 + half) * groups + group) * 8
                lanes = slice(group * 128, group * 128 + 128)
                subs = slice(half * 8, half * 8 + 8)
                tiles[0, first : first + 8, :] = size[subs, lanes]
                tiles[1, first : first + 8, :] = drive[subs, lanes]
                tiles[2, first : first + 8, :] = grad[subs, lanes]

    def relay(index, _):
        for sub in range(8):
            token = index * 8 + sub
            at = pl.ds(index * groups * 8 + sub, groups, stride=8)
            for kind, (held, out) in enumerate(((dts, dt_ref), (dxs, dx_ref), (gs, g_ref))):
                row = tiles[kind, at, :]
                held[step, token] = row
                out[0, token] = row
        return 0

    lax.fori_loop(0, rows // 8, relay, 0)

    @pl.when(step == chunks - 1)
    def _():
        batch = 4
        zero = jnp.zeros((groups, 128), F32)
        for lead in range(0, states, batch):
            pairs = [(n, v) for n in range(lead, lead + batch) for v in range(chunks)]
            rates = [-LOG2E * jnp.exp(decay_ref[v, n]) for n, v in pairs]

            def block(index, carry):
                state, run, head, total = (list(part) for part in carry)
                for sub in range(8):
                    token = index * 8 + sub
                    size = [dts[v, token] for v in range(chunks)]
                    drive = [dxs[v, token] for v in range(chunks)]
                    grad = [gs[v, token] for v in range(chunks)]
                    if lead == 0:
                        total = [a + b for a, b in zip(total, size)]
                    for k, (n, v) in enumerate(pairs):
                        factor = jnp.exp2(size[v] * rates[k])
                        state[k] = factor * state[k] + drive[v] * coef[n, token]
                        run[k] = run[k] * factor
                        head[k] = head[k] + run[k] * (grad[v] * coef[states + n, token])
                return state, run, head, total

            many = [zero] * len(pairs)
            state, run, head, total = lax.fori_loop(
                0,
                rows // 8,
                block,
                (many, [zero + 1.0] * len(pairs), many, [zero] * chunks),
            )
            for k, (n, v) in enumerate(pairs):
                fwd[v, n] = state[k]
                bwd[v, n] = head[k]
            if lead == 0:
                for v in range(chunks):
                    coarse = total[v].astype(BF).astype(F32)
                    for target in (fwd, bwd):
                        target[v, states] = coarse
                        target[v, states + 1] = total[v] - coarse
        place = lax.axis_index("ctx")
        for mask, message in enumerate(messages, 1):
            message[...] = jnp.where((place ^ mask) > place, fwd[...], bwd[...]).astype(BF)


def local_call(parts, step_weight, step_bias, decay, conv_out, gate, grad, states, places):
    rows, chans = conv_out.shape
    wide = parts[0].shape[1]
    low_rank = step_weight.shape[0]
    chunks, _, groups, _ = decay.shape
    width = groups * 128
    message = (chunks, states + 2, groups, 128)
    dense = (chunks, rows, groups, 128)
    big = pltpu.VMEM(dense, F32)
    return pl.pallas_call(
        functools.partial(local_kernel, low_rank, states, places),
        grid=(chunks,),
        in_specs=[
            whole((rows, wide)),
            whole((rows, wide)),
            columns(low_rank, width),
            columns(1, width),
            whole(decay.shape),
            columns(rows, width),
            columns(rows, width),
            columns(rows, width),
        ],
        out_specs=[
            *[pl.BlockSpec((1, rows, groups, 128), lambda i: (i, 0, 0, 0))] * 3,
            whole((2 * states, rows)),
            whole((rows, low_rank)),
        ]
        + [whole(message)] * (places - 1),
        out_shape=[
            *[sds(dense, F32)] * 3,
            sds((2 * states, rows), F32),
            sds((rows, low_rank), BF),
        ]
        + [sds(message, BF)] * (places - 1),
        scratch_shapes=[
            pltpu.VMEM((rows, 128), F32),
            pltpu.SMEM((2 * states, rows), F32),
            pltpu.VMEM((3, rows * groups, 128), F32),
            big,
            big,
            big,
            pltpu.VMEM(message, F32),
            pltpu.VMEM(message, F32),
            pltpu.SemaphoreType.DMA,
        ],
        compiler_params=params(),
        name="local_ends",
    )(*parts, step_weight, step_bias, decay, conv_out, gate, grad)


def fold_rows(products, base, groups, target, first):
    total = products[pl.ds(base, 8, stride=groups), :]
    for row in range(1, groups):
        total = total + products[pl.ds(base + row, 8, stride=groups), :]
    target[pl.ds(pl.multiple_of(first, 8), 8), :] = total


def scan_kernel(places, states, opening, *refs):
    (coef, dt_ref, dx_ref, g_ref, decay_ref, skips_ref) = refs[:6]
    (conv_ref, gate_ref, grad_ref, weight_ref, skip_ref) = refs[6:11]
    messages, refs = refs[11 : 10 + places], refs[10 + places :]
    if not opening:
        before_ref, refs = refs[0], refs[4:]
    (pre_ref, gate_out, scan_out, small_ref, part_ref) = refs[:5]
    refs = refs[5:]
    (ys, dds, qs, decayed, coef_out, coef_in, rate, decay_acc, acc, ends, products, factors) = refs
    rows = conv_ref.shape[0]
    groups = decay_ref.shape[2]
    low_rank = weight_ref.shape[0]
    span = groups * 8

    place = lax.axis_index("ctx")
    for n in range(states):
        rate[n] = -LOG2E * jnp.exp(decay_ref[0, n])
    ends[place] = jnp.zeros(ends.shape[1:], F32)
    for mask, message in enumerate(messages, 1):
        ends[place ^ mask] = message[0].astype(F32)
    totals = [ends[q, states] + ends[q, states + 1] for q in range(places)]
    state, carry = [], []
    for n in range(states):
        before = jnp.zeros((groups, 128), F32)
        after = jnp.zeros((groups, 128), F32)
        for q in range(places - 1):
            reached = jnp.exp2(rate[n] * totals[q]) * before + ends[q, n]
            before = jnp.where(q < place, reached, before)
        for q in range(places - 1, 0, -1):
            reached = jnp.exp2(rate[n] * totals[q]) * after + ends[q, n]
            after = jnp.where(q > place, reached, after)
        state.append(before)
        carry.append(after)

    def forward(index, state):
        state = list(state)
        for sub in range(8):
            token = index * 8 + sub
            at = pl.ds(index * span + sub, groups, stride=8)
            size, drive, grad = dt_ref[0, token], dx_ref[0, token], g_ref[0, token]
            result = jnp.zeros((groups, 128), F32)
            for lead in range(0, states, 8):
                base = (sub * states + lead) * groups
                for n in range(lead, lead + 8):
                    factor = jnp.exp2(size * rate[n])
                    kept = factor * state[n]
                    factors[token, n] = factor
                    decayed[token, n] = kept
                    state[n] = kept + drive * coef[n, token]
                    result = result + state[n] * coef[states + n, token]
                    row = base + (n - lead) * groups
                    products[row : row + groups, :] = state[n] * grad
                fold_rows(products, base, groups, coef_out, token * states + lead)
            ys[at, :] = result
        return state

    lax.fori_loop(0, rows // 8, forward, state)

    def backward(hop, both):
        carry, gathered = list(both[0]), list(both[1])
        index = rows // 8 - 1 - hop
        for sub in range(7, -1, -1):
            token = index * 8 + sub
            at = pl.ds(index * span + sub, groups, stride=8)
            size, drive, grad = dt_ref[0, token], dx_ref[0, token], g_ref[0, token]
            slope = jnp.zeros((groups, 128), F32)
            inner = jnp.zeros((groups, 128), F32)
            for lead in range(0, states, 8):
                base = (sub * states + lead) * groups
                for n in range(lead, lead + 8):
                    adjoint = carry[n] + grad * coef[states + n, token]
                    carry[n] = factors[token, n] * adjoint
                    weighted = adjoint * decayed[token, n] * (size * rate[n])
                    slope = slope + weighted
                    gathered[n] = gathered[n] + weighted
                    inner = inner + adjoint * coef[n, token]
                    row = base + (n - lead) * groups
                    products[row : row + groups, :] = adjoint * drive
                fold_rows(products, base, groups, coef_in, token * states + lead)
            tiny = 1.0 - 0.5 * size * (1.0 - size * (1.0 / 3.0) * (1.0 - 0.25 * size))
            ratio = jnp.where(size < 0.03, tiny, (1.0 - jnp.exp(-size)) / jnp.maximum(size, 0.03))
            dds[at, :] = (LN2 * slope + drive * inner) * ratio
            qs[at, :] = size * inner + skips_ref[0] * grad
        return carry, gathered

    zeros = [jnp.zeros((groups, 128), F32)] * states
    _, gathered = lax.fori_loop(0, rows // 8, backward, (carry, zeros))
    for n in range(states):
        decay_acc[n * groups : n * groups + groups, :] = gathered[n] * LN2

    for group in range(groups):
        pre_ref[rows : rows + states, group * 128 : group * 128 + 128] = decay_acc[
            pl.ds(group, states, stride=groups), :
        ].astype(BF)
    skip = skip_ref[...]
    bias_sum = jnp.zeros((1, conv_ref.shape[1]), F32)
    skip_sum = jnp.zeros((1, conv_ref.shape[1]), F32)
    for start in range(0, rows, 16):
        here = slice(start, start + 16)

        def natural(read):
            return jnp.concatenate(
                [
                    jnp.concatenate(
                        [
                            read(((start // 8 + half) * groups + group) * 8)
                            for group in range(groups)
                        ],
                        axis=1,
                    )
                    for half in range(2)
                ],
                axis=0,
            )

        d_pre = natural(lambda first: dds[first : first + 8, :])
        out = natural(lambda first: ys[first : first + 8, :])
        conv = conv_ref[here, :].astype(F32)
        gate = gate_ref[here, :].astype(F32)
        grad = grad_ref[here, :].astype(F32)
        sig = sigmoid(gate)
        scan_grad = grad * gate * sig
        pre_ref[here, :] = d_pre.astype(BF)
        bias_sum = bias_sum + jnp.sum(d_pre, axis=0, keepdims=True)
        skip_sum = skip_sum + jnp.sum(scan_grad * conv, axis=0, keepdims=True)
        scan_out[here, :] = natural(lambda first: qs[first : first + 8, :]).astype(BF)
        gate_out[here, :] = (
            grad * (out + skip * conv) * (sig * (1.0 + gate * (1.0 - sig)))
        ).astype(BF)
    small_ref[...] = jnp.concatenate(
        [bias_sum, skip_sum, jnp.zeros((6, bias_sum.shape[1]), F32)], axis=0
    )

    pre_bf = pre_ref[:rows, :]
    lanes = lax.broadcasted_iota(jnp.int32, (2 * states, 128), 0)
    coefs = jnp.zeros((2 * states, rows), F32)
    for n in range(states):
        at = pl.ds(n, rows, stride=states)
        for kind, source in enumerate((coef_in, coef_out)):
            pick = jnp.where(lanes == kind * states + n, 1.0, 0.0).astype(BF)
            coefs = coefs + dot(pick, source[at, :].astype(BF), NT)
    wide = dot(weight_ref[...], pre_bf, NT)

    ranks, coef_rows, block = low_rank // places, 2 * states // places, acc.shape[0] // places

    acc[...] = jnp.zeros_like(acc) if opening else before_ref[...]
    for q in range(places):
        at = q * block
        acc[at : at + ranks, :] += wide[q * ranks : (q + 1) * ranks, :]
        acc[at + ranks : at + ranks + coef_rows, :] += coefs[
            q * coef_rows : (q + 1) * coef_rows, :
        ]
    part_ref[...] = acc[...].astype(part_ref.dtype)


def padded(wide):
    return (wide + 127) // 128 * 128


def scan_call(
    places, chunk, coef, dense, decay, skips, conv_out, gate, grad, step_weight, skip, messages,
    previous,
):
    rows, chans = conv_out.shape
    low_rank = step_weight.shape[0]
    chunks, states, groups, _ = decay.shape
    width = groups * 128
    wide = padded(low_rank + 2 * states)
    lead = lambda *shape: pl.BlockSpec((1,) + shape, lambda i: (chunk,) + (0,) * len(shape))
    here = lambda height: pl.BlockSpec((height, width), lambda i: (0, chunk))
    tall = pltpu.VMEM((rows * groups, 128), F32)
    first, last = chunk == 0, chunk == chunks - 1
    in_specs = [
        pl.BlockSpec(memory_space=pltpu.SMEM),
        lead(rows, groups, 128),
        lead(rows, groups, 128),
        lead(rows, groups, 128),
        lead(states, groups, 128),
        lead(groups, 128),
        here(rows),
        here(rows),
        here(rows),
        here(low_rank),
        here(1),
    ]
    in_specs += [lead(states + 2, groups, 128)] * (places - 1)
    aliases = {}
    if not first:
        in_specs += [whole((wide, rows))] + [pl.BlockSpec(memory_space=pl.ANY)] * 3
        aliases = {11 + places: 1, 12 + places: 2, 13 + places: 3}
    return pl.pallas_call(
        functools.partial(scan_kernel, places, states, first),
        grid=(1,),
        in_specs=in_specs,
        out_specs=[
            whole((rows + states, width)),
            here(rows),
            here(rows),
            here(8),
            whole((wide, rows)),
        ],
        out_shape=[
            sds((rows + states, width), BF),
            sds((rows, chans), BF),
            sds((rows, chans), BF),
            sds((8, chans), F32),
            sds((wide, rows), BF if last else F32),
        ],
        scratch_shapes=[
            tall,
            tall,
            tall,
            pltpu.VMEM((rows, states, groups, 128), F32),
            pltpu.VMEM((rows * states, 128), F32),
            pltpu.VMEM((rows * states, 128), F32),
            pltpu.VMEM((states, groups, 128), F32),
            pltpu.VMEM((states * groups, 128), F32),
            pltpu.VMEM((wide, rows), F32),
            pltpu.VMEM((places, states + 2, groups, 128), F32),
            pltpu.VMEM((8 * states * groups, 128), F32),
            pltpu.VMEM((rows, states, groups, 128), F32),
        ],
        input_output_aliases=aliases,
        compiler_params=params(),
        name="scan_gradients",
    )(
        coef, *dense, decay, skips, conv_out, gate, grad, step_weight, skip, *messages, *previous
    )


def conv_grad_kernel(places, low_rank, back_a, back_b, proj_ref, scan_ref, small_in, input_ref, rim_ref, weight_ref, bias_ref,
                     out_ref, tail_ref, small_ref, ext, grad):
    taps = weight_ref.shape[0]
    rows = input_ref.shape[0]
    fill_extended(ext, rim_ref, input_ref, taps)
    wide = proj_ref.shape[0]
    block = back_a.shape[0] // places
    ranks, coef_rows = low_rank // places, (wide - low_rank) // places
    back = (back_a[...].astype(F32) + back_b[...].astype(F32)).astype(BF).astype(F32)
    order = [back[q * block : q * block + ranks, :] for q in range(places)]
    order += [back[q * block + ranks : q * block + ranks + coef_rows, :] for q in range(places)]
    d_xc = dot(jnp.concatenate(order, axis=0).astype(BF), proj_ref[...], TN)
    sums = [jnp.zeros((1, input_ref.shape[1]), F32) for _ in range(taps + 1)]
    for start in range(0, rows, 16):
        here = slice(start, start + 16)
        pre = conv_block(ext, weight_ref, bias_ref[...], taps, start, 16)
        sig = sigmoid(pre)
        value = (d_xc[here, :] + scan_ref[here, :].astype(F32)) * (sig * (1.0 + pre * (1.0 - sig)))
        grad[here, :] = value
        for tap in range(taps):
            first = 8 - (taps - 1) + tap + start
            sums[tap] = sums[tap] + jnp.sum(value * ext[first : first + 16, :], axis=0, keepdims=True)
        sums[taps] = sums[taps] + jnp.sum(value, axis=0, keepdims=True)
    grad[rows : rows + 8, :] = jnp.zeros((8, grad.shape[1]), F32)
    for start in range(0, rows, 16):
        total = jnp.zeros((16, grad.shape[1]), F32)
        for tap in range(taps):
            first = start + taps - 1 - tap
            total = total + weight_ref[tap : tap + 1, :] * grad[first : first + 16, :]
        out_ref[start : start + 16, :] = total.astype(BF)
    tail_ref[...] = total
    small_ref[...] = jnp.concatenate(
        sums + [small_in[0 : 7 - taps, :], grad[0:8, :]], axis=0
    ).astype(BF)


def conv_grad_call(places, low_rank, backs, proj_weight, scan_part, small, conv_input, rim, weight, bias):
    rows, chans = conv_input.shape
    taps = weight.shape[0]
    wide = proj_weight.shape[0]
    width = min(512, chans)
    return pl.pallas_call(
        functools.partial(conv_grad_kernel, places, low_rank),
        grid=(chans // width,),
        in_specs=[
            whole(backs[0].shape),
            whole(backs[1].shape),
            columns(wide, width),
            columns(rows, width),
            columns(8, width),
            columns(rows, width),
            columns(taps - 1, width),
            columns(taps, width),
            columns(1, width),
        ],
        out_specs=[columns(rows, width), columns(16, width), columns(16, width)],
        out_shape=[sds((rows, chans), BF), sds((16, chans), F32), sds((16, chans), BF)],
        scratch_shapes=[pltpu.VMEM((rows + 8, width), F32), pltpu.VMEM((rows + 8, width), F32)],
        compiler_params=params(),
        name="conv_gradients",
    )(*backs, proj_weight, scan_part, small, conv_input, rim, weight, bias)


def cut_kernel(places, back_a, back_b, *refs):
    cuts, (back,) = refs[:places], refs[places:]
    place = lax.axis_index("ctx")
    height = back.shape[0] // places
    back[...] = back_a[...].astype(F32) + back_b[...].astype(F32)
    for mask in range(places):
        cuts[mask][...] = back[pl.ds((place ^ mask) * height, height), :].astype(BF)


def cut_call(places, backs):
    wide, rows = backs[0].shape
    return pl.pallas_call(
        functools.partial(cut_kernel, places),
        out_shape=[sds((wide // places, rows), BF)] * places,
        scratch_shapes=[pltpu.VMEM((wide, rows), F32)],
        compiler_params=params(),
        name="cut_rows",
    )(*backs)


def step_kernel(ranks, near, *refs):
    lows, steps, (mine_ref, theirs_ref) = refs[:near], refs[near : 2 * near], refs[2 * near :]
    place = lax.axis_index("ctx")
    rows = lows[0].shape[1]
    pair = pl.ds(pl.multiple_of(lax.div(place, 2) * (2 * ranks), 16), 2 * ranks)
    odd = lax.rem(place, 2) == 1
    total = jnp.zeros((2 * ranks, mine_ref.shape[1]), F32)
    decay = jnp.zeros((mine_ref.shape[0] - ranks, mine_ref.shape[1]), F32)
    for low, step in zip(lows, steps):
        total = total + dot(low[pair, :], step[:rows, :])
        decay = decay + step[rows:, :].astype(F32)
    mine_ref[:ranks, :] = jnp.where(odd, total[ranks:, :], total[:ranks, :])
    theirs_ref[:ranks, :] = jnp.where(odd, total[:ranks, :], total[ranks:, :]).astype(BF)
    mine_ref[ranks:, :] = decay
    theirs_ref[ranks:, :] = decay.astype(BF)


def step_call(ranks, lows, steps):
    rows = lows[0].shape[1]
    tall, chans = steps[0].shape
    width = min(512, chans)
    height = ranks + tall - rows
    return pl.pallas_call(
        functools.partial(step_kernel, ranks, len(lows)),
        grid=(chans // width,),
        in_specs=[whole(lows[0].shape)] * len(lows) + [columns(tall, width)] * len(steps),
        out_specs=[columns(height, width)] * 2,
        out_shape=[sds((height, chans), F32), sds((height, chans), BF)],
        compiler_params=params(),
        name="step_products",
    )(*lows, *steps)


def rows_kernel(ranks, places, *refs):
    cuts, blocks, refs = refs[:places], refs[places : 2 * places], refs[2 * places :]
    products, (out_ref, coef_ref, step_ref, decay_ref) = refs[:-4], refs[-4:]
    total = jnp.zeros((cuts[0].shape[0], out_ref.shape[1]), F32)
    for cut, block in zip(cuts, blocks):
        total = total + dot(cut[...], block[...])
    out_ref[...] = total[:ranks, :]
    coef_ref[...] = total[ranks : ranks + coef_ref.shape[0], :]
    for chunk in range(len(products) // 2):

        @pl.when(pl.program_id(0) == chunk)
        def _():
            mine, theirs = products[2 * chunk : 2 * chunk + 2]
            step_ref[...] = mine[:ranks, :] + theirs[:ranks, :].astype(F32)
            decay_ref[...] = mine[ranks:, :] + theirs[ranks:, :].astype(F32)


def rows_call(ranks, coef_rows, cuts, blocks, products):
    rows, chans = blocks[0].shape
    height, width = products[0].shape
    heights = (ranks, coef_rows, ranks, height - ranks)
    return pl.pallas_call(
        functools.partial(rows_kernel, ranks, len(cuts)),
        grid=(chans // width,),
        in_specs=[whole(cuts[0].shape)] * len(cuts)
        + [columns(rows, width)] * len(blocks)
        + [whole((height, width))] * len(products),
        out_specs=[columns(height, width) for height in heights],
        out_shape=[sds((height, chans), F32) for height in heights],
        compiler_params=params(),
        name="row_gradients",
    )(*cuts, *blocks, *products)


def last_kernel(places, taps, *refs):
    (_, tail_ref, weight_ref) = refs[:3]
    late, refs = refs[3 : 3 + places], refs[3 + places :]
    (out_ref, conv_w, conv_b, step_b, skip, fix) = refs
    fix[...] = tail_ref[...]
    inside = lax.axis_index("ctx") < places - 1
    following = jnp.where(inside, late[places - 1][8:16, :].astype(F32), 0.0)
    for row in range(taps - 1):
        extra = jnp.zeros((1, fix.shape[1]), F32)
        for tap in range(row + 1):
            extra = extra + weight_ref[tap : tap + 1, :] * following[row - tap : row - tap + 1, :]
        at = 16 - (taps - 1) + row
        fix[at : at + 1, :] += extra
    out_ref[...] = fix[...].astype(BF)
    total = late[0][...].astype(F32)
    for part in late[1:]:
        total = total + part[...].astype(F32)
    conv_w[...] = total[:taps, :]
    conv_b[...] = total[taps : taps + 1, :]
    step_b[...] = total[taps + 1 : taps + 2, :]
    skip[...] = total[taps + 2 : taps + 3, :]


def last_call(main, tail, weight, late):
    rows, chans = main.shape
    taps = weight.shape[0]
    places = len(late)
    return pl.pallas_call(
        functools.partial(last_kernel, places, taps),
        grid=(1,),
        in_specs=[pl.BlockSpec(memory_space=pl.ANY), columns(16, chans), columns(taps, chans)]
        + [columns(16, chans)] * places,
        out_specs=[
            pl.BlockSpec((16, chans), lambda i: (rows // 16 - 1, i)),
            columns(taps, chans),
        ]
        + [columns(1, chans)] * 3,
        out_shape=[sds((rows, chans), BF), sds((taps, chans), F32)] + [sds((1, chans), F32)] * 3,
        scratch_shapes=[pltpu.VMEM((16, chans), F32)],
        input_output_aliases={0: 0},
        compiler_params=params(),
        name="last_rows",
    )(main, tail, weight, *late)


def exchange(block, axis):
    return lax.all_to_all(block, axis, split_axis=0, concat_axis=0, tiled=True)


def swap(block, axis, mask):
    return lax.ppermute(block, axis, [(i, i ^ mask) for i in range(lax.axis_size(axis))])


tie = lax.optimization_barrier


def spread(block):
    return [block] + [swap(block, "ctx", mask) for mask in range(1, min(lax.axis_size("ctx"), 3))]


def spread_on(blocks):
    places = lax.axis_size("ctx")
    if places == 4:
        return blocks + [swap(blocks[2], "ctx", 1)]
    return blocks + [swap(blocks[0], "ctx", mask) for mask in range(3, places)]


def gather_near(block):
    return [block] + [swap(block, "ctx", mask) for mask in range(2, lax.axis_size("ctx"), 2)]


def chan_sum(part):
    mask, peers = 1, lax.axis_size("chan")
    while True:
        other = swap(part, "chan", mask)
        mask *= 2
        if mask == peers:
            return part, other
        part = (part.astype(F32) + other.astype(F32)).astype(BF)


def body(
    conv_input,
    gate_input,
    out_grad,
    conv_weight,
    conv_bias,
    proj_weight,
    step_weight,
    step_bias,
    decay_log,
    skip_gain,
):
    rows, chans = conv_input.shape
    taps = conv_weight.shape[0]
    low_rank = step_weight.shape[0]
    states = decay_log.shape[0]
    places = lax.axis_size("ctx")
    groups = group_rows(chans)
    decay = decay_log.reshape(states, -1, groups, 128).transpose(1, 0, 2, 3)
    skips = skip_gain.reshape(-1, groups, 128)
    conv_bias = conv_bias[None, :]
    step_bias = step_bias[None, :]
    skip_gain = skip_gain[None, :]

    chunks = decay.shape[0]
    rim = shift(conv_input[rows - (taps - 1) :], "ctx", 1)
    conv_out, part = conv_call(conv_input, rim, conv_weight, conv_bias, proj_weight)
    blocks = spread(conv_out)
    parts = chan_sum(part)
    dt, dx, g, coef, low, *messages = local_call(
        parts, step_weight, step_bias, decay, conv_out, gate_input, out_grad, states, places
    )
    messages, blocks = tie((messages, blocks))
    messages = [swap(message, "ctx", mask) for mask, message in enumerate(messages, 1)]
    messages, blocks, low = tie((messages, blocks, low))
    blocks = spread_on(blocks)
    lows = gather_near(jnp.transpose(low))
    previous, steps = [], []
    for chunk in range(chunks):
        message, grad_gate, scan_part, small, part = scan_call(
            places, chunk, coef, (dt, dx, g), decay, skips, conv_out, gate_input, out_grad,
            step_weight, skip_gain, messages, previous,
        )
        previous = [part, grad_gate, scan_part, small]
        if chunk == 0:
            previous, blocks = tie((previous, blocks))
        else:
            previous, steps[-1], lows = tie((previous, steps[-1], lows))
        steps.append(gather_near(message))
    part, grad_gate, scan_part, small = previous
    ranks = low_rank // places
    products = []
    for step in steps[:-1]:
        mine, theirs = step_call(ranks, lows, step)
        products += [mine, swap(theirs, "ctx", 1)]
    backs = chan_sum(part)
    backs, products = tie((backs, products))
    cuts = cut_call(places, backs)
    cuts, lows = tie((cuts, lows))
    cuts = [cuts[0]] + [swap(cut, "ctx", mask) for mask, cut in enumerate(cuts[1:], 1)]
    mine, theirs = step_call(ranks, lows, steps[-1])
    backs, theirs = tie((backs, theirs))
    products += [mine, swap(theirs, "ctx", 1)]
    main, tail, sums = conv_grad_call(
        places, low_rank, backs, proj_weight, scan_part, small, conv_input, rim, conv_weight,
        conv_bias,
    )
    sums, cuts = tie((sums, cuts))
    late = [sums] + [rotate(sums, "ctx", hop) for hop in range(1, places)]
    grad_proj, grad_coef, grad_step, decay_grad = rows_call(
        ranks, 2 * states // places, cuts, blocks, products
    )
    late, grad_proj = tie((late, grad_proj))
    grad_input, conv_w, conv_b, step_b, skip = last_call(main, tail, conv_weight, late)
    return (
        grad_input,
        grad_gate,
        grad_proj,
        grad_coef,
        grad_step,
        conv_w,
        conv_b[0],
        step_b[0],
        decay_grad,
        skip[0],
    )


def solution(mesh):
    tokens, columns_, chan = P("ctx", "chan"), P(None, "chan"), P("chan")
    in_specs = (
        tokens, tokens, tokens, columns_, chan, columns_, columns_, chan, columns_, chan,
    )
    out_specs = (
        tokens, tokens, tokens, tokens, tokens, columns_, chan, chan, columns_, chan,
    )
    return jax.shard_map(body, mesh=mesh, in_specs=in_specs, out_specs=out_specs, check_vma=False)
```

```python
import functools

import jax
import jax.numpy as jnp
from jax import lax
from jax.experimental import pallas as pl
from jax.experimental.pallas import tpu as pltpu
from jax.sharding import PartitionSpec as P

BF = jnp.bfloat16
F32 = jnp.float32
LOG2E = 1.4426950408889634
LN2 = 0.6931471805599453
VMEM_BYTES = 56 * 1024 * 1024
NT = (((1,), (1,)), ((), ()))
TN = (((0,), (0,)), ((), ()))


def group_rows(chans):
    for rows in (8, 4, 2, 1):
        if chans % (rows * 128) == 0:
            return rows
    return 1


def dot(a, b, dims=(((1,), (0,)), ((), ()))):
    return lax.dot_general(a, b, dims, preferred_element_type=F32)


def params(**more):
    return pltpu.CompilerParams(vmem_limit_bytes=VMEM_BYTES, **more)


def sds(shape, dtype):
    return jax.ShapeDtypeStruct(shape, dtype)


def whole(shape):
    return pl.BlockSpec(shape, lambda i: (0,) * len(shape))


def columns(rows, width):
    return pl.BlockSpec((rows, width), lambda i: (0, i))


def sigmoid(v):
    return 0.5 + 0.5 * jnp.tanh(0.5 * v)


def rotate(block, axis, distance):
    count = lax.axis_size(axis)
    return lax.ppermute(block, axis, [(i, (i + distance) % count) for i in range(count)])


def shift(block, axis, distance):
    count = lax.axis_size(axis)
    route = [(i, i + distance) for i in range(count) if 0 <= i + distance < count]
    return lax.ppermute(block, axis, route)


def fill_extended(ext, rim_ref, input_ref, taps):
    rows = input_ref.shape[0]
    ext[8 - (taps - 1) : 8, :] = rim_ref[...].astype(F32)
    ext[8 : 8 + rows, :] = input_ref[...].astype(F32)


def conv_block(ext, weight, bias, taps, start, rows):
    total = bias + jnp.zeros((rows, ext.shape[1]), F32)
    for tap in range(taps):
        first = 8 - (taps - 1) + tap + start
        total = total + weight[tap : tap + 1, :] * ext[first : first + rows, :]
    return total


def conv_kernel(input_ref, rim_ref, weight_ref, bias_ref, proj_ref, out_ref, part_ref, ext, acc):
    step = pl.program_id(0)
    taps = weight_ref.shape[0]
    rows = input_ref.shape[0]
    fill_extended(ext, rim_ref, input_ref, taps)
    for start in range(0, rows, 16):
        pre = conv_block(ext, weight_ref, bias_ref[...], taps, start, 16)
        out_ref[start : start + 16, :] = (pre * sigmoid(pre)).astype(BF)
    part = dot(out_ref[...], proj_ref[...], NT)

    @pl.when(step == 0)
    def _():
        acc[...] = part

    @pl.when(step > 0)
    def _():
        acc[...] += part

    @pl.when(step == pl.num_programs(0) - 1)
    def _():
        part_ref[...] = acc[...].astype(BF)


def conv_call(conv_input, rim, weight, bias, proj_weight):
    rows, chans = conv_input.shape
    taps = weight.shape[0]
    wide = proj_weight.shape[0]
    width = min(512, chans)
    return pl.pallas_call(
        conv_kernel,
        grid=(chans // width,),
        in_specs=[
            columns(rows, width),
            columns(taps - 1, width),
            columns(taps, width),
            columns(1, width),
            columns(wide, width),
        ],
        out_specs=[columns(rows, width), whole((rows, wide))],
        out_shape=[sds((rows, chans), BF), sds((rows, wide), BF)],
        scratch_shapes=[pltpu.VMEM((rows + 8, width), F32), pltpu.VMEM((rows, wide), F32)],
        compiler_params=params(),
        name="conv_project",
    )(conv_input, rim, weight, bias, proj_weight)


def tile_rows(value, target, lead, groups):
    rows = value.shape[0]
    for block in range(rows // 8):
        for group in range(groups):
            first = (block * groups + group) * 8
            target[lead, first : first + 8, :] = value[
                block * 8 : block * 8 + 8, group * 128 : group * 128 + 128
            ]


def local_kernel(low_rank, states, places, *refs):
    parts, refs = refs[:2], refs[2:]
    (coef, weight_ref, bias_ref, decay_ref, conv_ref, gate_ref, grad_ref) = refs[:7]
    (dt_ref, dx_ref, g_ref, low) = refs[7:11]
    messages, refs = refs[11 : 10 + places], refs[10 + places :]
    (tiles, dts, dxs, gs, fwd, bwd) = refs
    step = pl.program_id(0)
    chunks = dts.shape[0]
    rows = conv_ref.shape[0]
    groups = decay_ref.shape[2]

    @pl.when(step == 0)
    def _():
        total = (parts[0][...].astype(F32) + parts[1][...].astype(F32)).astype(BF)
        low[...] = total[:, :low_rank]

    pre = dot(low[...], weight_ref[...]) + bias_ref[...]
    for start in range(0, rows, 16):
        here = slice(start, start + 16)
        p = pre[here, :]
        size = jnp.maximum(p, 0.0) + jnp.log1p(jnp.exp(-jnp.abs(p)))
        gate = gate_ref[here, :].astype(F32)
        grad = grad_ref[here, :].astype(F32) * gate * sigmoid(gate)
        drive = size * conv_ref[here, :].astype(F32)
        for half in range(2):
            for group in range(groups):
                first = ((start // 8 + half) * groups + group) * 8
                lanes = slice(group * 128, group * 128 + 128)
                subs = slice(half * 8, half * 8 + 8)
                tiles[0, first : first + 8, :] = size[subs, lanes]
                tiles[1, first : first + 8, :] = drive[subs, lanes]
                tiles[2, first : first + 8, :] = grad[subs, lanes]

    def relay(index, _):
        for sub in range(8):
            token = index * 8 + sub
            at = pl.ds(index * groups * 8 + sub, groups, stride=8)
            for kind, (held, out) in enumerate(((dts, dt_ref), (dxs, dx_ref), (gs, g_ref))):
                row = tiles[kind, at, :]
                held[step, token] = row
                out[0, token] = row
        return 0

    lax.fori_loop(0, rows // 8, relay, 0)

    @pl.when(step == chunks - 1)
    def _():
        batch = 4
        zero = jnp.zeros((groups, 128), F32)
        for lead in range(0, states, batch):
            pairs = [(n, v) for n in range(lead, lead + batch) for v in range(chunks)]
            rates = [-LOG2E * jnp.exp(decay_ref[v, n]) for n, v in pairs]

            def block(index, carry):
                state, run, head, total = (list(part) for part in carry)
                for sub in range(8):
                    token = index * 8 + sub
                    base = token * (2 * states)
                    size = [dts[v, token] for v in range(chunks)]
                    drive = [dxs[v, token] for v in range(chunks)]
                    grad = [gs[v, token] for v in range(chunks)]
                    if lead == 0:
                        total = [a + b for a, b in zip(total, size)]
                    for k, (n, v) in enumerate(pairs):
                        factor = jnp.exp2(size[v] * rates[k])
                        state[k] = factor * state[k] + drive[v] * coef[base + n]
                        run[k] = run[k] * factor
                        head[k] = head[k] + run[k] * (grad[v] * coef[base + (states + n)])
                return state, run, head, total

            many = [zero] * len(pairs)
            state, run, head, total = lax.fori_loop(
                0,
                rows // 8,
                block,
                (many, [zero + 1.0] * len(pairs), many, [zero] * chunks),
            )
            for k, (n, v) in enumerate(pairs):
                fwd[v, n] = state[k]
                bwd[v, n] = head[k]
            if lead == 0:
                for v in range(chunks):
                    coarse = total[v].astype(BF).astype(F32)
                    for target in (fwd, bwd):
                        target[v, states] = coarse
                        target[v, states + 1] = total[v] - coarse
        place = lax.axis_index("ctx")
        for mask, message in enumerate(messages, 1):
            message[...] = jnp.where((place ^ mask) > place, fwd[...], bwd[...]).astype(BF)


def local_call(parts, coef, step_weight, step_bias, decay, conv_out, gate, grad, states, places):
    rows, chans = conv_out.shape
    wide = parts[0].shape[1]
    low_rank = step_weight.shape[0]
    chunks, _, groups, _ = decay.shape
    width = groups * 128
    message = (chunks, states + 2, groups, 128)
    dense = (chunks, rows, groups, 128)
    big = pltpu.VMEM(dense, F32)
    return pl.pallas_call(
        functools.partial(local_kernel, low_rank, states, places),
        grid=(chunks,),
        in_specs=[
            whole((rows, wide)),
            whole((rows, wide)),
            pl.BlockSpec(memory_space=pltpu.SMEM),
            columns(low_rank, width),
            columns(1, width),
            whole(decay.shape),
            columns(rows, width),
            columns(rows, width),
            columns(rows, width),
        ],
        out_specs=[
            *[pl.BlockSpec((1, rows, groups, 128), lambda i: (i, 0, 0, 0))] * 3,
            whole((rows, low_rank)),
        ]
        + [whole(message)] * (places - 1),
        out_shape=[
            *[sds(dense, F32)] * 3,
            sds((rows, low_rank), BF),
        ]
        + [sds(message, BF)] * (places - 1),
        scratch_shapes=[
            pltpu.VMEM((3, rows * groups, 128), F32),
            big,
            big,
            big,
            pltpu.VMEM(message, F32),
            pltpu.VMEM(message, F32),
        ],
        compiler_params=params(),
        name="local_ends",
    )(*parts, coef, step_weight, step_bias, decay, conv_out, gate, grad)


def fold_rows(products, base, groups, target, first):
    total = products[pl.ds(base, 8, stride=groups), :]
    for row in range(1, groups):
        total = total + products[pl.ds(base + row, 8, stride=groups), :]
    target[pl.ds(pl.multiple_of(first, 8), 8), :] = total


def scan_kernel(places, states, opening, *refs):
    (coef, dt_ref, dx_ref, g_ref, decay_ref, skips_ref) = refs[:6]
    (conv_ref, gate_ref, grad_ref, weight_ref, skip_ref) = refs[6:11]
    messages, refs = refs[11 : 10 + places], refs[10 + places :]
    if not opening:
        before_ref, refs = refs[0], refs[4:]
    (pre_ref, gate_out, scan_out, small_ref, part_ref) = refs[:5]
    refs = refs[5:]
    (ys, dds, qs, decayed, coef_out, coef_in, rate, decay_acc, acc, ends, products, factors) = refs
    rows = conv_ref.shape[0]
    groups = decay_ref.shape[2]
    low_rank = weight_ref.shape[0]
    span = groups * 8

    place = lax.axis_index("ctx")
    for n in range(states):
        rate[n] = -LOG2E * jnp.exp(decay_ref[0, n])
    ends[place] = jnp.zeros(ends.shape[1:], F32)
    for mask, message in enumerate(messages, 1):
        ends[place ^ mask] = message[0].astype(F32)
    totals = [ends[q, states] + ends[q, states + 1] for q in range(places)]
    state, carry = [], []
    for n in range(states):
        before = jnp.zeros((groups, 128), F32)
        after = jnp.zeros((groups, 128), F32)
        for q in range(places - 1):
            reached = jnp.exp2(rate[n] * totals[q]) * before + ends[q, n]
            before = jnp.where(q < place, reached, before)
        for q in range(places - 1, 0, -1):
            reached = jnp.exp2(rate[n] * totals[q]) * after + ends[q, n]
            after = jnp.where(q > place, reached, after)
        state.append(before)
        carry.append(after)

    def forward(index, state):
        state = list(state)
        for sub in range(8):
            token = index * 8 + sub
            at = pl.ds(index * span + sub, groups, stride=8)
            scalar = token * (2 * states)
            size, drive, grad = dt_ref[0, token], dx_ref[0, token], g_ref[0, token]
            result = jnp.zeros((groups, 128), F32)
            for lead in range(0, states, 8):
                base = (sub * states + lead) * groups
                for n in range(lead, lead + 8):
                    factor = jnp.exp2(size * rate[n])
                    kept = factor * state[n]
                    factors[token, n] = factor
                    decayed[token, n] = kept
                    state[n] = kept + drive * coef[scalar + n]
                    result = result + state[n] * coef[scalar + (states + n)]
                    row = base + (n - lead) * groups
                    products[row : row + groups, :] = state[n] * grad
                fold_rows(products, base, groups, coef_out, token * states + lead)
            ys[at, :] = result
        return state

    lax.fori_loop(0, rows // 8, forward, state)

    def backward(hop, both):
        carry, gathered = list(both[0]), list(both[1])
        index = rows // 8 - 1 - hop
        for sub in range(7, -1, -1):
            token = index * 8 + sub
            at = pl.ds(index * span + sub, groups, stride=8)
            scalar = token * (2 * states)
            size, drive, grad = dt_ref[0, token], dx_ref[0, token], g_ref[0, token]
            slope = jnp.zeros((groups, 128), F32)
            inner = jnp.zeros((groups, 128), F32)
            for lead in range(0, states, 8):
                base = (sub * states + lead) * groups
                for n in range(lead, lead + 8):
                    adjoint = carry[n] + grad * coef[scalar + (states + n)]
                    carry[n] = factors[token, n] * adjoint
                    weighted = adjoint * decayed[token, n] * (size * rate[n])
                    slope = slope + weighted
                    gathered[n] = gathered[n] + weighted
                    inner = inner + adjoint * coef[scalar + n]
                    row = base + (n - lead) * groups
                    products[row : row + groups, :] = adjoint * drive
                fold_rows(products, base, groups, coef_in, token * states + lead)
            tiny = 1.0 - 0.5 * size * (1.0 - size * (1.0 / 3.0) * (1.0 - 0.25 * size))
            ratio = jnp.where(size < 0.03, tiny, (1.0 - jnp.exp(-size)) / jnp.maximum(size, 0.03))
            dds[at, :] = (LN2 * slope + drive * inner) * ratio
            qs[at, :] = size * inner + skips_ref[0] * grad
        return carry, gathered

    zeros = [jnp.zeros((groups, 128), F32)] * states
    _, gathered = lax.fori_loop(0, rows // 8, backward, (carry, zeros))
    for n in range(states):
        decay_acc[n * groups : n * groups + groups, :] = gathered[n] * LN2

    for group in range(groups):
        pre_ref[rows : rows + states, group * 128 : group * 128 + 128] = decay_acc[
            pl.ds(group, states, stride=groups), :
        ].astype(BF)
    skip = skip_ref[...]
    bias_sum = jnp.zeros((1, conv_ref.shape[1]), F32)
    skip_sum = jnp.zeros((1, conv_ref.shape[1]), F32)
    for start in range(0, rows, 16):
        here = slice(start, start + 16)

        def natural(read):
            return jnp.concatenate(
                [
                    jnp.concatenate(
                        [
                            read(((start // 8 + half) * groups + group) * 8)
                            for group in range(groups)
                        ],
                        axis=1,
                    )
                    for half in range(2)
                ],
                axis=0,
            )

        d_pre = natural(lambda first: dds[first : first + 8, :])
        out = natural(lambda first: ys[first : first + 8, :])
        conv = conv_ref[here, :].astype(F32)
        gate = gate_ref[here, :].astype(F32)
        grad = grad_ref[here, :].astype(F32)
        sig = sigmoid(gate)
        scan_grad = grad * gate * sig
        pre_ref[here, :] = d_pre.astype(BF)
        bias_sum = bias_sum + jnp.sum(d_pre, axis=0, keepdims=True)
        skip_sum = skip_sum + jnp.sum(scan_grad * conv, axis=0, keepdims=True)
        scan_out[here, :] = natural(lambda first: qs[first : first + 8, :]).astype(BF)
        gate_out[here, :] = (
            grad * (out + skip * conv) * (sig * (1.0 + gate * (1.0 - sig)))
        ).astype(BF)
    small_ref[...] = jnp.concatenate(
        [bias_sum, skip_sum, jnp.zeros((6, bias_sum.shape[1]), F32)], axis=0
    )

    pre_bf = pre_ref[:rows, :]
    lanes = lax.broadcasted_iota(jnp.int32, (2 * states, 128), 0)
    coefs = jnp.zeros((2 * states, rows), F32)
    for n in range(states):
        at = pl.ds(n, rows, stride=states)
        for kind, source in enumerate((coef_in, coef_out)):
            pick = jnp.where(lanes == kind * states + n, 1.0, 0.0).astype(BF)
            coefs = coefs + dot(pick, source[at, :].astype(BF), NT)
    wide = dot(weight_ref[...], pre_bf, NT)

    ranks, coef_rows, block = low_rank // places, 2 * states // places, acc.shape[0] // places

    acc[...] = jnp.zeros_like(acc) if opening else before_ref[...]
    for q in range(places):
        at = q * block
        acc[at : at + ranks, :] += wide[q * ranks : (q + 1) * ranks, :]
        acc[at + ranks : at + ranks + coef_rows, :] += coefs[
            q * coef_rows : (q + 1) * coef_rows, :
        ]
    part_ref[...] = acc[...].astype(part_ref.dtype)


def padded(wide):
    return (wide + 127) // 128 * 128


def scan_call(
    places, chunk, coef, dense, decay, skips, conv_out, gate, grad, step_weight, skip, messages,
    previous,
):
    rows, chans = conv_out.shape
    low_rank = step_weight.shape[0]
    chunks, states, groups, _ = decay.shape
    width = groups * 128
    wide = padded(low_rank + 2 * states)
    lead = lambda *shape: pl.BlockSpec((1,) + shape, lambda i: (chunk,) + (0,) * len(shape))
    here = lambda height: pl.BlockSpec((height, width), lambda i: (0, chunk))
    tall = pltpu.VMEM((rows * groups, 128), F32)
    first, last = chunk == 0, chunk == chunks - 1
    in_specs = [
        pl.BlockSpec(memory_space=pltpu.SMEM),
        lead(rows, groups, 128),
        lead(rows, groups, 128),
        lead(rows, groups, 128),
        lead(states, groups, 128),
        lead(groups, 128),
        here(rows),
        here(rows),
        here(rows),
        here(low_rank),
        here(1),
    ]
    in_specs += [lead(states + 2, groups, 128)] * (places - 1)
    aliases = {}
    if not first:
        in_specs += [whole((wide, rows))] + [pl.BlockSpec(memory_space=pl.ANY)] * 3
        aliases = {11 + places: 1, 12 + places: 2, 13 + places: 3}
    return pl.pallas_call(
        functools.partial(scan_kernel, places, states, first),
        grid=(1,),
        in_specs=in_specs,
        out_specs=[
            whole((rows + states, width)),
            here(rows),
            here(rows),
            here(8),
            whole((wide, rows)),
        ],
        out_shape=[
            sds((rows + states, width), BF),
            sds((rows, chans), BF),
            sds((rows, chans), BF),
            sds((8, chans), F32),
            sds((wide, rows), BF if last else F32),
        ],
        scratch_shapes=[
            tall,
            tall,
            tall,
            pltpu.VMEM((rows, states, groups, 128), F32),
            pltpu.VMEM((rows * states, 128), F32),
            pltpu.VMEM((rows * states, 128), F32),
            pltpu.VMEM((states, groups, 128), F32),
            pltpu.VMEM((states * groups, 128), F32),
            pltpu.VMEM((wide, rows), F32),
            pltpu.VMEM((places, states + 2, groups, 128), F32),
            pltpu.VMEM((8 * states * groups, 128), F32),
            pltpu.VMEM((rows, states, groups, 128), F32),
        ],
        input_output_aliases=aliases,
        compiler_params=params(),
        name="scan_gradients",
    )(
        coef, *dense, decay, skips, conv_out, gate, grad, step_weight, skip, *messages, *previous
    )


def conv_grad_kernel(places, low_rank, back_a, back_b, proj_ref, scan_ref, small_in, input_ref, rim_ref, weight_ref, bias_ref,
                     out_ref, tail_ref, small_ref, ext, grad):
    taps = weight_ref.shape[0]
    rows = input_ref.shape[0]
    fill_extended(ext, rim_ref, input_ref, taps)
    wide = proj_ref.shape[0]
    block = back_a.shape[0] // places
    ranks, coef_rows = low_rank // places, (wide - low_rank) // places
    back = (back_a[...].astype(F32) + back_b[...].astype(F32)).astype(BF).astype(F32)
    order = [back[q * block : q * block + ranks, :] for q in range(places)]
    order += [back[q * block + ranks : q * block + ranks + coef_rows, :] for q in range(places)]
    d_xc = dot(jnp.concatenate(order, axis=0).astype(BF), proj_ref[...], TN)
    sums = [jnp.zeros((1, input_ref.shape[1]), F32) for _ in range(taps + 1)]
    for start in range(0, rows, 16):
        here = slice(start, start + 16)
        pre = conv_block(ext, weight_ref, bias_ref[...], taps, start, 16)
        sig = sigmoid(pre)
        value = (d_xc[here, :] + scan_ref[here, :].astype(F32)) * (sig * (1.0 + pre * (1.0 - sig)))
        grad[here, :] = value
        for tap in range(taps):
            first = 8 - (taps - 1) + tap + start
            sums[tap] = sums[tap] + jnp.sum(value * ext[first : first + 16, :], axis=0, keepdims=True)
        sums[taps] = sums[taps] + jnp.sum(value, axis=0, keepdims=True)
    grad[rows : rows + 8, :] = jnp.zeros((8, grad.shape[1]), F32)
    for start in range(0, rows, 16):
        total = jnp.zeros((16, grad.shape[1]), F32)
        for tap in range(taps):
            first = start + taps - 1 - tap
            total = total + weight_ref[tap : tap + 1, :] * grad[first : first + 16, :]
        out_ref[start : start + 16, :] = total.astype(BF)
    tail_ref[...] = total
    small_ref[...] = jnp.concatenate(
        sums + [small_in[0 : 7 - taps, :], grad[0:8, :]], axis=0
    ).astype(BF)


def conv_grad_call(places, low_rank, backs, proj_weight, scan_part, small, conv_input, rim, weight, bias):
    rows, chans = conv_input.shape
    taps = weight.shape[0]
    wide = proj_weight.shape[0]
    width = min(512, chans)
    return pl.pallas_call(
        functools.partial(conv_grad_kernel, places, low_rank),
        grid=(chans // width,),
        in_specs=[
            whole(backs[0].shape),
            whole(backs[1].shape),
            columns(wide, width),
            columns(rows, width),
            columns(8, width),
            columns(rows, width),
            columns(taps - 1, width),
            columns(taps, width),
            columns(1, width),
        ],
        out_specs=[columns(rows, width), columns(16, width), columns(16, width)],
        out_shape=[sds((rows, chans), BF), sds((16, chans), F32), sds((16, chans), BF)],
        scratch_shapes=[pltpu.VMEM((rows + 8, width), F32), pltpu.VMEM((rows + 8, width), F32)],
        compiler_params=params(),
        name="conv_gradients",
    )(*backs, proj_weight, scan_part, small, conv_input, rim, weight, bias)


def cut_kernel(places, back_a, back_b, *refs):
    cuts, (back,) = refs[:places], refs[places:]
    place = lax.axis_index("ctx")
    height = back.shape[0] // places
    back[...] = back_a[...].astype(F32) + back_b[...].astype(F32)
    for mask in range(places):
        cuts[mask][...] = back[pl.ds((place ^ mask) * height, height), :].astype(BF)


def cut_call(places, backs):
    wide, rows = backs[0].shape
    return pl.pallas_call(
        functools.partial(cut_kernel, places),
        out_shape=[sds((wide // places, rows), BF)] * places,
        scratch_shapes=[pltpu.VMEM((wide, rows), F32)],
        compiler_params=params(),
        name="cut_rows",
    )(*backs)


def step_kernel(ranks, near, *refs):
    lows, steps, (mine_ref, theirs_ref) = refs[:near], refs[near : 2 * near], refs[2 * near :]
    place = lax.axis_index("ctx")
    rows = lows[0].shape[1]
    pair = pl.ds(pl.multiple_of(lax.div(place, 2) * (2 * ranks), 16), 2 * ranks)
    odd = lax.rem(place, 2) == 1
    total = jnp.zeros((2 * ranks, mine_ref.shape[1]), F32)
    decay = jnp.zeros((mine_ref.shape[0] - ranks, mine_ref.shape[1]), F32)
    for low, step in zip(lows, steps):
        total = total + dot(low[pair, :], step[:rows, :])
        decay = decay + step[rows:, :].astype(F32)
    mine_ref[:ranks, :] = jnp.where(odd, total[ranks:, :], total[:ranks, :])
    theirs_ref[:ranks, :] = jnp.where(odd, total[:ranks, :], total[ranks:, :]).astype(BF)
    mine_ref[ranks:, :] = decay
    theirs_ref[ranks:, :] = decay.astype(BF)


def step_call(ranks, lows, steps):
    rows = lows[0].shape[1]
    tall, chans = steps[0].shape
    width = min(512, chans)
    height = ranks + tall - rows
    return pl.pallas_call(
        functools.partial(step_kernel, ranks, len(lows)),
        grid=(chans // width,),
        in_specs=[whole(lows[0].shape)] * len(lows) + [columns(tall, width)] * len(steps),
        out_specs=[columns(height, width)] * 2,
        out_shape=[sds((height, chans), F32), sds((height, chans), BF)],
        compiler_params=params(),
        name="step_products",
    )(*lows, *steps)


def rows_kernel(ranks, places, *refs):
    cuts, blocks, refs = refs[:places], refs[places : 2 * places], refs[2 * places :]
    products, (out_ref, coef_ref, step_ref, decay_ref) = refs[:-4], refs[-4:]
    total = jnp.zeros((cuts[0].shape[0], out_ref.shape[1]), F32)
    for cut, block in zip(cuts, blocks):
        total = total + dot(cut[...], block[...])
    out_ref[...] = total[:ranks, :]
    coef_ref[...] = total[ranks : ranks + coef_ref.shape[0], :]
    for chunk in range(len(products) // 2):

        @pl.when(pl.program_id(0) == chunk)
        def _():
            mine, theirs = products[2 * chunk : 2 * chunk + 2]
            step_ref[...] = mine[:ranks, :] + theirs[:ranks, :].astype(F32)
            decay_ref[...] = mine[ranks:, :] + theirs[ranks:, :].astype(F32)


def rows_call(ranks, coef_rows, cuts, blocks, products):
    rows, chans = blocks[0].shape
    height, width = products[0].shape
    heights = (ranks, coef_rows, ranks, height - ranks)
    return pl.pallas_call(
        functools.partial(rows_kernel, ranks, len(cuts)),
        grid=(chans // width,),
        in_specs=[whole(cuts[0].shape)] * len(cuts)
        + [columns(rows, width)] * len(blocks)
        + [whole((height, width))] * len(products),
        out_specs=[columns(height, width) for height in heights],
        out_shape=[sds((height, chans), F32) for height in heights],
        compiler_params=params(),
        name="row_gradients",
    )(*cuts, *blocks, *products)


def last_kernel(places, taps, *refs):
    (_, tail_ref, weight_ref) = refs[:3]
    late, refs = refs[3 : 3 + places], refs[3 + places :]
    (out_ref, conv_w, conv_b, step_b, skip, fix) = refs
    fix[...] = tail_ref[...]
    inside = lax.axis_index("ctx") < places - 1
    following = jnp.where(inside, late[places - 1][8:16, :].astype(F32), 0.0)
    for row in range(taps - 1):
        extra = jnp.zeros((1, fix.shape[1]), F32)
        for tap in range(row + 1):
            extra = extra + weight_ref[tap : tap + 1, :] * following[row - tap : row - tap + 1, :]
        at = 16 - (taps - 1) + row
        fix[at : at + 1, :] += extra
    out_ref[...] = fix[...].astype(BF)
    total = late[0][...].astype(F32)
    for part in late[1:]:
        total = total + part[...].astype(F32)
    conv_w[...] = total[:taps, :]
    conv_b[...] = total[taps : taps + 1, :]
    step_b[...] = total[taps + 1 : taps + 2, :]
    skip[...] = total[taps + 2 : taps + 3, :]


def last_call(main, tail, weight, late):
    rows, chans = main.shape
    taps = weight.shape[0]
    places = len(late)
    return pl.pallas_call(
        functools.partial(last_kernel, places, taps),
        grid=(1,),
        in_specs=[pl.BlockSpec(memory_space=pl.ANY), columns(16, chans), columns(taps, chans)]
        + [columns(16, chans)] * places,
        out_specs=[
            pl.BlockSpec((16, chans), lambda i: (rows // 16 - 1, i)),
            columns(taps, chans),
        ]
        + [columns(1, chans)] * 3,
        out_shape=[sds((rows, chans), BF), sds((taps, chans), F32)] + [sds((1, chans), F32)] * 3,
        scratch_shapes=[pltpu.VMEM((16, chans), F32)],
        input_output_aliases={0: 0},
        compiler_params=params(),
        name="last_rows",
    )(main, tail, weight, *late)


def exchange(block, axis):
    return lax.all_to_all(block, axis, split_axis=0, concat_axis=0, tiled=True)


def swap(block, axis, mask):
    return lax.ppermute(block, axis, [(i, i ^ mask) for i in range(lax.axis_size(axis))])


tie = lax.optimization_barrier


def spread(block):
    return [block] + [swap(block, "ctx", mask) for mask in range(1, min(lax.axis_size("ctx"), 3))]


def spread_on(blocks):
    places = lax.axis_size("ctx")
    if places == 4:
        return blocks + [swap(blocks[2], "ctx", 1)]
    return blocks + [swap(blocks[0], "ctx", mask) for mask in range(3, places)]


def gather_near(block):
    return [block] + [swap(block, "ctx", mask) for mask in range(2, lax.axis_size("ctx"), 2)]


def chan_sum(part):
    mask, peers = 1, lax.axis_size("chan")
    while True:
        other = swap(part, "chan", mask)
        mask *= 2
        if mask == peers:
            return part, other
        part = (part.astype(F32) + other.astype(F32)).astype(BF)


def body(
    conv_input,
    gate_input,
    out_grad,
    conv_weight,
    conv_bias,
    proj_weight,
    step_weight,
    step_bias,
    decay_log,
    skip_gain,
):
    rows, chans = conv_input.shape
    taps = conv_weight.shape[0]
    low_rank = step_weight.shape[0]
    states = decay_log.shape[0]
    places = lax.axis_size("ctx")
    groups = group_rows(chans)
    decay = decay_log.reshape(states, -1, groups, 128).transpose(1, 0, 2, 3)
    skips = skip_gain.reshape(-1, groups, 128)
    conv_bias = conv_bias[None, :]
    step_bias = step_bias[None, :]
    skip_gain = skip_gain[None, :]

    chunks = decay.shape[0]
    rim = shift(conv_input[rows - (taps - 1) :], "ctx", 1)
    conv_out, part = conv_call(conv_input, rim, conv_weight, conv_bias, proj_weight)
    blocks = spread(conv_out)
    parts = chan_sum(part)
    coef = (parts[0][:, low_rank:].astype(F32) + parts[1][:, low_rank:].astype(F32)).astype(BF)
    coef = coef.astype(F32).reshape(-1)
    dt, dx, g, low, *messages = local_call(
        parts, coef, step_weight, step_bias, decay, conv_out, gate_input, out_grad, states, places
    )
    messages, blocks = tie((messages, blocks))
    messages = [swap(message, "ctx", mask) for mask, message in enumerate(messages, 1)]
    messages, blocks, low = tie((messages, blocks, low))
    blocks = spread_on(blocks)
    lows = gather_near(jnp.transpose(low))
    previous, steps = [], []
    for chunk in range(chunks):
        message, grad_gate, scan_part, small, part = scan_call(
            places, chunk, coef, (dt, dx, g), decay, skips, conv_out, gate_input, out_grad,
            step_weight, skip_gain, messages, previous,
        )
        previous = [part, grad_gate, scan_part, small]
        if chunk == 0:
            previous, blocks = tie((previous, blocks))
        else:
            previous, steps[-1], lows = tie((previous, steps[-1], lows))
        steps.append(gather_near(message))
    part, grad_gate, scan_part, small = previous
    ranks = low_rank // places
    products = []
    backs = chan_sum(part)
    if chunks > 1:
        near, lows = tie((backs[0], lows))
        backs = (near, backs[1])
    for step in steps[:-1]:
        mine, theirs = step_call(ranks, lows, step)
        products += [mine, swap(theirs, "ctx", 1)]
    cuts = cut_call(places, backs)
    cuts, lows = tie((cuts, lows))
    cuts = [cuts[0]] + [swap(cut, "ctx", mask) for mask, cut in enumerate(cuts[1:], 1)]
    mine, theirs = step_call(ranks, lows, steps[-1])
    backs, theirs = tie((backs, theirs))
    latest = [mine, swap(theirs, "ctx", 1)]
    main, tail, sums = conv_grad_call(
        places, low_rank, backs, proj_weight, scan_part, small, conv_input, rim, conv_weight,
        conv_bias,
    )
    sums, cuts, products = tie((sums, cuts, products))
    late = [sums] + [rotate(sums, "ctx", hop) for hop in range(1, places)]
    grad_proj, grad_coef, grad_step, decay_grad = rows_call(
        ranks, 2 * states // places, cuts, blocks, products + latest
    )
    late, grad_proj = tie((late, grad_proj))
    grad_input, conv_w, conv_b, step_b, skip = last_call(main, tail, conv_weight, late)
    return (
        grad_input,
        grad_gate,
        grad_proj,
        grad_coef,
        grad_step,
        conv_w,
        conv_b[0],
        step_b[0],
        decay_grad,
        skip[0],
    )


def solution(mesh):
    tokens, columns_, chan = P("ctx", "chan"), P(None, "chan"), P("chan")
    in_specs = (
        tokens, tokens, tokens, columns_, chan, columns_, columns_, chan, columns_, chan,
    )
    out_specs = (
        tokens, tokens, tokens, tokens, tokens, columns_, chan, chan, columns_, chan,
    )
    return jax.shard_map(body, mesh=mesh, in_specs=in_specs, out_specs=out_specs, check_vma=False)
```

```python
import functools

import jax
import jax.numpy as jnp
from jax import lax
from jax.experimental import pallas as pl
from jax.experimental.pallas import tpu as pltpu
from jax.sharding import PartitionSpec as P

BF = jnp.bfloat16
F32 = jnp.float32
LOG2E = 1.4426950408889634
LN2 = 0.6931471805599453
MIB = 1024 * 1024
NT = (((1,), (1,)), ((), ()))
TN = (((0,), (0,)), ((), ()))


def group_rows(chans):
    for rows in (8, 4, 2, 1):
        if chans % (rows * 128) == 0:
            return rows
    return 1


def dot(a, b, dims=(((1,), (0,)), ((), ()))):
    return lax.dot_general(a, b, dims, preferred_element_type=F32)


def params(mebibytes):
    return pltpu.CompilerParams(vmem_limit_bytes=mebibytes * MIB)


def sds(shape, dtype):
    return jax.ShapeDtypeStruct(shape, dtype)


def whole(shape):
    return pl.BlockSpec(shape, lambda i: (0,) * len(shape))


def columns(rows, width):
    return pl.BlockSpec((rows, width), lambda i: (0, i))


def sigmoid(v):
    return 0.5 + 0.5 * jnp.tanh(0.5 * v)


def rotate(block, axis, distance):
    count = lax.axis_size(axis)
    return lax.ppermute(block, axis, [(i, (i + distance) % count) for i in range(count)])


def shift(block, axis, distance):
    count = lax.axis_size(axis)
    route = [(i, i + distance) for i in range(count) if 0 <= i + distance < count]
    return lax.ppermute(block, axis, route)


def fill_extended(ext, rim_ref, input_ref, taps):
    rows = input_ref.shape[0]
    ext[8 - (taps - 1) : 8, :] = rim_ref[...].astype(F32)
    ext[8 : 8 + rows, :] = input_ref[...].astype(F32)


def conv_block(ext, weight, bias, taps, start, rows):
    total = bias + jnp.zeros((rows, ext.shape[1]), F32)
    for tap in range(taps):
        first = 8 - (taps - 1) + tap + start
        total = total + weight[tap : tap + 1, :] * ext[first : first + rows, :]
    return total


def conv_kernel(input_ref, rim_ref, weight_ref, bias_ref, proj_ref, out_ref, part_ref, ext, acc):
    step = pl.program_id(0)
    taps = weight_ref.shape[0]
    rows = input_ref.shape[0]
    fill_extended(ext, rim_ref, input_ref, taps)
    for start in range(0, rows, 16):
        pre = conv_block(ext, weight_ref, bias_ref[...], taps, start, 16)
        out_ref[start : start + 16, :] = (pre * sigmoid(pre)).astype(BF)
    part = dot(out_ref[...], proj_ref[...], NT)

    @pl.when(step == 0)
    def _():
        acc[...] = part

    @pl.when(step > 0)
    def _():
        acc[...] += part

    @pl.when(step == pl.num_programs(0) - 1)
    def _():
        part_ref[...] = acc[...].astype(BF)


def conv_call(conv_input, rim, weight, bias, proj_weight):
    rows, chans = conv_input.shape
    taps = weight.shape[0]
    wide = proj_weight.shape[0]
    width = min(1024, chans)
    return pl.pallas_call(
        conv_kernel,
        grid=(chans // width,),
        in_specs=[
            columns(rows, width),
            columns(taps - 1, width),
            columns(taps, width),
            columns(1, width),
            columns(wide, width),
        ],
        out_specs=[columns(rows, width), whole((rows, wide))],
        out_shape=[sds((rows, chans), BF), sds((rows, wide), BF)],
        scratch_shapes=[pltpu.VMEM((rows + 8, width), F32), pltpu.VMEM((rows, wide), F32)],
        compiler_params=params(16),
        name="conv_project",
    )(conv_input, rim, weight, bias, proj_weight)


def tile_rows(value, target, lead, groups):
    rows = value.shape[0]
    for block in range(rows // 8):
        for group in range(groups):
            first = (block * groups + group) * 8
            target[lead, first : first + 8, :] = value[
                block * 8 : block * 8 + 8, group * 128 : group * 128 + 128
            ]


def local_kernel(low_rank, states, places, *refs):
    parts, refs = refs[:2], refs[2:]
    (coef, weight_ref, bias_ref, decay_ref, conv_ref, gate_ref, grad_ref) = refs[:7]
    (dt_ref, dx_ref, g_ref, low) = refs[7:11]
    messages, refs = refs[11 : 10 + places], refs[10 + places :]
    (tiles, dts, dxs, gs, fwd, bwd) = refs
    step = pl.program_id(0)
    chunks = dts.shape[0]
    rows = conv_ref.shape[0]
    groups = decay_ref.shape[2]

    @pl.when(step == 0)
    def _():
        total = (parts[0][...].astype(F32) + parts[1][...].astype(F32)).astype(BF)
        low[...] = total[:, :low_rank]

    pre = dot(low[...], weight_ref[...]) + bias_ref[...]
    for start in range(0, rows, 16):
        here = slice(start, start + 16)
        p = pre[here, :]
        size = jnp.maximum(p, 0.0) + jnp.log1p(jnp.exp(-jnp.abs(p)))
        gate = gate_ref[here, :].astype(F32)
        grad = grad_ref[here, :].astype(F32) * gate * sigmoid(gate)
        drive = size * conv_ref[here, :].astype(F32)
        for half in range(2):
            for group in range(groups):
                first = ((start // 8 + half) * groups + group) * 8
                lanes = slice(group * 128, group * 128 + 128)
                subs = slice(half * 8, half * 8 + 8)
                tiles[0, first : first + 8, :] = size[subs, lanes]
                tiles[1, first : first + 8, :] = drive[subs, lanes]
                tiles[2, first : first + 8, :] = grad[subs, lanes]

    def relay(index, _):
        for sub in range(8):
            token = index * 8 + sub
            at = pl.ds(index * groups * 8 + sub, groups, stride=8)
            for kind, (held, out) in enumerate(((dts, dt_ref), (dxs, dx_ref), (gs, g_ref))):
                row = tiles[kind, at, :]
                held[step, token] = row
                out[0, token] = row
        return 0

    lax.fori_loop(0, rows // 8, relay, 0)

    @pl.when(step == chunks - 1)
    def _():
        batch = 4
        zero = jnp.zeros((groups, 128), F32)
        for lead in range(0, states, batch):
            pairs = [(n, v) for n in range(lead, lead + batch) for v in range(chunks)]
            rates = [-LOG2E * jnp.exp(decay_ref[v, n]) for n, v in pairs]

            def block(index, carry):
                state, run, head, total = (list(part) for part in carry)
                for sub in range(8):
                    token = index * 8 + sub
                    base = token * (2 * states)
                    size = [dts[v, token] for v in range(chunks)]
                    drive = [dxs[v, token] for v in range(chunks)]
                    grad = [gs[v, token] for v in range(chunks)]
                    if lead == 0:
                        total = [a + b for a, b in zip(total, size)]
                    for k, (n, v) in enumerate(pairs):
                        factor = jnp.exp2(size[v] * rates[k])
                        state[k] = factor * state[k] + drive[v] * coef[base + n]
                        run[k] = run[k] * factor
                        head[k] = head[k] + run[k] * (grad[v] * coef[base + (states + n)])
                return state, run, head, total

            many = [zero] * len(pairs)
            state, run, head, total = lax.fori_loop(
                0,
                rows // 8,
                block,
                (many, [zero + 1.0] * len(pairs), many, [zero] * chunks),
            )
            for k, (n, v) in enumerate(pairs):
                fwd[v, n] = state[k]
                bwd[v, n] = head[k]
            if lead == 0:
                for v in range(chunks):
                    coarse = total[v].astype(BF).astype(F32)
                    for target in (fwd, bwd):
                        target[v, states] = coarse
                        target[v, states + 1] = total[v] - coarse
        place = lax.axis_index("ctx")
        for mask, message in enumerate(messages, 1):
            message[...] = jnp.where((place ^ mask) > place, fwd[...], bwd[...]).astype(BF)


def local_call(parts, coef, step_weight, step_bias, decay, conv_out, gate, grad, states, places):
    rows, chans = conv_out.shape
    wide = parts[0].shape[1]
    low_rank = step_weight.shape[0]
    chunks, _, groups, _ = decay.shape
    width = groups * 128
    message = (chunks, states + 2, groups, 128)
    dense = (chunks, rows, groups, 128)
    big = pltpu.VMEM(dense, F32)
    return pl.pallas_call(
        functools.partial(local_kernel, low_rank, states, places),
        grid=(chunks,),
        in_specs=[
            whole((rows, wide)),
            whole((rows, wide)),
            pl.BlockSpec(memory_space=pltpu.SMEM),
            columns(low_rank, width),
            columns(1, width),
            whole(decay.shape),
            columns(rows, width),
            columns(rows, width),
            columns(rows, width),
        ],
        out_specs=[
            *[pl.BlockSpec((1, rows, groups, 128), lambda i: (i, 0, 0, 0))] * 3,
            whole((rows, low_rank)),
        ]
        + [whole(message)] * (places - 1),
        out_shape=[
            *[sds(dense, F32)] * 3,
            sds((rows, low_rank), BF),
        ]
        + [sds(message, BF)] * (places - 1),
        scratch_shapes=[
            pltpu.VMEM((3, rows * groups, 128), F32),
            big,
            big,
            big,
            pltpu.VMEM(message, F32),
            pltpu.VMEM(message, F32),
        ],
        compiler_params=params(26),
        name="local_ends",
    )(*parts, coef, step_weight, step_bias, decay, conv_out, gate, grad)


def fold_rows(products, base, groups, target, first):
    total = products[pl.ds(base, 8, stride=groups), :]
    for row in range(1, groups):
        total = total + products[pl.ds(base + row, 8, stride=groups), :]
    target[pl.ds(pl.multiple_of(first, 8), 8), :] = total


def scan_kernel(places, states, opening, *refs):
    (coef, dt_ref, dx_ref, g_ref, decay_ref, skips_ref) = refs[:6]
    (conv_ref, gate_ref, grad_ref, weight_ref, skip_ref) = refs[6:11]
    messages, refs = refs[11 : 10 + places], refs[10 + places :]
    if not opening:
        before_ref, refs = refs[0], refs[4:]
    (pre_ref, gate_out, scan_out, small_ref, part_ref) = refs[:5]
    refs = refs[5:]
    (ys, dds, qs, decayed, coef_out, coef_in, rate, decay_acc, acc, ends, products, factors) = refs
    rows = conv_ref.shape[0]
    groups = decay_ref.shape[2]
    low_rank = weight_ref.shape[0]
    span = groups * 8

    place = lax.axis_index("ctx")
    for n in range(states):
        rate[n] = -LOG2E * jnp.exp(decay_ref[0, n])
    ends[place] = jnp.zeros(ends.shape[1:], F32)
    for mask, message in enumerate(messages, 1):
        ends[place ^ mask] = message[0].astype(F32)
    totals = [ends[q, states] + ends[q, states + 1] for q in range(places)]
    state, carry = [], []
    for n in range(states):
        before = jnp.zeros((groups, 128), F32)
        after = jnp.zeros((groups, 128), F32)
        for q in range(places - 1):
            reached = jnp.exp2(rate[n] * totals[q]) * before + ends[q, n]
            before = jnp.where(q < place, reached, before)
        for q in range(places - 1, 0, -1):
            reached = jnp.exp2(rate[n] * totals[q]) * after + ends[q, n]
            after = jnp.where(q > place, reached, after)
        state.append(before)
        carry.append(after)

    def forward(index, state):
        state = list(state)
        for sub in range(8):
            token = index * 8 + sub
            at = pl.ds(index * span + sub, groups, stride=8)
            scalar = token * (2 * states)
            size, drive, grad = dt_ref[0, token], dx_ref[0, token], g_ref[0, token]
            result = jnp.zeros((groups, 128), F32)
            for lead in range(0, states, 8):
                base = (sub * states + lead) * groups
                for n in range(lead, lead + 8):
                    factor = jnp.exp2(size * rate[n])
                    kept = factor * state[n]
                    factors[token, n] = factor
                    decayed[token, n] = kept
                    state[n] = kept + drive * coef[scalar + n]
                    result = result + state[n] * coef[scalar + (states + n)]
                    row = base + (n - lead) * groups
                    products[row : row + groups, :] = state[n] * grad
                fold_rows(products, base, groups, coef_out, token * states + lead)
            ys[at, :] = result
        return state

    lax.fori_loop(0, rows // 8, forward, state)

    def backward(hop, both):
        carry, gathered = list(both[0]), list(both[1])
        index = rows // 8 - 1 - hop
        for sub in range(7, -1, -1):
            token = index * 8 + sub
            at = pl.ds(index * span + sub, groups, stride=8)
            scalar = token * (2 * states)
            size, drive, grad = dt_ref[0, token], dx_ref[0, token], g_ref[0, token]
            slope = jnp.zeros((groups, 128), F32)
            inner = jnp.zeros((groups, 128), F32)
            for lead in range(0, states, 8):
                base = (sub * states + lead) * groups
                for n in range(lead, lead + 8):
                    adjoint = carry[n] + grad * coef[scalar + (states + n)]
                    carry[n] = factors[token, n] * adjoint
                    weighted = adjoint * decayed[token, n] * (size * rate[n])
                    slope = slope + weighted
                    gathered[n] = gathered[n] + weighted
                    inner = inner + adjoint * coef[scalar + n]
                    row = base + (n - lead) * groups
                    products[row : row + groups, :] = adjoint * drive
                fold_rows(products, base, groups, coef_in, token * states + lead)
            tiny = 1.0 - 0.5 * size * (1.0 - size * (1.0 / 3.0) * (1.0 - 0.25 * size))
            ratio = jnp.where(size < 0.03, tiny, (1.0 - jnp.exp(-size)) / jnp.maximum(size, 0.03))
            dds[at, :] = (LN2 * slope + drive * inner) * ratio
            qs[at, :] = size * inner + skips_ref[0] * grad
        return carry, gathered

    zeros = [jnp.zeros((groups, 128), F32)] * states
    _, gathered = lax.fori_loop(0, rows // 8, backward, (carry, zeros))
    for n in range(states):
        decay_acc[n * groups : n * groups + groups, :] = gathered[n] * LN2

    for group in range(groups):
        pre_ref[rows : rows + states, group * 128 : group * 128 + 128] = decay_acc[
            pl.ds(group, states, stride=groups), :
        ].astype(BF)
    skip = skip_ref[...]
    bias_sum = jnp.zeros((1, conv_ref.shape[1]), F32)
    skip_sum = jnp.zeros((1, conv_ref.shape[1]), F32)
    for start in range(0, rows, 16):
        here = slice(start, start + 16)

        def natural(read):
            return jnp.concatenate(
                [
                    jnp.concatenate(
                        [
                            read(((start // 8 + half) * groups + group) * 8)
                            for group in range(groups)
                        ],
                        axis=1,
                    )
                    for half in range(2)
                ],
                axis=0,
            )

        d_pre = natural(lambda first: dds[first : first + 8, :])
        out = natural(lambda first: ys[first : first + 8, :])
        conv = conv_ref[here, :].astype(F32)
        gate = gate_ref[here, :].astype(F32)
        grad = grad_ref[here, :].astype(F32)
        sig = sigmoid(gate)
        scan_grad = grad * gate * sig
        pre_ref[here, :] = d_pre.astype(BF)
        bias_sum = bias_sum + jnp.sum(d_pre, axis=0, keepdims=True)
        skip_sum = skip_sum + jnp.sum(scan_grad * conv, axis=0, keepdims=True)
        scan_out[here, :] = natural(lambda first: qs[first : first + 8, :]).astype(BF)
        gate_out[here, :] = (
            grad * (out + skip * conv) * (sig * (1.0 + gate * (1.0 - sig)))
        ).astype(BF)
    small_ref[...] = jnp.concatenate(
        [bias_sum, skip_sum, jnp.zeros((6, bias_sum.shape[1]), F32)], axis=0
    )

    pre_bf = pre_ref[:rows, :]
    lanes = lax.broadcasted_iota(jnp.int32, (2 * states, 128), 0)
    coefs = jnp.zeros((2 * states, rows), F32)
    for n in range(states):
        at = pl.ds(n, rows, stride=states)
        for kind, source in enumerate((coef_in, coef_out)):
            pick = jnp.where(lanes == kind * states + n, 1.0, 0.0).astype(BF)
            coefs = coefs + dot(pick, source[at, :].astype(BF), NT)
    wide = dot(weight_ref[...], pre_bf, NT)

    ranks, coef_rows, block = low_rank // places, 2 * states // places, acc.shape[0] // places

    acc[...] = jnp.zeros_like(acc) if opening else before_ref[...]
    for q in range(places):
        at = q * block
        acc[at : at + ranks, :] += wide[q * ranks : (q + 1) * ranks, :]
        acc[at + ranks : at + ranks + coef_rows, :] += coefs[
            q * coef_rows : (q + 1) * coef_rows, :
        ]
    part_ref[...] = acc[...].astype(part_ref.dtype)


def padded(wide):
    return (wide + 127) // 128 * 128


def scan_call(
    places, chunk, coef, dense, decay, skips, conv_out, gate, grad, step_weight, skip, messages,
    previous,
):
    rows, chans = conv_out.shape
    low_rank = step_weight.shape[0]
    chunks, states, groups, _ = decay.shape
    width = groups * 128
    wide = padded(low_rank + 2 * states)
    lead = lambda *shape: pl.BlockSpec((1,) + shape, lambda i: (chunk,) + (0,) * len(shape))
    here = lambda height: pl.BlockSpec((height, width), lambda i: (0, chunk))
    tall = pltpu.VMEM((rows * groups, 128), F32)
    first, last = chunk == 0, chunk == chunks - 1
    in_specs = [
        pl.BlockSpec(memory_space=pltpu.SMEM),
        lead(rows, groups, 128),
        lead(rows, groups, 128),
        lead(rows, groups, 128),
        lead(states, groups, 128),
        lead(groups, 128),
        here(rows),
        here(rows),
        here(rows),
        here(low_rank),
        here(1),
    ]
    in_specs += [lead(states + 2, groups, 128)] * (places - 1)
    aliases = {}
    if not first:
        in_specs += [whole((wide, rows))] + [pl.BlockSpec(memory_space=pl.ANY)] * 3
        aliases = {11 + places: 1, 12 + places: 2, 13 + places: 3}
    return pl.pallas_call(
        functools.partial(scan_kernel, places, states, first),
        grid=(1,),
        in_specs=in_specs,
        out_specs=[
            whole((rows + states, width)),
            here(rows),
            here(rows),
            here(8),
            whole((wide, rows)),
        ],
        out_shape=[
            sds((rows + states, width), BF),
            sds((rows, chans), BF),
            sds((rows, chans), BF),
            sds((8, chans), F32),
            sds((wide, rows), BF if last else F32),
        ],
        scratch_shapes=[
            tall,
            tall,
            tall,
            pltpu.VMEM((rows, states, groups, 128), F32),
            pltpu.VMEM((rows * states, 128), F32),
            pltpu.VMEM((rows * states, 128), F32),
            pltpu.VMEM((states, groups, 128), F32),
            pltpu.VMEM((states * groups, 128), F32),
            pltpu.VMEM((wide, rows), F32),
            pltpu.VMEM((places, states + 2, groups, 128), F32),
            pltpu.VMEM((8 * states * groups, 128), F32),
            pltpu.VMEM((rows, states, groups, 128), F32),
        ],
        input_output_aliases=aliases,
        compiler_params=params(38),
        name="scan_gradients",
    )(
        coef, *dense, decay, skips, conv_out, gate, grad, step_weight, skip, *messages, *previous
    )


def conv_grad_kernel(places, low_rank, back_a, back_b, proj_ref, scan_ref, small_in, input_ref, rim_ref, weight_ref, bias_ref,
                     out_ref, tail_ref, small_ref, ext, grad, back_t):
    taps = weight_ref.shape[0]
    rows = input_ref.shape[0]
    fill_extended(ext, rim_ref, input_ref, taps)
    wide = proj_ref.shape[0]
    block = back_a.shape[0] // places
    ranks, coef_rows = low_rank // places, (wide - low_rank) // places

    @pl.when(pl.program_id(0) == 0)
    def _():
        back = back_a[...].astype(F32) + back_b[...].astype(F32)
        order = [back[q * block : q * block + ranks, :] for q in range(places)]
        order += [back[q * block + ranks : q * block + ranks + coef_rows, :] for q in range(places)]
        order += [jnp.zeros((padded(wide) - wide, back.shape[1]), F32)]
        back_t[...] = jnp.transpose(jnp.concatenate(order, axis=0))[:, :wide].astype(BF)

    d_xc = dot(back_t[...], proj_ref[...])
    sums = [jnp.zeros((1, input_ref.shape[1]), F32) for _ in range(taps + 1)]
    for start in range(0, rows, 16):
        here = slice(start, start + 16)
        pre = conv_block(ext, weight_ref, bias_ref[...], taps, start, 16)
        sig = sigmoid(pre)
        value = (d_xc[here, :] + scan_ref[here, :].astype(F32)) * (sig * (1.0 + pre * (1.0 - sig)))
        grad[here, :] = value
        for tap in range(taps):
            first = 8 - (taps - 1) + tap + start
            sums[tap] = sums[tap] + jnp.sum(value * ext[first : first + 16, :], axis=0, keepdims=True)
        sums[taps] = sums[taps] + jnp.sum(value, axis=0, keepdims=True)
    grad[rows : rows + 8, :] = jnp.zeros((8, grad.shape[1]), F32)
    for start in range(0, rows, 16):
        total = jnp.zeros((16, grad.shape[1]), F32)
        for tap in range(taps):
            first = start + taps - 1 - tap
            total = total + weight_ref[tap : tap + 1, :] * grad[first : first + 16, :]
        out_ref[start : start + 16, :] = total.astype(BF)
    tail_ref[...] = total
    small_ref[...] = jnp.concatenate(
        sums + [small_in[0 : 7 - taps, :], grad[0:8, :]], axis=0
    ).astype(BF)


def conv_grad_call(places, low_rank, backs, proj_weight, scan_part, small, conv_input, rim, weight, bias):
    rows, chans = conv_input.shape
    taps = weight.shape[0]
    wide = proj_weight.shape[0]
    width = min(1024, chans)
    return pl.pallas_call(
        functools.partial(conv_grad_kernel, places, low_rank),
        grid=(chans // width,),
        in_specs=[
            whole(backs[0].shape),
            whole(backs[1].shape),
            columns(wide, width),
            columns(rows, width),
            columns(8, width),
            columns(rows, width),
            columns(taps - 1, width),
            columns(taps, width),
            columns(1, width),
        ],
        out_specs=[columns(rows, width), columns(16, width), columns(16, width)],
        out_shape=[sds((rows, chans), BF), sds((16, chans), F32), sds((16, chans), BF)],
        scratch_shapes=[
            pltpu.VMEM((rows + 8, width), F32),
            pltpu.VMEM((rows + 8, width), F32),
            pltpu.VMEM((rows, wide), BF),
        ],
        compiler_params=params(18),
        name="conv_gradients",
    )(*backs, proj_weight, scan_part, small, conv_input, rim, weight, bias)


def cut_kernel(places, back_a, back_b, *refs):
    cuts, (back,) = refs[:places], refs[places:]
    place = lax.axis_index("ctx")
    height = back.shape[0] // places
    back[...] = back_a[...].astype(F32) + back_b[...].astype(F32)
    for mask in range(places):
        cuts[mask][...] = back[pl.ds((place ^ mask) * height, height), :].astype(BF)


def cut_call(places, backs):
    wide, rows = backs[0].shape
    return pl.pallas_call(
        functools.partial(cut_kernel, places),
        out_shape=[sds((wide // places, rows), BF)] * places,
        scratch_shapes=[pltpu.VMEM((wide, rows), F32)],
        compiler_params=params(8),
        name="cut_rows",
    )(*backs)


def step_kernel(ranks, near, *refs):
    lows, steps, (mine_ref, theirs_ref) = refs[:near], refs[near : 2 * near], refs[2 * near :]
    place = lax.axis_index("ctx")
    rows = lows[0].shape[1]
    pair = pl.ds(pl.multiple_of(lax.div(place, 2) * (2 * ranks), 16), 2 * ranks)
    odd = lax.rem(place, 2) == 1
    total = jnp.zeros((2 * ranks, mine_ref.shape[1]), F32)
    decay = jnp.zeros((mine_ref.shape[0] - ranks, mine_ref.shape[1]), F32)
    for low, step in zip(lows, steps):
        total = total + dot(low[pair, :], step[:rows, :])
        decay = decay + step[rows:, :].astype(F32)
    mine_ref[:ranks, :] = jnp.where(odd, total[ranks:, :], total[:ranks, :])
    theirs_ref[:ranks, :] = jnp.where(odd, total[:ranks, :], total[ranks:, :]).astype(BF)
    mine_ref[ranks:, :] = decay
    theirs_ref[ranks:, :] = decay.astype(BF)


def step_call(ranks, lows, steps):
    rows = lows[0].shape[1]
    tall, chans = steps[0].shape
    width = min(512, chans)
    height = ranks + tall - rows
    return pl.pallas_call(
        functools.partial(step_kernel, ranks, len(lows)),
        grid=(chans // width,),
        in_specs=[whole(lows[0].shape)] * len(lows) + [columns(tall, width)] * len(steps),
        out_specs=[columns(height, width)] * 2,
        out_shape=[sds((height, chans), F32), sds((height, chans), BF)],
        compiler_params=params(16),
        name="step_products",
    )(*lows, *steps)


def rows_kernel(ranks, places, *refs):
    cuts, blocks, refs = refs[:places], refs[places : 2 * places], refs[2 * places :]
    products, (out_ref, coef_ref, step_ref, decay_ref) = refs[:-4], refs[-4:]
    total = jnp.zeros((cuts[0].shape[0], out_ref.shape[1]), F32)
    for cut, block in zip(cuts, blocks):
        total = total + dot(cut[...], block[...])
    out_ref[...] = total[:ranks, :]
    coef_ref[...] = total[ranks : ranks + coef_ref.shape[0], :]
    for chunk in range(len(products) // 2):

        @pl.when(pl.program_id(0) == chunk)
        def _():
            mine, theirs = products[2 * chunk : 2 * chunk + 2]
            step_ref[...] = mine[:ranks, :] + theirs[:ranks, :].astype(F32)
            decay_ref[...] = mine[ranks:, :] + theirs[ranks:, :].astype(F32)


def rows_call(ranks, coef_rows, cuts, blocks, products):
    rows, chans = blocks[0].shape
    height, width = products[0].shape
    heights = (ranks, coef_rows, ranks, height - ranks)
    return pl.pallas_call(
        functools.partial(rows_kernel, ranks, len(cuts)),
        grid=(chans // width,),
        in_specs=[whole(cuts[0].shape)] * len(cuts)
        + [columns(rows, width)] * len(blocks)
        + [whole((height, width))] * len(products),
        out_specs=[columns(height, width) for height in heights],
        out_shape=[sds((height, chans), F32) for height in heights],
        compiler_params=params(20),
        name="row_gradients",
    )(*cuts, *blocks, *products)


def last_kernel(places, taps, *refs):
    (_, tail_ref, weight_ref) = refs[:3]
    late, refs = refs[3 : 3 + places], refs[3 + places :]
    (out_ref, conv_w, conv_b, step_b, skip, fix) = refs
    fix[...] = tail_ref[...]
    inside = lax.axis_index("ctx") < places - 1
    following = jnp.where(inside, late[places - 1][8:16, :].astype(F32), 0.0)
    for row in range(taps - 1):
        extra = jnp.zeros((1, fix.shape[1]), F32)
        for tap in range(row + 1):
            extra = extra + weight_ref[tap : tap + 1, :] * following[row - tap : row - tap + 1, :]
        at = 16 - (taps - 1) + row
        fix[at : at + 1, :] += extra
    out_ref[...] = fix[...].astype(BF)
    total = late[0][...].astype(F32)
    for part in late[1:]:
        total = total + part[...].astype(F32)
    conv_w[...] = total[:taps, :]
    conv_b[...] = total[taps : taps + 1, :]
    step_b[...] = total[taps + 1 : taps + 2, :]
    skip[...] = total[taps + 2 : taps + 3, :]


def last_call(main, tail, weight, late):
    rows, chans = main.shape
    taps = weight.shape[0]
    places = len(late)
    return pl.pallas_call(
        functools.partial(last_kernel, places, taps),
        grid=(1,),
        in_specs=[pl.BlockSpec(memory_space=pl.ANY), columns(16, chans), columns(taps, chans)]
        + [columns(16, chans)] * places,
        out_specs=[
            pl.BlockSpec((16, chans), lambda i: (rows // 16 - 1, i)),
            columns(taps, chans),
        ]
        + [columns(1, chans)] * 3,
        out_shape=[sds((rows, chans), BF), sds((taps, chans), F32)] + [sds((1, chans), F32)] * 3,
        scratch_shapes=[pltpu.VMEM((16, chans), F32)],
        input_output_aliases={0: 0},
        compiler_params=params(8),
        name="last_rows",
    )(main, tail, weight, *late)


def exchange(block, axis):
    return lax.all_to_all(block, axis, split_axis=0, concat_axis=0, tiled=True)


def swap(block, axis, mask):
    return lax.ppermute(block, axis, [(i, i ^ mask) for i in range(lax.axis_size(axis))])


tie = lax.optimization_barrier


def spread(block):
    return [block] + [swap(block, "ctx", mask) for mask in range(1, min(lax.axis_size("ctx"), 3))]


def spread_on(blocks):
    places = lax.axis_size("ctx")
    if places == 4:
        return blocks + [swap(blocks[2], "ctx", 1)]
    return blocks + [swap(blocks[0], "ctx", mask) for mask in range(3, places)]


def gather_near(block):
    return [block] + [swap(block, "ctx", mask) for mask in range(2, lax.axis_size("ctx"), 2)]


def chan_sum(part):
    mask, peers = 1, lax.axis_size("chan")
    while True:
        other = swap(part, "chan", mask)
        mask *= 2
        if mask == peers:
            return part, other
        part = (part.astype(F32) + other.astype(F32)).astype(BF)


def body(
    conv_input,
    gate_input,
    out_grad,
    conv_weight,
    conv_bias,
    proj_weight,
    step_weight,
    step_bias,
    decay_log,
    skip_gain,
):
    rows, chans = conv_input.shape
    taps = conv_weight.shape[0]
    low_rank = step_weight.shape[0]
    states = decay_log.shape[0]
    places = lax.axis_size("ctx")
    groups = group_rows(chans)
    decay = decay_log.reshape(states, -1, groups, 128).transpose(1, 0, 2, 3)
    skips = skip_gain.reshape(-1, groups, 128)
    conv_bias = conv_bias[None, :]
    step_bias = step_bias[None, :]
    skip_gain = skip_gain[None, :]

    chunks = decay.shape[0]
    rim = shift(conv_input[rows - (taps - 1) :], "ctx", 1)
    conv_out, part = conv_call(conv_input, rim, conv_weight, conv_bias, proj_weight)
    blocks = spread(conv_out)
    parts = chan_sum(part)
    coef = (parts[0][:, low_rank:].astype(F32) + parts[1][:, low_rank:].astype(F32)).astype(BF)
    coef = coef.astype(F32).reshape(-1)
    dt, dx, g, low, *messages = local_call(
        parts, coef, step_weight, step_bias, decay, conv_out, gate_input, out_grad, states, places
    )
    messages = [swap(message, "ctx", mask) for mask, message in enumerate(messages, 1)]
    messages, blocks, low = tie((messages, blocks, low))
    blocks = spread_on(blocks)
    lows = gather_near(jnp.transpose(low))
    previous, steps = [], []
    for chunk in range(chunks):
        message, grad_gate, scan_part, small, part = scan_call(
            places, chunk, coef, (dt, dx, g), decay, skips, conv_out, gate_input, out_grad,
            step_weight, skip_gain, messages, previous,
        )
        previous = [part, grad_gate, scan_part, small]
        if chunk == 0:
            previous, blocks = tie((previous, blocks))
        else:
            previous, steps[-1], lows = tie((previous, steps[-1], lows))
        steps.append(gather_near(message))
    part, grad_gate, scan_part, small = previous
    ranks = low_rank // places
    products = []
    backs = chan_sum(part)
    if chunks > 1:
        near, lows = tie((backs[0], lows))
        backs = (near, backs[1])
    for step in steps[:-1]:
        mine, theirs = step_call(ranks, lows, step)
        products += [mine, swap(theirs, "ctx", 1)]
    cuts = cut_call(places, backs)
    cuts, lows = tie((cuts, lows))
    cuts = [cuts[0]] + [swap(cut, "ctx", mask) for mask, cut in enumerate(cuts[1:], 1)]
    mine, theirs = step_call(ranks, lows, steps[-1])
    backs, theirs = tie((backs, theirs))
    latest = [mine, swap(theirs, "ctx", 1)]
    main, tail, sums = conv_grad_call(
        places, low_rank, backs, proj_weight, scan_part, small, conv_input, rim, conv_weight,
        conv_bias,
    )
    sums, cuts, products = tie((sums, cuts, products))
    late = [sums] + [rotate(sums, "ctx", hop) for hop in range(1, places)]
    grad_proj, grad_coef, grad_step, decay_grad = rows_call(
        ranks, 2 * states // places, cuts, blocks, products + latest
    )
    late, grad_proj = tie((late, grad_proj))
    grad_input, conv_w, conv_b, step_b, skip = last_call(main, tail, conv_weight, late)
    return (
        grad_input,
        grad_gate,
        grad_proj,
        grad_coef,
        grad_step,
        conv_w,
        conv_b[0],
        step_b[0],
        decay_grad,
        skip[0],
    )


def solution(mesh):
    tokens, columns_, chan = P("ctx", "chan"), P(None, "chan"), P("chan")
    in_specs = (
        tokens, tokens, tokens, columns_, chan, columns_, columns_, chan, columns_, chan,
    )
    out_specs = (
        tokens, tokens, tokens, tokens, tokens, columns_, chan, chan, columns_, chan,
    )
    return jax.shard_map(body, mesh=mesh, in_specs=in_specs, out_specs=out_specs, check_vma=False)
```

```python
import functools

import jax
import jax.numpy as jnp
from jax import lax
from jax.experimental import pallas as pl
from jax.experimental.pallas import tpu as pltpu
from jax.sharding import PartitionSpec as P

BF = jnp.bfloat16
F32 = jnp.float32
LOG2E = 1.4426950408889634
LN2 = 0.6931471805599453
MIB = 1024 * 1024
NT = (((1,), (1,)), ((), ()))
TN = (((0,), (0,)), ((), ()))


def group_rows(chans):
    for rows in (8, 4, 2, 1):
        if chans % (rows * 128) == 0:
            return rows
    return 1


def dot(a, b, dims=(((1,), (0,)), ((), ()))):
    return lax.dot_general(a, b, dims, preferred_element_type=F32)


def params(mebibytes):
    return pltpu.CompilerParams(vmem_limit_bytes=mebibytes * MIB)


def sds(shape, dtype):
    return jax.ShapeDtypeStruct(shape, dtype)


def whole(shape):
    return pl.BlockSpec(shape, lambda i: (0,) * len(shape))


def columns(rows, width):
    return pl.BlockSpec((rows, width), lambda i: (0, i))


def sigmoid(v):
    return 0.5 + 0.5 * jnp.tanh(0.5 * v)


def rotate(block, axis, distance):
    count = lax.axis_size(axis)
    return lax.ppermute(block, axis, [(i, (i + distance) % count) for i in range(count)])


def shift(block, axis, distance):
    count = lax.axis_size(axis)
    route = [(i, i + distance) for i in range(count) if 0 <= i + distance < count]
    return lax.ppermute(block, axis, route)


def fill_extended(ext, rim_ref, input_ref, taps):
    rows = input_ref.shape[0]
    ext[8 - (taps - 1) : 8, :] = rim_ref[...].astype(F32)
    ext[8 : 8 + rows, :] = input_ref[...].astype(F32)


def conv_block(ext, weight, bias, taps, start, rows):
    total = bias + jnp.zeros((rows, ext.shape[1]), F32)
    for tap in range(taps):
        first = 8 - (taps - 1) + tap + start
        total = total + weight[tap : tap + 1, :] * ext[first : first + rows, :]
    return total


def conv_kernel(input_ref, rim_ref, weight_ref, bias_ref, proj_ref, out_ref, part_ref, ext, acc):
    step = pl.program_id(0)
    taps = weight_ref.shape[0]
    rows = input_ref.shape[0]
    fill_extended(ext, rim_ref, input_ref, taps)
    for start in range(0, rows, 16):
        pre = conv_block(ext, weight_ref, bias_ref[...], taps, start, 16)
        out_ref[start : start + 16, :] = (pre * sigmoid(pre)).astype(BF)
    part = dot(out_ref[...], proj_ref[...], NT)

    @pl.when(step == 0)
    def _():
        acc[...] = part

    @pl.when(step > 0)
    def _():
        acc[...] += part

    @pl.when(step == pl.num_programs(0) - 1)
    def _():
        part_ref[...] = acc[...].astype(BF)


def conv_call(conv_input, rim, weight, bias, proj_weight):
    rows, chans = conv_input.shape
    taps = weight.shape[0]
    wide = proj_weight.shape[0]
    width = min(1024, chans)
    return pl.pallas_call(
        conv_kernel,
        grid=(chans // width,),
        in_specs=[
            columns(rows, width),
            columns(taps - 1, width),
            columns(taps, width),
            columns(1, width),
            columns(wide, width),
        ],
        out_specs=[columns(rows, width), whole((rows, wide))],
        out_shape=[sds((rows, chans), BF), sds((rows, wide), BF)],
        scratch_shapes=[pltpu.VMEM((rows + 8, width), F32), pltpu.VMEM((rows, wide), F32)],
        compiler_params=params(58),
        name="conv_project",
    )(conv_input, rim, weight, bias, proj_weight)


def tile_rows(value, target, lead, groups):
    rows = value.shape[0]
    for block in range(rows // 8):
        for group in range(groups):
            first = (block * groups + group) * 8
            target[lead, first : first + 8, :] = value[
                block * 8 : block * 8 + 8, group * 128 : group * 128 + 128
            ]


def local_kernel(low_rank, states, places, *refs):
    parts, refs = refs[:2], refs[2:]
    (coef, weight_ref, bias_ref, decay_ref, conv_ref, gate_ref, grad_ref) = refs[:7]
    (dt_ref, dx_ref, g_ref, low) = refs[7:11]
    messages, refs = refs[11 : 10 + places], refs[10 + places :]
    (tiles, dts, dxs, gs, fwd, bwd) = refs
    step = pl.program_id(0)
    chunks = dts.shape[0]
    rows = conv_ref.shape[0]
    groups = decay_ref.shape[2]

    @pl.when(step == 0)
    def _():
        total = (parts[0][...].astype(F32) + parts[1][...].astype(F32)).astype(BF)
        low[...] = total[:, :low_rank]

    pre = dot(low[...], weight_ref[...]) + bias_ref[...]
    for start in range(0, rows, 16):
        here = slice(start, start + 16)
        p = pre[here, :]
        size = jnp.maximum(p, 0.0) + jnp.log1p(jnp.exp(-jnp.abs(p)))
        gate = gate_ref[here, :].astype(F32)
        grad = grad_ref[here, :].astype(F32) * gate * sigmoid(gate)
        drive = size * conv_ref[here, :].astype(F32)
        for half in range(2):
            for group in range(groups):
                first = ((start // 8 + half) * groups + group) * 8
                lanes = slice(group * 128, group * 128 + 128)
                subs = slice(half * 8, half * 8 + 8)
                tiles[0, first : first + 8, :] = size[subs, lanes]
                tiles[1, first : first + 8, :] = drive[subs, lanes]
                tiles[2, first : first + 8, :] = grad[subs, lanes]

    def relay(index, _):
        for sub in range(8):
            token = index * 8 + sub
            at = pl.ds(index * groups * 8 + sub, groups, stride=8)
            for kind, (held, out) in enumerate(((dts, dt_ref), (dxs, dx_ref), (gs, g_ref))):
                row = tiles[kind, at, :]
                held[step, token] = row
                out[0, token] = row
        return 0

    lax.fori_loop(0, rows // 8, relay, 0)

    @pl.when(step == chunks - 1)
    def _():
        batch = 4
        zero = jnp.zeros((groups, 128), F32)
        for lead in range(0, states, batch):
            pairs = [(n, v) for n in range(lead, lead + batch) for v in range(chunks)]
            rates = [-LOG2E * jnp.exp(decay_ref[v, n]) for n, v in pairs]

            def block(index, carry):
                state, run, head, total = (list(part) for part in carry)
                for sub in range(8):
                    token = index * 8 + sub
                    base = token * (2 * states)
                    size = [dts[v, token] for v in range(chunks)]
                    drive = [dxs[v, token] for v in range(chunks)]
                    grad = [gs[v, token] for v in range(chunks)]
                    if lead == 0:
                        total = [a + b for a, b in zip(total, size)]
                    for k, (n, v) in enumerate(pairs):
                        factor = jnp.exp2(size[v] * rates[k])
                        state[k] = factor * state[k] + drive[v] * coef[base + n]
                        run[k] = run[k] * factor
                        head[k] = head[k] + run[k] * (grad[v] * coef[base + (states + n)])
                return state, run, head, total

            many = [zero] * len(pairs)
            state, run, head, total = lax.fori_loop(
                0,
                rows // 8,
                block,
                (many, [zero + 1.0] * len(pairs), many, [zero] * chunks),
            )
            for k, (n, v) in enumerate(pairs):
                fwd[v, n] = state[k]
                bwd[v, n] = head[k]
            if lead == 0:
                for v in range(chunks):
                    coarse = total[v].astype(BF).astype(F32)
                    for target in (fwd, bwd):
                        target[v, states] = coarse
                        target[v, states + 1] = total[v] - coarse
        place = lax.axis_index("ctx")
        for mask, message in enumerate(messages, 1):
            message[...] = jnp.where((place ^ mask) > place, fwd[...], bwd[...]).astype(BF)


def local_call(parts, coef, step_weight, step_bias, decay, conv_out, gate, grad, states, places):
    rows, chans = conv_out.shape
    wide = parts[0].shape[1]
    low_rank = step_weight.shape[0]
    chunks, _, groups, _ = decay.shape
    width = groups * 128
    message = (chunks, states + 2, groups, 128)
    dense = (chunks, rows, groups, 128)
    big = pltpu.VMEM(dense, F32)
    return pl.pallas_call(
        functools.partial(local_kernel, low_rank, states, places),
        grid=(chunks,),
        in_specs=[
            whole((rows, wide)),
            whole((rows, wide)),
            pl.BlockSpec(memory_space=pltpu.SMEM),
            columns(low_rank, width),
            columns(1, width),
            whole(decay.shape),
            columns(rows, width),
            columns(rows, width),
            columns(rows, width),
        ],
        out_specs=[
            *[pl.BlockSpec((1, rows, groups, 128), lambda i: (i, 0, 0, 0))] * 3,
            whole((rows, low_rank)),
        ]
        + [whole(message)] * (places - 1),
        out_shape=[
            *[sds(dense, F32)] * 3,
            sds((rows, low_rank), BF),
        ]
        + [sds(message, BF)] * (places - 1),
        scratch_shapes=[
            pltpu.VMEM((3, rows * groups, 128), F32),
            big,
            big,
            big,
            pltpu.VMEM(message, F32),
            pltpu.VMEM(message, F32),
        ],
        compiler_params=params(58),
        name="local_ends",
    )(*parts, coef, step_weight, step_bias, decay, conv_out, gate, grad)


def fold_rows(products, base, groups, target, first):
    total = products[pl.ds(base, 8, stride=groups), :]
    for row in range(1, groups):
        total = total + products[pl.ds(base + row, 8, stride=groups), :]
    target[pl.ds(pl.multiple_of(first, 8), 8), :] = total


def scan_kernel(places, states, opening, *refs):
    (coef, dt_ref, dx_ref, g_ref, decay_ref, skips_ref) = refs[:6]
    (conv_ref, gate_ref, grad_ref, weight_ref, skip_ref) = refs[6:11]
    messages, refs = refs[11 : 10 + places], refs[10 + places :]
    if not opening:
        before_ref, refs = refs[0], refs[4:]
    (pre_ref, gate_out, scan_out, small_ref, part_ref) = refs[:5]
    refs = refs[5:]
    (ys, dds, qs, decayed, coef_out, coef_in, rate, decay_acc, acc, ends, products, factors) = refs
    rows = conv_ref.shape[0]
    groups = decay_ref.shape[2]
    low_rank = weight_ref.shape[0]
    span = groups * 8

    place = lax.axis_index("ctx")
    for n in range(states):
        rate[n] = -LOG2E * jnp.exp(decay_ref[0, n])
    ends[place] = jnp.zeros(ends.shape[1:], F32)
    for mask, message in enumerate(messages, 1):
        ends[place ^ mask] = message[0].astype(F32)
    totals = [ends[q, states] + ends[q, states + 1] for q in range(places)]
    state, carry = [], []
    for n in range(states):
        before = jnp.zeros((groups, 128), F32)
        after = jnp.zeros((groups, 128), F32)
        for q in range(places - 1):
            reached = jnp.exp2(rate[n] * totals[q]) * before + ends[q, n]
            before = jnp.where(q < place, reached, before)
        for q in range(places - 1, 0, -1):
            reached = jnp.exp2(rate[n] * totals[q]) * after + ends[q, n]
            after = jnp.where(q > place, reached, after)
        state.append(before)
        carry.append(after)

    def forward(index, state):
        state = list(state)
        for sub in range(8):
            token = index * 8 + sub
            at = pl.ds(index * span + sub, groups, stride=8)
            scalar = token * (2 * states)
            size, drive, grad = dt_ref[0, token], dx_ref[0, token], g_ref[0, token]
            result = jnp.zeros((groups, 128), F32)
            for lead in range(0, states, 8):
                base = (sub * states + lead) * groups
                for n in range(lead, lead + 8):
                    factor = jnp.exp2(size * rate[n])
                    kept = factor * state[n]
                    factors[token, n] = factor
                    decayed[token, n] = kept
                    state[n] = kept + drive * coef[scalar + n]
                    result = result + state[n] * coef[scalar + (states + n)]
                    row = base + (n - lead) * groups
                    products[row : row + groups, :] = state[n] * grad
                fold_rows(products, base, groups, coef_out, token * states + lead)
            ys[at, :] = result
        return state

    lax.fori_loop(0, rows // 8, forward, state)

    def backward(hop, both):
        carry, gathered = list(both[0]), list(both[1])
        index = rows // 8 - 1 - hop
        for sub in range(7, -1, -1):
            token = index * 8 + sub
            at = pl.ds(index * span + sub, groups, stride=8)
            scalar = token * (2 * states)
            size, drive, grad = dt_ref[0, token], dx_ref[0, token], g_ref[0, token]
            slope = jnp.zeros((groups, 128), F32)
            inner = jnp.zeros((groups, 128), F32)
            for lead in range(0, states, 8):
                base = (sub * states + lead) * groups
                for n in range(lead, lead + 8):
                    adjoint = carry[n] + grad * coef[scalar + (states + n)]
                    carry[n] = factors[token, n] * adjoint
                    weighted = adjoint * decayed[token, n] * (size * rate[n])
                    slope = slope + weighted
                    gathered[n] = gathered[n] + weighted
                    inner = inner + adjoint * coef[scalar + n]
                    row = base + (n - lead) * groups
                    products[row : row + groups, :] = adjoint * drive
                fold_rows(products, base, groups, coef_in, token * states + lead)
            tiny = 1.0 - 0.5 * size * (1.0 - size * (1.0 / 3.0) * (1.0 - 0.25 * size))
            ratio = jnp.where(size < 0.03, tiny, (1.0 - jnp.exp(-size)) / jnp.maximum(size, 0.03))
            dds[at, :] = (LN2 * slope + drive * inner) * ratio
            qs[at, :] = size * inner + skips_ref[0] * grad
        return carry, gathered

    zeros = [jnp.zeros((groups, 128), F32)] * states
    _, gathered = lax.fori_loop(0, rows // 8, backward, (carry, zeros))
    for n in range(states):
        decay_acc[n * groups : n * groups + groups, :] = gathered[n] * LN2

    for group in range(groups):
        pre_ref[rows : rows + states, group * 128 : group * 128 + 128] = decay_acc[
            pl.ds(group, states, stride=groups), :
        ].astype(BF)
    skip = skip_ref[...]
    bias_sum = jnp.zeros((1, conv_ref.shape[1]), F32)
    skip_sum = jnp.zeros((1, conv_ref.shape[1]), F32)
    for start in range(0, rows, 16):
        here = slice(start, start + 16)

        def natural(read):
            return jnp.concatenate(
                [
                    jnp.concatenate(
                        [
                            read(((start // 8 + half) * groups + group) * 8)
                            for group in range(groups)
                        ],
                        axis=1,
                    )
                    for half in range(2)
                ],
                axis=0,
            )

        d_pre = natural(lambda first: dds[first : first + 8, :])
        out = natural(lambda first: ys[first : first + 8, :])
        conv = conv_ref[here, :].astype(F32)
        gate = gate_ref[here, :].astype(F32)
        grad = grad_ref[here, :].astype(F32)
        sig = sigmoid(gate)
        scan_grad = grad * gate * sig
        pre_ref[here, :] = d_pre.astype(BF)
        bias_sum = bias_sum + jnp.sum(d_pre, axis=0, keepdims=True)
        skip_sum = skip_sum + jnp.sum(scan_grad * conv, axis=0, keepdims=True)
        scan_out[here, :] = natural(lambda first: qs[first : first + 8, :]).astype(BF)
        gate_out[here, :] = (
            grad * (out + skip * conv) * (sig * (1.0 + gate * (1.0 - sig)))
        ).astype(BF)
    small_ref[...] = jnp.concatenate(
        [bias_sum, skip_sum, jnp.zeros((6, bias_sum.shape[1]), F32)], axis=0
    )

    pre_bf = pre_ref[:rows, :]
    lanes = lax.broadcasted_iota(jnp.int32, (2 * states, 128), 0)
    coefs = jnp.zeros((2 * states, rows), F32)
    for n in range(states):
        at = pl.ds(n, rows, stride=states)
        for kind, source in enumerate((coef_in, coef_out)):
            pick = jnp.where(lanes == kind * states + n, 1.0, 0.0).astype(BF)
            coefs = coefs + dot(pick, source[at, :].astype(BF), NT)
    wide = dot(weight_ref[...], pre_bf, NT)

    ranks, coef_rows, block = low_rank // places, 2 * states // places, acc.shape[0] // places

    acc[...] = jnp.zeros_like(acc) if opening else before_ref[...]
    for q in range(places):
        at = q * block
        acc[at : at + ranks, :] += wide[q * ranks : (q + 1) * ranks, :]
        acc[at + ranks : at + ranks + coef_rows, :] += coefs[
            q * coef_rows : (q + 1) * coef_rows, :
        ]
    part_ref[...] = acc[...].astype(part_ref.dtype)


def padded(wide):
    return (wide + 127) // 128 * 128


def scan_call(
    places, chunk, coef, dense, decay, skips, conv_out, gate, grad, step_weight, skip, messages,
    previous,
):
    rows, chans = conv_out.shape
    low_rank = step_weight.shape[0]
    chunks, states, groups, _ = decay.shape
    width = groups * 128
    wide = padded(low_rank + 2 * states)
    lead = lambda *shape: pl.BlockSpec((1,) + shape, lambda i: (chunk,) + (0,) * len(shape))
    here = lambda height: pl.BlockSpec((height, width), lambda i: (0, chunk))
    tall = pltpu.VMEM((rows * groups, 128), F32)
    first, last = chunk == 0, chunk == chunks - 1
    in_specs = [
        pl.BlockSpec(memory_space=pltpu.SMEM),
        lead(rows, groups, 128),
        lead(rows, groups, 128),
        lead(rows, groups, 128),
        lead(states, groups, 128),
        lead(groups, 128),
        here(rows),
        here(rows),
        here(rows),
        here(low_rank),
        here(1),
    ]
    in_specs += [lead(states + 2, groups, 128)] * (places - 1)
    aliases = {}
    if not first:
        in_specs += [whole((wide, rows))] + [pl.BlockSpec(memory_space=pl.ANY)] * 3
        aliases = {11 + places: 1, 12 + places: 2, 13 + places: 3}
    return pl.pallas_call(
        functools.partial(scan_kernel, places, states, first),
        grid=(1,),
        in_specs=in_specs,
        out_specs=[
            whole((rows + states, width)),
            here(rows),
            here(rows),
            here(8),
            whole((wide, rows)),
        ],
        out_shape=[
            sds((rows + states, width), BF),
            sds((rows, chans), BF),
            sds((rows, chans), BF),
            sds((8, chans), F32),
            sds((wide, rows), BF if last else F32),
        ],
        scratch_shapes=[
            tall,
            tall,
            tall,
            pltpu.VMEM((rows, states, groups, 128), F32),
            pltpu.VMEM((rows * states, 128), F32),
            pltpu.VMEM((rows * states, 128), F32),
            pltpu.VMEM((states, groups, 128), F32),
            pltpu.VMEM((states * groups, 128), F32),
            pltpu.VMEM((wide, rows), F32),
            pltpu.VMEM((places, states + 2, groups, 128), F32),
            pltpu.VMEM((8 * states * groups, 128), F32),
            pltpu.VMEM((rows, states, groups, 128), F32),
        ],
        input_output_aliases=aliases,
        compiler_params=params(58),
        name="scan_gradients",
    )(
        coef, *dense, decay, skips, conv_out, gate, grad, step_weight, skip, *messages, *previous
    )


def conv_grad_kernel(places, low_rank, back_a, back_b, proj_ref, scan_ref, small_in, input_ref, rim_ref, weight_ref, bias_ref,
                     out_ref, tail_ref, small_ref, ext, grad, back_t):
    taps = weight_ref.shape[0]
    rows = input_ref.shape[0]
    fill_extended(ext, rim_ref, input_ref, taps)
    wide = proj_ref.shape[0]
    block = back_a.shape[0] // places
    ranks, coef_rows = low_rank // places, (wide - low_rank) // places

    @pl.when(pl.program_id(0) == 0)
    def _():
        back = back_a[...].astype(F32) + back_b[...].astype(F32)
        order = [back[q * block : q * block + ranks, :] for q in range(places)]
        order += [back[q * block + ranks : q * block + ranks + coef_rows, :] for q in range(places)]
        order += [jnp.zeros((padded(wide) - wide, back.shape[1]), F32)]
        back_t[...] = jnp.transpose(jnp.concatenate(order, axis=0))[:, :wide].astype(BF)

    d_xc = dot(back_t[...], proj_ref[...])
    sums = [jnp.zeros((1, input_ref.shape[1]), F32) for _ in range(taps + 1)]
    for start in range(0, rows, 16):
        here = slice(start, start + 16)
        pre = conv_block(ext, weight_ref, bias_ref[...], taps, start, 16)
        sig = sigmoid(pre)
        value = (d_xc[here, :] + scan_ref[here, :].astype(F32)) * (sig * (1.0 + pre * (1.0 - sig)))
        grad[here, :] = value
        for tap in range(taps):
            first = 8 - (taps - 1) + tap + start
            sums[tap] = sums[tap] + jnp.sum(value * ext[first : first + 16, :], axis=0, keepdims=True)
        sums[taps] = sums[taps] + jnp.sum(value, axis=0, keepdims=True)
    grad[rows : rows + 8, :] = jnp.zeros((8, grad.shape[1]), F32)
    for start in range(0, rows, 16):
        total = jnp.zeros((16, grad.shape[1]), F32)
        for tap in range(taps):
            first = start + taps - 1 - tap
            total = total + weight_ref[tap : tap + 1, :] * grad[first : first + 16, :]
        out_ref[start : start + 16, :] = total.astype(BF)
    tail_ref[...] = total
    small_ref[...] = jnp.concatenate(
        sums + [small_in[0 : 7 - taps, :], grad[0:8, :]], axis=0
    ).astype(BF)


def conv_grad_call(places, low_rank, backs, proj_weight, scan_part, small, conv_input, rim, weight, bias):
    rows, chans = conv_input.shape
    taps = weight.shape[0]
    wide = proj_weight.shape[0]
    width = min(1024, chans)
    return pl.pallas_call(
        functools.partial(conv_grad_kernel, places, low_rank),
        grid=(chans // width,),
        in_specs=[
            whole(backs[0].shape),
            whole(backs[1].shape),
            columns(wide, width),
            columns(rows, width),
            columns(8, width),
            columns(rows, width),
            columns(taps - 1, width),
            columns(taps, width),
            columns(1, width),
        ],
        out_specs=[columns(rows, width), columns(16, width), columns(16, width)],
        out_shape=[sds((rows, chans), BF), sds((16, chans), F32), sds((16, chans), BF)],
        scratch_shapes=[
            pltpu.VMEM((rows + 8, width), F32),
            pltpu.VMEM((rows + 8, width), F32),
            pltpu.VMEM((rows, wide), BF),
        ],
        compiler_params=params(18),
        name="conv_gradients",
    )(*backs, proj_weight, scan_part, small, conv_input, rim, weight, bias)


def cut_kernel(places, back_a, back_b, *refs):
    cuts, (back,) = refs[:places], refs[places:]
    place = lax.axis_index("ctx")
    height = back.shape[0] // places
    back[...] = back_a[...].astype(F32) + back_b[...].astype(F32)
    for mask in range(places):
        cuts[mask][...] = back[pl.ds((place ^ mask) * height, height), :].astype(BF)


def cut_call(places, backs):
    wide, rows = backs[0].shape
    return pl.pallas_call(
        functools.partial(cut_kernel, places),
        out_shape=[sds((wide // places, rows), BF)] * places,
        scratch_shapes=[pltpu.VMEM((wide, rows), F32)],
        compiler_params=params(8),
        name="cut_rows",
    )(*backs)


def step_kernel(ranks, near, *refs):
    lows, steps, (mine_ref, theirs_ref) = refs[:near], refs[near : 2 * near], refs[2 * near :]
    place = lax.axis_index("ctx")
    rows = lows[0].shape[1]
    pair = pl.ds(pl.multiple_of(lax.div(place, 2) * (2 * ranks), 16), 2 * ranks)
    odd = lax.rem(place, 2) == 1
    total = jnp.zeros((2 * ranks, mine_ref.shape[1]), F32)
    decay = jnp.zeros((mine_ref.shape[0] - ranks, mine_ref.shape[1]), F32)
    for low, step in zip(lows, steps):
        total = total + dot(low[pair, :], step[:rows, :])
        decay = decay + step[rows:, :].astype(F32)
    mine_ref[:ranks, :] = jnp.where(odd, total[ranks:, :], total[:ranks, :])
    theirs_ref[:ranks, :] = jnp.where(odd, total[:ranks, :], total[ranks:, :]).astype(BF)
    mine_ref[ranks:, :] = decay
    theirs_ref[ranks:, :] = decay.astype(BF)


def step_call(ranks, lows, steps):
    rows = lows[0].shape[1]
    tall, chans = steps[0].shape
    width = min(512, chans)
    height = ranks + tall - rows
    return pl.pallas_call(
        functools.partial(step_kernel, ranks, len(lows)),
        grid=(chans // width,),
        in_specs=[whole(lows[0].shape)] * len(lows) + [columns(tall, width)] * len(steps),
        out_specs=[columns(height, width)] * 2,
        out_shape=[sds((height, chans), F32), sds((height, chans), BF)],
        compiler_params=params(16),
        name="step_products",
    )(*lows, *steps)


def rows_kernel(ranks, places, *refs):
    cuts, blocks, (out_ref, coef_ref) = refs[:places], refs[places:-2], refs[-2:]
    total = jnp.zeros((cuts[0].shape[0], out_ref.shape[1]), F32)
    for cut, block in zip(cuts, blocks):
        total = total + dot(cut[...], block[...])
    out_ref[...] = total[:ranks, :]
    coef_ref[...] = total[ranks : ranks + coef_ref.shape[0], :]


def rows_call(ranks, coef_rows, cuts, blocks):
    rows, chans = blocks[0].shape
    width = min(1024, chans)
    return pl.pallas_call(
        functools.partial(rows_kernel, ranks, len(cuts)),
        grid=(chans // width,),
        in_specs=[whole(cuts[0].shape)] * len(cuts) + [columns(rows, width)] * len(blocks),
        out_specs=[columns(ranks, width), columns(coef_rows, width)],
        out_shape=[sds((ranks, chans), F32), sds((coef_rows, chans), F32)],
        compiler_params=params(16),
        name="row_gradients",
    )(*cuts, *blocks)


def total_kernel(*refs):
    products, (step_ref, decay_ref) = refs[:-2], refs[-2:]
    ranks = step_ref.shape[0]
    for chunk in range(len(products) // 2):

        @pl.when(pl.program_id(0) == chunk)
        def _():
            mine, theirs = products[2 * chunk : 2 * chunk + 2]
            step_ref[...] = mine[:ranks, :] + theirs[:ranks, :].astype(F32)
            decay_ref[...] = mine[ranks:, :] + theirs[ranks:, :].astype(F32)


def total_call(ranks, products):
    height, width = products[0].shape
    chunks = len(products) // 2
    heights = (ranks, height - ranks)
    return pl.pallas_call(
        total_kernel,
        grid=(chunks,),
        in_specs=[whole((height, width))] * len(products),
        out_specs=[columns(tall, width) for tall in heights],
        out_shape=[sds((tall, chunks * width), F32) for tall in heights],
        compiler_params=params(12),
        name="step_gradients",
    )(*products)


def last_kernel(places, taps, *refs):
    (_, tail_ref, weight_ref) = refs[:3]
    late, refs = refs[3 : 3 + places], refs[3 + places :]
    (out_ref, conv_w, conv_b, step_b, skip, fix) = refs
    fix[...] = tail_ref[...]
    inside = lax.axis_index("ctx") < places - 1
    following = jnp.where(inside, late[places - 1][8:16, :].astype(F32), 0.0)
    for row in range(taps - 1):
        extra = jnp.zeros((1, fix.shape[1]), F32)
        for tap in range(row + 1):
            extra = extra + weight_ref[tap : tap + 1, :] * following[row - tap : row - tap + 1, :]
        at = 16 - (taps - 1) + row
        fix[at : at + 1, :] += extra
    out_ref[...] = fix[...].astype(BF)
    total = late[0][...].astype(F32)
    for part in late[1:]:
        total = total + part[...].astype(F32)
    conv_w[...] = total[:taps, :]
    conv_b[...] = total[taps : taps + 1, :]
    step_b[...] = total[taps + 1 : taps + 2, :]
    skip[...] = total[taps + 2 : taps + 3, :]


def last_call(main, tail, weight, late):
    rows, chans = main.shape
    taps = weight.shape[0]
    places = len(late)
    return pl.pallas_call(
        functools.partial(last_kernel, places, taps),
        grid=(1,),
        in_specs=[pl.BlockSpec(memory_space=pl.ANY), columns(16, chans), columns(taps, chans)]
        + [columns(16, chans)] * places,
        out_specs=[
            pl.BlockSpec((16, chans), lambda i: (rows // 16 - 1, i)),
            columns(taps, chans),
        ]
        + [columns(1, chans)] * 3,
        out_shape=[sds((rows, chans), BF), sds((taps, chans), F32)] + [sds((1, chans), F32)] * 3,
        scratch_shapes=[pltpu.VMEM((16, chans), F32)],
        input_output_aliases={0: 0},
        compiler_params=params(8),
        name="last_rows",
    )(main, tail, weight, *late)


def exchange(block, axis):
    return lax.all_to_all(block, axis, split_axis=0, concat_axis=0, tiled=True)


def swap(block, axis, mask):
    return lax.ppermute(block, axis, [(i, i ^ mask) for i in range(lax.axis_size(axis))])


tie = lax.optimization_barrier


def spread(block):
    return [block] + [swap(block, "ctx", mask) for mask in range(1, min(lax.axis_size("ctx"), 3))]


def spread_on(blocks):
    places = lax.axis_size("ctx")
    if places == 4:
        return blocks + [swap(blocks[2], "ctx", 1)]
    return blocks + [swap(blocks[0], "ctx", mask) for mask in range(3, places)]


def gather_near(block):
    return [block] + [swap(block, "ctx", mask) for mask in range(2, lax.axis_size("ctx"), 2)]


def chan_sum(part):
    mask, peers = 1, lax.axis_size("chan")
    while True:
        other = swap(part, "chan", mask)
        mask *= 2
        if mask == peers:
            return part, other
        part = (part.astype(F32) + other.astype(F32)).astype(BF)


def body(
    conv_input,
    gate_input,
    out_grad,
    conv_weight,
    conv_bias,
    proj_weight,
    step_weight,
    step_bias,
    decay_log,
    skip_gain,
):
    rows, chans = conv_input.shape
    taps = conv_weight.shape[0]
    low_rank = step_weight.shape[0]
    states = decay_log.shape[0]
    places = lax.axis_size("ctx")
    groups = group_rows(chans)
    decay = decay_log.reshape(states, -1, groups, 128).transpose(1, 0, 2, 3)
    skips = skip_gain.reshape(-1, groups, 128)
    conv_bias = conv_bias[None, :]
    step_bias = step_bias[None, :]
    skip_gain = skip_gain[None, :]

    chunks = decay.shape[0]
    rim = shift(conv_input[rows - (taps - 1) :], "ctx", 1)
    conv_out, part = conv_call(conv_input, rim, conv_weight, conv_bias, proj_weight)
    blocks = spread(conv_out)
    parts = chan_sum(part)
    coef = (parts[0][:, low_rank:].astype(F32) + parts[1][:, low_rank:].astype(F32)).astype(BF)
    coef = coef.astype(F32).reshape(-1)
    dt, dx, g, low, *messages = local_call(
        parts, coef, step_weight, step_bias, decay, conv_out, gate_input, out_grad, states, places
    )
    messages = [swap(message, "ctx", mask) for mask, message in enumerate(messages, 1)]
    messages, blocks, low = tie((messages, blocks, low))
    blocks = spread_on(blocks)
    lows = gather_near(jnp.transpose(low))
    previous, steps = [], []
    for chunk in range(chunks):
        message, grad_gate, scan_part, small, part = scan_call(
            places, chunk, coef, (dt, dx, g), decay, skips, conv_out, gate_input, out_grad,
            step_weight, skip_gain, messages, previous,
        )
        previous = [part, grad_gate, scan_part, small]
        if chunk == 0:
            previous, blocks = tie((previous, blocks))
        else:
            previous, steps[-1], lows = tie((previous, steps[-1], lows))
        steps.append(gather_near(message))
    part, grad_gate, scan_part, small = previous
    ranks = low_rank // places
    products = []
    backs = chan_sum(part)
    if chunks > 1:
        near, lows = tie((backs[0], lows))
        backs = (near, backs[1])
    for step in steps[:-1]:
        mine, theirs = step_call(ranks, lows, step)
        products += [mine, swap(theirs, "ctx", 1)]
    cuts = cut_call(places, backs)
    cuts = [cuts[0]] + [swap(cut, "ctx", mask) for mask, cut in enumerate(cuts[1:], 1)]
    main, tail, sums = conv_grad_call(
        places, low_rank, backs, proj_weight, scan_part, small, conv_input, rim, conv_weight,
        conv_bias,
    )
    sums, cuts, products, steps[-1], lows = tie((sums, cuts, products, steps[-1], lows))
    mine, theirs = step_call(ranks, lows, steps[-1])
    products += [mine, swap(theirs, "ctx", 1)]
    late = [sums] + [rotate(sums, "ctx", hop) for hop in range(1, places)]
    grad_proj, grad_coef = rows_call(ranks, 2 * states // places, cuts, blocks)
    products, grad_proj = tie((products, grad_proj))
    grad_step, decay_grad = total_call(ranks, products)
    late, grad_step = tie((late, grad_step))
    grad_input, conv_w, conv_b, step_b, skip = last_call(main, tail, conv_weight, late)
    return (
        grad_input,
        grad_gate,
        grad_proj,
        grad_coef,
        grad_step,
        conv_w,
        conv_b[0],
        step_b[0],
        decay_grad,
        skip[0],
    )


def solution(mesh):
    tokens, columns_, chan = P("ctx", "chan"), P(None, "chan"), P("chan")
    in_specs = (
        tokens, tokens, tokens, columns_, chan, columns_, columns_, chan, columns_, chan,
    )
    out_specs = (
        tokens, tokens, tokens, tokens, tokens, columns_, chan, chan, columns_, chan,
    )
    return jax.shard_map(body, mesh=mesh, in_specs=in_specs, out_specs=out_specs, check_vma=False)
```

```python
import functools

import jax
import jax.numpy as jnp
from jax import lax
from jax.experimental import pallas as pl
from jax.experimental.pallas import tpu as pltpu
from jax.sharding import PartitionSpec as P

BF = jnp.bfloat16
F32 = jnp.float32
LOG2E = 1.4426950408889634
LN2 = 0.6931471805599453
MIB = 1024 * 1024
NT = (((1,), (1,)), ((), ()))
TN = (((0,), (0,)), ((), ()))


def group_rows(chans):
    for rows in (8, 4, 2, 1):
        if chans % (rows * 128) == 0:
            return rows
    return 1


def dot(a, b, dims=(((1,), (0,)), ((), ()))):
    return lax.dot_general(a, b, dims, preferred_element_type=F32)


def params(mebibytes):
    return pltpu.CompilerParams(vmem_limit_bytes=mebibytes * MIB)


def sds(shape, dtype):
    return jax.ShapeDtypeStruct(shape, dtype)


def whole(shape):
    return pl.BlockSpec(shape, lambda i: (0,) * len(shape))


def columns(rows, width):
    return pl.BlockSpec((rows, width), lambda i: (0, i))


def sigmoid(v):
    return 0.5 + 0.5 * jnp.tanh(0.5 * v)


def rotate(block, axis, distance):
    count = lax.axis_size(axis)
    return lax.ppermute(block, axis, [(i, (i + distance) % count) for i in range(count)])


def shift(block, axis, distance):
    count = lax.axis_size(axis)
    route = [(i, i + distance) for i in range(count) if 0 <= i + distance < count]
    return lax.ppermute(block, axis, route)


def fill_extended(ext, rim_ref, input_ref, taps):
    rows = input_ref.shape[0]
    ext[8 - (taps - 1) : 8, :] = rim_ref[...].astype(F32)
    ext[8 : 8 + rows, :] = input_ref[...].astype(F32)


def conv_block(ext, weight, bias, taps, start, rows):
    total = bias + jnp.zeros((rows, ext.shape[1]), F32)
    for tap in range(taps):
        first = 8 - (taps - 1) + tap + start
        total = total + weight[tap : tap + 1, :] * ext[first : first + rows, :]
    return total


def conv_kernel(input_ref, rim_ref, weight_ref, bias_ref, proj_ref, out_ref, part_ref, ext, acc):
    step = pl.program_id(0)
    taps = weight_ref.shape[0]
    rows = input_ref.shape[0]
    fill_extended(ext, rim_ref, input_ref, taps)
    for start in range(0, rows, 16):
        pre = conv_block(ext, weight_ref, bias_ref[...], taps, start, 16)
        out_ref[start : start + 16, :] = (pre * sigmoid(pre)).astype(BF)
    part = dot(out_ref[...], proj_ref[...], NT)

    @pl.when(step == 0)
    def _():
        acc[...] = part

    @pl.when(step > 0)
    def _():
        acc[...] += part

    @pl.when(step == pl.num_programs(0) - 1)
    def _():
        part_ref[...] = acc[...].astype(BF)


def conv_call(conv_input, rim, weight, bias, proj_weight):
    rows, chans = conv_input.shape
    taps = weight.shape[0]
    wide = proj_weight.shape[0]
    width = min(1024, chans)
    return pl.pallas_call(
        conv_kernel,
        grid=(chans // width,),
        in_specs=[
            columns(rows, width),
            columns(taps - 1, width),
            columns(taps, width),
            columns(1, width),
            columns(wide, width),
        ],
        out_specs=[columns(rows, width), whole((rows, wide))],
        out_shape=[sds((rows, chans), BF), sds((rows, wide), BF)],
        scratch_shapes=[pltpu.VMEM((rows + 8, width), F32), pltpu.VMEM((rows, wide), F32)],
        compiler_params=params(58),
        name="conv_project",
    )(conv_input, rim, weight, bias, proj_weight)


def tile_rows(value, target, lead, groups):
    rows = value.shape[0]
    for block in range(rows // 8):
        for group in range(groups):
            first = (block * groups + group) * 8
            target[lead, first : first + 8, :] = value[
                block * 8 : block * 8 + 8, group * 128 : group * 128 + 128
            ]


def local_kernel(low_rank, states, places, *refs):
    parts, refs = refs[:2], refs[2:]
    (coef, weight_ref, bias_ref, decay_ref, conv_ref, gate_ref, grad_ref) = refs[:7]
    (dt_ref, dx_ref, g_ref, low) = refs[7:11]
    messages, refs = refs[11 : 10 + places], refs[10 + places :]
    (tiles, dts, dxs, gs, fwd, bwd) = refs
    step = pl.program_id(0)
    chunks = dts.shape[0]
    rows = conv_ref.shape[0]
    groups = decay_ref.shape[2]

    @pl.when(step == 0)
    def _():
        total = (parts[0][...].astype(F32) + parts[1][...].astype(F32)).astype(BF)
        low[...] = total[:, :low_rank]

    pre = dot(low[...], weight_ref[...]) + bias_ref[...]
    for start in range(0, rows, 16):
        here = slice(start, start + 16)
        p = pre[here, :]
        size = jnp.maximum(p, 0.0) + jnp.log1p(jnp.exp(-jnp.abs(p)))
        gate = gate_ref[here, :].astype(F32)
        grad = grad_ref[here, :].astype(F32) * gate * sigmoid(gate)
        drive = size * conv_ref[here, :].astype(F32)
        for half in range(2):
            for group in range(groups):
                first = ((start // 8 + half) * groups + group) * 8
                lanes = slice(group * 128, group * 128 + 128)
                subs = slice(half * 8, half * 8 + 8)
                tiles[0, first : first + 8, :] = size[subs, lanes]
                tiles[1, first : first + 8, :] = drive[subs, lanes]
                tiles[2, first : first + 8, :] = grad[subs, lanes]

    def relay(index, _):
        for sub in range(8):
            token = index * 8 + sub
            at = pl.ds(index * groups * 8 + sub, groups, stride=8)
            for kind, (held, out) in enumerate(((dts, dt_ref), (dxs, dx_ref), (gs, g_ref))):
                row = tiles[kind, at, :]
                held[step, token] = row
                out[0, token] = row
        return 0

    lax.fori_loop(0, rows // 8, relay, 0)

    @pl.when(step == chunks - 1)
    def _():
        batch = 4
        zero = jnp.zeros((groups, 128), F32)
        for lead in range(0, states, batch):
            pairs = [(n, v) for n in range(lead, lead + batch) for v in range(chunks)]
            rates = [-LOG2E * jnp.exp(decay_ref[v, n]) for n, v in pairs]

            def block(index, carry):
                state, run, head, total = (list(part) for part in carry)
                for sub in range(8):
                    token = index * 8 + sub
                    base = token * (2 * states)
                    size = [dts[v, token] for v in range(chunks)]
                    drive = [dxs[v, token] for v in range(chunks)]
                    grad = [gs[v, token] for v in range(chunks)]
                    if lead == 0:
                        total = [a + b for a, b in zip(total, size)]
                    for k, (n, v) in enumerate(pairs):
                        factor = jnp.exp2(size[v] * rates[k])
                        state[k] = factor * state[k] + drive[v] * coef[base + n]
                        run[k] = run[k] * factor
                        head[k] = head[k] + run[k] * (grad[v] * coef[base + (states + n)])
                return state, run, head, total

            many = [zero] * len(pairs)
            state, run, head, total = lax.fori_loop(
                0,
                rows // 8,
                block,
                (many, [zero + 1.0] * len(pairs), many, [zero] * chunks),
            )
            for k, (n, v) in enumerate(pairs):
                fwd[v, n] = state[k]
                bwd[v, n] = head[k]
            if lead == 0:
                for v in range(chunks):
                    coarse = total[v].astype(BF).astype(F32)
                    for target in (fwd, bwd):
                        target[v, states] = coarse
                        target[v, states + 1] = total[v] - coarse
        place = lax.axis_index("ctx")
        for mask, message in enumerate(messages, 1):
            message[...] = jnp.where((place ^ mask) > place, fwd[...], bwd[...]).astype(BF)


def local_call(parts, coef, step_weight, step_bias, decay, conv_out, gate, grad, states, places):
    rows, chans = conv_out.shape
    wide = parts[0].shape[1]
    low_rank = step_weight.shape[0]
    chunks, _, groups, _ = decay.shape
    width = groups * 128
    message = (chunks, states + 2, groups, 128)
    dense = (chunks, rows, groups, 128)
    big = pltpu.VMEM(dense, F32)
    return pl.pallas_call(
        functools.partial(local_kernel, low_rank, states, places),
        grid=(chunks,),
        in_specs=[
            whole((rows, wide)),
            whole((rows, wide)),
            pl.BlockSpec(memory_space=pltpu.SMEM),
            columns(low_rank, width),
            columns(1, width),
            whole(decay.shape),
            columns(rows, width),
            columns(rows, width),
            columns(rows, width),
        ],
        out_specs=[
            *[pl.BlockSpec((1, rows, groups, 128), lambda i: (i, 0, 0, 0))] * 3,
            whole((rows, low_rank)),
        ]
        + [whole(message)] * (places - 1),
        out_shape=[
            *[sds(dense, F32)] * 3,
            sds((rows, low_rank), BF),
        ]
        + [sds(message, BF)] * (places - 1),
        scratch_shapes=[
            pltpu.VMEM((3, rows * groups, 128), F32),
            big,
            big,
            big,
            pltpu.VMEM(message, F32),
            pltpu.VMEM(message, F32),
        ],
        compiler_params=params(58),
        name="local_ends",
    )(*parts, coef, step_weight, step_bias, decay, conv_out, gate, grad)


def fold_rows(products, base, groups, target, first):
    total = products[pl.ds(base, 8, stride=groups), :]
    for row in range(1, groups):
        total = total + products[pl.ds(base + row, 8, stride=groups), :]
    target[pl.ds(pl.multiple_of(first, 8), 8), :] = total


def scan_kernel(places, states, opening, *refs):
    (coef, dt_ref, dx_ref, g_ref, decay_ref, skips_ref) = refs[:6]
    (conv_ref, gate_ref, grad_ref, weight_ref, skip_ref) = refs[6:11]
    messages, refs = refs[11 : 10 + places], refs[10 + places :]
    if not opening:
        before_ref, refs = refs[0], refs[4:]
    (pre_ref, gate_out, scan_out, small_ref, part_ref) = refs[:5]
    refs = refs[5:]
    (ys, dds, qs, decayed, coef_out, coef_in, rate, decay_acc, acc, ends, products, factors) = refs
    rows = conv_ref.shape[0]
    groups = decay_ref.shape[2]
    low_rank = weight_ref.shape[0]
    span = groups * 8

    place = lax.axis_index("ctx")
    for n in range(states):
        rate[n] = -LOG2E * jnp.exp(decay_ref[0, n])
    ends[place] = jnp.zeros(ends.shape[1:], F32)
    for mask, message in enumerate(messages, 1):
        ends[place ^ mask] = message[0].astype(F32)
    totals = [ends[q, states] + ends[q, states + 1] for q in range(places)]
    state, carry = [], []
    for n in range(states):
        before = jnp.zeros((groups, 128), F32)
        after = jnp.zeros((groups, 128), F32)
        for q in range(places - 1):
            reached = jnp.exp2(rate[n] * totals[q]) * before + ends[q, n]
            before = jnp.where(q < place, reached, before)
        for q in range(places - 1, 0, -1):
            reached = jnp.exp2(rate[n] * totals[q]) * after + ends[q, n]
            after = jnp.where(q > place, reached, after)
        state.append(before)
        carry.append(after)

    def forward(index, state):
        state = list(state)
        for sub in range(8):
            token = index * 8 + sub
            at = pl.ds(index * span + sub, groups, stride=8)
            scalar = token * (2 * states)
            size, drive, grad = dt_ref[0, token], dx_ref[0, token], g_ref[0, token]
            result = jnp.zeros((groups, 128), F32)
            for lead in range(0, states, 8):
                base = (sub * states + lead) * groups
                for n in range(lead, lead + 8):
                    factor = jnp.exp2(size * rate[n])
                    kept = factor * state[n]
                    factors[token, n] = factor
                    decayed[token, n] = kept
                    state[n] = kept + drive * coef[scalar + n]
                    result = result + state[n] * coef[scalar + (states + n)]
                    row = base + (n - lead) * groups
                    products[row : row + groups, :] = state[n] * grad
                fold_rows(products, base, groups, coef_out, token * states + lead)
            ys[at, :] = result
        return state

    lax.fori_loop(0, rows // 8, forward, state)

    def backward(hop, both):
        carry, gathered = list(both[0]), list(both[1])
        index = rows // 8 - 1 - hop
        for sub in range(7, -1, -1):
            token = index * 8 + sub
            at = pl.ds(index * span + sub, groups, stride=8)
            scalar = token * (2 * states)
            size, drive, grad = dt_ref[0, token], dx_ref[0, token], g_ref[0, token]
            slope = jnp.zeros((groups, 128), F32)
            inner = jnp.zeros((groups, 128), F32)
            for lead in range(0, states, 8):
                base = (sub * states + lead) * groups
                for n in range(lead, lead + 8):
                    adjoint = carry[n] + grad * coef[scalar + (states + n)]
                    carry[n] = factors[token, n] * adjoint
                    weighted = adjoint * decayed[token, n] * (size * rate[n])
                    slope = slope + weighted
                    gathered[n] = gathered[n] + weighted
                    inner = inner + adjoint * coef[scalar + n]
                    row = base + (n - lead) * groups
                    products[row : row + groups, :] = adjoint * drive
                fold_rows(products, base, groups, coef_in, token * states + lead)
            tiny = 1.0 - 0.5 * size * (1.0 - size * (1.0 / 3.0) * (1.0 - 0.25 * size))
            ratio = jnp.where(size < 0.03, tiny, (1.0 - jnp.exp(-size)) / jnp.maximum(size, 0.03))
            dds[at, :] = (LN2 * slope + drive * inner) * ratio
            qs[at, :] = size * inner + skips_ref[0] * grad
        return carry, gathered

    zeros = [jnp.zeros((groups, 128), F32)] * states
    _, gathered = lax.fori_loop(0, rows // 8, backward, (carry, zeros))
    for n in range(states):
        decay_acc[n * groups : n * groups + groups, :] = gathered[n] * LN2

    for group in range(groups):
        pre_ref[rows : rows + states, group * 128 : group * 128 + 128] = decay_acc[
            pl.ds(group, states, stride=groups), :
        ].astype(BF)
    skip = skip_ref[...]
    bias_sum = jnp.zeros((1, conv_ref.shape[1]), F32)
    skip_sum = jnp.zeros((1, conv_ref.shape[1]), F32)
    for start in range(0, rows, 16):
        here = slice(start, start + 16)

        def natural(read):
            return jnp.concatenate(
                [
                    jnp.concatenate(
                        [
                            read(((start // 8 + half) * groups + group) * 8)
                            for group in range(groups)
                        ],
                        axis=1,
                    )
                    for half in range(2)
                ],
                axis=0,
            )

        d_pre = natural(lambda first: dds[first : first + 8, :])
        out = natural(lambda first: ys[first : first + 8, :])
        conv = conv_ref[here, :].astype(F32)
        gate = gate_ref[here, :].astype(F32)
        grad = grad_ref[here, :].astype(F32)
        sig = sigmoid(gate)
        scan_grad = grad * gate * sig
        pre_ref[here, :] = d_pre.astype(BF)
        bias_sum = bias_sum + jnp.sum(d_pre, axis=0, keepdims=True)
        skip_sum = skip_sum + jnp.sum(scan_grad * conv, axis=0, keepdims=True)
        scan_out[here, :] = natural(lambda first: qs[first : first + 8, :]).astype(BF)
        gate_out[here, :] = (
            grad * (out + skip * conv) * (sig * (1.0 + gate * (1.0 - sig)))
        ).astype(BF)
    small_ref[...] = jnp.concatenate(
        [bias_sum, skip_sum, jnp.zeros((6, bias_sum.shape[1]), F32)], axis=0
    )

    pre_bf = pre_ref[:rows, :]
    lanes = lax.broadcasted_iota(jnp.int32, (2 * states, 128), 0)
    coefs = jnp.zeros((2 * states, rows), F32)
    for n in range(states):
        at = pl.ds(n, rows, stride=states)
        for kind, source in enumerate((coef_in, coef_out)):
            pick = jnp.where(lanes == kind * states + n, 1.0, 0.0).astype(BF)
            coefs = coefs + dot(pick, source[at, :].astype(BF), NT)
    wide = dot(weight_ref[...], pre_bf, NT)

    ranks, coef_rows, block = low_rank // places, 2 * states // places, acc.shape[0] // places

    acc[...] = jnp.zeros_like(acc) if opening else before_ref[...]
    for q in range(places):
        at = q * block
        acc[at : at + ranks, :] += wide[q * ranks : (q + 1) * ranks, :]
        acc[at + ranks : at + ranks + coef_rows, :] += coefs[
            q * coef_rows : (q + 1) * coef_rows, :
        ]
    part_ref[...] = acc[...].astype(part_ref.dtype)


def padded(wide):
    return (wide + 127) // 128 * 128


def scan_call(
    places, chunk, coef, dense, decay, skips, conv_out, gate, grad, step_weight, skip, messages,
    previous,
):
    rows, chans = conv_out.shape
    low_rank = step_weight.shape[0]
    chunks, states, groups, _ = decay.shape
    width = groups * 128
    wide = (low_rank + 2 * states) // places
    wide = (wide + 15) // 16 * 16 * places
    lead = lambda *shape: pl.BlockSpec((1,) + shape, lambda i: (chunk,) + (0,) * len(shape))
    here = lambda height: pl.BlockSpec((height, width), lambda i: (0, chunk))
    tall = pltpu.VMEM((rows * groups, 128), F32)
    first, last = chunk == 0, chunk == chunks - 1
    in_specs = [
        pl.BlockSpec(memory_space=pltpu.SMEM),
        lead(rows, groups, 128),
        lead(rows, groups, 128),
        lead(rows, groups, 128),
        lead(states, groups, 128),
        lead(groups, 128),
        here(rows),
        here(rows),
        here(rows),
        here(low_rank),
        here(1),
    ]
    in_specs += [lead(states + 2, groups, 128)] * (places - 1)
    aliases = {}
    if not first:
        in_specs += [whole((wide, rows))] + [pl.BlockSpec(memory_space=pl.ANY)] * 3
        aliases = {11 + places: 1, 12 + places: 2, 13 + places: 3}
    return pl.pallas_call(
        functools.partial(scan_kernel, places, states, first),
        grid=(1,),
        in_specs=in_specs,
        out_specs=[
            whole((rows + states, width)),
            here(rows),
            here(rows),
            here(8),
            whole((wide, rows)),
        ],
        out_shape=[
            sds((rows + states, width), BF),
            sds((rows, chans), BF),
            sds((rows, chans), BF),
            sds((8, chans), F32),
            sds((wide, rows), BF if last else F32),
        ],
        scratch_shapes=[
            tall,
            tall,
            tall,
            pltpu.VMEM((rows, states, groups, 128), F32),
            pltpu.VMEM((rows * states, 128), F32),
            pltpu.VMEM((rows * states, 128), F32),
            pltpu.VMEM((states, groups, 128), F32),
            pltpu.VMEM((states * groups, 128), F32),
            pltpu.VMEM((wide, rows), F32),
            pltpu.VMEM((places, states + 2, groups, 128), F32),
            pltpu.VMEM((8 * states * groups, 128), F32),
            pltpu.VMEM((rows, states, groups, 128), F32),
        ],
        input_output_aliases=aliases,
        compiler_params=params(58),
        name="scan_gradients",
    )(
        coef, *dense, decay, skips, conv_out, gate, grad, step_weight, skip, *messages, *previous
    )


def conv_grad_kernel(places, low_rank, back_a, back_b, proj_ref, scan_ref, small_in, input_ref, rim_ref, weight_ref, bias_ref,
                     out_ref, tail_ref, small_ref, ext, grad, back_t):
    taps = weight_ref.shape[0]
    rows = input_ref.shape[0]
    fill_extended(ext, rim_ref, input_ref, taps)
    wide = proj_ref.shape[0]
    block = back_a.shape[0] // places
    ranks, coef_rows = low_rank // places, (wide - low_rank) // places

    @pl.when(pl.program_id(0) == 0)
    def _():
        back = back_a[...].astype(F32) + back_b[...].astype(F32)
        order = [back[q * block : q * block + ranks, :] for q in range(places)]
        order += [back[q * block + ranks : q * block + ranks + coef_rows, :] for q in range(places)]
        order += [jnp.zeros((padded(wide) - wide, back.shape[1]), F32)]
        back_t[...] = jnp.transpose(jnp.concatenate(order, axis=0))[:, :wide].astype(BF)

    d_xc = dot(back_t[...], proj_ref[...])
    sums = [jnp.zeros((1, input_ref.shape[1]), F32) for _ in range(taps + 1)]
    for start in range(0, rows, 16):
        here = slice(start, start + 16)
        pre = conv_block(ext, weight_ref, bias_ref[...], taps, start, 16)
        sig = sigmoid(pre)
        value = (d_xc[here, :] + scan_ref[here, :].astype(F32)) * (sig * (1.0 + pre * (1.0 - sig)))
        grad[here, :] = value
        for tap in range(taps):
            first = 8 - (taps - 1) + tap + start
            sums[tap] = sums[tap] + jnp.sum(value * ext[first : first + 16, :], axis=0, keepdims=True)
        sums[taps] = sums[taps] + jnp.sum(value, axis=0, keepdims=True)
    grad[rows : rows + 8, :] = jnp.zeros((8, grad.shape[1]), F32)
    for start in range(0, rows, 16):
        total = jnp.zeros((16, grad.shape[1]), F32)
        for tap in range(taps):
            first = start + taps - 1 - tap
            total = total + weight_ref[tap : tap + 1, :] * grad[first : first + 16, :]
        out_ref[start : start + 16, :] = total.astype(BF)
    tail_ref[...] = total
    small_ref[...] = jnp.concatenate(
        sums + [small_in[0 : 7 - taps, :], grad[0:8, :]], axis=0
    ).astype(BF)


def conv_grad_call(places, low_rank, backs, proj_weight, scan_part, small, conv_input, rim, weight, bias):
    rows, chans = conv_input.shape
    taps = weight.shape[0]
    wide = proj_weight.shape[0]
    width = min(1024, chans)
    return pl.pallas_call(
        functools.partial(conv_grad_kernel, places, low_rank),
        grid=(chans // width,),
        in_specs=[
            whole(backs[0].shape),
            whole(backs[1].shape),
            columns(wide, width),
            columns(rows, width),
            columns(8, width),
            columns(rows, width),
            columns(taps - 1, width),
            columns(taps, width),
            columns(1, width),
        ],
        out_specs=[columns(rows, width), columns(16, width), columns(16, width)],
        out_shape=[sds((rows, chans), BF), sds((16, chans), F32), sds((16, chans), BF)],
        scratch_shapes=[
            pltpu.VMEM((rows + 8, width), F32),
            pltpu.VMEM((rows + 8, width), F32),
            pltpu.VMEM((rows, wide), BF),
        ],
        compiler_params=params(18),
        name="conv_gradients",
    )(*backs, proj_weight, scan_part, small, conv_input, rim, weight, bias)


def cut_kernel(places, back_a, back_b, *refs):
    cuts, (back,) = refs[:places], refs[places:]
    place = lax.axis_index("ctx")
    height = back.shape[0] // places
    back[...] = back_a[...].astype(F32) + back_b[...].astype(F32)
    for mask in range(places):
        cuts[mask][...] = back[pl.ds((place ^ mask) * height, height), :].astype(BF)


def cut_call(places, backs):
    wide, rows = backs[0].shape
    return pl.pallas_call(
        functools.partial(cut_kernel, places),
        out_shape=[sds((wide // places, rows), BF)] * places,
        scratch_shapes=[pltpu.VMEM((wide, rows), F32)],
        compiler_params=params(8),
        name="cut_rows",
    )(*backs)


def step_kernel(ranks, near, *refs):
    lows, steps, (mine_ref, theirs_ref) = refs[:near], refs[near : 2 * near], refs[2 * near :]
    place = lax.axis_index("ctx")
    rows = lows[0].shape[1]
    pair = pl.ds(pl.multiple_of(lax.div(place, 2) * (2 * ranks), 16), 2 * ranks)
    odd = lax.rem(place, 2) == 1
    total = jnp.zeros((2 * ranks, mine_ref.shape[1]), F32)
    decay = jnp.zeros((mine_ref.shape[0] - ranks, mine_ref.shape[1]), F32)
    for low, step in zip(lows, steps):
        total = total + dot(low[pair, :], step[:rows, :])
        decay = decay + step[rows:, :].astype(F32)
    mine_ref[:ranks, :] = jnp.where(odd, total[ranks:, :], total[:ranks, :])
    theirs_ref[:ranks, :] = jnp.where(odd, total[:ranks, :], total[ranks:, :]).astype(BF)
    mine_ref[ranks:, :] = decay
    theirs_ref[ranks:, :] = decay.astype(BF)


def step_call(ranks, lows, steps):
    rows = lows[0].shape[1]
    tall, chans = steps[0].shape
    width = min(512, chans)
    height = ranks + tall - rows
    return pl.pallas_call(
        functools.partial(step_kernel, ranks, len(lows)),
        grid=(chans // width,),
        in_specs=[whole(lows[0].shape)] * len(lows) + [columns(tall, width)] * len(steps),
        out_specs=[columns(height, width)] * 2,
        out_shape=[sds((height, chans), F32), sds((height, chans), BF)],
        compiler_params=params(16),
        name="step_products",
    )(*lows, *steps)


def rows_kernel(ranks, places, *refs):
    cuts, blocks, (out_ref, coef_ref) = refs[:places], refs[places:-2], refs[-2:]
    total = jnp.zeros((cuts[0].shape[0], out_ref.shape[1]), F32)
    for cut, block in zip(cuts, blocks):
        total = total + dot(cut[...], block[...])
    out_ref[...] = total[:ranks, :]
    coef_ref[...] = total[ranks : ranks + coef_ref.shape[0], :]


def rows_call(ranks, coef_rows, cuts, blocks):
    rows, chans = blocks[0].shape
    width = min(1024, chans)
    return pl.pallas_call(
        functools.partial(rows_kernel, ranks, len(cuts)),
        grid=(chans // width,),
        in_specs=[whole(cuts[0].shape)] * len(cuts) + [columns(rows, width)] * len(blocks),
        out_specs=[columns(ranks, width), columns(coef_rows, width)],
        out_shape=[sds((ranks, chans), F32), sds((coef_rows, chans), F32)],
        compiler_params=params(16),
        name="row_gradients",
    )(*cuts, *blocks)


def total_kernel(*refs):
    products, (step_ref, decay_ref) = refs[:-2], refs[-2:]
    ranks = step_ref.shape[0]
    for chunk in range(len(products) // 2):

        @pl.when(pl.program_id(0) == chunk)
        def _():
            mine, theirs = products[2 * chunk : 2 * chunk + 2]
            step_ref[...] = mine[:ranks, :] + theirs[:ranks, :].astype(F32)
            decay_ref[...] = mine[ranks:, :] + theirs[ranks:, :].astype(F32)


def total_call(ranks, products):
    height, width = products[0].shape
    chunks = len(products) // 2
    heights = (ranks, height - ranks)
    return pl.pallas_call(
        total_kernel,
        grid=(chunks,),
        in_specs=[whole((height, width))] * len(products),
        out_specs=[columns(tall, width) for tall in heights],
        out_shape=[sds((tall, chunks * width), F32) for tall in heights],
        compiler_params=params(12),
        name="step_gradients",
    )(*products)


def last_kernel(places, taps, *refs):
    (_, tail_ref, weight_ref) = refs[:3]
    late, refs = refs[3 : 3 + places], refs[3 + places :]
    (out_ref, conv_w, conv_b, step_b, skip, fix) = refs
    fix[...] = tail_ref[...]
    inside = lax.axis_index("ctx") < places - 1
    following = jnp.where(inside, late[places - 1][8:16, :].astype(F32), 0.0)
    for row in range(taps - 1):
        extra = jnp.zeros((1, fix.shape[1]), F32)
        for tap in range(row + 1):
            extra = extra + weight_ref[tap : tap + 1, :] * following[row - tap : row - tap + 1, :]
        at = 16 - (taps - 1) + row
        fix[at : at + 1, :] += extra
    out_ref[...] = fix[...].astype(BF)
    total = late[0][...].astype(F32)
    for part in late[1:]:
        total = total + part[...].astype(F32)
    conv_w[...] = total[:taps, :]
    conv_b[...] = total[taps : taps + 1, :]
    step_b[...] = total[taps + 1 : taps + 2, :]
    skip[...] = total[taps + 2 : taps + 3, :]


def last_call(main, tail, weight, late):
    rows, chans = main.shape
    taps = weight.shape[0]
    places = len(late)
    return pl.pallas_call(
        functools.partial(last_kernel, places, taps),
        grid=(1,),
        in_specs=[pl.BlockSpec(memory_space=pl.ANY), columns(16, chans), columns(taps, chans)]
        + [columns(16, chans)] * places,
        out_specs=[
            pl.BlockSpec((16, chans), lambda i: (rows // 16 - 1, i)),
            columns(taps, chans),
        ]
        + [columns(1, chans)] * 3,
        out_shape=[sds((rows, chans), BF), sds((taps, chans), F32)] + [sds((1, chans), F32)] * 3,
        scratch_shapes=[pltpu.VMEM((16, chans), F32)],
        input_output_aliases={0: 0},
        compiler_params=params(8),
        name="last_rows",
    )(main, tail, weight, *late)


def exchange(block, axis):
    return lax.all_to_all(block, axis, split_axis=0, concat_axis=0, tiled=True)


def swap(block, axis, mask):
    return lax.ppermute(block, axis, [(i, i ^ mask) for i in range(lax.axis_size(axis))])


tie = lax.optimization_barrier


def spread(block):
    return [block] + [swap(block, "ctx", mask) for mask in range(1, min(lax.axis_size("ctx"), 3))]


def spread_on(blocks):
    places = lax.axis_size("ctx")
    if places == 4:
        return blocks + [swap(blocks[2], "ctx", 1)]
    return blocks + [swap(blocks[0], "ctx", mask) for mask in range(3, places)]


def gather_near(block):
    return [block] + [swap(block, "ctx", mask) for mask in range(2, lax.axis_size("ctx"), 2)]


def chan_sum(part):
    mask, peers = 1, lax.axis_size("chan")
    while True:
        other = swap(part, "chan", mask)
        mask *= 2
        if mask == peers:
            return part, other
        part = (part.astype(F32) + other.astype(F32)).astype(BF)


def body(
    conv_input,
    gate_input,
    out_grad,
    conv_weight,
    conv_bias,
    proj_weight,
    step_weight,
    step_bias,
    decay_log,
    skip_gain,
):
    rows, chans = conv_input.shape
    taps = conv_weight.shape[0]
    low_rank = step_weight.shape[0]
    states = decay_log.shape[0]
    places = lax.axis_size("ctx")
    groups = group_rows(chans)
    decay = decay_log.reshape(states, -1, groups, 128).transpose(1, 0, 2, 3)
    skips = skip_gain.reshape(-1, groups, 128)
    conv_bias = conv_bias[None, :]
    step_bias = step_bias[None, :]
    skip_gain = skip_gain[None, :]

    chunks = decay.shape[0]
    rim = shift(conv_input[rows - (taps - 1) :], "ctx", 1)
    conv_out, part = conv_call(conv_input, rim, conv_weight, conv_bias, proj_weight)
    blocks = spread(conv_out)
    parts = chan_sum(part)
    coef = (parts[0][:, low_rank:].astype(F32) + parts[1][:, low_rank:].astype(F32)).astype(BF)
    coef = coef.astype(F32).reshape(-1)
    dt, dx, g, low, *messages = local_call(
        parts, coef, step_weight, step_bias, decay, conv_out, gate_input, out_grad, states, places
    )
    messages = [swap(message, "ctx", mask) for mask, message in enumerate(messages, 1)]
    messages, blocks, low = tie((messages, blocks, low))
    blocks = spread_on(blocks)
    low = jnp.transpose(low)
    previous, steps = [], []
    for chunk in range(chunks):
        message, grad_gate, scan_part, small, part = scan_call(
            places, chunk, coef, (dt, dx, g), decay, skips, conv_out, gate_input, out_grad,
            step_weight, skip_gain, messages, previous,
        )
        previous = [part, grad_gate, scan_part, small]
        if chunk == 0:
            previous, blocks = tie((previous, blocks))
        else:
            previous, steps[-1], low = tie((previous, steps[-1], low))
        steps.append(gather_near(message))
    part, grad_gate, scan_part, small = previous
    ranks = low_rank // places
    products = []
    backs = chan_sum(part)
    lows = gather_near(low)
    backs, lows = tie((backs, lows))
    for step in steps[:-1]:
        mine, theirs = step_call(ranks, lows, step)
        products += [mine, swap(theirs, "ctx", 1)]
    cuts = cut_call(places, backs)
    cuts = [cuts[0]] + [swap(cut, "ctx", mask) for mask, cut in enumerate(cuts[1:], 1)]
    main, tail, sums = conv_grad_call(
        places, low_rank, backs, proj_weight, scan_part, small, conv_input, rim, conv_weight,
        conv_bias,
    )
    sums, cuts, products, steps[-1], lows = tie((sums, cuts, products, steps[-1], lows))
    mine, theirs = step_call(ranks, lows, steps[-1])
    products += [mine, swap(theirs, "ctx", 1)]
    late = [sums] + [rotate(sums, "ctx", hop) for hop in range(1, places)]
    grad_proj, grad_coef = rows_call(ranks, 2 * states // places, cuts, blocks)
    products, grad_proj = tie((products, grad_proj))
    grad_step, decay_grad = total_call(ranks, products)
    late, grad_step = tie((late, grad_step))
    grad_input, conv_w, conv_b, step_b, skip = last_call(main, tail, conv_weight, late)
    return (
        grad_input,
        grad_gate,
        grad_proj,
        grad_coef,
        grad_step,
        conv_w,
        conv_b[0],
        step_b[0],
        decay_grad,
        skip[0],
    )


def solution(mesh):
    tokens, columns_, chan = P("ctx", "chan"), P(None, "chan"), P("chan")
    in_specs = (
        tokens, tokens, tokens, columns_, chan, columns_, columns_, chan, columns_, chan,
    )
    out_specs = (
        tokens, tokens, tokens, tokens, tokens, columns_, chan, chan, columns_, chan,
    )
    return jax.shard_map(body, mesh=mesh, in_specs=in_specs, out_specs=out_specs, check_vma=False)
```

```python
import functools

import jax
import jax.numpy as jnp
from jax import lax
from jax.experimental import pallas as pl
from jax.experimental.pallas import tpu as pltpu
from jax.sharding import PartitionSpec as P

BF = jnp.bfloat16
F32 = jnp.float32
LOG2E = 1.4426950408889634
LN2 = 0.6931471805599453
MIB = 1024 * 1024
NT = (((1,), (1,)), ((), ()))
TN = (((0,), (0,)), ((), ()))


def group_rows(chans):
    for rows in (8, 4, 2, 1):
        if chans % (rows * 128) == 0:
            return rows
    return 1


def dot(a, b, dims=(((1,), (0,)), ((), ()))):
    return lax.dot_general(a, b, dims, preferred_element_type=F32)


def params(mebibytes):
    return pltpu.CompilerParams(vmem_limit_bytes=mebibytes * MIB)


def sds(shape, dtype):
    return jax.ShapeDtypeStruct(shape, dtype)


def whole(shape):
    return pl.BlockSpec(shape, lambda i: (0,) * len(shape))


def columns(rows, width):
    return pl.BlockSpec((rows, width), lambda i: (0, i))


def sigmoid(v):
    return 0.5 + 0.5 * jnp.tanh(0.5 * v)


def rotate(block, axis, distance):
    count = lax.axis_size(axis)
    return lax.ppermute(block, axis, [(i, (i + distance) % count) for i in range(count)])


def shift(block, axis, distance):
    count = lax.axis_size(axis)
    route = [(i, i + distance) for i in range(count) if 0 <= i + distance < count]
    return lax.ppermute(block, axis, route)


def fill_extended(ext, rim_ref, input_ref, taps):
    rows = input_ref.shape[0]
    ext[8 - (taps - 1) : 8, :] = rim_ref[...].astype(F32)
    ext[8 : 8 + rows, :] = input_ref[...].astype(F32)


def conv_block(ext, weight, bias, taps, start, rows):
    total = bias + jnp.zeros((rows, ext.shape[1]), F32)
    for tap in range(taps):
        first = 8 - (taps - 1) + tap + start
        total = total + weight[tap : tap + 1, :] * ext[first : first + rows, :]
    return total


def conv_kernel(input_ref, rim_ref, weight_ref, bias_ref, proj_ref, out_ref, part_ref, ext, acc):
    step = pl.program_id(0)
    taps = weight_ref.shape[0]
    rows = input_ref.shape[0]
    fill_extended(ext, rim_ref, input_ref, taps)
    for start in range(0, rows, 16):
        pre = conv_block(ext, weight_ref, bias_ref[...], taps, start, 16)
        out_ref[start : start + 16, :] = (pre * sigmoid(pre)).astype(BF)
    part = dot(out_ref[...], proj_ref[...], NT)

    @pl.when(step == 0)
    def _():
        acc[...] = part

    @pl.when(step > 0)
    def _():
        acc[...] += part

    @pl.when(step == pl.num_programs(0) - 1)
    def _():
        part_ref[...] = acc[...].astype(BF)


def conv_call(conv_input, rim, weight, bias, proj_weight):
    rows, chans = conv_input.shape
    taps = weight.shape[0]
    wide = proj_weight.shape[0]
    width = min(1024, chans)
    return pl.pallas_call(
        conv_kernel,
        grid=(chans // width,),
        in_specs=[
            columns(rows, width),
            columns(taps - 1, width),
            columns(taps, width),
            columns(1, width),
            columns(wide, width),
        ],
        out_specs=[columns(rows, width), whole((rows, wide))],
        out_shape=[sds((rows, chans), BF), sds((rows, wide), BF)],
        scratch_shapes=[pltpu.VMEM((rows + 8, width), F32), pltpu.VMEM((rows, wide), F32)],
        compiler_params=params(58),
        name="conv_project",
    )(conv_input, rim, weight, bias, proj_weight)


def tile_rows(value, target, lead, groups):
    rows = value.shape[0]
    for block in range(rows // 8):
        for group in range(groups):
            first = (block * groups + group) * 8
            target[lead, first : first + 8, :] = value[
                block * 8 : block * 8 + 8, group * 128 : group * 128 + 128
            ]


def local_kernel(low_rank, states, places, *refs):
    parts, refs = refs[:2], refs[2:]
    (coef, weight_ref, bias_ref, decay_ref, conv_ref, gate_ref, grad_ref) = refs[:7]
    (dt_ref, dx_ref, g_ref, low) = refs[7:11]
    messages, refs = refs[11 : 10 + places], refs[10 + places :]
    (tiles, dts, dxs, gs, fwd, bwd) = refs
    step = pl.program_id(0)
    chunks = dts.shape[0]
    rows = conv_ref.shape[0]
    groups = decay_ref.shape[2]

    @pl.when(step == 0)
    def _():
        total = (parts[0][...].astype(F32) + parts[1][...].astype(F32)).astype(BF)
        low[...] = total[:, :low_rank]

    pre = dot(low[...], weight_ref[...]) + bias_ref[...]
    for start in range(0, rows, 16):
        here = slice(start, start + 16)
        p = pre[here, :]
        size = jnp.maximum(p, 0.0) + jnp.log1p(jnp.exp(-jnp.abs(p)))
        gate = gate_ref[here, :].astype(F32)
        grad = grad_ref[here, :].astype(F32) * gate * sigmoid(gate)
        drive = size * conv_ref[here, :].astype(F32)
        for half in range(2):
            for group in range(groups):
                first = ((start // 8 + half) * groups + group) * 8
                lanes = slice(group * 128, group * 128 + 128)
                subs = slice(half * 8, half * 8 + 8)
                tiles[0, first : first + 8, :] = size[subs, lanes]
                tiles[1, first : first + 8, :] = drive[subs, lanes]
                tiles[2, first : first + 8, :] = grad[subs, lanes]

    def relay(index, _):
        for sub in range(8):
            token = index * 8 + sub
            at = pl.ds(index * groups * 8 + sub, groups, stride=8)
            for kind, (held, out) in enumerate(((dts, dt_ref), (dxs, dx_ref), (gs, g_ref))):
                row = tiles[kind, at, :]
                held[step, token] = row
                out[0, token] = row
        return 0

    lax.fori_loop(0, rows // 8, relay, 0)

    @pl.when(step == chunks - 1)
    def _():
        batch = 4
        zero = jnp.zeros((groups, 128), F32)
        for lead in range(0, states, batch):
            pairs = [(n, v) for n in range(lead, lead + batch) for v in range(chunks)]
            rates = [-LOG2E * jnp.exp(decay_ref[v, n]) for n, v in pairs]

            def block(index, carry):
                state, run, head, total = (list(part) for part in carry)
                for sub in range(8):
                    token = index * 8 + sub
                    base = token * (2 * states)
                    size = [dts[v, token] for v in range(chunks)]
                    drive = [dxs[v, token] for v in range(chunks)]
                    grad = [gs[v, token] for v in range(chunks)]
                    if lead == 0:
                        total = [a + b for a, b in zip(total, size)]
                    for k, (n, v) in enumerate(pairs):
                        factor = jnp.exp2(size[v] * rates[k])
                        state[k] = factor * state[k] + drive[v] * coef[base + n]
                        run[k] = run[k] * factor
                        head[k] = head[k] + run[k] * (grad[v] * coef[base + (states + n)])
                return state, run, head, total

            many = [zero] * len(pairs)
            state, run, head, total = lax.fori_loop(
                0,
                rows // 8,
                block,
                (many, [zero + 1.0] * len(pairs), many, [zero] * chunks),
            )
            for k, (n, v) in enumerate(pairs):
                fwd[v, n] = state[k]
                bwd[v, n] = head[k]
            if lead == 0:
                for v in range(chunks):
                    coarse = total[v].astype(BF).astype(F32)
                    for target in (fwd, bwd):
                        target[v, states] = coarse
                        target[v, states + 1] = total[v] - coarse
        place = lax.axis_index("ctx")
        for mask, message in enumerate(messages, 1):
            message[...] = jnp.where((place ^ mask) > place, fwd[...], bwd[...]).astype(BF)


def local_call(parts, coef, step_weight, step_bias, decay, conv_out, gate, grad, states, places):
    rows, chans = conv_out.shape
    wide = parts[0].shape[1]
    low_rank = step_weight.shape[0]
    chunks, _, groups, _ = decay.shape
    width = groups * 128
    message = (chunks, states + 2, groups, 128)
    dense = (chunks, rows, groups, 128)
    big = pltpu.VMEM(dense, F32)
    return pl.pallas_call(
        functools.partial(local_kernel, low_rank, states, places),
        grid=(chunks,),
        in_specs=[
            whole((rows, wide)),
            whole((rows, wide)),
            pl.BlockSpec(memory_space=pltpu.SMEM),
            columns(low_rank, width),
            columns(1, width),
            whole(decay.shape),
            columns(rows, width),
            columns(rows, width),
            columns(rows, width),
        ],
        out_specs=[
            *[pl.BlockSpec((1, rows, groups, 128), lambda i: (i, 0, 0, 0))] * 3,
            whole((rows, low_rank)),
        ]
        + [whole(message)] * (places - 1),
        out_shape=[
            *[sds(dense, F32)] * 3,
            sds((rows, low_rank), BF),
        ]
        + [sds(message, BF)] * (places - 1),
        scratch_shapes=[
            pltpu.VMEM((3, rows * groups, 128), F32),
            big,
            big,
            big,
            pltpu.VMEM(message, F32),
            pltpu.VMEM(message, F32),
        ],
        compiler_params=params(58),
        name="local_ends",
    )(*parts, coef, step_weight, step_bias, decay, conv_out, gate, grad)


def fold_rows(products, base, groups, target, first):
    total = products[pl.ds(base, 8, stride=groups), :]
    for row in range(1, groups):
        total = total + products[pl.ds(base + row, 8, stride=groups), :]
    target[pl.ds(pl.multiple_of(first, 8), 8), :] = total


def scan_kernel(places, states, opening, *refs):
    (coef, dt_ref, dx_ref, g_ref, decay_ref, skips_ref) = refs[:6]
    (conv_ref, gate_ref, grad_ref, weight_ref, skip_ref) = refs[6:11]
    messages, refs = refs[11 : 10 + places], refs[10 + places :]
    if not opening:
        before_ref, refs = refs[0], refs[4:]
    (pre_ref, gate_out, scan_out, small_ref, part_ref) = refs[:5]
    refs = refs[5:]
    (ys, dds, qs, decayed, coef_out, coef_in, rate, decay_acc, acc, ends, products, factors) = refs
    rows = conv_ref.shape[0]
    groups = decay_ref.shape[2]
    low_rank = weight_ref.shape[0]
    span = groups * 8

    place = lax.axis_index("ctx")
    for n in range(states):
        rate[n] = -LOG2E * jnp.exp(decay_ref[0, n])
    ends[place] = jnp.zeros(ends.shape[1:], F32)
    for mask, message in enumerate(messages, 1):
        ends[place ^ mask] = message[0].astype(F32)
    totals = [ends[q, states] + ends[q, states + 1] for q in range(places)]
    state, carry = [], []
    for n in range(states):
        before = jnp.zeros((groups, 128), F32)
        after = jnp.zeros((groups, 128), F32)
        for q in range(places - 1):
            reached = jnp.exp2(rate[n] * totals[q]) * before + ends[q, n]
            before = jnp.where(q < place, reached, before)
        for q in range(places - 1, 0, -1):
            reached = jnp.exp2(rate[n] * totals[q]) * after + ends[q, n]
            after = jnp.where(q > place, reached, after)
        state.append(before)
        carry.append(after)

    def forward(index, state):
        state = list(state)
        for sub in range(8):
            token = index * 8 + sub
            at = pl.ds(index * span + sub, groups, stride=8)
            scalar = token * (2 * states)
            size, drive, grad = dt_ref[0, token], dx_ref[0, token], g_ref[0, token]
            result = jnp.zeros((groups, 128), F32)
            for lead in range(0, states, 8):
                base = (sub * states + lead) * groups
                for n in range(lead, lead + 8):
                    factor = jnp.exp2(size * rate[n])
                    kept = factor * state[n]
                    factors[token, n] = factor
                    decayed[token, n] = kept
                    state[n] = kept + drive * coef[scalar + n]
                    result = result + state[n] * coef[scalar + (states + n)]
                    row = base + (n - lead) * groups
                    products[row : row + groups, :] = state[n] * grad
                fold_rows(products, base, groups, coef_out, token * states + lead)
            ys[at, :] = result
        return state

    lax.fori_loop(0, rows // 8, forward, state)

    def backward(hop, both):
        carry, gathered = list(both[0]), list(both[1])
        index = rows // 8 - 1 - hop
        for sub in range(7, -1, -1):
            token = index * 8 + sub
            at = pl.ds(index * span + sub, groups, stride=8)
            scalar = token * (2 * states)
            size, drive, grad = dt_ref[0, token], dx_ref[0, token], g_ref[0, token]
            slope = jnp.zeros((groups, 128), F32)
            inner = jnp.zeros((groups, 128), F32)
            for lead in range(0, states, 8):
                base = (sub * states + lead) * groups
                for n in range(lead, lead + 8):
                    adjoint = carry[n] + grad * coef[scalar + (states + n)]
                    carry[n] = factors[token, n] * adjoint
                    weighted = adjoint * decayed[token, n] * (size * rate[n])
                    slope = slope + weighted
                    gathered[n] = gathered[n] + weighted
                    inner = inner + adjoint * coef[scalar + n]
                    row = base + (n - lead) * groups
                    products[row : row + groups, :] = adjoint * drive
                fold_rows(products, base, groups, coef_in, token * states + lead)
            tiny = 1.0 - 0.5 * size * (1.0 - size * (1.0 / 3.0) * (1.0 - 0.25 * size))
            ratio = jnp.where(size < 0.03, tiny, (1.0 - jnp.exp(-size)) / jnp.maximum(size, 0.03))
            dds[at, :] = (LN2 * slope + drive * inner) * ratio
            qs[at, :] = size * inner + skips_ref[0] * grad
        return carry, gathered

    zeros = [jnp.zeros((groups, 128), F32)] * states
    _, gathered = lax.fori_loop(0, rows // 8, backward, (carry, zeros))
    for n in range(states):
        decay_acc[n * groups : n * groups + groups, :] = gathered[n] * LN2

    for group in range(groups):
        pre_ref[rows : rows + states, group * 128 : group * 128 + 128] = decay_acc[
            pl.ds(group, states, stride=groups), :
        ].astype(BF)
    skip = skip_ref[...]
    bias_sum = jnp.zeros((1, conv_ref.shape[1]), F32)
    skip_sum = jnp.zeros((1, conv_ref.shape[1]), F32)
    for start in range(0, rows, 16):
        here = slice(start, start + 16)

        def natural(read):
            return jnp.concatenate(
                [
                    jnp.concatenate(
                        [
                            read(((start // 8 + half) * groups + group) * 8)
                            for group in range(groups)
                        ],
                        axis=1,
                    )
                    for half in range(2)
                ],
                axis=0,
            )

        d_pre = natural(lambda first: dds[first : first + 8, :])
        out = natural(lambda first: ys[first : first + 8, :])
        conv = conv_ref[here, :].astype(F32)
        gate = gate_ref[here, :].astype(F32)
        grad = grad_ref[here, :].astype(F32)
        sig = sigmoid(gate)
        scan_grad = grad * gate * sig
        pre_ref[here, :] = d_pre.astype(BF)
        bias_sum = bias_sum + jnp.sum(d_pre, axis=0, keepdims=True)
        skip_sum = skip_sum + jnp.sum(scan_grad * conv, axis=0, keepdims=True)
        scan_out[here, :] = natural(lambda first: qs[first : first + 8, :]).astype(BF)
        gate_out[here, :] = (
            grad * (out + skip * conv) * (sig * (1.0 + gate * (1.0 - sig)))
        ).astype(BF)
    small_ref[...] = jnp.concatenate(
        [bias_sum, skip_sum, jnp.zeros((6, bias_sum.shape[1]), F32)], axis=0
    )

    pre_bf = pre_ref[:rows, :]
    lanes = lax.broadcasted_iota(jnp.int32, (2 * states, 128), 0)
    coefs = jnp.zeros((2 * states, rows), F32)
    for n in range(states):
        at = pl.ds(n, rows, stride=states)
        for kind, source in enumerate((coef_in, coef_out)):
            pick = jnp.where(lanes == kind * states + n, 1.0, 0.0).astype(BF)
            coefs = coefs + dot(pick, source[at, :].astype(BF), NT)
    wide = dot(weight_ref[...], pre_bf, NT)

    ranks, coef_rows, block = low_rank // places, 2 * states // places, acc.shape[0] // places

    acc[...] = jnp.zeros_like(acc) if opening else before_ref[...]
    for q in range(places):
        at = q * block
        acc[at : at + ranks, :] += wide[q * ranks : (q + 1) * ranks, :]
        acc[at + ranks : at + ranks + coef_rows, :] += coefs[
            q * coef_rows : (q + 1) * coef_rows, :
        ]
    part_ref[...] = acc[...].astype(part_ref.dtype)


def padded(wide):
    return (wide + 127) // 128 * 128


def scan_call(
    places, chunk, coef, dense, decay, skips, conv_out, gate, grad, step_weight, skip, messages,
    previous,
):
    rows, chans = conv_out.shape
    low_rank = step_weight.shape[0]
    chunks, states, groups, _ = decay.shape
    width = groups * 128
    wide = (low_rank + 2 * states) // places
    wide = (wide + 15) // 16 * 16 * places
    lead = lambda *shape: pl.BlockSpec((1,) + shape, lambda i: (chunk,) + (0,) * len(shape))
    here = lambda height: pl.BlockSpec((height, width), lambda i: (0, chunk))
    tall = pltpu.VMEM((rows * groups, 128), F32)
    first, last = chunk == 0, chunk == chunks - 1
    in_specs = [
        pl.BlockSpec(memory_space=pltpu.SMEM),
        lead(rows, groups, 128),
        lead(rows, groups, 128),
        lead(rows, groups, 128),
        lead(states, groups, 128),
        lead(groups, 128),
        here(rows),
        here(rows),
        here(rows),
        here(low_rank),
        here(1),
    ]
    in_specs += [lead(states + 2, groups, 128)] * (places - 1)
    aliases = {}
    if not first:
        in_specs += [whole((wide, rows))] + [pl.BlockSpec(memory_space=pl.ANY)] * 3
        aliases = {11 + places: 1, 12 + places: 2, 13 + places: 3}
    return pl.pallas_call(
        functools.partial(scan_kernel, places, states, first),
        grid=(1,),
        in_specs=in_specs,
        out_specs=[
            whole((rows + states, width)),
            here(rows),
            here(rows),
            here(8),
            whole((wide, rows)),
        ],
        out_shape=[
            sds((rows + states, width), BF),
            sds((rows, chans), BF),
            sds((rows, chans), BF),
            sds((8, chans), F32),
            sds((wide, rows), BF if last else F32),
        ],
        scratch_shapes=[
            tall,
            tall,
            tall,
            pltpu.VMEM((rows, states, groups, 128), F32),
            pltpu.VMEM((rows * states, 128), F32),
            pltpu.VMEM((rows * states, 128), F32),
            pltpu.VMEM((states, groups, 128), F32),
            pltpu.VMEM((states * groups, 128), F32),
            pltpu.VMEM((wide, rows), F32),
            pltpu.VMEM((places, states + 2, groups, 128), F32),
            pltpu.VMEM((8 * states * groups, 128), F32),
            pltpu.VMEM((rows, states, groups, 128), F32),
        ],
        input_output_aliases=aliases,
        compiler_params=params(58),
        name="scan_gradients",
    )(
        coef, *dense, decay, skips, conv_out, gate, grad, step_weight, skip, *messages, *previous
    )


def conv_grad_kernel(places, low_rank, back_a, back_b, proj_ref, scan_ref, small_in, input_ref, rim_ref, weight_ref, bias_ref,
                     out_ref, tail_ref, small_ref, ext, grad, back_t):
    taps = weight_ref.shape[0]
    rows = input_ref.shape[0]
    fill_extended(ext, rim_ref, input_ref, taps)
    wide = proj_ref.shape[0]
    block = back_a.shape[0] // places
    ranks, coef_rows = low_rank // places, (wide - low_rank) // places

    @pl.when(pl.program_id(0) == 0)
    def _():
        back = back_a[...].astype(F32) + back_b[...].astype(F32)
        order = [back[q * block : q * block + ranks, :] for q in range(places)]
        order += [back[q * block + ranks : q * block + ranks + coef_rows, :] for q in range(places)]
        order += [jnp.zeros((padded(wide) - wide, back.shape[1]), F32)]
        back_t[...] = jnp.transpose(jnp.concatenate(order, axis=0))[:, :wide].astype(BF)

    d_xc = dot(back_t[...], proj_ref[...])
    sums = [jnp.zeros((1, input_ref.shape[1]), F32) for _ in range(taps + 1)]
    for start in range(0, rows, 16):
        here = slice(start, start + 16)
        pre = conv_block(ext, weight_ref, bias_ref[...], taps, start, 16)
        sig = sigmoid(pre)
        value = (d_xc[here, :] + scan_ref[here, :].astype(F32)) * (sig * (1.0 + pre * (1.0 - sig)))
        grad[here, :] = value
        for tap in range(taps):
            first = 8 - (taps - 1) + tap + start
            sums[tap] = sums[tap] + jnp.sum(value * ext[first : first + 16, :], axis=0, keepdims=True)
        sums[taps] = sums[taps] + jnp.sum(value, axis=0, keepdims=True)
    grad[rows : rows + 8, :] = jnp.zeros((8, grad.shape[1]), F32)
    for start in range(0, rows, 16):
        total = jnp.zeros((16, grad.shape[1]), F32)
        for tap in range(taps):
            first = start + taps - 1 - tap
            total = total + weight_ref[tap : tap + 1, :] * grad[first : first + 16, :]
        out_ref[start : start + 16, :] = total.astype(BF)
    tail_ref[...] = total
    small_ref[...] = jnp.concatenate(
        sums + [small_in[0 : 7 - taps, :], grad[0:8, :]], axis=0
    ).astype(BF)


def conv_grad_call(places, low_rank, backs, proj_weight, scan_part, small, conv_input, rim, weight, bias):
    rows, chans = conv_input.shape
    taps = weight.shape[0]
    wide = proj_weight.shape[0]
    width = min(1024, chans)
    return pl.pallas_call(
        functools.partial(conv_grad_kernel, places, low_rank),
        grid=(chans // width,),
        in_specs=[
            whole(backs[0].shape),
            whole(backs[1].shape),
            columns(wide, width),
            columns(rows, width),
            columns(8, width),
            columns(rows, width),
            columns(taps - 1, width),
            columns(taps, width),
            columns(1, width),
        ],
        out_specs=[columns(rows, width), columns(16, width), columns(16, width)],
        out_shape=[sds((rows, chans), BF), sds((16, chans), F32), sds((16, chans), BF)],
        scratch_shapes=[
            pltpu.VMEM((rows + 8, width), F32),
            pltpu.VMEM((rows + 8, width), F32),
            pltpu.VMEM((rows, wide), BF),
        ],
        compiler_params=params(18),
        name="conv_gradients",
    )(*backs, proj_weight, scan_part, small, conv_input, rim, weight, bias)


def cut_kernel(places, back_a, back_b, *refs):
    cuts, (back,) = refs[:places], refs[places:]
    place = lax.axis_index("ctx")
    height = back.shape[0] // places
    back[...] = back_a[...].astype(F32) + back_b[...].astype(F32)
    for mask in range(places):
        cuts[mask][...] = back[pl.ds((place ^ mask) * height, height), :].astype(BF)


def cut_call(places, backs):
    wide, rows = backs[0].shape
    return pl.pallas_call(
        functools.partial(cut_kernel, places),
        out_shape=[sds((wide // places, rows), BF)] * places,
        scratch_shapes=[pltpu.VMEM((wide, rows), F32)],
        compiler_params=params(8),
        name="cut_rows",
    )(*backs)


def step_kernel(ranks, near, *refs):
    lows, steps, (mine_ref, theirs_ref) = refs[:near], refs[near : 2 * near], refs[2 * near :]
    place = lax.axis_index("ctx")
    rows = lows[0].shape[1]
    odd = lax.rem(place, 2) == 1
    total = jnp.zeros((2 * ranks, mine_ref.shape[1]), F32)
    decay = jnp.zeros((mine_ref.shape[0] - ranks, mine_ref.shape[1]), F32)
    for low, step in zip(lows, steps):
        total = total + dot(low[...], step[:rows, :])
        decay = decay + step[rows:, :].astype(F32)
    mine_ref[:ranks, :] = jnp.where(odd, total[ranks:, :], total[:ranks, :])
    theirs_ref[:ranks, :] = jnp.where(odd, total[:ranks, :], total[ranks:, :]).astype(BF)
    mine_ref[ranks:, :] = decay
    theirs_ref[ranks:, :] = decay.astype(BF)


def step_call(ranks, lows, steps):
    rows = lows[0].shape[1]
    tall, chans = steps[0].shape
    width = min(512, chans)
    height = ranks + tall - rows
    return pl.pallas_call(
        functools.partial(step_kernel, ranks, len(lows)),
        grid=(chans // width,),
        in_specs=[whole(lows[0].shape)] * len(lows) + [columns(tall, width)] * len(steps),
        out_specs=[columns(height, width)] * 2,
        out_shape=[sds((height, chans), F32), sds((height, chans), BF)],
        compiler_params=params(16),
        name="step_products",
    )(*lows, *steps)


def rows_kernel(ranks, places, *refs):
    cuts, blocks, (out_ref, coef_ref) = refs[:places], refs[places:-2], refs[-2:]
    total = jnp.zeros((cuts[0].shape[0], out_ref.shape[1]), F32)
    for cut, block in zip(cuts, blocks):
        total = total + dot(cut[...], block[...])
    out_ref[...] = total[:ranks, :]
    coef_ref[...] = total[ranks : ranks + coef_ref.shape[0], :]


def rows_call(ranks, coef_rows, cuts, blocks):
    rows, chans = blocks[0].shape
    width = min(1024, chans)
    return pl.pallas_call(
        functools.partial(rows_kernel, ranks, len(cuts)),
        grid=(chans // width,),
        in_specs=[whole(cuts[0].shape)] * len(cuts) + [columns(rows, width)] * len(blocks),
        out_specs=[columns(ranks, width), columns(coef_rows, width)],
        out_shape=[sds((ranks, chans), F32), sds((coef_rows, chans), F32)],
        compiler_params=params(16),
        name="row_gradients",
    )(*cuts, *blocks)


def total_kernel(*refs):
    products, (step_ref, decay_ref) = refs[:-2], refs[-2:]
    ranks = step_ref.shape[0]
    for chunk in range(len(products) // 2):

        @pl.when(pl.program_id(0) == chunk)
        def _():
            mine, theirs = products[2 * chunk : 2 * chunk + 2]
            step_ref[...] = mine[:ranks, :] + theirs[:ranks, :].astype(F32)
            decay_ref[...] = mine[ranks:, :] + theirs[ranks:, :].astype(F32)


def total_call(ranks, products):
    height, width = products[0].shape
    chunks = len(products) // 2
    heights = (ranks, height - ranks)
    return pl.pallas_call(
        total_kernel,
        grid=(chunks,),
        in_specs=[whole((height, width))] * len(products),
        out_specs=[columns(tall, width) for tall in heights],
        out_shape=[sds((tall, chunks * width), F32) for tall in heights],
        compiler_params=params(12),
        name="step_gradients",
    )(*products)


def last_kernel(places, taps, *refs):
    (_, tail_ref, weight_ref) = refs[:3]
    late, refs = refs[3 : 3 + places], refs[3 + places :]
    (out_ref, conv_w, conv_b, step_b, skip, fix) = refs
    fix[...] = tail_ref[...]
    inside = lax.axis_index("ctx") < places - 1
    following = jnp.where(inside, late[places - 1][8:16, :].astype(F32), 0.0)
    for row in range(taps - 1):
        extra = jnp.zeros((1, fix.shape[1]), F32)
        for tap in range(row + 1):
            extra = extra + weight_ref[tap : tap + 1, :] * following[row - tap : row - tap + 1, :]
        at = 16 - (taps - 1) + row
        fix[at : at + 1, :] += extra
    out_ref[...] = fix[...].astype(BF)
    total = late[0][...].astype(F32)
    for part in late[1:]:
        total = total + part[...].astype(F32)
    conv_w[...] = total[:taps, :]
    conv_b[...] = total[taps : taps + 1, :]
    step_b[...] = total[taps + 1 : taps + 2, :]
    skip[...] = total[taps + 2 : taps + 3, :]


def last_call(main, tail, weight, late):
    rows, chans = main.shape
    taps = weight.shape[0]
    places = len(late)
    return pl.pallas_call(
        functools.partial(last_kernel, places, taps),
        grid=(1,),
        in_specs=[pl.BlockSpec(memory_space=pl.ANY), columns(16, chans), columns(taps, chans)]
        + [columns(16, chans)] * places,
        out_specs=[
            pl.BlockSpec((16, chans), lambda i: (rows // 16 - 1, i)),
            columns(taps, chans),
        ]
        + [columns(1, chans)] * 3,
        out_shape=[sds((rows, chans), BF), sds((taps, chans), F32)] + [sds((1, chans), F32)] * 3,
        scratch_shapes=[pltpu.VMEM((16, chans), F32)],
        input_output_aliases={0: 0},
        compiler_params=params(8),
        name="last_rows",
    )(main, tail, weight, *late)


def exchange(block, axis):
    return lax.all_to_all(block, axis, split_axis=0, concat_axis=0, tiled=True)


def swap(block, axis, mask):
    return lax.ppermute(block, axis, [(i, i ^ mask) for i in range(lax.axis_size(axis))])


tie = lax.optimization_barrier


def spread(block):
    return [block] + [swap(block, "ctx", mask) for mask in range(1, min(lax.axis_size("ctx"), 3))]


def spread_on(blocks):
    places = lax.axis_size("ctx")
    if places == 4:
        return blocks + [swap(blocks[2], "ctx", 1)]
    return blocks + [swap(blocks[0], "ctx", mask) for mask in range(3, places)]


def gather_near(block):
    return [block] + [swap(block, "ctx", mask) for mask in range(2, lax.axis_size("ctx"), 2)]


def chan_sum(part):
    mask, peers = 1, lax.axis_size("chan")
    while True:
        other = swap(part, "chan", mask)
        mask *= 2
        if mask == peers:
            return part, other
        part = (part.astype(F32) + other.astype(F32)).astype(BF)


def body(
    conv_input,
    gate_input,
    out_grad,
    conv_weight,
    conv_bias,
    proj_weight,
    step_weight,
    step_bias,
    decay_log,
    skip_gain,
):
    rows, chans = conv_input.shape
    taps = conv_weight.shape[0]
    low_rank = step_weight.shape[0]
    states = decay_log.shape[0]
    places = lax.axis_size("ctx")
    groups = group_rows(chans)
    decay = decay_log.reshape(states, -1, groups, 128).transpose(1, 0, 2, 3)
    skips = skip_gain.reshape(-1, groups, 128)
    conv_bias = conv_bias[None, :]
    step_bias = step_bias[None, :]
    skip_gain = skip_gain[None, :]

    chunks = decay.shape[0]
    rim = shift(conv_input[rows - (taps - 1) :], "ctx", 1)
    conv_out, part = conv_call(conv_input, rim, conv_weight, conv_bias, proj_weight)
    blocks = spread(conv_out)
    parts = chan_sum(part)
    coef = (parts[0][:, low_rank:].astype(F32) + parts[1][:, low_rank:].astype(F32)).astype(BF)
    coef = coef.astype(F32).reshape(-1)
    dt, dx, g, low, *messages = local_call(
        parts, coef, step_weight, step_bias, decay, conv_out, gate_input, out_grad, states, places
    )
    messages = [swap(message, "ctx", mask) for mask, message in enumerate(messages, 1)]
    messages, blocks, low = tie((messages, blocks, low))
    blocks = spread_on(blocks)
    ranks = low_rank // places
    lows = [
        lax.dynamic_slice_in_dim(
            jnp.transpose(low), ((lax.axis_index("ctx") ^ mask) // 2) * 2 * ranks, 2 * ranks
        )
        for mask in range(0, places, 2)
    ]
    lows = lows[:1] + [swap(rows_, "ctx", 2 * k) for k, rows_ in enumerate(lows[1:], 1)]
    previous, steps = [], []
    for chunk in range(chunks):
        message, grad_gate, scan_part, small, part = scan_call(
            places, chunk, coef, (dt, dx, g), decay, skips, conv_out, gate_input, out_grad,
            step_weight, skip_gain, messages, previous,
        )
        previous = [part, grad_gate, scan_part, small]
        if chunk == 0:
            previous, blocks = tie((previous, blocks))
        else:
            previous, steps[-1], lows = tie((previous, steps[-1], lows))
        steps.append(gather_near(message))
    part, grad_gate, scan_part, small = previous
    ranks = low_rank // places
    products = []
    backs = chan_sum(part)
    if chunks > 1:
        near, lows = tie((backs[0], lows))
        backs = (near, backs[1])
    for step in steps[:-1]:
        mine, theirs = step_call(ranks, lows, step)
        products += [mine, swap(theirs, "ctx", 1)]
    cuts = cut_call(places, backs)
    cuts = [cuts[0]] + [swap(cut, "ctx", mask) for mask, cut in enumerate(cuts[1:], 1)]
    main, tail, sums = conv_grad_call(
        places, low_rank, backs, proj_weight, scan_part, small, conv_input, rim, conv_weight,
        conv_bias,
    )
    sums, cuts, products, steps[-1], lows = tie((sums, cuts, products, steps[-1], lows))
    mine, theirs = step_call(ranks, lows, steps[-1])
    products += [mine, swap(theirs, "ctx", 1)]
    late = [sums] + [rotate(sums, "ctx", hop) for hop in range(1, places)]
    grad_proj, grad_coef = rows_call(ranks, 2 * states // places, cuts, blocks)
    products, grad_proj = tie((products, grad_proj))
    grad_step, decay_grad = total_call(ranks, products)
    late, grad_step = tie((late, grad_step))
    grad_input, conv_w, conv_b, step_b, skip = last_call(main, tail, conv_weight, late)
    return (
        grad_input,
        grad_gate,
        grad_proj,
        grad_coef,
        grad_step,
        conv_w,
        conv_b[0],
        step_b[0],
        decay_grad,
        skip[0],
    )


def solution(mesh):
    tokens, columns_, chan = P("ctx", "chan"), P(None, "chan"), P("chan")
    in_specs = (
        tokens, tokens, tokens, columns_, chan, columns_, columns_, chan, columns_, chan,
    )
    out_specs = (
        tokens, tokens, tokens, tokens, tokens, columns_, chan, chan, columns_, chan,
    )
    return jax.shard_map(body, mesh=mesh, in_specs=in_specs, out_specs=out_specs, check_vma=False)
```
